32 devices in a mesh: member: 2 (over y), gridy: 4 (over x, core), gridx: 4 (over z).
Axes of the slice: x: 2, y: 2, z: 4, core: 2. Of those that a mesh axis runs over, the one named last changes fastest.
Arguments:
- temp: float32 [4, 4, 256, 1024], P('member', None, 'gridy', 'gridx'), may hold values from -6 to 6
- salt: float32 [4, 4, 256, 1024], P('member', None, 'gridy', 'gridx'), may hold values from -6 to 6
- uvel: float32 [4, 4, 256, 1024], P('member', None, 'gridy', 'gridx'), may hold values from -3 to 3
- vvel: float32 [4, 4, 256, 1024], P('member', None, 'gridy', 'gridx'), may hold values from -3 to 3
- eta: float32 [4, 256, 1024], P('member', 'gridy', 'gridx'), may hold values from -6 to 6
- land_mask: int32 [256, 1024], P('gridy', 'gridx'), may hold values 0 or 1
- clone_source: int32 [4], P('member'), may hold values from 0 to 3
Outputs:
- new_temp: float32 [4, 4, 256, 1024], P('member', None, 'gridy', 'gridx')
- new_salt: float32 [4, 4, 256, 1024], P('member', None, 'gridy', 'gridx')
- new_uvel: float32 [4, 4, 256, 1024], P('member', None, 'gridy', 'gridx')
- new_vvel: float32 [4, 4, 256, 1024], P('member', None, 'gridy', 'gridx')
- new_eta: float32 [4, 256, 1024], P('member', 'gridy', 'gridx')
- overturning: float32 [4, 4, 256], P('member', None, 'gridy')
- clone_weight: float32 [4], P('member')
The draws below stay inside these ranges and needn't reach their ends.
All inputs are finite; a program needn't handle non-finite values. No bound on the sum of `land_mask` on one device may be relied on, other than what follows from the above.
Results may differ from the reference program's by a relative error of at most 0.0001.
Values sent between devices are 32-bit elements; how exact they have to be, the bound alone decides.
No kernel may reach another device: no remote copies, remote signals or barrier semaphores. Data moves between devices by JAX's collectives and lax.ppermute only.
A program may use at most 128 MiB of HBM per device.

```python
import jax
import jax.numpy as jnp
from jax import lax

LEV = 4
STEPS = 2
ITERS = 3
MEMBERS = 4
NY = 256
NX = 1024


def plant(drawn, rng, least, largest):
    longest = drawn.shape.index(max(drawn.shape))
    spots = []
    for shift in (0, 1):
        where = [jax.random.randint(jax.random.fold_in(rng, axis), (), 0, length) for axis, length in enumerate(drawn.shape)]
        where[longest] = (where[longest] + shift) % drawn.shape[longest]
        spots.append(tuple(where))
    return drawn.at[spots[0]].set(least).at[spots[1]].set(largest)


def block_levels(own_key, dims, cuts, smallest, largest):
    def one(position, shards_of):
        heights = jax.random.uniform(jax.random.fold_in(jax.random.fold_in(own_key, 6), position), (shards_of,), jnp.float32, smallest / len(cuts), largest / len(cuts))
        return jnp.repeat(jnp.exp(heights), dims[position] // shards_of).reshape((-1,) + (1,) * (len(dims) - position - 1))

    factor_of = one(*cuts[0])
    for cut in cuts[1:]:
        factor_of = factor_of * one(*cut)
    return factor_of


def noise(rng, extent, scale, limit, shards=(), held_as=jnp.bfloat16):
    result = scale * jax.random.normal(rng, extent, jnp.float32)
    if shards:
        result = result * block_levels(rng, extent, shards, -0.22, 0.18)
    return jnp.clip(result, -limit, limit).astype(held_as)


def setup_inputs(seed: int = 0) -> dict:
    seeds = jax.random.split(jax.random.key(seed), 8)
    temp = noise(seeds[0], (MEMBERS, LEV, NY, NX), 1.0, 6.0, ((0, 2), (2, 4), (3, 4)), jnp.float32)
    salt = noise(seeds[1], (MEMBERS, LEV, NY, NX), 1.0, 6.0, ((0, 2), (2, 4), (3, 4)), jnp.float32)
    uvel = noise(seeds[2], (MEMBERS, LEV, NY, NX), 0.5, 3.0, ((0, 2), (2, 4), (3, 4)), jnp.float32)
    vvel = noise(seeds[3], (MEMBERS, LEV, NY, NX), 0.5, 3.0, ((0, 2), (2, 4), (3, 4)), jnp.float32)
    eta = noise(seeds[4], (MEMBERS, NY, NX), 1.0, 6.0, ((0, 2), (1, 4), (2, 4)), jnp.float32)
    land_mask = plant((jax.random.randint(seeds[5], (NY, NX), 0, 4) < 3).astype(jnp.int32), jax.random.fold_in(seeds[5], 1), 0, 1)
    clone_source = plant(jax.random.randint(seeds[6], (MEMBERS,), 0, MEMBERS), jax.random.fold_in(seeds[6], 1), 0, MEMBERS - 1).astype(jnp.int32)
    return dict(temp=temp, salt=salt, uvel=uvel, vvel=vvel, eta=eta, land_mask=land_mask, clone_source=clone_source)


ALPHA_T = 0.8
BETA_S = 0.6
PRESS_K = 0.25
STEP_DT = 0.1
KAPPA = 0.1
VISCOSITY = 0.1
DRAG_K = 0.05
CORI_K = 1.0
SURF_C = 4.0
DIV_K = 0.5
GRAV_K = 0.5

def east(field):
    return jnp.roll(field, -1, axis=-1)

def west(field):
    return jnp.roll(field, 1, axis=-1)

def north(field):
    zero_row = jnp.zeros_like(field[..., :1, :])
    return jnp.concatenate([field[..., 1:, :], zero_row], axis=-2)

def south(field):
    zero_row = jnp.zeros_like(field[..., :1, :])
    return jnp.concatenate([zero_row, field[..., :-1, :]], axis=-2)

def laplace(field):
    return east(field) + west(field) + north(field) + south(field) - 4.0 * field

def pressure(temp, salt):
    return PRESS_K * jnp.cumsum(BETA_S * salt - ALPHA_T * temp, axis=0)

def surface_apply(field):
    return (1.0 + 4.0 * SURF_C) * field - SURF_C * (east(field) + west(field) + north(field) + south(field))

def surface_solve(rhs):
    solution = jnp.zeros_like(rhs)
    residual = rhs
    direction = rhs
    norm_now = jnp.sum(residual * residual)
    for count in range(ITERS):
        image = surface_apply(direction)
        alpha = norm_now / jnp.sum(direction * image)
        solution = solution + alpha * direction
        residual = residual - alpha * image
        norm_next = jnp.sum(residual * residual)
        direction = residual + norm_next / norm_now * direction
        norm_now = norm_next
    return solution

def member_window(fields, ocean, coriolis):
    temp, salt, uvel, vvel, eta = fields
    for count in range(STEPS):
        press = pressure(temp, salt)
        temp_next = ocean * (temp - STEP_DT * 0.5 * (uvel * (east(temp) - west(temp)) + vvel * (north(temp) - south(temp))) + KAPPA * laplace(temp))
        salt_next = ocean * (salt - STEP_DT * 0.5 * (uvel * (east(salt) - west(salt)) + vvel * (north(salt) - south(salt))) + KAPPA * laplace(salt))
        ustar = ocean * (uvel + STEP_DT * (coriolis * vvel - 0.5 * (east(press) - west(press)) - DRAG_K * uvel) + VISCOSITY * laplace(uvel))
        vstar = ocean * (vvel + STEP_DT * (-coriolis * uvel - 0.5 * (north(press) - south(press)) - DRAG_K * vvel) + VISCOSITY * laplace(vvel))
        trans_u = lax.optimization_barrier(jnp.sum(ustar, axis=0))
        trans_v = lax.optimization_barrier(jnp.sum(vstar, axis=0))
        rhs = eta - DIV_K * 0.5 * (east(trans_u) - west(trans_u) + (north(trans_v) - south(trans_v)))
        eta = surface_solve(rhs)
        uvel = ocean * (ustar - GRAV_K * 0.5 * (east(eta) - west(eta)))
        vvel = ocean * (vstar - GRAV_K * 0.5 * (north(eta) - south(eta)))
        temp = temp_next
        salt = salt_next
    zonal = lax.optimization_barrier(jnp.sum(vvel, axis=2))
    overturn = jnp.cumsum(zonal, axis=0) / jnp.sqrt(jnp.float32(NX))
    latitude = (jnp.arange(NY).astype(jnp.float32) + 0.5) / NY
    score = jnp.sum(overturn * latitude[None, :]) / jnp.sqrt(jnp.float32(LEV * NY))
    return (temp, salt, uvel, vvel, eta, overturn, score)

def reference(temp, salt, uvel, vvel, eta, land_mask, clone_source):
    ocean = land_mask.astype(jnp.float32)
    rows = jnp.arange(NY).astype(jnp.float32) + 0.5
    coriolis = (CORI_K * (2.0 * rows / NY - 1.0))[:, None]
    results = lax.map(lambda fields: member_window(fields, ocean, coriolis), (temp, salt, uvel, vvel, eta))
    temp_f, salt_f, uvel_f, vvel_f, eta_f, overturn, score = results
    new_temp = jnp.take(temp_f, clone_source, axis=0)
    new_salt = jnp.take(salt_f, clone_source, axis=0)
    new_uvel = jnp.take(uvel_f, clone_source, axis=0)
    new_vvel = jnp.take(vvel_f, clone_source, axis=0)
    new_eta = jnp.take(eta_f, clone_source, axis=0)
    clone_weight = jnp.take(score, clone_source, axis=0) - jnp.mean(score)
    return (new_temp, new_salt, new_uvel, new_vvel, new_eta, overturn, clone_weight)
```

```python
import functools

import jax
import jax.numpy as jnp
from jax import lax
from jax.experimental import pallas as pl
from jax.experimental.pallas import tpu as pltpu
from jax.sharding import PartitionSpec as P

STEPS = 2
ITERS = 3

ALPHA_T = 0.8
BETA_S = 0.6
PRESS_K = 0.25
STEP_DT = 0.1
KAPPA = 0.1
VISCOSITY = 0.1
DRAG_K = 0.05
CORI_K = 1.0
SURF_C = 4.0
DIV_K = 0.5
GRAV_K = 0.5

ADV = STEP_DT * 0.5
DIV = DIV_K * 0.5
GRAV = GRAV_K * 0.5

WIDE = 10
TOP = 24
CHUNK = 16
LANE = 128
PER_GROUP = 11
PAIRS = [(a, b) for a in range(4) for b in range(a, 4)]
SUMS = 6 + 6 * len(PAIRS)
SUM_ROWS = -(-SUMS // 8) * 8
SUM_LANES = SUM_ROWS // 8
VMEM_LIMIT = 56 * 1024 * 1024


def rim_place(plane):
    group, place = divmod(plane, PER_GROUP)
    if place < 6:
        return group, 0, (2 * place + 1) * WIDE
    return group, 1, (2 * (place - 6) + 2) * WIDE


def groups_of(planes):
    return -(-planes // PER_GROUP)


def lanes_like(shape):
    return lax.broadcasted_iota(jnp.int32, shape, len(shape) - 1)


def load_plane(fields, m, plane, levels):
    if plane < 4 * levels:
        return fields[plane // levels][m, plane % levels]
    if plane == 4 * levels:
        return fields[4][m]
    return fields[5][...].astype(jnp.float32)


def pack_kernel(levels, temp, salt, uvel, vvel, eta, mask, to_west, to_east, to_north, to_south, *corners):
    members, _, rows, cols = temp.shape
    planes = 4 * levels + 2
    fields = (temp, salt, uvel, vvel, eta, mask)
    lane = lanes_like((rows, LANE))
    for m in range(members):
        west_parts = [None] * groups_of(planes)
        east_parts = [None] * groups_of(planes)
        for plane in range(planes):
            value = load_plane(fields, m, plane, levels)
            group, _, start = rim_place(plane)
            both = jnp.where(lane < WIDE, value[:, :LANE], value[:, cols - LANE :])
            both = pltpu.roll(both, start, 1)
            is_west = (lane >= start) & (lane < start + WIDE)
            is_east = (lane >= start - WIDE) & (lane < start)
            zero = jnp.zeros_like(both)
            west_parts[group] = jnp.where(is_west, both, zero if west_parts[group] is None else west_parts[group])
            east_parts[group] = jnp.where(is_east, both, zero if east_parts[group] is None else east_parts[group])
            to_south[m, plane * WIDE : (plane + 1) * WIDE, :] = value[:WIDE]
            to_north[m, plane * WIDE : (plane + 1) * WIDE, :] = value[rows - WIDE :]
        for group in range(groups_of(planes)):
            where = slice(group * LANE, (group + 1) * LANE)
            to_west[m, :, where] = west_parts[group]
            to_east[m, :, where] = east_parts[group]
            corners[0][m, :, where] = west_parts[group][:CHUNK]
            corners[1][m, :, where] = west_parts[group][rows - CHUNK :]
            corners[2][m, :, where] = east_parts[group][:CHUNK]
            corners[3][m, :, where] = east_parts[group][rows - CHUNK :]


def whole(count):
    return [pl.BlockSpec(memory_space=pltpu.VMEM)] * count


def pack_rims(temp, salt, uvel, vvel, eta, mask):
    members, levels, rows, cols = temp.shape
    planes = 4 * levels + 2
    wide = groups_of(planes) * LANE
    row_pack = -(-planes * WIDE // 8) * 8
    side = jax.ShapeDtypeStruct((members, rows, wide), jnp.float32)
    line = jax.ShapeDtypeStruct((members, row_pack, cols), jnp.float32)
    corner = jax.ShapeDtypeStruct((members, CHUNK, wide), jnp.float32)
    return pl.pallas_call(
        functools.partial(pack_kernel, levels),
        out_shape=(side, side, line, line, corner, corner, corner, corner),
        in_specs=whole(6),
        out_specs=tuple(whole(8)),
        compiler_params=pltpu.CompilerParams(vmem_limit_bytes=VMEM_LIMIT),
        name="pack_rims",
    )(temp, salt, uvel, vvel, eta, mask)


def east_west(value):
    width = value.shape[-1]
    return pltpu.roll(value, width - 1, 1), pltpu.roll(value, 1, 1)


def chunks(first, last):
    return [(a, min(a + CHUNK, last)) for a in range(first, last, CHUNK)]


def assemble(ext, fields, rims, m, levels):
    from_east, from_west, from_north, from_south, ne, nw, se, sw = rims
    planes = 4 * levels + 2
    rows, cols = fields[5].shape
    bands = [(TOP - CHUNK, se, sw, 0, CHUNK)]
    bands += [(TOP + a, from_east, from_west, a, CHUNK) for a in range(0, rows, CHUNK)]
    bands += [(TOP + rows, ne, nw, 0, CHUNK)]
    for group in range(groups_of(planes)):
        where = slice(group * LANE, (group + 1) * LANE)
        for at, east_ref, west_ref, start, size in bands:
            east = east_ref[m, start : start + size, where]
            west = west_ref[m, start : start + size, where]
            slot = lanes_like(east.shape) // WIDE
            odd = (slot & 1) == 1
            joined = (jnp.where(odd, east, west), jnp.where(odd, west, east))
            for plane in range(group * PER_GROUP, min((group + 1) * PER_GROUP, planes)):
                _, kind, offset = rim_place(plane)
                ext[plane, at : at + size, cols : cols + LANE] = pltpu.roll(joined[kind], LANE - offset, 1)
    for plane in range(planes):
        ext[plane, TOP : TOP + rows, :cols] = load_plane(fields, m, plane, levels)
        ext[plane, TOP - WIDE : TOP, :cols] = from_south[m, plane * WIDE : (plane + 1) * WIDE, :]
        ext[plane, TOP + rows : TOP + rows + WIDE, :cols] = from_north[m, plane * WIDE : (plane + 1) * WIDE, :]


def fill_rows(cor, inside, first_row, total_rows):
    shape = (CHUNK, cor.shape[1])
    for a in range(0, cor.shape[0], CHUNK):
        row = first_row + (a - TOP) + lax.broadcasted_iota(jnp.int32, shape, 0)
        latitude = row.astype(jnp.float32) + 0.5
        cor[a : a + CHUNK, :] = CORI_K * (2.0 * latitude / total_rows - 1.0)
        inside[a : a + CHUNK, :] = jnp.where((row >= 0) & (row < total_rows), 1.0, 0.0)


class Planes:
    def __init__(self, ref, names):
        self.ref, self.names = ref, names

    def get(self, name, a, b):
        return self.ref[self.names.index(name), a:b, :]

    def put(self, name, a, b, value):
        self.ref[self.names.index(name), a:b, :] = value

    def sides(self, name, a, b):
        here = self.get(name, a, b)
        east, west = east_west(here)
        return here, east, west, self.get(name, a + 1, b + 1), self.get(name, a - 1, b - 1)

    def lap(self, name, a, b):
        here, east, west, north, south = self.sides(name, a, b)
        return east + west + north + south - 4.0 * here


def momentum(ocean, cor, u, v, pu, pv, lap_u, lap_v):
    new_u = ocean * (u + STEP_DT * (cor * v - 0.5 * pu - DRAG_K * u) + VISCOSITY * lap_u)
    new_v = ocean * (v + STEP_DT * (-cor * u - 0.5 * pv - DRAG_K * v) + VISCOSITY * lap_v)
    return new_u, new_v


def surface_start(ext, work, cor, inside, levels, rows):
    ocean_at = 4 * levels + 1
    low, high = TOP - CHUNK, TOP + rows + CHUNK
    near_low, near_high = TOP - 8, TOP + rows + 8
    for a, b in chunks(low, high):
        su = sv = sp = None
        for l in range(levels):
            dens = BETA_S * ext[levels + l, a:b, :] - ALPHA_T * ext[l, a:b, :]
            work.put("d%d" % l, a, b, dens)
            u, v = ext[2 * levels + l, a:b, :], ext[3 * levels + l, a:b, :]
            weighted = (PRESS_K * (levels - l)) * dens
            su, sv, sp = (u, v, weighted) if l == 0 else (su + u, sv + v, sp + weighted)
        work.put("su", a, b, su)
        work.put("sv", a, b, sv)
        work.put("sp", a, b, sp)
    for a, b in chunks(near_low, near_high):
        carried = None
        for l in range(levels):
            _, east, west, north, south = work.sides("d%d" % l, a, b)
            term = ext[2 * levels + l, a:b, :] * (east - west) + ext[3 * levels + l, a:b, :] * (north - south)
            term = (PRESS_K * (levels - l)) * term
            carried = term if l == 0 else carried + term
        here, east, west, north, south = work.sides("sp", a, b)
        lap = east + west + north + south - 4.0 * here
        work.put("q", a, b, ext[ocean_at, a:b, :] * (here - ADV * carried + KAPPA * lap))
    for a, b in chunks(low, high):
        ocean = ext[ocean_at, a:b, :]
        _, pe, pw, pn, ps = work.sides("sp", a, b)
        new_u, new_v = momentum(
            ocean, cor[a:b, :], work.get("su", a, b), work.get("sv", a, b),
            pe - pw, pn - ps, work.lap("su", a, b), work.lap("sv", a, b),
        )
        work.put("tu", a, b, new_u)
        work.put("tv", a, b, new_v)
    for a, b in chunks(near_low, near_high):
        work.put("v0", a, b, inside[a:b, :] * (ext[4 * levels, a:b, :] - divergence(work, "tu", "tv", a, b)))


def divergence(work, u_name, v_name, a, b):
    east, west = east_west(work.get(u_name, a, b))
    return DIV * (east - west + (work.get(v_name, a + 1, b + 1) - work.get(v_name, a - 1, b - 1)))


def around(work, name, a, b):
    _, east, west, north, south = work.sides(name, a, b)
    return east + west + north + south


def powers(work, inside, first, second, third, low, high):
    for a, b in chunks(low, high):
        work.put(second, a, b, inside[a:b, :] * around(work, first, a, b))
    for a, b in chunks(low, high):
        work.put(third, a, b, inside[a:b, :] * (around(work, second, a, b) - 4.0 * work.get(first, a, b)))


def surface_next(work, ext, cor, inside, levels, rows, u_name, v_name, eta_name, with_press, out_name):
    low, high = TOP - 8, TOP + rows + 8
    ocean_at = 4 * levels + 1
    for a, b in chunks(low, high):
        if with_press:
            _, pe, pw, pn, ps = work.sides("q", a, b)
            pu, pv = pe - pw, pn - ps
        else:
            pu = pv = 0.0
        new_u, new_v = momentum(
            ext[ocean_at, a:b, :], cor[a:b, :], work.get(u_name, a, b), work.get(v_name, a, b),
            pu, pv, work.lap(u_name, a, b), work.lap(v_name, a, b),
        )
        work.put("t2u", a, b, new_u)
        work.put("t2v", a, b, new_v)
    for a, b in chunks(low, high):
        div = divergence(work, "t2u", "t2v", a, b)
        value = -div if eta_name is None else work.get(eta_name, a, b) - div
        work.put(out_name, a, b, inside[a:b, :] * value)


def surface_push(work, ext, levels, rows, eta_name, u_name, v_name, base):
    ocean_at = 4 * levels + 1
    for a, b in chunks(TOP - 8, TOP + rows + 8):
        ocean = ext[ocean_at, a:b, :]
        _, east, west, north, south = work.sides(eta_name, a, b)
        push_u = -(levels * GRAV) * ocean * (east - west)
        push_v = -(levels * GRAV) * ocean * (north - south)
        if base:
            push_u, push_v = work.get("tu", a, b) + push_u, work.get("tv", a, b) + push_v
        work.put(u_name, a, b, push_u)
        work.put(v_name, a, b, push_v)


SUM_NAMES = ["d0", "d1", "d2", "d3", "su", "sv", "sp", "q", "tu", "tv", "v0", "v1", "v2", "v3", "pu", "pv", "t2u", "t2v"]
SUM_NAMES += ["w%d_%d" % (i, k) for i in range(4) for k in range(4)]


def sums_kernel(levels, total_rows, place, *refs):
    fields, rims, out, scratch = refs[:6], refs[6:14], refs[14], refs[15:]
    ext, planes, cor, inside, red = scratch
    members = fields[0].shape[0]
    rows, cols = fields[5].shape
    work = Planes(planes, SUM_NAMES)
    fill_rows(cor, inside, place[0], total_rows)
    red[...] = jnp.zeros_like(red)

    def one(m, carry):
        assemble(ext, fields, rims, m, levels)
        surface_start(ext, work, cor, inside, levels, rows)
        low, high = TOP - 8, TOP + rows + 8
        powers(work, inside, "v0", "v1", "v2", low, high)
        for a, b in chunks(TOP, TOP + rows):
            work.put("v3", a, b, around(work, "v2", a, b))
        surface_next(work, ext, cor, inside, levels, rows, "tu", "tv", None, True, "w0_0")
        for k in range(1, 4):
            name = "v%d" % (k - 1)
            surface_push(work, ext, levels, rows, name, "pu", "pv", False)
            surface_next(work, ext, cor, inside, levels, rows, "pu", "pv", name, False, "w0_%d" % k)
        for k in range(4):
            powers(work, inside, "w0_%d" % k, "w1_%d" % k, "w2_%d" % k, low, high)
            for a, b in chunks(TOP, TOP + rows):
                work.put("w3_%d" % k, a, b, around(work, "w2_%d" % k, a, b))

        def put_sum(at, first, second):
            total = None
            for a, b in chunks(TOP, TOP + rows):
                x = planes[SUM_NAMES.index(first), a:b, :cols]
                y = planes[SUM_NAMES.index(second), a:b, :cols]
                total = x * y if total is None else total + x * y
            line = jnp.sum(total, axis=0, keepdims=True)
            folded = line[:, :LANE]
            for c in range(LANE, cols, LANE):
                folded = folded + line[:, c : c + LANE]
            red[m, at : at + 1, :] = folded

        for i in range(6):
            put_sum(i, "v%d" % (i // 2), "v%d" % (i - i // 2))
            for p, (a, b) in enumerate(PAIRS):
                put_sum(6 + i * len(PAIRS) + p, "w%d_%d" % (i // 2, a), "w%d_%d" % (i - i // 2, b))
        return carry

    lax.fori_loop(0, members, one, 0)
    lane = lanes_like((8, LANE))
    tile = jnp.zeros((8, LANE), jnp.float32)
    for m in range(members):
        total = jnp.sum(red[m], axis=1, keepdims=True)
        for q in range(SUM_LANES):
            tile = jnp.where(lane == m * SUM_LANES + q, total[8 * q : 8 * q + 8], tile)
    out[...] = tile


def plane_shape(rows, cols):
    return (2 * TOP + rows, cols + LANE)


def local_sums(place, fields, rims, total_rows):
    members, levels, rows, cols = fields[0].shape
    shape = plane_shape(rows, cols)
    return pl.pallas_call(
        functools.partial(sums_kernel, levels, total_rows),
        out_shape=jax.ShapeDtypeStruct((8, LANE), jnp.float32),
        in_specs=[pl.BlockSpec(memory_space=pltpu.SMEM)] + whole(14),
        out_specs=pl.BlockSpec(memory_space=pltpu.VMEM),
        scratch_shapes=[
            pltpu.VMEM((4 * levels + 2,) + shape, jnp.float32),
            pltpu.VMEM((len(SUM_NAMES),) + shape, jnp.float32),
            pltpu.VMEM(shape, jnp.float32),
            pltpu.VMEM(shape, jnp.float32),
            pltpu.VMEM((members, SUM_ROWS, LANE), jnp.float32),
        ],
        compiler_params=pltpu.CompilerParams(vmem_limit_bytes=VMEM_LIMIT),
        name="local_sums",
    )(place, *fields, *rims)


def krylov(moment):
    n00, n01, n11, n12, n22, x22 = moment
    n02 = n11 - 4.0 * n00
    main, near = 1.0 + 4.0 * SURF_C, SURF_C
    g00 = main * n00 - near * n01
    g01 = main * n01 - near * n11
    g02 = main * n02 - near * n12
    g11 = main * n11 - near * (n12 + 4.0 * n01)
    g12 = main * n12 - near * (n22 + 4.0 * n02)
    g22 = main * n22 - near * x22
    l1, l2 = g01 / g00, g02 / g00
    d1 = g11 - l1 * g01
    d1 = jnp.where(d1 > 3e-7 * g11, d1, jnp.inf)
    e = g12 - l1 * g02
    l12 = e / d1
    d2 = g22 - l2 * g02 - l12 * e
    d2 = jnp.where(d2 > 3e-7 * g22, d2, jnp.inf)
    z0 = n00
    z1 = n01 - l1 * z0
    z2 = n02 - l2 * z0 - l12 * z1
    y2 = z2 / d2
    y1 = z1 / d1 - l12 * y2
    y0 = z0 / g00 - l1 * y1 - l2 * y2
    return [y0, y1, y2]


def weights(read):
    first = krylov([read(i) for i in range(6)])
    lifted = [None] + first
    second = []
    for i in range(6):
        total = None
        for p, (a, b) in enumerate(PAIRS):
            term = read(6 + i * len(PAIRS) + p)
            for k in (a, b):
                if k:
                    term = term * lifted[k]
            if a != b:
                term = 2.0 * term
            total = term if total is None else total + term
        second.append(total)
    return first, krylov(second)


RUN_NAMES = ["d0", "d1", "d2", "d3", "su", "sv", "sp", "q", "tu", "tv", "v0", "v1", "v2", "pu", "pv", "t2u", "t2v"]
RUN_NAMES += ["eta1", "w0", "w1", "w2", "eta2", "p", "p2"]


def combine(work, factors, names, out_name, a, b):
    total = None
    for factor, name in zip(factors, names):
        term = factor * work.get(name, a, b)
        total = term if total is None else total + term
    work.put(out_name, a, b, total)


def advance_kernel(levels, total_rows, place, sums, *refs):
    fields, rims = refs[:6], refs[6:14]
    new_temp, new_salt, new_uvel, new_vvel, new_eta, zonal = refs[14:20]
    ext, planes, after, cor, inside = refs[20:]
    members = fields[0].shape[0]
    rows, cols = fields[5].shape
    ocean_at = 4 * levels + 1
    work = Planes(planes, RUN_NAMES)
    fill_rows(cor, inside, place[0], total_rows)
    zonal[...] = jnp.zeros_like(zonal)
    low, high = TOP - 8, TOP + rows + 8

    def one(m, carry):
        assemble(ext, fields, rims, m, levels)

        def read(i):
            return jnp.full((1, 1), sums[i % 8, m * SUM_LANES + i // 8], jnp.float32)

        first, second = weights(read)
        surface_start(ext, work, cor, inside, levels, rows)
        powers(work, inside, "v0", "v1", "v2", low, high)
        for a, b in chunks(low, high):
            combine(work, first, ("v0", "v1", "v2"), "eta1", a, b)
        surface_push(work, ext, levels, rows, "eta1", "pu", "pv", True)
        surface_next(work, ext, cor, inside, levels, rows, "pu", "pv", "eta1", True, "w0")
        powers(work, inside, "w0", "w1", "w2", low, high)
        for a, b in chunks(low, high):
            combine(work, second, ("w0", "w1", "w2"), "eta2", a, b)
        for a, b in chunks(TOP, TOP + rows):
            new_eta[m, a - TOP : b - TOP, :] = work.get("eta2", a, b)[:, :cols]
        for a, b in chunks(low, high):
            ocean = ext[ocean_at, a:b, :]
            for name, to_u, to_v in (("eta1", "pu", "pv"), ("eta2", "t2u", "t2v")):
                _, east, west, north, south = work.sides(name, a, b)
                work.put(to_u, a, b, GRAV * ocean * (east - west))
                work.put(to_v, a, b, GRAV * ocean * (north - south))
        for a, b in chunks(TOP - CHUNK, TOP + rows + CHUNK):
            work.put("p", a, b, jnp.zeros((b - a, cols + LANE), jnp.float32))
            work.put("p2", a, b, jnp.zeros((b - a, cols + LANE), jnp.float32))

        def sides(ref, at, a, b):
            here = ref[at, a:b, :]
            east, west = east_west(here)
            north, south = ref[at, a + 1 : b + 1, :], ref[at, a - 1 : b - 1, :]
            return here, east - west, north - south, east + west + north + south - 4.0 * here

        def step(ref, l, press, a, b):
            ocean = ext[ocean_at, a:b, :]
            temp, temp_x, temp_y, temp_l = sides(ref, l, a, b)
            salt, salt_x, salt_y, salt_l = sides(ref, levels + l, a, b)
            u, _, _, u_l = sides(ref, 2 * levels + l, a, b)
            v, _, _, v_l = sides(ref, 3 * levels + l, a, b)
            _, pe, pw, pn, ps = work.sides(press, a, b)
            temp = ocean * (temp - ADV * (u * temp_x + v * temp_y) + KAPPA * temp_l)
            salt = ocean * (salt - ADV * (u * salt_x + v * salt_y) + KAPPA * salt_l)
            u, v = momentum(ocean, cor[a:b, :], u, v, pe - pw, pn - ps, u_l, v_l)
            return temp, salt, u, v

        def add_press(ref, l, press, a, b):
            dens = BETA_S * ref[levels + l, a:b, :] - ALPHA_T * ref[l, a:b, :]
            work.put(press, a, b, work.get(press, a, b) + PRESS_K * dens)

        def level(l, carry):
            for a, b in chunks(TOP - CHUNK, TOP + rows + CHUNK):
                add_press(ext, l, "p", a, b)
            for a, b in chunks(low, high):
                temp, salt, u, v = step(ext, l, "p", a, b)
                after[l, a:b, :] = temp
                after[levels + l, a:b, :] = salt
                after[2 * levels + l, a:b, :] = u - work.get("pu", a, b)
                after[3 * levels + l, a:b, :] = v - work.get("pv", a, b)
            for a, b in chunks(low, high):
                add_press(after, l, "p2", a, b)
            for a, b in chunks(TOP, TOP + rows):
                temp, salt, u, v = step(after, l, "p2", a, b)
                u = u - work.get("t2u", a, b)
                v = v - work.get("t2v", a, b)
                here = slice(a - TOP, b - TOP)
                new_temp[m, l, here, :] = temp[:, :cols]
                new_salt[m, l, here, :] = salt[:, :cols]
                new_uvel[m, l, here, :] = u[:, :cols]
                new_vvel[m, l, here, :] = v[:, :cols]
                total = jnp.sum(v[:, :cols], axis=1, keepdims=True)
                lane = lanes_like((b - a, LANE))
                zonal[here, :] = jnp.where(lane == m * levels + l, total, zonal[here, :])
            return carry

        lax.fori_loop(0, levels, level, 0)
        return carry

    lax.fori_loop(0, members, one, 0)


def advance(place, sums, fields, rims, total_rows):
    members, levels, rows, cols = fields[0].shape
    shape = plane_shape(rows, cols)
    volume = jax.ShapeDtypeStruct((members, levels, rows, cols), jnp.float32)
    surface = jax.ShapeDtypeStruct((members, rows, cols), jnp.float32)
    return pl.pallas_call(
        functools.partial(advance_kernel, levels, total_rows),
        out_shape=(volume,) * 4 + (surface, jax.ShapeDtypeStruct((rows, LANE), jnp.float32)),
        in_specs=[pl.BlockSpec(memory_space=pltpu.SMEM)] * 2 + whole(14),
        out_specs=tuple(whole(6)),
        scratch_shapes=[
            pltpu.VMEM((4 * levels + 2,) + shape, jnp.float32),
            pltpu.VMEM((len(RUN_NAMES),) + shape, jnp.float32),
            pltpu.VMEM((4 * levels,) + shape, jnp.float32),
            pltpu.VMEM(shape, jnp.float32),
            pltpu.VMEM(shape, jnp.float32),
        ],
        compiler_params=pltpu.CompilerParams(vmem_limit_bytes=VMEM_LIMIT),
        name="advance",
    )(place, sums, *fields, *rims)


def exchange_rims(packed):
    to_west, to_east, to_north, to_south, west_low, west_high, east_low, east_high = packed
    count_y, count_x = lax.axis_size("gridy"), lax.axis_size("gridx")

    def move(value, north, east):
        pairs = []
        for j in range(count_y):
            for i in range(count_x):
                if 0 <= j + north < count_y:
                    pairs.append((j * count_x + i, (j + north) * count_x + (i + east) % count_x))
        return lax.ppermute(value, ("gridy", "gridx"), pairs)

    return (
        move(to_west, 0, -1),
        move(to_east, 0, 1),
        move(to_south, -1, 0),
        move(to_north, 1, 0),
        move(west_low, -1, -1),
        move(east_low, -1, 1),
        move(west_high, 1, -1),
        move(east_high, 1, 1),
    )


def total_over(value, axis):
    count = lax.axis_size(axis)
    if count <= 4:
        moved = [
            lax.ppermute(value, axis, [(i, (i + shift) % count) for i in range(count)]) for shift in range(1, count)
        ]
        for part in moved:
            value = value + part
        return value
    step = 1
    while step < count:
        if count % (2 * step):
            return lax.psum(value, axis)
        value = value + lax.ppermute(value, axis, [(i, i ^ step) for i in range(count)])
        step *= 2
    return value


def swap_members(value):
    return lax.all_gather(value, "member", axis=0, tiled=True)


def shards(temp, salt, uvel, vvel, eta, land_mask, clone_source):
    members, levels, rows, cols = temp.shape
    tile_row = lax.axis_index("gridy")
    total_rows = rows * lax.axis_size("gridy")
    total_cols = cols * lax.axis_size("gridx")
    place = (tile_row * rows).astype(jnp.int32).reshape(1)
    fields = (temp, salt, uvel, vvel, eta, land_mask)
    rims = exchange_rims(pack_rims(*fields))
    sums = local_sums(place, fields, rims, total_rows)
    sums = total_over(total_over(sums, "gridx"), "gridy")
    *state, zonal = advance(place, sums, fields, rims, total_rows)
    side = lax.axis_index("member")
    count = lax.axis_size("member")
    every = [lax.all_gather(value, "member", axis=0, tiled=True) for value in state]
    picked = [jnp.take(value, clone_source, axis=0) for value in every]

    zonal_whole = total_over(zonal, "gridx")[:, : members * levels].reshape(rows, members, levels)
    zonal_whole = jnp.transpose(zonal_whole, (1, 2, 0))
    zonal_scale = 1.0 / jnp.sqrt(jnp.float32(total_cols))
    score_scale = 1.0 / jnp.sqrt(jnp.float32(levels * total_rows))
    latitude = (tile_row * rows + jnp.arange(rows, dtype=jnp.int32)).astype(jnp.float32) + 0.5
    overturn = jnp.cumsum(zonal_whole, axis=1) * zonal_scale
    score = total_over(jnp.sum(overturn * (latitude / total_rows), axis=(1, 2)) * score_scale, "gridy")
    every_score = lax.all_gather(score, "member", axis=0, tiled=True)
    clone_weight = jnp.take(every_score, clone_source, axis=0) - jnp.mean(every_score)
    return (*picked, overturn, clone_weight)


def solution(mesh):
    volume = P("member", None, "gridy", "gridx")
    in_specs = (volume,) * 4 + (P("member", "gridy", "gridx"), P("gridy", "gridx"), P("member"))
    out_specs = (volume,) * 4 + (P("member", "gridy", "gridx"), P("member", None, "gridy"), P("member"))
    return jax.shard_map(shards, mesh=mesh, in_specs=in_specs, out_specs=out_specs, check_vma=False)
```

```python
import functools

import jax
import jax.numpy as jnp
from jax import lax
from jax.experimental import pallas as pl
from jax.experimental.pallas import tpu as pltpu
from jax.sharding import PartitionSpec as P

STEPS = 2
ITERS = 3

ALPHA_T = 0.8
BETA_S = 0.6
PRESS_K = 0.25
STEP_DT = 0.1
KAPPA = 0.1
VISCOSITY = 0.1
DRAG_K = 0.05
CORI_K = 1.0
SURF_C = 4.0
DIV_K = 0.5
GRAV_K = 0.5

ADV = STEP_DT * 0.5
DIV = DIV_K * 0.5
GRAV = GRAV_K * 0.5

WIDE = 10
TOP = 24
CHUNK = 16
LANE = 128
PER_GROUP = 11
PAIRS = [(a, b) for a in range(4) for b in range(a, 4)]
SUMS = 6 + 6 * len(PAIRS)
SUM_ROWS = -(-SUMS // 8) * 8
SUM_LANES = SUM_ROWS // 8
VMEM_LIMIT = 56 * 1024 * 1024


def rim_place(plane):
    group, place = divmod(plane, PER_GROUP)
    if place < 6:
        return group, 0, (2 * place + 1) * WIDE
    return group, 1, (2 * (place - 6) + 2) * WIDE


def groups_of(planes):
    return -(-planes // PER_GROUP)


def lanes_like(shape):
    return lax.broadcasted_iota(jnp.int32, shape, len(shape) - 1)


def load_plane(fields, m, plane, levels):
    if plane < 4 * levels:
        return fields[plane // levels][m, plane % levels]
    if plane == 4 * levels:
        return fields[4][m]
    return fields[5][...].astype(jnp.float32)


def pack_kernel(levels, temp, salt, uvel, vvel, eta, mask, to_west, to_east, to_north, to_south):
    members, _, rows, cols = temp.shape
    planes = 4 * levels + 2
    fields = (temp, salt, uvel, vvel, eta, mask)
    lane = lanes_like((rows, LANE))
    for m in range(members):
        west_parts = [None] * groups_of(planes)
        east_parts = [None] * groups_of(planes)
        for plane in range(planes):
            value = load_plane(fields, m, plane, levels)
            group, _, start = rim_place(plane)
            both = jnp.where(lane < WIDE, value[:, :LANE], value[:, cols - LANE :])
            both = pltpu.roll(both, start, 1)
            is_west = (lane >= start) & (lane < start + WIDE)
            is_east = (lane >= start - WIDE) & (lane < start)
            zero = jnp.zeros_like(both)
            west_parts[group] = jnp.where(is_west, both, zero if west_parts[group] is None else west_parts[group])
            east_parts[group] = jnp.where(is_east, both, zero if east_parts[group] is None else east_parts[group])
            to_south[m, plane * WIDE : (plane + 1) * WIDE, :] = value[:WIDE]
            to_north[m, plane * WIDE : (plane + 1) * WIDE, :] = value[rows - WIDE :]
        for group in range(groups_of(planes)):
            where = slice(group * LANE, (group + 1) * LANE)
            to_west[m, :, where] = west_parts[group]
            to_east[m, :, where] = east_parts[group]


def whole(count):
    return [pl.BlockSpec(memory_space=pltpu.VMEM)] * count


def pack_rims(temp, salt, uvel, vvel, eta, mask):
    members, levels, rows, cols = temp.shape
    planes = 4 * levels + 2
    wide = groups_of(planes) * LANE
    row_pack = -(-planes * WIDE // 8) * 8
    side = jax.ShapeDtypeStruct((members, rows, wide), jnp.float32)
    line = jax.ShapeDtypeStruct((members, row_pack, cols), jnp.float32)
    return pl.pallas_call(
        functools.partial(pack_kernel, levels),
        out_shape=(side, side, line, line),
        in_specs=whole(6),
        out_specs=tuple(whole(4)),
        compiler_params=pltpu.CompilerParams(vmem_limit_bytes=VMEM_LIMIT),
        name="pack_rims",
    )(temp, salt, uvel, vvel, eta, mask)


def east_west(value):
    width = value.shape[-1]
    return pltpu.roll(value, width - 1, 1), pltpu.roll(value, 1, 1)


def chunks(first, last):
    return [(a, min(a + CHUNK, last)) for a in range(first, last, CHUNK)]


def assemble(ext, fields, rims, m, levels):
    from_east, from_west, from_north, from_south, north_sides, south_sides = rims
    planes = 4 * levels + 2
    rows, cols = fields[5].shape
    wide = groups_of(planes) * LANE
    for group in range(groups_of(planes)):
        where = slice(group * LANE, (group + 1) * LANE)
        where_west = slice(wide + group * LANE, wide + (group + 1) * LANE)
        bands = [(TOP - CHUNK, south_sides[m, :, where], south_sides[m, :, where_west])]
        for a in range(0, rows, CHUNK):
            bands.append((TOP + a, from_east[m, a : a + CHUNK, where], from_west[m, a : a + CHUNK, where]))
        bands.append((TOP + rows, north_sides[m, :, where], north_sides[m, :, where_west]))
        for at, east, west in bands:
            odd = ((lanes_like(east.shape) // WIDE) & 1) == 1
            joined = (jnp.where(odd, east, west), jnp.where(odd, west, east))
            for plane in range(group * PER_GROUP, min((group + 1) * PER_GROUP, planes)):
                _, kind, offset = rim_place(plane)
                ext[plane, at : at + CHUNK, cols : cols + LANE] = pltpu.roll(joined[kind], LANE - offset, 1)
    for plane in range(planes):
        ext[plane, TOP : TOP + rows, :cols] = load_plane(fields, m, plane, levels)
        ext[plane, TOP - WIDE : TOP, :cols] = from_south[m, plane * WIDE : (plane + 1) * WIDE, :]
        ext[plane, TOP + rows : TOP + rows + WIDE, :cols] = from_north[m, plane * WIDE : (plane + 1) * WIDE, :]


def fill_rows(cor, inside, first_row, total_rows):
    shape = (CHUNK, cor.shape[1])
    for a in range(0, cor.shape[0], CHUNK):
        row = first_row + (a - TOP) + lax.broadcasted_iota(jnp.int32, shape, 0)
        latitude = row.astype(jnp.float32) + 0.5
        cor[a : a + CHUNK, :] = CORI_K * (2.0 * latitude / total_rows - 1.0)
        inside[a : a + CHUNK, :] = jnp.where((row >= 0) & (row < total_rows), 1.0, 0.0)


class Planes:
    def __init__(self, ref, names):
        self.ref, self.names = ref, names

    def get(self, name, a, b):
        return self.ref[self.names.index(name), a:b, :]

    def put(self, name, a, b, value):
        self.ref[self.names.index(name), a:b, :] = value

    def sides(self, name, a, b):
        here = self.get(name, a, b)
        east, west = east_west(here)
        return here, east, west, self.get(name, a + 1, b + 1), self.get(name, a - 1, b - 1)

    def lap(self, name, a, b):
        here, east, west, north, south = self.sides(name, a, b)
        return east + west + north + south - 4.0 * here


def momentum(ocean, cor, u, v, pu, pv, lap_u, lap_v):
    new_u = ocean * (u + STEP_DT * (cor * v - 0.5 * pu - DRAG_K * u) + VISCOSITY * lap_u)
    new_v = ocean * (v + STEP_DT * (-cor * u - 0.5 * pv - DRAG_K * v) + VISCOSITY * lap_v)
    return new_u, new_v


def surface_start(ext, work, cor, inside, levels, rows):
    ocean_at = 4 * levels + 1
    low, high = TOP - CHUNK, TOP + rows + CHUNK
    near_low, near_high = TOP - 8, TOP + rows + 8
    for a, b in chunks(low, high):
        su = sv = sp = None
        for l in range(levels):
            dens = BETA_S * ext[levels + l, a:b, :] - ALPHA_T * ext[l, a:b, :]
            work.put("d%d" % l, a, b, dens)
            u, v = ext[2 * levels + l, a:b, :], ext[3 * levels + l, a:b, :]
            weighted = (PRESS_K * (levels - l)) * dens
            su, sv, sp = (u, v, weighted) if l == 0 else (su + u, sv + v, sp + weighted)
        work.put("su", a, b, su)
        work.put("sv", a, b, sv)
        work.put("sp", a, b, sp)
    for a, b in chunks(near_low, near_high):
        carried = None
        for l in range(levels):
            _, east, west, north, south = work.sides("d%d" % l, a, b)
            term = ext[2 * levels + l, a:b, :] * (east - west) + ext[3 * levels + l, a:b, :] * (north - south)
            term = (PRESS_K * (levels - l)) * term
            carried = term if l == 0 else carried + term
        here, east, west, north, south = work.sides("sp", a, b)
        lap = east + west + north + south - 4.0 * here
        work.put("q", a, b, ext[ocean_at, a:b, :] * (here - ADV * carried + KAPPA * lap))
    for a, b in chunks(low, high):
        ocean = ext[ocean_at, a:b, :]
        _, pe, pw, pn, ps = work.sides("sp", a, b)
        new_u, new_v = momentum(
            ocean, cor[a:b, :], work.get("su", a, b), work.get("sv", a, b),
            pe - pw, pn - ps, work.lap("su", a, b), work.lap("sv", a, b),
        )
        work.put("tu", a, b, new_u)
        work.put("tv", a, b, new_v)
    for a, b in chunks(near_low, near_high):
        work.put("v0", a, b, inside[a:b, :] * (ext[4 * levels, a:b, :] - divergence(work, "tu", "tv", a, b)))


def divergence(work, u_name, v_name, a, b):
    east, west = east_west(work.get(u_name, a, b))
    return DIV * (east - west + (work.get(v_name, a + 1, b + 1) - work.get(v_name, a - 1, b - 1)))


def around(work, name, a, b):
    _, east, west, north, south = work.sides(name, a, b)
    return east + west + north + south


def powers(work, inside, first, second, third, low, high):
    for a, b in chunks(low, high):
        work.put(second, a, b, inside[a:b, :] * around(work, first, a, b))
    for a, b in chunks(low, high):
        work.put(third, a, b, inside[a:b, :] * (around(work, second, a, b) - 4.0 * work.get(first, a, b)))


def surface_next(work, ext, cor, inside, levels, rows, u_name, v_name, eta_name, with_press, out_name):
    low, high = TOP - 8, TOP + rows + 8
    ocean_at = 4 * levels + 1
    for a, b in chunks(low, high):
        if with_press:
            _, pe, pw, pn, ps = work.sides("q", a, b)
            pu, pv = pe - pw, pn - ps
        else:
            pu = pv = 0.0
        new_u, new_v = momentum(
            ext[ocean_at, a:b, :], cor[a:b, :], work.get(u_name, a, b), work.get(v_name, a, b),
            pu, pv, work.lap(u_name, a, b), work.lap(v_name, a, b),
        )
        work.put("t2u", a, b, new_u)
        work.put("t2v", a, b, new_v)
    for a, b in chunks(low, high):
        div = divergence(work, "t2u", "t2v", a, b)
        value = -div if eta_name is None else work.get(eta_name, a, b) - div
        work.put(out_name, a, b, inside[a:b, :] * value)


def surface_push(work, ext, levels, rows, eta_name, u_name, v_name, base):
    ocean_at = 4 * levels + 1
    for a, b in chunks(TOP - 8, TOP + rows + 8):
        ocean = ext[ocean_at, a:b, :]
        _, east, west, north, south = work.sides(eta_name, a, b)
        push_u = -(levels * GRAV) * ocean * (east - west)
        push_v = -(levels * GRAV) * ocean * (north - south)
        if base:
            push_u, push_v = work.get("tu", a, b) + push_u, work.get("tv", a, b) + push_v
        work.put(u_name, a, b, push_u)
        work.put(v_name, a, b, push_v)


SUM_NAMES = ["d0", "d1", "d2", "d3", "su", "sv", "sp", "q", "tu", "tv", "v0", "v1", "v2", "v3", "pu", "pv", "t2u", "t2v"]
SUM_NAMES += ["w%d_%d" % (i, k) for i in range(4) for k in range(4)]


def sums_kernel(levels, total_rows, place, *refs):
    fields, rims, out, scratch = refs[:6], refs[6:12], refs[12], refs[13:]
    ext, planes, cor, inside, red = scratch
    members = fields[0].shape[0]
    rows, cols = fields[5].shape
    work = Planes(planes, SUM_NAMES)
    fill_rows(cor, inside, place[0], total_rows)
    red[...] = jnp.zeros_like(red)

    def one(m, carry):
        assemble(ext, fields, rims, m, levels)
        surface_start(ext, work, cor, inside, levels, rows)
        low, high = TOP - 8, TOP + rows + 8
        powers(work, inside, "v0", "v1", "v2", low, high)
        for a, b in chunks(TOP, TOP + rows):
            work.put("v3", a, b, around(work, "v2", a, b))
        surface_next(work, ext, cor, inside, levels, rows, "tu", "tv", None, True, "w0_0")
        for k in range(1, 4):
            name = "v%d" % (k - 1)
            surface_push(work, ext, levels, rows, name, "pu", "pv", False)
            surface_next(work, ext, cor, inside, levels, rows, "pu", "pv", name, False, "w0_%d" % k)
        for k in range(4):
            powers(work, inside, "w0_%d" % k, "w1_%d" % k, "w2_%d" % k, low, high)
            for a, b in chunks(TOP, TOP + rows):
                work.put("w3_%d" % k, a, b, around(work, "w2_%d" % k, a, b))

        def put_sum(at, first, second):
            total = None
            for a, b in chunks(TOP, TOP + rows):
                x = planes[SUM_NAMES.index(first), a:b, :cols]
                y = planes[SUM_NAMES.index(second), a:b, :cols]
                total = x * y if total is None else total + x * y
            line = jnp.sum(total, axis=0, keepdims=True)
            folded = line[:, :LANE]
            for c in range(LANE, cols, LANE):
                folded = folded + line[:, c : c + LANE]
            red[m, at : at + 1, :] = folded

        for i in range(6):
            put_sum(i, "v%d" % (i // 2), "v%d" % (i - i // 2))
            for p, (a, b) in enumerate(PAIRS):
                put_sum(6 + i * len(PAIRS) + p, "w%d_%d" % (i // 2, a), "w%d_%d" % (i - i // 2, b))
        return carry

    lax.fori_loop(0, members, one, 0)
    lane = lanes_like((8, LANE))
    tile = jnp.zeros((8, LANE), jnp.float32)
    for m in range(members):
        total = jnp.sum(red[m], axis=1, keepdims=True)
        for q in range(SUM_LANES):
            tile = jnp.where(lane == m * SUM_LANES + q, total[8 * q : 8 * q + 8], tile)
    out[...] = tile


def plane_shape(rows, cols):
    return (2 * TOP + rows, cols + LANE)


def local_sums(place, fields, rims, total_rows):
    members, levels, rows, cols = fields[0].shape
    shape = plane_shape(rows, cols)
    return pl.pallas_call(
        functools.partial(sums_kernel, levels, total_rows),
        out_shape=jax.ShapeDtypeStruct((8, LANE), jnp.float32),
        in_specs=[pl.BlockSpec(memory_space=pltpu.SMEM)] + whole(12),
        out_specs=pl.BlockSpec(memory_space=pltpu.VMEM),
        scratch_shapes=[
            pltpu.VMEM((4 * levels + 2,) + shape, jnp.float32),
            pltpu.VMEM((len(SUM_NAMES),) + shape, jnp.float32),
            pltpu.VMEM(shape, jnp.float32),
            pltpu.VMEM(shape, jnp.float32),
            pltpu.VMEM((members, SUM_ROWS, LANE), jnp.float32),
        ],
        compiler_params=pltpu.CompilerParams(vmem_limit_bytes=VMEM_LIMIT),
        cost_estimate=pl.CostEstimate(flops=10**8, bytes_accessed=4 * 10**6, transcendentals=0),
        name="local_sums",
    )(place, *fields, *rims)


def krylov(moment):
    n00, n01, n11, n12, n22, x22 = moment
    n02 = n11 - 4.0 * n00
    main, near = 1.0 + 4.0 * SURF_C, SURF_C
    g00 = main * n00 - near * n01
    g01 = main * n01 - near * n11
    g02 = main * n02 - near * n12
    g11 = main * n11 - near * (n12 + 4.0 * n01)
    g12 = main * n12 - near * (n22 + 4.0 * n02)
    g22 = main * n22 - near * x22
    l1, l2 = g01 / g00, g02 / g00
    d1 = g11 - l1 * g01
    d1 = jnp.where(d1 > 3e-7 * g11, d1, jnp.inf)
    e = g12 - l1 * g02
    l12 = e / d1
    d2 = g22 - l2 * g02 - l12 * e
    d2 = jnp.where(d2 > 3e-7 * g22, d2, jnp.inf)
    z0 = n00
    z1 = n01 - l1 * z0
    z2 = n02 - l2 * z0 - l12 * z1
    y2 = z2 / d2
    y1 = z1 / d1 - l12 * y2
    y0 = z0 / g00 - l1 * y1 - l2 * y2
    return [y0, y1, y2]


def weights(read):
    first = krylov([read(i) for i in range(6)])
    lifted = [None] + first
    second = []
    for i in range(6):
        total = None
        for p, (a, b) in enumerate(PAIRS):
            term = read(6 + i * len(PAIRS) + p)
            for k in (a, b):
                if k:
                    term = term * lifted[k]
            if a != b:
                term = 2.0 * term
            total = term if total is None else total + term
        second.append(total)
    return first, krylov(second)


RUN_NAMES = ["d0", "d1", "d2", "d3", "su", "sv", "sp", "q", "tu", "tv", "v0", "v1", "v2", "pu", "pv", "t2u", "t2v"]
RUN_NAMES += ["eta1", "w0", "w1", "w2", "eta2", "p", "p2"]


def combine(work, factors, names, out_name, a, b):
    total = None
    for factor, name in zip(factors, names):
        term = factor * work.get(name, a, b)
        total = term if total is None else total + term
    work.put(out_name, a, b, total)


def advance_kernel(levels, total_rows, place, sums, *refs):
    fields, rims = refs[:6], refs[6:12]
    out, zonal = refs[12:14]
    ext, planes, after, cor, inside = refs[14:]
    rows, cols = fields[5].shape
    ocean_at = 4 * levels + 1
    member = place[1]
    work = Planes(planes, RUN_NAMES)
    fill_rows(cor, inside, place[0], total_rows)
    low, high = TOP - 8, TOP + rows + 8
    assemble(ext, fields, rims, 0, levels)

    def read(i):
        return jnp.full((1, 1), sums[i % 8, member * SUM_LANES + i // 8], jnp.float32)

    first, second = weights(read)
    surface_start(ext, work, cor, inside, levels, rows)
    powers(work, inside, "v0", "v1", "v2", low, high)
    for a, b in chunks(low, high):
        combine(work, first, ("v0", "v1", "v2"), "eta1", a, b)
    surface_push(work, ext, levels, rows, "eta1", "pu", "pv", True)
    surface_next(work, ext, cor, inside, levels, rows, "pu", "pv", "eta1", True, "w0")
    powers(work, inside, "w0", "w1", "w2", low, high)
    for a, b in chunks(low, high):
        combine(work, second, ("w0", "w1", "w2"), "eta2", a, b)
    for a, b in chunks(TOP, TOP + rows):
        out[4 * levels, a - TOP : b - TOP, :] = work.get("eta2", a, b)[:, :cols]
    for a, b in chunks(low, high):
        ocean = ext[ocean_at, a:b, :]
        for name, to_u, to_v in (("eta1", "pu", "pv"), ("eta2", "t2u", "t2v")):
            _, east, west, north, south = work.sides(name, a, b)
            work.put(to_u, a, b, GRAV * ocean * (east - west))
            work.put(to_v, a, b, GRAV * ocean * (north - south))
        cor[a:b, :] = STEP_DT * cor[a:b, :]
    for a, b in chunks(TOP - CHUNK, TOP + rows + CHUNK):
        work.put("p", a, b, jnp.zeros((b - a, cols + LANE), jnp.float32))
        work.put("p2", a, b, jnp.zeros((b - a, cols + LANE), jnp.float32))
    zonal[...] = jnp.zeros_like(zonal)

    def step(ref, l, press, a, b, width):
        def sides(value, above, below):
            east, west = east_west(value)
            east, west = east[:, :width], west[:, :width]
            north, south = above[:, :width], below[:, :width]
            return value[:, :width], east, west, north, south

        def of(at):
            return sides(ref[at, a:b, :], ref[at, a + 1 : b + 1, :], ref[at, a - 1 : b - 1, :])

        ocean = ext[ocean_at, a:b, :width]
        coriolis = cor[a:b, :width]
        u, east, west, north, south = of(2 * levels + l)
        around_u = (east + west) + (north + south)
        v, east, west, north, south = of(3 * levels + l)
        around_v = (east + west) + (north + south)
        _, pe, pw, pn, ps = sides(work.get(press, a, b), work.get(press, a + 1, b + 1), work.get(press, a - 1, b - 1))
        keep = 1.0 - STEP_DT * DRAG_K - 4.0 * VISCOSITY
        new_u = ocean * ((keep * u + VISCOSITY * around_u) + (coriolis * v - (pe - pw)))
        new_v = ocean * ((keep * v + VISCOSITY * around_v) - (coriolis * u + (pn - ps)))
        flow_u, flow_v = ADV * u, ADV * v
        results = []
        for at in (l, levels + l):
            here, east, west, north, south = of(at)
            carried = flow_u * (east - west) + flow_v * (north - south)
            spread = (1.0 - 4.0 * KAPPA) * here + KAPPA * ((east + west) + (north + south))
            results.append(ocean * (spread - carried))
        return results[0], results[1], new_u, new_v

    def add_press(ref, l, press, a, b):
        factor = PRESS_K * 0.5 * STEP_DT
        dens = (factor * BETA_S) * ref[levels + l, a:b, :] - (factor * ALPHA_T) * ref[l, a:b, :]
        work.put(press, a, b, work.get(press, a, b) + dens)

    def level(l, carry):
        for a in range(TOP - CHUNK, TOP + rows + CHUNK, 8):
            add_press(ext, l, "p", a, a + 8)
        for a in range(low, high, 8):
            temp, salt, u, v = step(ext, l, "p", a, a + 8, cols + LANE)
            after[l, a : a + 8, :] = temp
            after[levels + l, a : a + 8, :] = salt
            after[2 * levels + l, a : a + 8, :] = u - work.get("pu", a, a + 8)
            after[3 * levels + l, a : a + 8, :] = v - work.get("pv", a, a + 8)
        for a in range(low, high, 8):
            add_press(after, l, "p2", a, a + 8)
        for a in range(TOP, TOP + rows, 8):
            temp, salt, u, v = step(after, l, "p2", a, a + 8, cols)
            here = slice(a - TOP, a - TOP + 8)
            v = v - work.get("t2v", a, a + 8)[:, :cols]
            out[l, here, :] = temp
            out[levels + l, here, :] = salt
            out[2 * levels + l, here, :] = u - work.get("t2u", a, a + 8)[:, :cols]
            out[3 * levels + l, here, :] = v
            total = jnp.sum(v, axis=1, keepdims=True)
            lane = lanes_like((8, LANE))
            zonal[here, :] = jnp.where(lane == member * levels + l, total, zonal[here, :])
        return carry

    lax.fori_loop(0, levels, level, 0)


def advance(place, sums, fields, rims, total_rows):
    members, levels, rows, cols = fields[0].shape
    shape = plane_shape(rows, cols)

    def of_member(value):
        rest = value.shape[1:]
        return pl.BlockSpec((1,) + rest, lambda i, place: (place[1],) + (0,) * len(rest))

    def fixed(dims):
        return pl.BlockSpec(dims, lambda i, place: (0,) * len(dims))

    mask_spec = fixed(fields[5].shape)
    final = (4 * levels + 1, rows, cols)
    return pl.pallas_call(
        functools.partial(advance_kernel, levels, total_rows),
        out_shape=(jax.ShapeDtypeStruct(final, jnp.float32), jax.ShapeDtypeStruct((rows, LANE), jnp.float32)),
        grid_spec=pltpu.PrefetchScalarGridSpec(
            num_scalar_prefetch=1,
            grid=(1,),
            in_specs=[pl.BlockSpec(memory_space=pltpu.SMEM)]
            + [of_member(value) for value in fields[:5]]
            + [mask_spec]
            + [of_member(value) for value in rims],
            out_specs=(fixed(final), fixed((rows, LANE))),
            scratch_shapes=[
                pltpu.VMEM((4 * levels + 2,) + shape, jnp.float32),
                pltpu.VMEM((len(RUN_NAMES),) + shape, jnp.float32),
                pltpu.VMEM((4 * levels,) + shape, jnp.float32),
                pltpu.VMEM(shape, jnp.float32),
                pltpu.VMEM(shape, jnp.float32),
            ],
        ),
        compiler_params=pltpu.CompilerParams(vmem_limit_bytes=VMEM_LIMIT),
        cost_estimate=pl.CostEstimate(flops=10**8, bytes_accessed=4 * 10**6, transcendentals=0),
        name="advance",
    )(place, sums, *fields, *rims)


def pick_kernel(levels, choice, *refs):
    count = len(refs) - 6
    sources, outs, sem = refs[:count], refs[count : count + 5], refs[count + 5]
    slots = outs[0].shape[0]

    def parts(s, source):
        for f in range(4):
            yield source.at[pl.ds(f * levels, levels)], outs[f].at[s]
        yield source.at[4 * levels], outs[4].at[s]

    for s in range(slots):
        for k in range(count):

            @pl.when(choice[s] == k)
            def _():
                for i, (source, target) in enumerate(parts(s, sources[k])):
                    pltpu.make_async_copy(source, target, sem.at[s, i]).start()

    for s in range(slots):
        for i, (source, target) in enumerate(parts(s, sources[0])):
            pltpu.make_async_copy(source, target, sem.at[s, i]).wait()


def pick(choice, sources, slots, levels):
    _, rows, cols = sources[0].shape
    volume = jax.ShapeDtypeStruct((slots, levels, rows, cols), jnp.float32)
    surface = jax.ShapeDtypeStruct((slots, rows, cols), jnp.float32)
    return pl.pallas_call(
        functools.partial(pick_kernel, levels),
        out_shape=(volume,) * 4 + (surface,),
        in_specs=[pl.BlockSpec(memory_space=pltpu.SMEM)] + [pl.BlockSpec(memory_space=pl.ANY)] * len(sources),
        out_specs=(pl.BlockSpec(memory_space=pl.ANY),) * 5,
        scratch_shapes=[pltpu.SemaphoreType.DMA((slots, 5))],
        name="pick",
    )(choice, *sources)


def shift(value, axis, by, wrap):
    count = lax.axis_size(axis)
    pairs = [(i, (i + by) % count) for i in range(count) if wrap or 0 <= i + by < count]
    return lax.ppermute(value, axis, pairs)


def exchange_rims(packed):
    to_west, to_east, to_north, to_south = packed
    rows = to_west.shape[1]
    from_east, from_west = shift(to_west, "gridx", -1, True), shift(to_east, "gridx", 1, True)
    from_north, from_south = shift(to_south, "gridy", -1, False), shift(to_north, "gridy", 1, False)
    low = jnp.concatenate([from_east[:, :CHUNK], from_west[:, :CHUNK]], axis=2)
    high = jnp.concatenate([from_east[:, rows - CHUNK :], from_west[:, rows - CHUNK :]], axis=2)
    north_sides, south_sides = shift(low, "gridy", -1, False), shift(high, "gridy", 1, False)
    return from_east, from_west, from_north, from_south, north_sides, south_sides


def total_over(value, axis):
    count = lax.axis_size(axis)
    if count & (count - 1):
        return lax.psum(value, axis)
    step = 1
    while step < count:
        value = value + lax.ppermute(value, axis, [(i, i ^ step) for i in range(count)])
        step *= 2
    return value


def swap(value):
    return lax.ppermute(value, "member", [(0, 1), (1, 0)])


def first_and_both(wanted, side, members):
    away = wanted // members != side
    index = wanted - (1 - side) * members
    takes = [jnp.any(away & (index == m)) for m in range(members)]
    return jnp.where(takes[0], 0, 1).astype(jnp.int32), takes[0] & takes[1]


def shards(temp, salt, uvel, vvel, eta, land_mask, clone_source):
    members, levels, rows, cols = temp.shape
    assert members == 2 and lax.axis_size("member") == 2
    tile_row, side = lax.axis_index("gridy"), lax.axis_index("member")
    total_rows = rows * lax.axis_size("gridy")
    total_cols = cols * lax.axis_size("gridx")
    their_source = swap(clone_source)
    here_first, here_both = first_and_both(clone_source, side, members)
    sent_first, sent_both = first_and_both(their_source, 1 - side, members)

    first_row = (tile_row * rows).astype(jnp.int32)
    fields = (temp, salt, uvel, vvel, eta, land_mask)
    rims = exchange_rims(pack_rims(*fields))
    sums = local_sums(first_row.reshape(1), fields, rims, total_rows)
    sums = total_over(total_over(sums, "gridx"), "gridy")

    sent, sent_zonal = advance(jnp.stack([first_row, sent_first]), sums, fields, rims, total_rows)
    arrived = swap(sent)
    other, other_zonal = advance(jnp.stack([first_row, 1 - sent_first]), sums, fields, rims, total_rows)

    zonal_whole = total_over(sent_zonal + other_zonal, "gridx")[:, : members * levels].reshape(rows, members, levels)
    zonal_whole = jnp.transpose(zonal_whole, (1, 2, 0))
    zonal_scale = 1.0 / jnp.sqrt(jnp.float32(total_cols))
    score_scale = 1.0 / jnp.sqrt(jnp.float32(levels * total_rows))
    latitude = (tile_row * rows + jnp.arange(rows, dtype=jnp.int32)).astype(jnp.float32) + 0.5
    overturn = jnp.cumsum(zonal_whole, axis=1) * zonal_scale
    score = total_over(jnp.sum(overturn * (latitude / total_rows), axis=(1, 2)) * score_scale, "gridy")
    their_score = swap(score)
    every_score = jnp.where(side == 0, jnp.concatenate([score, their_score]), jnp.concatenate([their_score, score]))
    clone_weight = jnp.take(every_score, clone_source, axis=0) - jnp.mean(every_score)

    away = clone_source // members != side
    index = clone_source % members
    choice = jnp.where(away, jnp.where(index == here_first, 2, 3), jnp.where(index == sent_first, 0, 1))
    choice = choice.astype(jnp.int32)

    def with_second():
        return pick(choice, (sent, other, arrived, swap(other)), members, levels)

    def without_second():
        return pick(choice, (sent, other, arrived), members, levels)

    picked = lax.cond(here_both | sent_both, with_second, without_second)
    return (*picked, overturn, clone_weight)


def solution(mesh):
    volume = P("member", None, "gridy", "gridx")
    in_specs = (volume,) * 4 + (P("member", "gridy", "gridx"), P("gridy", "gridx"), P("member"))
    out_specs = (volume,) * 4 + (P("member", "gridy", "gridx"), P("member", None, "gridy"), P("member"))
    return jax.shard_map(shards, mesh=mesh, in_specs=in_specs, out_specs=out_specs, check_vma=False)
```

```python
import functools

import jax
import jax.numpy as jnp
from jax import lax
from jax.experimental import pallas as pl
from jax.experimental.pallas import tpu as pltpu
from jax.sharding import PartitionSpec as P

STEPS = 2
ITERS = 3

ALPHA_T = 0.8
BETA_S = 0.6
PRESS_K = 0.25
STEP_DT = 0.1
KAPPA = 0.1
VISCOSITY = 0.1
DRAG_K = 0.05
CORI_K = 1.0
SURF_C = 4.0
DIV_K = 0.5
GRAV_K = 0.5

ADV = STEP_DT * 0.5
DIV = DIV_K * 0.5
GRAV = GRAV_K * 0.5

WIDE = 10
TOP = 24
CHUNK = 16
LANE = 128
PER_GROUP = 11
PAIRS = [(a, b) for a in range(4) for b in range(a, 4)]
SUMS = 6 + 6 * len(PAIRS)
SUM_ROWS = -(-SUMS // 8) * 8
SUM_LANES = SUM_ROWS // 8
VMEM_LIMIT = 24 * 1024 * 1024


def rim_place(plane):
    group, place = divmod(plane, PER_GROUP)
    if place < 6:
        return group, 0, (2 * place + 1) * WIDE
    return group, 1, (2 * (place - 6) + 2) * WIDE


def groups_of(planes):
    return -(-planes // PER_GROUP)


def lanes_like(shape):
    return lax.broadcasted_iota(jnp.int32, shape, len(shape) - 1)


def load_plane(fields, m, plane, levels):
    if plane < 4 * levels:
        return fields[plane // levels][m, plane % levels]
    if plane == 4 * levels:
        return fields[4][m]
    return fields[5][...].astype(jnp.float32)


def pack_kernel(levels, temp, salt, uvel, vvel, eta, mask, to_west, to_east, to_north, to_south):
    members, _, rows, cols = temp.shape
    planes = 4 * levels + 2
    fields = (temp, salt, uvel, vvel, eta, mask)
    lane = lanes_like((rows, LANE))
    for m in range(members):
        west_parts = [None] * groups_of(planes)
        east_parts = [None] * groups_of(planes)
        for plane in range(planes):
            value = load_plane(fields, m, plane, levels)
            group, _, start = rim_place(plane)
            both = jnp.where(lane < WIDE, value[:, :LANE], value[:, cols - LANE :])
            both = pltpu.roll(both, start, 1)
            is_west = (lane >= start) & (lane < start + WIDE)
            is_east = (lane >= start - WIDE) & (lane < start)
            zero = jnp.zeros_like(both)
            west_parts[group] = jnp.where(is_west, both, zero if west_parts[group] is None else west_parts[group])
            east_parts[group] = jnp.where(is_east, both, zero if east_parts[group] is None else east_parts[group])
            to_south[m, plane * WIDE : (plane + 1) * WIDE, :] = value[:WIDE]
            to_north[m, plane * WIDE : (plane + 1) * WIDE, :] = value[rows - WIDE :]
        for group in range(groups_of(planes)):
            where = slice(group * LANE, (group + 1) * LANE)
            to_west[m, :, where] = west_parts[group]
            to_east[m, :, where] = east_parts[group]


def whole(count):
    return [pl.BlockSpec(memory_space=pltpu.VMEM)] * count


def pack_rims(temp, salt, uvel, vvel, eta, mask):
    members, levels, rows, cols = temp.shape
    planes = 4 * levels + 2
    wide = groups_of(planes) * LANE
    row_pack = -(-planes * WIDE // 8) * 8
    side = jax.ShapeDtypeStruct((members, rows, wide), jnp.float32)
    line = jax.ShapeDtypeStruct((members, row_pack, cols), jnp.float32)
    return pl.pallas_call(
        functools.partial(pack_kernel, levels),
        out_shape=(side, side, line, line),
        in_specs=whole(6),
        out_specs=tuple(whole(4)),
        compiler_params=pltpu.CompilerParams(vmem_limit_bytes=VMEM_LIMIT),
        name="pack_rims",
    )(temp, salt, uvel, vvel, eta, mask)


def east_west(value):
    width = value.shape[-1]
    return pltpu.roll(value, width - 1, 1), pltpu.roll(value, 1, 1)


def chunks(first, last):
    return [(a, min(a + CHUNK, last)) for a in range(first, last, CHUNK)]


def assemble(ext, fields, rims, m, levels):
    from_east, from_west, from_north, from_south, north_sides, south_sides = rims
    planes = 4 * levels + 2
    rows, cols = fields[5].shape
    wide = groups_of(planes) * LANE
    for group in range(groups_of(planes)):
        where = slice(group * LANE, (group + 1) * LANE)
        where_west = slice(wide + group * LANE, wide + (group + 1) * LANE)
        bands = [(TOP - CHUNK, south_sides[m, :, where], south_sides[m, :, where_west])]
        for a in range(0, rows, CHUNK):
            bands.append((TOP + a, from_east[m, a : a + CHUNK, where], from_west[m, a : a + CHUNK, where]))
        bands.append((TOP + rows, north_sides[m, :, where], north_sides[m, :, where_west]))
        for at, east, west in bands:
            odd = ((lanes_like(east.shape) // WIDE) & 1) == 1
            joined = (jnp.where(odd, east, west), jnp.where(odd, west, east))
            for plane in range(group * PER_GROUP, min((group + 1) * PER_GROUP, planes)):
                _, kind, offset = rim_place(plane)
                ext[plane, at : at + CHUNK, cols : cols + LANE] = pltpu.roll(joined[kind], LANE - offset, 1)
    for plane in range(planes):
        ext[plane, TOP : TOP + rows, :cols] = load_plane(fields, m, plane, levels)
        ext[plane, TOP - WIDE : TOP, :cols] = from_south[m, plane * WIDE : (plane + 1) * WIDE, :]
        ext[plane, TOP + rows : TOP + rows + WIDE, :cols] = from_north[m, plane * WIDE : (plane + 1) * WIDE, :]


def fill_rows(cor, inside, first_row, total_rows):
    shape = (CHUNK, cor.shape[1])
    for a in range(0, cor.shape[0], CHUNK):
        row = first_row + (a - TOP) + lax.broadcasted_iota(jnp.int32, shape, 0)
        latitude = row.astype(jnp.float32) + 0.5
        cor[a : a + CHUNK, :] = CORI_K * (2.0 * latitude / total_rows - 1.0)
        inside[a : a + CHUNK, :] = jnp.where((row >= 0) & (row < total_rows), 1.0, 0.0)


class Planes:
    def __init__(self, ref, names):
        self.ref, self.names = ref, names

    def get(self, name, a, b):
        return self.ref[self.names.index(name), a:b, :]

    def put(self, name, a, b, value):
        self.ref[self.names.index(name), a:b, :] = value

    def sides(self, name, a, b):
        here = self.get(name, a, b)
        east, west = east_west(here)
        return here, east, west, self.get(name, a + 1, b + 1), self.get(name, a - 1, b - 1)

    def lap(self, name, a, b):
        here, east, west, north, south = self.sides(name, a, b)
        return east + west + north + south - 4.0 * here


def momentum(ocean, cor, u, v, pu, pv, lap_u, lap_v):
    new_u = ocean * (u + STEP_DT * (cor * v - 0.5 * pu - DRAG_K * u) + VISCOSITY * lap_u)
    new_v = ocean * (v + STEP_DT * (-cor * u - 0.5 * pv - DRAG_K * v) + VISCOSITY * lap_v)
    return new_u, new_v


def surface_start(ext, work, cor, inside, levels, rows):
    ocean_at = 4 * levels + 1
    low, high = TOP - CHUNK, TOP + rows + CHUNK
    near_low, near_high = TOP - 8, TOP + rows + 8
    for a, b in chunks(low, high):
        su = sv = sp = None
        for l in range(levels):
            dens = BETA_S * ext[levels + l, a:b, :] - ALPHA_T * ext[l, a:b, :]
            work.put("d%d" % l, a, b, dens)
            u, v = ext[2 * levels + l, a:b, :], ext[3 * levels + l, a:b, :]
            weighted = (PRESS_K * (levels - l)) * dens
            su, sv, sp = (u, v, weighted) if l == 0 else (su + u, sv + v, sp + weighted)
        work.put("su", a, b, su)
        work.put("sv", a, b, sv)
        work.put("sp", a, b, sp)
    for a, b in chunks(near_low, near_high):
        carried = None
        for l in range(levels):
            _, east, west, north, south = work.sides("d%d" % l, a, b)
            term = ext[2 * levels + l, a:b, :] * (east - west) + ext[3 * levels + l, a:b, :] * (north - south)
            term = (PRESS_K * (levels - l)) * term
            carried = term if l == 0 else carried + term
        here, east, west, north, south = work.sides("sp", a, b)
        lap = east + west + north + south - 4.0 * here
        work.put("q", a, b, ext[ocean_at, a:b, :] * (here - ADV * carried + KAPPA * lap))
    for a, b in chunks(low, high):
        ocean = ext[ocean_at, a:b, :]
        _, pe, pw, pn, ps = work.sides("sp", a, b)
        new_u, new_v = momentum(
            ocean, cor[a:b, :], work.get("su", a, b), work.get("sv", a, b),
            pe - pw, pn - ps, work.lap("su", a, b), work.lap("sv", a, b),
        )
        work.put("tu", a, b, new_u)
        work.put("tv", a, b, new_v)
    for a, b in chunks(near_low, near_high):
        work.put("v0", a, b, inside[a:b, :] * (ext[4 * levels, a:b, :] - divergence(work, "tu", "tv", a, b)))


def divergence(work, u_name, v_name, a, b):
    east, west = east_west(work.get(u_name, a, b))
    return DIV * (east - west + (work.get(v_name, a + 1, b + 1) - work.get(v_name, a - 1, b - 1)))


def around(work, name, a, b):
    _, east, west, north, south = work.sides(name, a, b)
    return east + west + north + south


def powers(work, inside, first, second, third, low, high):
    for a, b in chunks(low, high):
        work.put(second, a, b, inside[a:b, :] * around(work, first, a, b))
    for a, b in chunks(low, high):
        work.put(third, a, b, inside[a:b, :] * (around(work, second, a, b) - 4.0 * work.get(first, a, b)))


def surface_next(work, ext, cor, inside, levels, rows, u_name, v_name, eta_name, with_press, out_name):
    low, high = TOP - 8, TOP + rows + 8
    ocean_at = 4 * levels + 1
    for a, b in chunks(low, high):
        if with_press:
            _, pe, pw, pn, ps = work.sides("q", a, b)
            pu, pv = pe - pw, pn - ps
        else:
            pu = pv = 0.0
        new_u, new_v = momentum(
            ext[ocean_at, a:b, :], cor[a:b, :], work.get(u_name, a, b), work.get(v_name, a, b),
            pu, pv, work.lap(u_name, a, b), work.lap(v_name, a, b),
        )
        work.put("t2u", a, b, new_u)
        work.put("t2v", a, b, new_v)
    for a, b in chunks(low, high):
        div = divergence(work, "t2u", "t2v", a, b)
        value = -div if eta_name is None else work.get(eta_name, a, b) - div
        work.put(out_name, a, b, inside[a:b, :] * value)


def surface_push(work, ext, levels, rows, eta_name, u_name, v_name, base):
    ocean_at = 4 * levels + 1
    for a, b in chunks(TOP - 8, TOP + rows + 8):
        ocean = ext[ocean_at, a:b, :]
        _, east, west, north, south = work.sides(eta_name, a, b)
        push_u = -(levels * GRAV) * ocean * (east - west)
        push_v = -(levels * GRAV) * ocean * (north - south)
        if base:
            push_u, push_v = work.get("tu", a, b) + push_u, work.get("tv", a, b) + push_v
        work.put(u_name, a, b, push_u)
        work.put(v_name, a, b, push_v)


SUM_NAMES = ["d0", "d1", "d2", "d3", "su", "sv", "sp", "q", "tu", "tv", "v0", "v1", "v2", "v3", "pu", "pv", "t2u", "t2v"]
SUM_NAMES += ["w%d_%d" % (i, k) for i in range(4) for k in range(4)]


def sums_kernel(levels, total_rows, place, *refs):
    fields, rims, out, scratch = refs[:6], refs[6:12], refs[12], refs[13:]
    ext, planes, cor, inside, red = scratch
    members = fields[0].shape[0]
    rows, cols = fields[5].shape
    work = Planes(planes, SUM_NAMES)
    fill_rows(cor, inside, place[0], total_rows)
    red[...] = jnp.zeros_like(red)

    def one(m, carry):
        assemble(ext, fields, rims, m, levels)
        surface_start(ext, work, cor, inside, levels, rows)
        low, high = TOP - 8, TOP + rows + 8
        powers(work, inside, "v0", "v1", "v2", low, high)
        for a, b in chunks(TOP, TOP + rows):
            work.put("v3", a, b, around(work, "v2", a, b))
        surface_next(work, ext, cor, inside, levels, rows, "tu", "tv", None, True, "w0_0")
        for k in range(1, 4):
            name = "v%d" % (k - 1)
            surface_push(work, ext, levels, rows, name, "pu", "pv", False)
            surface_next(work, ext, cor, inside, levels, rows, "pu", "pv", name, False, "w0_%d" % k)
        for k in range(4):
            powers(work, inside, "w0_%d" % k, "w1_%d" % k, "w2_%d" % k, low, high)
            for a, b in chunks(TOP, TOP + rows):
                work.put("w3_%d" % k, a, b, around(work, "w2_%d" % k, a, b))

        def put_sum(at, first, second):
            total = None
            for a, b in chunks(TOP, TOP + rows):
                x = planes[SUM_NAMES.index(first), a:b, :cols]
                y = planes[SUM_NAMES.index(second), a:b, :cols]
                total = x * y if total is None else total + x * y
            line = jnp.sum(total, axis=0, keepdims=True)
            folded = line[:, :LANE]
            for c in range(LANE, cols, LANE):
                folded = folded + line[:, c : c + LANE]
            red[m, at : at + 1, :] = folded

        for i in range(6):
            put_sum(i, "v%d" % (i // 2), "v%d" % (i - i // 2))
            for p, (a, b) in enumerate(PAIRS):
                put_sum(6 + i * len(PAIRS) + p, "w%d_%d" % (i // 2, a), "w%d_%d" % (i - i // 2, b))
        return carry

    lax.fori_loop(0, members, one, 0)
    lane = lanes_like((8, LANE))
    tile = jnp.zeros((8, LANE), jnp.float32)
    for m in range(members):
        total = jnp.sum(red[m], axis=1, keepdims=True)
        for q in range(SUM_LANES):
            tile = jnp.where(lane == m * SUM_LANES + q, total[8 * q : 8 * q + 8], tile)
    for i in range(out.shape[0]):
        out[i] = tile


def plane_shape(rows, cols):
    return (2 * TOP + rows, cols + LANE)


def local_sums(place, fields, rims, total_rows, copies):
    members, levels, rows, cols = fields[0].shape
    shape = plane_shape(rows, cols)
    return pl.pallas_call(
        functools.partial(sums_kernel, levels, total_rows),
        out_shape=jax.ShapeDtypeStruct((copies, 8, LANE), jnp.float32),
        in_specs=[pl.BlockSpec(memory_space=pltpu.SMEM)] + whole(12),
        out_specs=pl.BlockSpec(memory_space=pltpu.VMEM),
        scratch_shapes=[
            pltpu.VMEM((4 * levels + 2,) + shape, jnp.float32),
            pltpu.VMEM((len(SUM_NAMES),) + shape, jnp.float32),
            pltpu.VMEM(shape, jnp.float32),
            pltpu.VMEM(shape, jnp.float32),
            pltpu.VMEM((members, SUM_ROWS, LANE), jnp.float32),
        ],
        compiler_params=pltpu.CompilerParams(vmem_limit_bytes=VMEM_LIMIT),
        cost_estimate=pl.CostEstimate(flops=10**8, bytes_accessed=4 * 10**6, transcendentals=0),
        name="local_sums",
    )(place, *fields, *rims)


def krylov(moment):
    n00, n01, n11, n12, n22, x22 = moment
    n02 = n11 - 4.0 * n00
    main, near = 1.0 + 4.0 * SURF_C, SURF_C
    g00 = main * n00 - near * n01
    g01 = main * n01 - near * n11
    g02 = main * n02 - near * n12
    g11 = main * n11 - near * (n12 + 4.0 * n01)
    g12 = main * n12 - near * (n22 + 4.0 * n02)
    g22 = main * n22 - near * x22
    l1, l2 = g01 / g00, g02 / g00
    d1 = g11 - l1 * g01
    d1 = jnp.where(d1 > 3e-7 * g11, d1, jnp.inf)
    e = g12 - l1 * g02
    l12 = e / d1
    d2 = g22 - l2 * g02 - l12 * e
    d2 = jnp.where(d2 > 3e-7 * g22, d2, jnp.inf)
    z0 = n00
    z1 = n01 - l1 * z0
    z2 = n02 - l2 * z0 - l12 * z1
    y2 = z2 / d2
    y1 = z1 / d1 - l12 * y2
    y0 = z0 / g00 - l1 * y1 - l2 * y2
    return [y0, y1, y2]


def weights(read):
    first = krylov([read(i) for i in range(6)])
    lifted = [None] + first
    second = []
    for i in range(6):
        total = None
        for p, (a, b) in enumerate(PAIRS):
            term = read(6 + i * len(PAIRS) + p)
            for k in (a, b):
                if k:
                    term = term * lifted[k]
            if a != b:
                term = 2.0 * term
            total = term if total is None else total + term
        second.append(total)
    return first, krylov(second)


RUN_NAMES = ["d0", "d1", "d2", "d3", "su", "sv", "sp", "q", "tu", "tv", "v0", "v1", "v2", "pu", "pv", "t2u", "t2v"]
RUN_NAMES += ["eta1", "w0", "w1", "w2", "eta2", "p", "p2"]


def combine(work, factors, names, out_name, a, b):
    total = None
    for factor, name in zip(factors, names):
        term = factor * work.get(name, a, b)
        total = term if total is None else total + term
    work.put(out_name, a, b, total)


def advance_kernel(levels, total_rows, place, tiles, *refs):
    fields, rims = refs[:6], refs[6:12]
    out, zonal = refs[12:14]
    ext, planes, after, cor, inside, tile, sums, sem = refs[14:]
    rows, cols = fields[5].shape
    ocean_at = 4 * levels + 1
    member = place[1]
    work = Planes(planes, RUN_NAMES)
    fill_rows(cor, inside, place[0], total_rows)
    low, high = TOP - 8, TOP + rows + 8
    total = tiles[0]
    for i in range(1, tiles.shape[0]):
        total = total + tiles[i]
    tile[...] = total
    copy = pltpu.make_async_copy(tile, sums, sem)
    copy.start()
    assemble(ext, fields, rims, 0, levels)
    copy.wait()

    def read(i):
        return jnp.full((1, 1), sums[i % 8, member * SUM_LANES + i // 8], jnp.float32)

    first, second = weights(read)
    surface_start(ext, work, cor, inside, levels, rows)
    powers(work, inside, "v0", "v1", "v2", low, high)
    for a, b in chunks(low, high):
        combine(work, first, ("v0", "v1", "v2"), "eta1", a, b)
    surface_push(work, ext, levels, rows, "eta1", "pu", "pv", True)
    surface_next(work, ext, cor, inside, levels, rows, "pu", "pv", "eta1", True, "w0")
    powers(work, inside, "w0", "w1", "w2", low, high)
    for a, b in chunks(low, high):
        combine(work, second, ("w0", "w1", "w2"), "eta2", a, b)
    for a, b in chunks(TOP, TOP + rows):
        out[4 * levels, a - TOP : b - TOP, :] = work.get("eta2", a, b)[:, :cols]
    for a, b in chunks(low, high):
        ocean = ext[ocean_at, a:b, :]
        for name, to_u, to_v in (("eta1", "pu", "pv"), ("eta2", "t2u", "t2v")):
            _, east, west, north, south = work.sides(name, a, b)
            work.put(to_u, a, b, GRAV * ocean * (east - west))
            work.put(to_v, a, b, GRAV * ocean * (north - south))
        cor[a:b, :] = STEP_DT * cor[a:b, :]
    for a, b in chunks(TOP - CHUNK, TOP + rows + CHUNK):
        work.put("p", a, b, jnp.zeros((b - a, cols + LANE), jnp.float32))
        work.put("p2", a, b, jnp.zeros((b - a, cols + LANE), jnp.float32))
    zonal[...] = jnp.zeros_like(zonal)

    def step(ref, l, press, a, b, width):
        def sides(value, above, below):
            east, west = east_west(value)
            east, west = east[:, :width], west[:, :width]
            north, south = above[:, :width], below[:, :width]
            return value[:, :width], east, west, north, south

        def of(at):
            return sides(ref[at, a:b, :], ref[at, a + 1 : b + 1, :], ref[at, a - 1 : b - 1, :])

        ocean = ext[ocean_at, a:b, :width]
        coriolis = cor[a:b, :width]
        u, east, west, north, south = of(2 * levels + l)
        around_u = (east + west) + (north + south)
        v, east, west, north, south = of(3 * levels + l)
        around_v = (east + west) + (north + south)
        _, pe, pw, pn, ps = sides(work.get(press, a, b), work.get(press, a + 1, b + 1), work.get(press, a - 1, b - 1))
        keep = 1.0 - STEP_DT * DRAG_K - 4.0 * VISCOSITY
        new_u = ocean * ((keep * u + VISCOSITY * around_u) + (coriolis * v - (pe - pw)))
        new_v = ocean * ((keep * v + VISCOSITY * around_v) - (coriolis * u + (pn - ps)))
        flow_u, flow_v = ADV * u, ADV * v
        results = []
        for at in (l, levels + l):
            here, east, west, north, south = of(at)
            carried = flow_u * (east - west) + flow_v * (north - south)
            spread = (1.0 - 4.0 * KAPPA) * here + KAPPA * ((east + west) + (north + south))
            results.append(ocean * (spread - carried))
        return results[0], results[1], new_u, new_v

    def add_press(ref, l, press, a, b):
        factor = PRESS_K * 0.5 * STEP_DT
        dens = (factor * BETA_S) * ref[levels + l, a:b, :] - (factor * ALPHA_T) * ref[l, a:b, :]
        work.put(press, a, b, work.get(press, a, b) + dens)

    def level(l, carry):
        for a in range(TOP - CHUNK, TOP + rows + CHUNK, 8):
            add_press(ext, l, "p", a, a + 8)
        for a in range(low, high, 8):
            temp, salt, u, v = step(ext, l, "p", a, a + 8, cols + LANE)
            after[l, a : a + 8, :] = temp
            after[levels + l, a : a + 8, :] = salt
            after[2 * levels + l, a : a + 8, :] = u - work.get("pu", a, a + 8)
            after[3 * levels + l, a : a + 8, :] = v - work.get("pv", a, a + 8)
        for a in range(low, high, 8):
            add_press(after, l, "p2", a, a + 8)
        for a in range(TOP, TOP + rows, 8):
            temp, salt, u, v = step(after, l, "p2", a, a + 8, cols)
            here = slice(a - TOP, a - TOP + 8)
            v = v - work.get("t2v", a, a + 8)[:, :cols]
            out[l, here, :] = temp
            out[levels + l, here, :] = salt
            out[2 * levels + l, here, :] = u - work.get("t2u", a, a + 8)[:, :cols]
            out[3 * levels + l, here, :] = v
            total = jnp.sum(v, axis=1, keepdims=True)
            lane = lanes_like((8, LANE))
            zonal[here, :] = jnp.where(lane == member * levels + l, total, zonal[here, :])
        return carry

    lax.fori_loop(0, levels, level, 0)


def advance(place, tiles, fields, rims, total_rows):
    members, levels, rows, cols = fields[0].shape
    shape = plane_shape(rows, cols)

    def of_member(value):
        rest = value.shape[1:]
        return pl.BlockSpec((1,) + rest, lambda i, place: (place[1],) + (0,) * len(rest))

    def fixed(dims):
        return pl.BlockSpec(dims, lambda i, place: (0,) * len(dims))

    mask_spec = fixed(fields[5].shape)
    final = (4 * levels + 1, rows, cols)
    return pl.pallas_call(
        functools.partial(advance_kernel, levels, total_rows),
        out_shape=(jax.ShapeDtypeStruct(final, jnp.float32), jax.ShapeDtypeStruct((rows, LANE), jnp.float32)),
        grid_spec=pltpu.PrefetchScalarGridSpec(
            num_scalar_prefetch=1,
            grid=(1,),
            in_specs=[fixed(tiles.shape)]
            + [of_member(value) for value in fields[:5]]
            + [mask_spec]
            + [of_member(value) for value in rims],
            out_specs=(fixed(final), fixed((rows, LANE))),
            scratch_shapes=[
                pltpu.VMEM((4 * levels + 2,) + shape, jnp.float32),
                pltpu.VMEM((len(RUN_NAMES),) + shape, jnp.float32),
                pltpu.VMEM((4 * levels,) + shape, jnp.float32),
                pltpu.VMEM(shape, jnp.float32),
                pltpu.VMEM(shape, jnp.float32),
                pltpu.VMEM((8, LANE), jnp.float32),
                pltpu.SMEM((8, LANE), jnp.float32),
                pltpu.SemaphoreType.DMA,
            ],
        ),
        compiler_params=pltpu.CompilerParams(vmem_limit_bytes=VMEM_LIMIT),
        cost_estimate=pl.CostEstimate(flops=10**8, bytes_accessed=4 * 10**6, transcendentals=0),
        name="advance",
    )(place, tiles, *fields, *rims)


def pick_kernel(levels, choice, *refs):
    count = len(refs) - 6
    sources, outs, sem = refs[:count], refs[count : count + 5], refs[count + 5]
    slots = outs[0].shape[0]

    def parts(s, source):
        for f in range(4):
            yield source.at[pl.ds(f * levels, levels)], outs[f].at[s]
        yield source.at[4 * levels], outs[4].at[s]

    for s in range(slots):
        for k in range(count):

            @pl.when(choice[s] == k)
            def _():
                for i, (source, target) in enumerate(parts(s, sources[k])):
                    pltpu.make_async_copy(source, target, sem.at[s, i]).start()

    for s in range(slots):
        for i, (source, target) in enumerate(parts(s, sources[0])):
            pltpu.make_async_copy(source, target, sem.at[s, i]).wait()


def pick(choice, sources, slots, levels):
    _, rows, cols = sources[0].shape
    volume = jax.ShapeDtypeStruct((slots, levels, rows, cols), jnp.float32)
    surface = jax.ShapeDtypeStruct((slots, rows, cols), jnp.float32)
    return pl.pallas_call(
        functools.partial(pick_kernel, levels),
        out_shape=(volume,) * 4 + (surface,),
        in_specs=[pl.BlockSpec(memory_space=pltpu.SMEM)] + [pl.BlockSpec(memory_space=pl.ANY)] * len(sources),
        out_specs=(pl.BlockSpec(memory_space=pl.ANY),) * 5,
        scratch_shapes=[pltpu.SemaphoreType.DMA((slots, 5))],
        name="pick",
    )(choice, *sources)


def shift(value, axis, by, wrap):
    count = lax.axis_size(axis)
    pairs = [(i, (i + by) % count) for i in range(count) if wrap or 0 <= i + by < count]
    return lax.ppermute(value, axis, pairs)


def exchange_rims(packed):
    to_west, to_east, to_north, to_south = packed
    rows = to_west.shape[1]
    from_east, from_west = shift(to_west, "gridx", -1, True), shift(to_east, "gridx", 1, True)
    from_north, from_south = shift(to_south, "gridy", -1, False), shift(to_north, "gridy", 1, False)
    low = jnp.concatenate([from_east[:, :CHUNK], from_west[:, :CHUNK]], axis=2)
    high = jnp.concatenate([from_east[:, rows - CHUNK :], from_west[:, rows - CHUNK :]], axis=2)
    north_sides, south_sides = shift(low, "gridy", -1, False), shift(high, "gridy", 1, False)
    return from_east, from_west, from_north, from_south, north_sides, south_sides


def from_all(tiles, axes):
    return lax.all_to_all(tiles, axes, split_axis=0, concat_axis=0, tiled=True)


def swap(value):
    return lax.ppermute(value, "member", [(0, 1), (1, 0)])


def first_and_both(wanted, side, members):
    away = wanted // members != side
    index = wanted - (1 - side) * members
    takes = [jnp.any(away & (index == m)) for m in range(members)]
    return jnp.where(takes[0], 0, 1).astype(jnp.int32), takes[0] & takes[1]


def shards(temp, salt, uvel, vvel, eta, land_mask, clone_source):
    members, levels, rows, cols = temp.shape
    assert members == 2 and lax.axis_size("member") == 2
    tile_row, side = lax.axis_index("gridy"), lax.axis_index("member")
    total_rows = rows * lax.axis_size("gridy")
    total_cols = cols * lax.axis_size("gridx")
    their_source = swap(clone_source)
    here_first, here_both = first_and_both(clone_source, side, members)
    sent_first, sent_both = first_and_both(their_source, 1 - side, members)

    first_row = (tile_row * rows).astype(jnp.int32)
    fields = (temp, salt, uvel, vvel, eta, land_mask)
    rims = exchange_rims(pack_rims(*fields))
    grid = lax.axis_size(("gridy", "gridx"))
    tiles = from_all(local_sums(first_row.reshape(1), fields, rims, total_rows, grid), ("gridy", "gridx"))

    sent, sent_zonal = advance(jnp.stack([first_row, sent_first]), tiles, fields, rims, total_rows)
    arrived = swap(sent)

    def rest():
        other, other_zonal = advance(jnp.stack([first_row, 1 - sent_first]), tiles, fields, rims, total_rows)
        zonal = jnp.transpose((sent_zonal + other_zonal)[:, : members * levels])
        everywhere = ("member", "gridy", "gridx")
        count_y, count_x = lax.axis_size("gridy"), lax.axis_size("gridx")
        zonal = from_all(jnp.broadcast_to(zonal[None], (2 * grid,) + zonal.shape), everywhere)
        zonal = zonal.reshape(2, count_y, count_x, members, levels, rows)
        overturn = jnp.cumsum(jnp.sum(zonal, axis=2), axis=3) * (1.0 / jnp.sqrt(jnp.float32(total_cols)))
        latitude = (jnp.arange(total_rows, dtype=jnp.float32) + 0.5).reshape(count_y, 1, 1, rows) / total_rows
        score = jnp.sum(overturn * latitude, axis=(1, 3, 4)) * (1.0 / jnp.sqrt(jnp.float32(levels * total_rows)))
        score = score.reshape(-1)
        weight = jnp.take(score, clone_source, axis=0) - jnp.mean(score)
        return other, overturn[side, tile_row], weight

    def nothing():
        return jnp.zeros_like(sent), jnp.zeros((members, levels, rows), jnp.float32), jnp.zeros((members,), jnp.float32)

    other, overturn, clone_weight = lax.cond(tile_row < lax.axis_size("gridy"), rest, nothing)

    away = clone_source // members != side
    index = clone_source % members
    choice = jnp.where(away, jnp.where(index == here_first, 2, 3), jnp.where(index == sent_first, 0, 1))
    choice = choice.astype(jnp.int32)

    def with_second():
        return pick(choice, (sent, other, arrived, swap(other)), members, levels)

    def without_second():
        return pick(choice, (sent, other, arrived), members, levels)

    picked = lax.cond(here_both | sent_both, with_second, without_second)
    return (*picked, overturn, clone_weight)


def solution(mesh):
    volume = P("member", None, "gridy", "gridx")
    in_specs = (volume,) * 4 + (P("member", "gridy", "gridx"), P("gridy", "gridx"), P("member"))
    out_specs = (volume,) * 4 + (P("member", "gridy", "gridx"), P("member", None, "gridy"), P("member"))
    return jax.shard_map(shards, mesh=mesh, in_specs=in_specs, out_specs=out_specs, check_vma=False)
```

```python
import functools

import jax
import jax.numpy as jnp
from jax import lax
from jax.experimental import pallas as pl
from jax.experimental.pallas import tpu as pltpu
from jax.sharding import PartitionSpec as P

STEPS = 2
ITERS = 3

ALPHA_T = 0.8
BETA_S = 0.6
PRESS_K = 0.25
STEP_DT = 0.1
KAPPA = 0.1
VISCOSITY = 0.1
DRAG_K = 0.05
CORI_K = 1.0
SURF_C = 4.0
DIV_K = 0.5
GRAV_K = 0.5

ADV = STEP_DT * 0.5
DIV = DIV_K * 0.5
GRAV = GRAV_K * 0.5

WIDE = 10
TOP = 24
CHUNK = 16
LANE = 128
PER_GROUP = 11
PAIRS = [(a, b) for a in range(4) for b in range(a, 4)]
SUMS = 6 + 6 * len(PAIRS)
SUM_ROWS = -(-SUMS // 8) * 8
SUM_LANES = SUM_ROWS // 8
VMEM_LIMIT = 24 * 1024 * 1024


def rim_place(plane):
    group, place = divmod(plane, PER_GROUP)
    if place < 6:
        return group, 0, (2 * place + 1) * WIDE
    return group, 1, (2 * (place - 6) + 2) * WIDE


def groups_of(planes):
    return -(-planes // PER_GROUP)


def lanes_like(shape):
    return lax.broadcasted_iota(jnp.int32, shape, len(shape) - 1)


def load_plane(fields, m, plane, levels):
    if plane < 4 * levels:
        return fields[plane // levels][m, plane % levels]
    if plane == 4 * levels:
        return fields[4][m]
    return fields[5][...].astype(jnp.float32)


def pack_kernel(levels, temp, salt, uvel, vvel, eta, mask, to_west, to_east, to_north, to_south):
    members, _, rows, cols = temp.shape
    planes = 4 * levels + 2
    fields = (temp, salt, uvel, vvel, eta, mask)
    lane = lanes_like((rows, LANE))
    for m in range(members):
        west_parts = [None] * groups_of(planes)
        east_parts = [None] * groups_of(planes)
        for plane in range(planes):
            value = load_plane(fields, m, plane, levels)
            group, _, start = rim_place(plane)
            both = jnp.where(lane < WIDE, value[:, :LANE], value[:, cols - LANE :])
            both = pltpu.roll(both, start, 1)
            is_west = (lane >= start) & (lane < start + WIDE)
            is_east = (lane >= start - WIDE) & (lane < start)
            zero = jnp.zeros_like(both)
            west_parts[group] = jnp.where(is_west, both, zero if west_parts[group] is None else west_parts[group])
            east_parts[group] = jnp.where(is_east, both, zero if east_parts[group] is None else east_parts[group])
            to_south[m, plane * WIDE : (plane + 1) * WIDE, :] = value[:WIDE]
            to_north[m, plane * WIDE : (plane + 1) * WIDE, :] = value[rows - WIDE :]
        for group in range(groups_of(planes)):
            where = slice(group * LANE, (group + 1) * LANE)
            to_west[m, :, where] = west_parts[group]
            to_east[m, :, where] = east_parts[group]


def whole(count):
    return [pl.BlockSpec(memory_space=pltpu.VMEM)] * count


def pack_rims(temp, salt, uvel, vvel, eta, mask):
    members, levels, rows, cols = temp.shape
    planes = 4 * levels + 2
    wide = groups_of(planes) * LANE
    row_pack = -(-planes * WIDE // 8) * 8
    side = jax.ShapeDtypeStruct((members, rows, wide), jnp.float32)
    line = jax.ShapeDtypeStruct((members, row_pack, cols), jnp.float32)
    return pl.pallas_call(
        functools.partial(pack_kernel, levels),
        out_shape=(side, side, line, line),
        in_specs=whole(6),
        out_specs=tuple(whole(4)),
        compiler_params=pltpu.CompilerParams(vmem_limit_bytes=VMEM_LIMIT),
        name="pack_rims",
    )(temp, salt, uvel, vvel, eta, mask)


def east_west(value):
    width = value.shape[-1]
    return pltpu.roll(value, width - 1, 1), pltpu.roll(value, 1, 1)


def chunks(first, last):
    return [(a, min(a + CHUNK, last)) for a in range(first, last, CHUNK)]


def assemble(ext, fields, rims, m, levels):
    from_east, from_west, from_north, from_south, north_sides, south_sides = rims
    planes = 4 * levels + 2
    rows, cols = fields[5].shape
    wide = groups_of(planes) * LANE
    for group in range(groups_of(planes)):
        where = slice(group * LANE, (group + 1) * LANE)
        where_west = slice(wide + group * LANE, wide + (group + 1) * LANE)
        bands = [(TOP - CHUNK, south_sides[m, :, where], south_sides[m, :, where_west])]
        for a in range(0, rows, CHUNK):
            bands.append((TOP + a, from_east[m, a : a + CHUNK, where], from_west[m, a : a + CHUNK, where]))
        bands.append((TOP + rows, north_sides[m, :, where], north_sides[m, :, where_west]))
        for at, east, west in bands:
            odd = ((lanes_like(east.shape) // WIDE) & 1) == 1
            joined = (jnp.where(odd, east, west), jnp.where(odd, west, east))
            for plane in range(group * PER_GROUP, min((group + 1) * PER_GROUP, planes)):
                _, kind, offset = rim_place(plane)
                ext[plane, at : at + CHUNK, cols : cols + LANE] = pltpu.roll(joined[kind], LANE - offset, 1)
    for plane in range(planes):
        ext[plane, TOP : TOP + rows, :cols] = load_plane(fields, m, plane, levels)
        ext[plane, TOP - WIDE : TOP, :cols] = from_south[m, plane * WIDE : (plane + 1) * WIDE, :]
        ext[plane, TOP + rows : TOP + rows + WIDE, :cols] = from_north[m, plane * WIDE : (plane + 1) * WIDE, :]


def fill_rows(turn, inside, first_row, total_rows):
    shape = (CHUNK, turn.shape[1])
    for a in range(0, turn.shape[0], CHUNK):
        row = first_row + (a - TOP) + lax.broadcasted_iota(jnp.int32, shape, 0)
        latitude = row.astype(jnp.float32) + 0.5
        turn[a : a + CHUNK, :] = STEP_DT * CORI_K * (2.0 * latitude / total_rows - 1.0)
        inside[a : a + CHUNK, :] = jnp.where((row >= 0) & (row < total_rows), 1.0, 0.0)


KEPT = ["tu", "tv", "q", "v0", "v1", "v2"]
KEEP_FLOW = 1.0 - STEP_DT * DRAG_K - 4.0 * VISCOSITY
KEEP_TRACER = 1.0 - 4.0 * KAPPA
PRESS_SCALE = PRESS_K * 0.5 * STEP_DT


class Planes:
    def __init__(self, levels, rows, turn, inside):
        self.levels, self.rows, self.turn, self.inside = levels, rows, turn, inside
        self.views = {}

    def add(self, ref, names, lead=()):
        for i, name in enumerate(names):
            self.views[name] = ref.at[lead + (i,)]

    def get(self, name, a, b):
        return self.views[name][a:b, :]

    def put(self, name, a, b, value):
        self.views[name][a:b, :] = value

    def sides(self, name, a, b):
        here = self.get(name, a, b)
        east, west = east_west(here)
        return here, east, west, self.get(name, a + 1, b + 1), self.get(name, a - 1, b - 1)

    def slopes(self, name, a, b):
        _, east, west, north, south = self.sides(name, a, b)
        return east - west, north - south

    def around(self, name, a, b):
        here, east, west, north, south = self.sides(name, a, b)
        return here, (east + west) + (north + south)

    def main(self):
        return chunks(TOP, TOP + self.rows)

    def near(self):
        return [(TOP - 8, TOP)] + self.main() + [(TOP + self.rows, TOP + self.rows + 8)]

    def masked(self, a, b, value):
        if a >= TOP and b <= TOP + self.rows:
            return value
        return self.inside[a:b, :] * value

    def divergence(self, u_name, v_name, a, b):
        east, west = east_west(self.get(u_name, a, b))
        return DIV * ((east - west) + (self.get(v_name, a + 1, b + 1) - self.get(v_name, a - 1, b - 1)))

    def flow(self, u_name, v_name, press, out_u, out_v, a, b):
        ocean, turn = self.get("ocean", a, b), self.turn[a:b, :]
        u, around_u = self.around(u_name, a, b)
        v, around_v = self.around(v_name, a, b)
        push_u, push_v = turn * v, turn * u
        if press:
            slope_x, slope_y = self.slopes(press, a, b)
            push_u, push_v = push_u - slope_x, push_v + slope_y
        self.put(out_u, a, b, ocean * ((KEEP_FLOW * u + VISCOSITY * around_u) + push_u))
        self.put(out_v, a, b, ocean * ((KEEP_FLOW * v + VISCOSITY * around_v) - push_v))

    def powers(self, first, second, third):
        for a, b in self.near():
            self.put(second, a, b, self.masked(a, b, self.around(first, a, b)[1]))
        for a, b in self.near():
            value = self.around(second, a, b)[1] - 4.0 * self.get(first, a, b)
            self.put(third, a, b, self.masked(a, b, value))

    def next_right_side(self, u_name, v_name, eta_name, press, out_name):
        for a, b in self.near():
            self.flow(u_name, v_name, press, "t2u", "t2v", a, b)
        for a, b in self.near():
            div = self.divergence("t2u", "t2v", a, b)
            value = self.get(eta_name, a, b) - div if eta_name else -div
            self.put(out_name, a, b, self.masked(a, b, value))


def scaled(factor, value):
    return value if factor == 1.0 else factor * value


def surface_start(ext, work):
    levels = work.levels
    low, high = TOP - CHUNK, TOP + work.rows + CHUNK
    for a, b in chunks(low, high):
        su = sv = sp = None
        for l in range(levels):
            factor = PRESS_SCALE * (levels - l)
            dens = (factor * BETA_S) * ext[levels + l, a:b, :] - (factor * ALPHA_T) * ext[l, a:b, :]
            work.put("d%d" % l, a, b, dens)
            u, v = ext[2 * levels + l, a:b, :], ext[3 * levels + l, a:b, :]
            su, sv, sp = (u, v, dens) if l == 0 else (su + u, sv + v, sp + dens)
        work.put("su", a, b, su)
        work.put("sv", a, b, sv)
        work.put("sp", a, b, sp)
    for a, b in work.near():
        carried = None
        for l in range(levels):
            slope_x, slope_y = work.slopes("d%d" % l, a, b)
            term = ext[2 * levels + l, a:b, :] * slope_x + ext[3 * levels + l, a:b, :] * slope_y
            carried = term if l == 0 else carried + term
        here, around = work.around("sp", a, b)
        work.put("q", a, b, work.get("ocean", a, b) * ((KEEP_TRACER * here + KAPPA * around) - ADV * carried))
    for a, b in chunks(low, high):
        work.flow("su", "sv", "sp", "tu", "tv", a, b)
    for a, b in work.near():
        work.put("v0", a, b, work.masked(a, b, work.get("eta", a, b) - work.divergence("tu", "tv", a, b)))


SUM_NAMES = ["su", "sv", "sp", "v3", "pu", "pv", "t2u", "t2v"] + ["w%d_%d" % (i, k) for i in range(4) for k in range(4)]
SOURCE_LANE = LANE - 8


def sums_kernel(levels, total_rows, place, source, *refs):
    fields, rims, out, kept = refs[:6], refs[6:12], refs[12], refs[13]
    planes, turn, inside, red = refs[14:]
    members = fields[0].shape[0]
    rows, cols = fields[5].shape
    fill_rows(turn, inside, place[0], total_rows)
    red[...] = jnp.zeros_like(red)

    def one(m, carry):
        ext = kept.at[m]
        work = Planes(levels, rows, turn, inside)
        work.add(planes, SUM_NAMES + ["d%d" % l for l in range(levels)])
        work.add(kept, ["ext%d" % i for i in range(4 * levels)] + ["eta", "ocean"] + KEPT, (m,))
        assemble(ext, fields, rims, m, levels)
        surface_start(ext, work)
        work.powers("v0", "v1", "v2")
        for a, b in work.main():
            work.put("v3", a, b, work.around("v2", a, b)[1])
        work.next_right_side("tu", "tv", None, "q", "w0_0")
        for k in range(1, 4):
            name = "v%d" % (k - 1)
            for a, b in work.near():
                ocean = work.get("ocean", a, b)
                slope_x, slope_y = work.slopes(name, a, b)
                work.put("pu", a, b, scaled(-levels * GRAV, ocean * slope_x))
                work.put("pv", a, b, scaled(-levels * GRAV, ocean * slope_y))
            work.next_right_side("pu", "pv", name, None, "w0_%d" % k)
        for k in range(4):
            work.powers("w0_%d" % k, "w1_%d" % k, "w2_%d" % k)
            for a, b in work.main():
                work.put("w3_%d" % k, a, b, work.around("w2_%d" % k, a, b)[1])

        def put_sums(at, first, second, pairs):
            totals = [None] * len(pairs)
            for a in range(TOP, TOP + rows, 8):
                xs = [work.get(name, a, a + 8)[:, :cols] for name in first]
                ys = [work.get(name, a, a + 8)[:, :cols] for name in second]
                for p, (i, j) in enumerate(pairs):
                    term = xs[i] * ys[j]
                    totals[p] = term if totals[p] is None else totals[p] + term
            for p, total in enumerate(totals):
                folded = total[:, :LANE]
                for c in range(LANE, cols, LANE):
                    folded = folded + total[:, c : c + LANE]
                red[m, at + p : at + p + 1, :] = jnp.sum(folded, axis=0, keepdims=True)

        for i in range(6):
            low, high = i // 2, i - i // 2
            put_sums(i, ["v%d" % low], ["v%d" % high], [(0, 0)])
            names = [["w%d_%d" % (which, k) for k in range(4)] for which in (low, high)]
            put_sums(6 + i * len(PAIRS), names[0], names[1], PAIRS)
        return carry

    lax.fori_loop(0, members, one, 0)
    lane = lanes_like((8, LANE))
    tile = jnp.zeros((8, LANE), jnp.float32)
    for m in range(members):
        total = jnp.sum(red[m], axis=1, keepdims=True)
        for q in range(SUM_LANES):
            tile = jnp.where(lane == m * SUM_LANES + q, total[8 * q : 8 * q + 8], tile)
        tile = jnp.where(lane == SOURCE_LANE + m, source[m].astype(jnp.float32), tile)
    for i in range(out.shape[0]):
        out[i] = tile


def plane_shape(rows, cols):
    return (2 * TOP + rows, cols + LANE)


def local_sums(place, source, fields, rims, total_rows, copies):
    members, levels, rows, cols = fields[0].shape
    assert members * SUM_LANES <= SOURCE_LANE and members <= 8
    shape = plane_shape(rows, cols)
    kept = (members, 4 * levels + 2 + len(KEPT)) + shape
    return pl.pallas_call(
        functools.partial(sums_kernel, levels, total_rows),
        out_shape=(jax.ShapeDtypeStruct((copies, 8, LANE), jnp.float32), jax.ShapeDtypeStruct(kept, jnp.float32)),
        in_specs=[pl.BlockSpec(memory_space=pltpu.SMEM)] * 2 + whole(12),
        out_specs=tuple(whole(2)),
        scratch_shapes=[
            pltpu.VMEM((len(SUM_NAMES) + levels,) + shape, jnp.float32),
            pltpu.VMEM(shape, jnp.float32),
            pltpu.VMEM(shape, jnp.float32),
            pltpu.VMEM((members, SUM_ROWS, LANE), jnp.float32),
        ],
        compiler_params=pltpu.CompilerParams(vmem_limit_bytes=VMEM_LIMIT),
        cost_estimate=pl.CostEstimate(flops=10**8, bytes_accessed=4 * 10**6, transcendentals=0),
        name="local_sums",
    )(place, source, *fields, *rims)


def krylov(moment):
    n00, n01, n11, n12, n22, x22 = moment
    n02 = n11 - 4.0 * n00
    main, near = 1.0 + 4.0 * SURF_C, SURF_C
    g00 = main * n00 - near * n01
    g01 = main * n01 - near * n11
    g02 = main * n02 - near * n12
    g11 = main * n11 - near * (n12 + 4.0 * n01)
    g12 = main * n12 - near * (n22 + 4.0 * n02)
    g22 = main * n22 - near * x22
    l1, l2 = g01 / g00, g02 / g00
    d1 = g11 - l1 * g01
    d1 = jnp.where(d1 > 3e-7 * g11, d1, jnp.inf)
    e = g12 - l1 * g02
    l12 = e / d1
    d2 = g22 - l2 * g02 - l12 * e
    d2 = jnp.where(d2 > 3e-7 * g22, d2, jnp.inf)
    z0 = n00
    z1 = n01 - l1 * z0
    z2 = n02 - l2 * z0 - l12 * z1
    y2 = z2 / d2
    y1 = z1 / d1 - l12 * y2
    y0 = z0 / g00 - l1 * y1 - l2 * y2
    return [y0, y1, y2]


def weights(read):
    first = krylov([read(i) for i in range(6)])
    lifted = [None] + first
    second = []
    for i in range(6):
        total = None
        for p, (a, b) in enumerate(PAIRS):
            term = read(6 + i * len(PAIRS) + p)
            for k in (a, b):
                if k:
                    term = term * lifted[k]
            if a != b:
                term = 2.0 * term
            total = term if total is None else total + term
        second.append(total)
    return first, krylov(second)


RUN_NAMES = ["pu", "pv", "t2u", "t2v", "eta1", "w0", "w1", "w2", "eta2", "p", "p2", "gu1", "gv1", "gu2", "gv2"]


def advance_kernel(levels, total_rows, is_first, place, tiles, kept, out, zonal, planes, after, turn, inside, staged, sums, sem):
    rows, cols = out.shape[1:]
    members = kept.shape[0]
    grid = tiles.shape[0] // 2
    side = place[1]
    total = tiles[side * grid]
    for i in range(1, grid):
        total = total + tiles[side * grid + i]
    staged[0] = total
    staged[1] = tiles[(1 - side) * grid]
    copy = pltpu.make_async_copy(staged, sums, sem)
    copy.start()
    fill_rows(turn, inside, place[0], total_rows)
    zonal[...] = jnp.zeros_like(zonal)
    copy.wait()
    wanted = (side * members).astype(jnp.float32)
    is_zero = (sums[1, 0, SOURCE_LANE] == wanted) | (sums[1, 0, SOURCE_LANE + 1] == wanted)
    member = jnp.where(is_zero, 0, 1) if is_first else jnp.where(is_zero, 1, 0)
    ext = kept.at[member]
    work = Planes(levels, rows, turn, inside)
    work.add(planes, RUN_NAMES)
    work.add(kept, ["ext%d" % i for i in range(4 * levels)] + ["eta", "ocean"] + KEPT, (member,))

    def read(i):
        return jnp.full((1, 1), sums[0, i % 8, member * SUM_LANES + i // 8], jnp.float32)

    def combine(factors, names, out_name):
        for a, b in work.near():
            value = None
            for factor, name in zip(factors, names):
                term = factor * work.get(name, a, b)
                value = term if value is None else value + term
            work.put(out_name, a, b, value)

    first, second = weights(read)
    combine(first, ("v0", "v1", "v2"), "eta1")
    for a, b in work.near():
        ocean = work.get("ocean", a, b)
        slope_x, slope_y = work.slopes("eta1", a, b)
        slope_x, slope_y = GRAV * ocean * slope_x, GRAV * ocean * slope_y
        work.put("gu1", a, b, slope_x)
        work.put("gv1", a, b, slope_y)
        work.put("pu", a, b, work.get("tu", a, b) - levels * slope_x)
        work.put("pv", a, b, work.get("tv", a, b) - levels * slope_y)
    work.next_right_side("pu", "pv", "eta1", "q", "w0")
    work.powers("w0", "w1", "w2")
    combine(second, ("w0", "w1", "w2"), "eta2")
    for a, b in work.main():
        ocean = work.get("ocean", a, b)
        slope_x, slope_y = work.slopes("eta2", a, b)
        work.put("gu2", a, b, GRAV * ocean * slope_x)
        work.put("gv2", a, b, GRAV * ocean * slope_y)
        out[4 * levels, a - TOP : b - TOP, :] = work.get("eta2", a, b)[:, :cols]
    low, high = TOP - 8, TOP + rows + 8
    for a, b in chunks(TOP - CHUNK, TOP + rows + CHUNK):
        work.put("p", a, b, jnp.zeros((b - a, cols + LANE), jnp.float32))
        work.put("p2", a, b, jnp.zeros((b - a, cols + LANE), jnp.float32))

    def step(ref, l, press, a, b, width):
        def of(view):
            here = view[a:b, :]
            east, west = east_west(here)
            return here[:, :width], east[:, :width], west[:, :width], view[a + 1 : b + 1, :width], view[a - 1 : b - 1, :width]

        ocean = work.views["ocean"][a:b, :width]
        coriolis = turn[a:b, :width]
        u, east, west, north, south = of(ref.at[2 * levels + l])
        around_u = (east + west) + (north + south)
        v, east, west, north, south = of(ref.at[3 * levels + l])
        around_v = (east + west) + (north + south)
        _, east, west, north, south = of(work.views[press])
        new_u = ocean * ((KEEP_FLOW * u + VISCOSITY * around_u) + (coriolis * v - (east - west)))
        new_v = ocean * ((KEEP_FLOW * v + VISCOSITY * around_v) - (coriolis * u + (north - south)))
        flow_u, flow_v = ADV * u, ADV * v
        results = []
        for at in (l, levels + l):
            here, east, west, north, south = of(ref.at[at])
            carried = flow_u * (east - west) + flow_v * (north - south)
            spread = KEEP_TRACER * here + KAPPA * ((east + west) + (north + south))
            results.append(ocean * (spread - carried))
        return results[0], results[1], new_u, new_v

    def add_press(ref, l, press, a, b):
        dens = (PRESS_SCALE * BETA_S) * ref[levels + l, a:b, :] - (PRESS_SCALE * ALPHA_T) * ref[l, a:b, :]
        work.put(press, a, b, work.get(press, a, b) + dens)

    def level(l, carry):
        for a in range(TOP - CHUNK, TOP + rows + CHUNK, 8):
            add_press(ext, l, "p", a, a + 8)
        for a in range(low, high, 8):
            temp, salt, u, v = step(ext, l, "p", a, a + 8, cols + LANE)
            after[l, a : a + 8, :] = temp
            after[levels + l, a : a + 8, :] = salt
            after[2 * levels + l, a : a + 8, :] = u - work.get("gu1", a, a + 8)
            after[3 * levels + l, a : a + 8, :] = v - work.get("gv1", a, a + 8)
        for a in range(low, high, 8):
            add_press(after, l, "p2", a, a + 8)
        for a in range(TOP, TOP + rows, 8):
            temp, salt, u, v = step(after, l, "p2", a, a + 8, cols)
            here = slice(a - TOP, a - TOP + 8)
            v = v - work.get("gv2", a, a + 8)[:, :cols]
            out[l, here, :] = temp
            out[levels + l, here, :] = salt
            out[2 * levels + l, here, :] = u - work.get("gu2", a, a + 8)[:, :cols]
            out[3 * levels + l, here, :] = v
            row_sum = jnp.sum(v, axis=1, keepdims=True)
            zonal[here, :] = jnp.where(lanes_like((8, LANE)) == member * levels + l, row_sum, zonal[here, :])
        return carry

    lax.fori_loop(0, levels, level, 0)


def advance(is_first, place, tiles, kept, levels, rows, cols, total_rows):
    shape = plane_shape(rows, cols)
    return pl.pallas_call(
        functools.partial(advance_kernel, levels, total_rows, is_first),
        out_shape=(
            jax.ShapeDtypeStruct((4 * levels + 1, rows, cols), jnp.float32),
            jax.ShapeDtypeStruct((rows, LANE), jnp.float32),
        ),
        in_specs=[pl.BlockSpec(memory_space=pltpu.SMEM)] + whole(2),
        out_specs=tuple(whole(2)),
        scratch_shapes=[
            pltpu.VMEM((len(RUN_NAMES),) + shape, jnp.float32),
            pltpu.VMEM((4 * levels,) + shape, jnp.float32),
            pltpu.VMEM(shape, jnp.float32),
            pltpu.VMEM(shape, jnp.float32),
            pltpu.VMEM((2, 8, LANE), jnp.float32),
            pltpu.SMEM((2, 8, LANE), jnp.float32),
            pltpu.SemaphoreType.DMA,
        ],
        compiler_params=pltpu.CompilerParams(vmem_limit_bytes=VMEM_LIMIT),
        cost_estimate=pl.CostEstimate(flops=10**8, bytes_accessed=4 * 10**6, transcendentals=0),
        name="advance",
    )(place, tiles, kept)


def pick_kernel(levels, choice, *refs):
    count = len(refs) - 6
    sources, outs, sem = refs[:count], refs[count : count + 5], refs[count + 5]
    slots = outs[0].shape[0]

    def parts(s, source):
        for f in range(4):
            yield source.at[pl.ds(f * levels, levels)], outs[f].at[s]
        yield source.at[4 * levels], outs[4].at[s]

    for s in range(slots):
        for k in range(count):

            @pl.when(choice[s] == k)
            def _():
                for i, (source, target) in enumerate(parts(s, sources[k])):
                    pltpu.make_async_copy(source, target, sem.at[s, i]).start()

    for s in range(slots):
        for i, (source, target) in enumerate(parts(s, sources[0])):
            pltpu.make_async_copy(source, target, sem.at[s, i]).wait()


def pick(choice, sources, slots, levels):
    _, rows, cols = sources[0].shape
    volume = jax.ShapeDtypeStruct((slots, levels, rows, cols), jnp.float32)
    surface = jax.ShapeDtypeStruct((slots, rows, cols), jnp.float32)
    return pl.pallas_call(
        functools.partial(pick_kernel, levels),
        out_shape=(volume,) * 4 + (surface,),
        in_specs=[pl.BlockSpec(memory_space=pltpu.SMEM)] + [pl.BlockSpec(memory_space=pltpu.HBM)] * len(sources),
        out_specs=(pl.BlockSpec(memory_space=pl.ANY),) * 5,
        scratch_shapes=[pltpu.SemaphoreType.DMA((slots, 5))],
        name="pick",
    )(choice, *sources)


def shift(value, axis, by, wrap):
    count = lax.axis_size(axis)
    pairs = [(i, (i + by) % count) for i in range(count) if wrap or 0 <= i + by < count]
    return lax.ppermute(value, axis, pairs)


def exchange_rims(packed):
    to_west, to_east, to_north, to_south = packed
    rows = to_west.shape[1]
    from_east, from_west = shift(to_west, "gridx", -1, True), shift(to_east, "gridx", 1, True)
    from_north, from_south = shift(to_south, "gridy", -1, False), shift(to_north, "gridy", 1, False)
    low = jnp.concatenate([from_east[:, :CHUNK], from_west[:, :CHUNK]], axis=2)
    high = jnp.concatenate([from_east[:, rows - CHUNK :], from_west[:, rows - CHUNK :]], axis=2)
    north_sides, south_sides = shift(low, "gridy", -1, False), shift(high, "gridy", 1, False)
    return from_east, from_west, from_north, from_south, north_sides, south_sides


def from_all(tiles, axes):
    return lax.all_to_all(tiles, axes, split_axis=0, concat_axis=0, tiled=True)


def swap(value):
    return lax.ppermute(value, "member", [(0, 1), (1, 0)])


def first_and_both(wanted, side, members):
    away = wanted // members != side
    index = wanted - (1 - side) * members
    takes = [jnp.any(away & (index == m)) for m in range(members)]
    return jnp.where(takes[0], 0, 1).astype(jnp.int32), takes[0] & takes[1]


def shards(temp, salt, uvel, vvel, eta, land_mask, clone_source):
    members, levels, rows, cols = temp.shape
    assert members == 2 and lax.axis_size("member") == 2
    tile_row, side = lax.axis_index("gridy"), lax.axis_index("member")
    count_y, count_x = lax.axis_size("gridy"), lax.axis_size("gridx")
    grid = count_y * count_x
    total_rows, total_cols = rows * count_y, cols * count_x
    everywhere = ("member", "gridy", "gridx")

    place = jnp.stack([tile_row * rows, side]).astype(jnp.int32)
    fields = (temp, salt, uvel, vvel, eta, land_mask)
    rims = exchange_rims(pack_rims(*fields))
    tiles, kept = local_sums(place, clone_source, fields, rims, total_rows, 2 * grid)
    tiles = from_all(tiles, everywhere)

    sent, sent_zonal = advance(True, place, tiles, kept, levels, rows, cols, total_rows)
    arrived = swap(sent)

    def rest():
        other, other_zonal = advance(False, place, tiles, kept, levels, rows, cols, total_rows)
        zonal = jnp.transpose((sent_zonal + other_zonal)[:, : members * levels])
        zonal = from_all(jnp.broadcast_to(zonal[None], (2 * grid,) + zonal.shape), everywhere)
        zonal = zonal.reshape(2, count_y, count_x, members, levels, rows)
        overturn = jnp.cumsum(jnp.sum(zonal, axis=2), axis=3) * (1.0 / jnp.sqrt(jnp.float32(total_cols)))
        latitude = (jnp.arange(total_rows, dtype=jnp.float32) + 0.5).reshape(count_y, 1, 1, rows) / total_rows
        score = jnp.sum(overturn * latitude, axis=(1, 3, 4)) * (1.0 / jnp.sqrt(jnp.float32(levels * total_rows)))
        score = score.reshape(-1)
        weight = jnp.take(score, clone_source, axis=0) - jnp.mean(score)
        return other, overturn[side, tile_row], weight

    def nothing():
        return jnp.zeros_like(sent), jnp.zeros((members, levels, rows), jnp.float32), jnp.zeros((members,), jnp.float32)

    other, overturn, clone_weight = lax.cond(place[0] < total_rows, rest, nothing)

    their_source = tiles[(1 - side) * grid, 0, SOURCE_LANE : SOURCE_LANE + members].astype(jnp.int32)
    here_first, here_both = first_and_both(clone_source, side, members)
    sent_first, sent_both = first_and_both(their_source, 1 - side, members)
    away = clone_source // members != side
    index = clone_source % members
    choice = jnp.where(away, jnp.where(index == here_first, 2, 3), jnp.where(index == sent_first, 0, 1))
    choice = choice.astype(jnp.int32)

    def with_second():
        return pick(choice, (sent, other, arrived, swap(other)), members, levels)

    def without_second():
        return pick(choice, (sent, other, arrived), members, levels)

    picked = lax.cond(here_both | sent_both, with_second, without_second)
    return (*picked, overturn, clone_weight)


def solution(mesh):
    volume = P("member", None, "gridy", "gridx")
    in_specs = (volume,) * 4 + (P("member", "gridy", "gridx"), P("gridy", "gridx"), P("member"))
    out_specs = (volume,) * 4 + (P("member", "gridy", "gridx"), P("member", None, "gridy"), P("member"))
    return jax.shard_map(shards, mesh=mesh, in_specs=in_specs, out_specs=out_specs, check_vma=False)
```

```python
import functools

import jax
import jax.numpy as jnp
from jax import lax
from jax.experimental import pallas as pl
from jax.experimental.pallas import tpu as pltpu
from jax.sharding import PartitionSpec as P

STEPS = 2
ITERS = 3

ALPHA_T = 0.8
BETA_S = 0.6
PRESS_K = 0.25
STEP_DT = 0.1
KAPPA = 0.1
VISCOSITY = 0.1
DRAG_K = 0.05
CORI_K = 1.0
SURF_C = 4.0
DIV_K = 0.5
GRAV_K = 0.5

ADV = STEP_DT * 0.5
DIV = DIV_K * 0.5
GRAV = GRAV_K * 0.5

WIDE = 10
TOP = 24
CHUNK = 16
LANE = 128
PER_GROUP = 11
PAIRS = [(a, b) for a in range(4) for b in range(a, 4)]
SUMS = 6 + 6 * len(PAIRS)
VMEM_LIMIT = 24 * 1024 * 1024
WHOLE_VMEM = 60 * 1024 * 1024


def rim_place(plane):
    group, place = divmod(plane, PER_GROUP)
    if place < 6:
        return group, 0, (2 * place + 1) * WIDE
    return group, 1, (2 * (place - 6) + 2) * WIDE


def groups_of(planes):
    return -(-planes // PER_GROUP)


def lanes_like(shape):
    return lax.broadcasted_iota(jnp.int32, shape, len(shape) - 1)


def fetches(fields, planes_of, mask_to, sems, levels):
    members = fields[0].shape[0]
    per_member = []
    for m in range(members):
        parts = [(fields[f].at[m], planes_of(m, pl.ds(f * levels, levels))) for f in range(4)]
        parts.append((fields[4].at[m], planes_of(m, 4 * levels)))
        per_member.append([pltpu.make_async_copy(*part, sems.at[m, i]) for i, part in enumerate(parts)])
    mask_copy = pltpu.make_async_copy(fields[5], mask_to, sems.at[0, 5])
    mask_copy.start()
    for copies in per_member:
        for copy in copies:
            copy.start()
    mask_copy.wait()
    return per_member


def pack_kernel(levels, *refs):
    fields, (to_west, to_east, to_north, to_south), (held, mask, sems) = refs[:6], refs[6:10], refs[10:]
    members, _, rows, cols = held.shape
    planes = 4 * levels + 2
    copies = fetches(fields, lambda m, at: held.at[m, at], mask, sems, levels)
    lane = lanes_like((rows, LANE))
    for m in range(members):
        for copy in copies[m]:
            copy.wait()
        west_parts = [None] * groups_of(planes)
        east_parts = [None] * groups_of(planes)
        for plane in range(planes):
            value = held[m, plane] if plane < planes - 1 else mask[...].astype(jnp.float32)
            group, _, start = rim_place(plane)
            both = jnp.where(lane < WIDE, value[:, :LANE], value[:, cols - LANE :])
            both = pltpu.roll(both, start, 1)
            is_west = (lane >= start) & (lane < start + WIDE)
            is_east = (lane >= start - WIDE) & (lane < start)
            zero = jnp.zeros_like(both)
            west_parts[group] = jnp.where(is_west, both, zero if west_parts[group] is None else west_parts[group])
            east_parts[group] = jnp.where(is_east, both, zero if east_parts[group] is None else east_parts[group])
            to_south[m, plane * WIDE : (plane + 1) * WIDE, :] = value[:WIDE]
            to_north[m, plane * WIDE : (plane + 1) * WIDE, :] = value[rows - WIDE :]
        for group in range(groups_of(planes)):
            where = slice(group * LANE, (group + 1) * LANE)
            to_west[m, :, where] = west_parts[group]
            to_east[m, :, where] = east_parts[group]


def whole(count):
    return [pl.BlockSpec(memory_space=pltpu.VMEM)] * count


def in_hbm(count):
    return [pl.BlockSpec(memory_space=pltpu.HBM)] * count


def in_smem(count):
    return [pl.BlockSpec(memory_space=pltpu.SMEM)] * count


def pack_rims(temp, salt, uvel, vvel, eta, mask):
    members, levels, rows, cols = temp.shape
    planes = 4 * levels + 2
    wide = groups_of(planes) * LANE
    row_pack = -(-planes * WIDE // 8) * 8
    side = jax.ShapeDtypeStruct((members, rows, wide), jnp.float32)
    line = jax.ShapeDtypeStruct((members, row_pack, cols), jnp.float32)
    return pl.pallas_call(
        functools.partial(pack_kernel, levels),
        out_shape=(side, side, line, line),
        in_specs=in_hbm(6),
        out_specs=tuple(whole(4)),
        scratch_shapes=[
            pltpu.VMEM((members, planes - 1, rows, cols), jnp.float32),
            pltpu.VMEM((rows, cols), jnp.int32),
            pltpu.SemaphoreType.DMA((members, 6)),
        ],
        compiler_params=pltpu.CompilerParams(vmem_limit_bytes=WHOLE_VMEM),
        name="pack_rims",
    )(temp, salt, uvel, vvel, eta, mask)


def east_west(value):
    width = value.shape[-1]
    return pltpu.roll(value, width - 1, 1), pltpu.roll(value, 1, 1)


def chunks(first, last):
    return [(a, min(a + CHUNK, last)) for a in range(first, last, CHUNK)]


def assemble(ext, mask, rims, m, levels, keep_north, keep_south):
    from_east, from_west, from_north, from_south, north_sides, south_sides = rims
    planes = 4 * levels + 2
    rows, cols = mask.shape
    wide = groups_of(planes) * LANE
    for group in range(groups_of(planes)):
        where = slice(group * LANE, (group + 1) * LANE)
        where_west = slice(wide + group * LANE, wide + (group + 1) * LANE)
        bands = [(TOP - CHUNK, keep_south * south_sides[m, :, where], keep_south * south_sides[m, :, where_west])]
        for a in range(0, rows, CHUNK):
            bands.append((TOP + a, from_east[m, a : a + CHUNK, where], from_west[m, a : a + CHUNK, where]))
        bands.append((TOP + rows, keep_north * north_sides[m, :, where], keep_north * north_sides[m, :, where_west]))
        for at, east, west in bands:
            odd = ((lanes_like(east.shape) // WIDE) & 1) == 1
            joined = (jnp.where(odd, east, west), jnp.where(odd, west, east))
            for plane in range(group * PER_GROUP, min((group + 1) * PER_GROUP, planes)):
                _, kind, offset = rim_place(plane)
                ext[plane, at : at + CHUNK, cols : cols + LANE] = pltpu.roll(joined[kind], LANE - offset, 1)
    ext[planes - 1, TOP : TOP + rows, :cols] = mask[...].astype(jnp.float32)
    for plane in range(planes):
        at = slice(plane * WIDE, (plane + 1) * WIDE)
        ext[plane, TOP - WIDE : TOP, :cols] = keep_south * from_south[m, at, :]
        ext[plane, TOP + rows : TOP + rows + WIDE, :cols] = keep_north * from_north[m, at, :]


def fill_rows(turn, inside, first_row, total_rows):
    shape = (CHUNK, turn.shape[1])
    for a in range(0, turn.shape[0], CHUNK):
        row = first_row + (a - TOP) + lax.broadcasted_iota(jnp.int32, shape, 0)
        latitude = row.astype(jnp.float32) + 0.5
        turn[a : a + CHUNK, :] = STEP_DT * CORI_K * (2.0 * latitude / total_rows - 1.0)
        inside[a : a + CHUNK, :] = jnp.where((row >= 0) & (row < total_rows), 1.0, 0.0)


KEPT = ["tu", "tv", "q", "v0", "v1", "v2"]
KEEP_FLOW = 1.0 - STEP_DT * DRAG_K - 4.0 * VISCOSITY
KEEP_TRACER = 1.0 - 4.0 * KAPPA
PRESS_SCALE = PRESS_K * 0.5 * STEP_DT


class Planes:
    def __init__(self, levels, rows, turn, inside):
        self.levels, self.rows, self.turn, self.inside = levels, rows, turn, inside
        self.views = {}

    def add(self, ref, names, lead=()):
        for i, name in enumerate(names):
            self.views[name] = ref.at[lead + (i,)]

    def get(self, name, a, b):
        return self.views[name][a:b, :]

    def put(self, name, a, b, value):
        self.views[name][a:b, :] = value

    def sides(self, name, a, b):
        here = self.get(name, a, b)
        east, west = east_west(here)
        return here, east, west, self.get(name, a + 1, b + 1), self.get(name, a - 1, b - 1)

    def slopes(self, name, a, b):
        _, east, west, north, south = self.sides(name, a, b)
        return east - west, north - south

    def around(self, name, a, b):
        here, east, west, north, south = self.sides(name, a, b)
        return here, (east + west) + (north + south)

    def main(self):
        return chunks(TOP, TOP + self.rows)

    def near(self):
        return [(TOP - 8, TOP)] + self.main() + [(TOP + self.rows, TOP + self.rows + 8)]

    def masked(self, a, b, value):
        if a >= TOP and b <= TOP + self.rows:
            return value
        return self.inside[a:b, :] * value

    def divergence(self, u_name, v_name, a, b):
        east, west = east_west(self.get(u_name, a, b))
        return DIV * ((east - west) + (self.get(v_name, a + 1, b + 1) - self.get(v_name, a - 1, b - 1)))

    def flow(self, u_name, v_name, press, out_u, out_v, a, b):
        ocean, turn = self.get("ocean", a, b), self.turn[a:b, :]
        u, around_u = self.around(u_name, a, b)
        v, around_v = self.around(v_name, a, b)
        push_u, push_v = turn * v, turn * u
        if press:
            slope_x, slope_y = self.slopes(press, a, b)
            push_u, push_v = push_u - slope_x, push_v + slope_y
        self.put(out_u, a, b, ocean * ((KEEP_FLOW * u + VISCOSITY * around_u) + push_u))
        self.put(out_v, a, b, ocean * ((KEEP_FLOW * v + VISCOSITY * around_v) - push_v))

    def powers(self, first, second, third):
        for a, b in self.near():
            self.put(second, a, b, self.masked(a, b, self.around(first, a, b)[1]))
        for a, b in self.near():
            value = self.around(second, a, b)[1] - 4.0 * self.get(first, a, b)
            self.put(third, a, b, self.masked(a, b, value))

    def next_right_side(self, u_name, v_name, eta_name, press, out_name):
        for a, b in self.near():
            self.flow(u_name, v_name, press, "t2u", "t2v", a, b)
        for a, b in self.near():
            div = self.divergence("t2u", "t2v", a, b)
            value = self.get(eta_name, a, b) - div if eta_name else -div
            self.put(out_name, a, b, self.masked(a, b, value))


def scaled(factor, value):
    return value if factor == 1.0 else factor * value


def surface_start(ext, work):
    levels = work.levels
    low, high = TOP - CHUNK, TOP + work.rows + CHUNK
    for a, b in chunks(low, high):
        su = sv = sp = None
        for l in range(levels):
            factor = PRESS_SCALE * (levels - l)
            dens = (factor * BETA_S) * ext[levels + l, a:b, :] - (factor * ALPHA_T) * ext[l, a:b, :]
            work.put("d%d" % l, a, b, dens)
            u, v = ext[2 * levels + l, a:b, :], ext[3 * levels + l, a:b, :]
            su, sv, sp = (u, v, dens) if l == 0 else (su + u, sv + v, sp + dens)
        work.put("su", a, b, su)
        work.put("sv", a, b, sv)
        work.put("sp", a, b, sp)
    for a, b in work.near():
        carried = None
        for l in range(levels):
            slope_x, slope_y = work.slopes("d%d" % l, a, b)
            term = ext[2 * levels + l, a:b, :] * slope_x + ext[3 * levels + l, a:b, :] * slope_y
            carried = term if l == 0 else carried + term
        here, around = work.around("sp", a, b)
        work.put("q", a, b, work.get("ocean", a, b) * ((KEEP_TRACER * here + KAPPA * around) - ADV * carried))
    for a, b in chunks(low, high):
        work.flow("su", "sv", "sp", "tu", "tv", a, b)
    for a, b in work.near():
        work.put("v0", a, b, work.masked(a, b, work.get("eta", a, b) - work.divergence("tu", "tv", a, b)))


SUM_NAMES = ["su", "sv", "sp", "v3", "pu", "pv", "t2u", "t2v"] + ["w%d_%d" % (i, k) for i in range(4) for k in range(4)]
SOURCE_LANE = LANE - 8


def sums_kernel(levels, total_rows, source, *refs):
    fields, rims, out, kept = refs[:6], refs[6:12], refs[12], refs[13]
    planes, turn, inside, red, mask, sems = refs[14:]
    members = kept.shape[0]
    rows, cols = mask.shape
    copies = fetches(fields, lambda m, at: kept.at[m, at, pl.ds(TOP, rows), pl.ds(0, cols)], mask, sems, levels)
    tile_row = lax.axis_index("gridy")
    keep_south = jnp.where(tile_row > 0, 1.0, 0.0).astype(jnp.float32)
    keep_north = jnp.where(tile_row * rows + rows < total_rows, 1.0, 0.0).astype(jnp.float32)
    fill_rows(turn, inside, tile_row * rows, total_rows)
    red[...] = jnp.zeros_like(red)
    for m in range(members):
        assemble(kept.at[m], mask, rims, m, levels, keep_north, keep_south)
    for copy in sum(copies, []):
        copy.wait()

    def one(m, carry):
        ext = kept.at[m]
        work = Planes(levels, rows, turn, inside)
        work.add(planes, SUM_NAMES + ["d%d" % l for l in range(levels)])
        work.add(kept, ["ext%d" % i for i in range(4 * levels)] + ["eta", "ocean"] + KEPT, (m,))
        surface_start(ext, work)
        work.powers("v0", "v1", "v2")
        for a, b in work.main():
            work.put("v3", a, b, work.around("v2", a, b)[1])
        work.next_right_side("tu", "tv", None, "q", "w0_0")
        for k in range(1, 4):
            name = "v%d" % (k - 1)
            for a, b in work.near():
                ocean = work.get("ocean", a, b)
                slope_x, slope_y = work.slopes(name, a, b)
                work.put("pu", a, b, scaled(-levels * GRAV, ocean * slope_x))
                work.put("pv", a, b, scaled(-levels * GRAV, ocean * slope_y))
            work.next_right_side("pu", "pv", name, None, "w0_%d" % k)
        for k in range(4):
            work.powers("w0_%d" % k, "w1_%d" % k, "w2_%d" % k)
            for a, b in work.main():
                work.put("w3_%d" % k, a, b, work.around("w2_%d" % k, a, b)[1])

        def put_sums(at, first, second, pairs):
            totals = [None] * len(pairs)
            for a in range(TOP, TOP + rows, 8):
                xs = [work.get(name, a, a + 8)[:, :cols] for name in first]
                ys = [work.get(name, a, a + 8)[:, :cols] for name in second]
                for p, (i, j) in enumerate(pairs):
                    term = xs[i] * ys[j]
                    totals[p] = term if totals[p] is None else totals[p] + term
            for p, total in enumerate(totals):
                folded = total[:, :LANE]
                for c in range(LANE, cols, LANE):
                    folded = folded + total[:, c : c + LANE]
                red[m, at + p : at + p + 1, :] = jnp.sum(folded, axis=0, keepdims=True)

        for i in range(6):
            low, high = i // 2, i - i // 2
            put_sums(i, ["v%d" % low], ["v%d" % high], [(0, 0)])
            names = [["w%d_%d" % (which, k) for k in range(4)] for which in (low, high)]
            put_sums(6 + i * len(PAIRS), names[0], names[1], PAIRS)
        return carry

    lax.fori_loop(0, members, one, 0)
    lane = lanes_like((1, LANE))
    for m in range(members):
        line = jnp.sum(jnp.transpose(red[m]), axis=0, keepdims=True)
        for slot in range(members):
            line = jnp.where(lane == SOURCE_LANE + slot, source[slot].astype(jnp.float32), line)
        for i in range(out.shape[0]):
            out[i, m : m + 1, :] = line


def plane_shape(rows, cols):
    return (2 * TOP + rows, cols + LANE)


def local_sums(source, fields, rims, total_rows, copies):
    members, levels, rows, cols = fields[0].shape
    assert SUMS <= SOURCE_LANE and members <= 8
    shape = plane_shape(rows, cols)
    kept = (members, 4 * levels + 2 + len(KEPT)) + shape
    return pl.pallas_call(
        functools.partial(sums_kernel, levels, total_rows),
        out_shape=(jax.ShapeDtypeStruct((copies, members, LANE), jnp.float32), jax.ShapeDtypeStruct(kept, jnp.float32)),
        in_specs=in_smem(1) + in_hbm(6) + whole(6),
        out_specs=tuple(whole(2)),
        scratch_shapes=[
            pltpu.VMEM((len(SUM_NAMES) + levels,) + shape, jnp.float32),
            pltpu.VMEM(shape, jnp.float32),
            pltpu.VMEM(shape, jnp.float32),
            pltpu.VMEM((members, LANE, LANE), jnp.float32),
            pltpu.VMEM((rows, cols), jnp.int32),
            pltpu.SemaphoreType.DMA((members, 6)),
        ],
        compiler_params=pltpu.CompilerParams(vmem_limit_bytes=VMEM_LIMIT),
        cost_estimate=pl.CostEstimate(flops=10**8, bytes_accessed=4 * 10**6, transcendentals=0),
        name="local_sums",
    )(source, *fields, *rims)


def krylov(moment):
    n00, n01, n11, n12, n22, x22 = moment
    n02 = n11 - 4.0 * n00
    main, near = 1.0 + 4.0 * SURF_C, SURF_C
    g00 = main * n00 - near * n01
    g01 = main * n01 - near * n11
    g02 = main * n02 - near * n12
    g11 = main * n11 - near * (n12 + 4.0 * n01)
    g12 = main * n12 - near * (n22 + 4.0 * n02)
    g22 = main * n22 - near * x22
    l1, l2 = g01 / g00, g02 / g00
    d1 = g11 - l1 * g01
    d1 = jnp.where(d1 > 3e-7 * g11, d1, jnp.inf)
    e = g12 - l1 * g02
    l12 = e / d1
    d2 = g22 - l2 * g02 - l12 * e
    d2 = jnp.where(d2 > 3e-7 * g22, d2, jnp.inf)
    z0 = n00
    z1 = n01 - l1 * z0
    z2 = n02 - l2 * z0 - l12 * z1
    y2 = z2 / d2
    y1 = z1 / d1 - l12 * y2
    y0 = z0 / g00 - l1 * y1 - l2 * y2
    return [y0, y1, y2]


def weights(read):
    first = krylov([read(i) for i in range(6)])
    lifted = [None] + first
    second = []
    for i in range(6):
        total = None
        for p, (a, b) in enumerate(PAIRS):
            term = read(6 + i * len(PAIRS) + p)
            for k in (a, b):
                if k:
                    term = term * lifted[k]
            if a != b:
                term = 2.0 * term
            total = term if total is None else total + term
        second.append(total)
    return first, krylov(second)


RUN_NAMES = ["pu", "pv", "t2u", "t2v", "eta1", "w0", "w1", "w2", "eta2", "p", "p2", "gu1", "gv1", "gu2", "gv2"]


def whether(*conditions):
    result = jnp.int32(0)
    for condition in conditions:
        result = jnp.where(condition, 1, result)
    return result


def choose(source, theirs, side, members, info):
    mine, away = side * members, (1 - side) * members
    sent = [whether(*[theirs[slot] == (mine + m).astype(jnp.float32) for slot in range(members)]) for m in range(2)]
    here = [whether(*[source[slot] == away + m for slot in range(members)]) for m in range(2)]
    first_sent, first_here = 1 - sent[0], 1 - here[0]
    for slot in range(members):
        own = jnp.where(source[slot] - mine == first_sent, 0, 1)
        far = jnp.where(source[slot] - away == first_here, 2, 3)
        info[slot] = jnp.where((source[slot] >= mine) & (source[slot] < mine + members), own, far)
    info[members] = jnp.maximum(sent[0] * sent[1], here[0] * here[1])
    info[members + 1] = jnp.int32(1)
    return first_sent


def advance_kernel(levels, total_rows, is_first, *refs):
    if is_first:
        source, tiles, kept, out, zonal, info = refs[:6]
    else:
        info, tiles, kept, zonal_before, out, spread = refs[:6]
    planes, after, turn, inside, staged, sums, sem = refs[6:13]
    rows, cols = out.shape[1:]
    members = kept.shape[0]
    grid = tiles.shape[0] // 2
    side, tile_row = lax.axis_index("member"), lax.axis_index("gridy")
    total = tiles[side * grid]
    for i in range(1, grid):
        total = total + tiles[side * grid + i]
    staged[0, 0:members, :] = total
    staged[1, 0:members, :] = tiles[(1 - side) * grid]
    copy = pltpu.make_async_copy(staged, sums, sem)
    copy.start()
    fill_rows(turn, inside, tile_row * rows, total_rows)
    if not is_first:
        zonal = refs[13]
    zonal[...] = jnp.zeros_like(zonal) if is_first else zonal_before[...]
    copy.wait()
    theirs = [sums[1, 0, SOURCE_LANE + slot] for slot in range(members)]
    if is_first:
        member = choose(source, theirs, side, members, info)
    else:
        member = whether(*[theirs[slot] == (side * members).astype(jnp.float32) for slot in range(members)])
    ext = kept.at[member]
    work = Planes(levels, rows, turn, inside)
    work.add(planes, RUN_NAMES)
    work.add(kept, ["ext%d" % i for i in range(4 * levels)] + ["eta", "ocean"] + KEPT, (member,))

    def read(i):
        return jnp.full((1, 1), sums[0, member, i], jnp.float32)

    def combine(factors, names, out_name):
        for a, b in work.near():
            value = None
            for factor, name in zip(factors, names):
                term = factor * work.get(name, a, b)
                value = term if value is None else value + term
            work.put(out_name, a, b, value)

    first, second = weights(read)
    combine(first, ("v0", "v1", "v2"), "eta1")
    for a, b in work.near():
        ocean = work.get("ocean", a, b)
        slope_x, slope_y = work.slopes("eta1", a, b)
        slope_x, slope_y = GRAV * ocean * slope_x, GRAV * ocean * slope_y
        work.put("gu1", a, b, slope_x)
        work.put("gv1", a, b, slope_y)
        work.put("pu", a, b, work.get("tu", a, b) - levels * slope_x)
        work.put("pv", a, b, work.get("tv", a, b) - levels * slope_y)
    work.next_right_side("pu", "pv", "eta1", "q", "w0")
    work.powers("w0", "w1", "w2")
    combine(second, ("w0", "w1", "w2"), "eta2")
    for a, b in work.main():
        ocean = work.get("ocean", a, b)
        slope_x, slope_y = work.slopes("eta2", a, b)
        work.put("gu2", a, b, GRAV * ocean * slope_x)
        work.put("gv2", a, b, GRAV * ocean * slope_y)
        out[4 * levels, a - TOP : b - TOP, :] = work.get("eta2", a, b)[:, :cols]
    low, high = TOP - 8, TOP + rows + 8
    for a, b in chunks(TOP - CHUNK, TOP + rows + CHUNK):
        work.put("p", a, b, jnp.zeros((b - a, cols + LANE), jnp.float32))
        work.put("p2", a, b, jnp.zeros((b - a, cols + LANE), jnp.float32))

    def step(ref, l, press, a, b, width):
        def of(view):
            here = view[a:b, :]
            east, west = east_west(here)
            return here[:, :width], east[:, :width], west[:, :width], view[a + 1 : b + 1, :width], view[a - 1 : b - 1, :width]

        ocean = work.views["ocean"][a:b, :width]
        coriolis = turn[a:b, :width]
        u, east, west, north, south = of(ref.at[2 * levels + l])
        around_u = (east + west) + (north + south)
        v, east, west, north, south = of(ref.at[3 * levels + l])
        around_v = (east + west) + (north + south)
        _, east, west, north, south = of(work.views[press])
        new_u = ocean * ((KEEP_FLOW * u + VISCOSITY * around_u) + (coriolis * v - (east - west)))
        new_v = ocean * ((KEEP_FLOW * v + VISCOSITY * around_v) - (coriolis * u + (north - south)))
        flow_u, flow_v = ADV * u, ADV * v
        results = []
        for at in (l, levels + l):
            here, east, west, north, south = of(ref.at[at])
            carried = flow_u * (east - west) + flow_v * (north - south)
            spread = KEEP_TRACER * here + KAPPA * ((east + west) + (north + south))
            results.append(ocean * (spread - carried))
        return results[0], results[1], new_u, new_v

    def add_press(ref, l, press, a, b):
        dens = (PRESS_SCALE * BETA_S) * ref[levels + l, a:b, :] - (PRESS_SCALE * ALPHA_T) * ref[l, a:b, :]
        work.put(press, a, b, work.get(press, a, b) + dens)

    def level(l, carry):
        for a in range(TOP - CHUNK, TOP + rows + CHUNK, 8):
            add_press(ext, l, "p", a, a + 8)
        for a in range(low, high, 8):
            temp, salt, u, v = step(ext, l, "p", a, a + 8, cols + LANE)
            after[l, a : a + 8, :] = temp
            after[levels + l, a : a + 8, :] = salt
            after[2 * levels + l, a : a + 8, :] = u - work.get("gu1", a, a + 8)
            after[3 * levels + l, a : a + 8, :] = v - work.get("gv1", a, a + 8)
        for a in range(low, high, 8):
            add_press(after, l, "p2", a, a + 8)
        for a in range(TOP, TOP + rows, 8):
            temp, salt, u, v = step(after, l, "p2", a, a + 8, cols)
            here = slice(a - TOP, a - TOP + 8)
            v = v - work.get("gv2", a, a + 8)[:, :cols]
            out[l, here, :] = temp
            out[levels + l, here, :] = salt
            out[2 * levels + l, here, :] = u - work.get("gu2", a, a + 8)[:, :cols]
            out[3 * levels + l, here, :] = v
            row_sum = jnp.sum(v, axis=1, keepdims=True)
            zonal[here, :] = jnp.where(lanes_like((8, LANE)) == member * levels + l, row_sum, zonal[here, :])
        return carry

    lax.fori_loop(0, levels, level, 0)
    if not is_first:
        square = jnp.concatenate([zonal[...]] + [jnp.zeros_like(zonal)] * (LANE // rows - 1), axis=0)
        turned = jnp.transpose(square)[: members * levels]
        line = turned[:levels]
        for m in range(1, members):
            line = line + pltpu.roll(turned, m * rows, 1)[m * levels : (m + 1) * levels]
        for i in range(spread.shape[0]):
            spread[i] = line


def advance(is_first, small, tiles, kept, zonal, rows, cols, total_rows):
    members, planes = kept.shape[:2]
    levels = (planes - 2 - len(KEPT)) // 4
    assert members * rows == LANE and members * levels == 8
    shape = plane_shape(rows, cols)
    zonal_shape = jax.ShapeDtypeStruct((rows, LANE), jnp.float32)
    out_shape = [jax.ShapeDtypeStruct((4 * levels + 1, rows, cols), jnp.float32)]
    if is_first:
        out_shape += [zonal_shape, jax.ShapeDtypeStruct((members + 2,), jnp.int32)]
    else:
        out_shape += [jax.ShapeDtypeStruct((tiles.shape[0], levels, members * rows), jnp.float32)]
    return pl.pallas_call(
        functools.partial(advance_kernel, levels, total_rows, is_first),
        out_shape=tuple(out_shape),
        in_specs=in_smem(1) + whole(2 if is_first else 3),
        out_specs=tuple(whole(2) + (in_smem(1) if is_first else [])),
        scratch_shapes=[
            pltpu.VMEM((len(RUN_NAMES),) + shape, jnp.float32),
            pltpu.VMEM((4 * levels,) + shape, jnp.float32),
            pltpu.VMEM(shape, jnp.float32),
            pltpu.VMEM(shape, jnp.float32),
            pltpu.VMEM((2, 8, LANE), jnp.float32),
            pltpu.SMEM((2, 8, LANE), jnp.float32),
            pltpu.SemaphoreType.DMA,
        ]
        + ([] if is_first else [pltpu.VMEM((rows, LANE), jnp.float32)]),
        compiler_params=pltpu.CompilerParams(vmem_limit_bytes=VMEM_LIMIT),
        cost_estimate=pl.CostEstimate(flops=10**8, bytes_accessed=4 * 10**6, transcendentals=0),
        name="advance",
    )(small, tiles, kept, *([] if is_first else [zonal]))


def finish_kernel(count_y, count_x, total_cols, source, spread, overturn, weight, held):
    members, levels, rows = overturn.shape
    shape = spread.shape[1:]
    total_rows = rows * count_y
    lane = lanes_like(shape)
    member_of = lane // rows
    scores = []
    for side in range(2):
        weighted = None
        for y in range(count_y):
            at = (side * count_y + y) * count_x
            total = spread[at]
            for x in range(1, count_x):
                total = total + spread[at + x]
            lines = [total[0:1]]
            for l in range(1, levels):
                lines.append(lines[-1] + total[l : l + 1])
            whole_line = jnp.concatenate(lines, axis=0) * (total_cols**-0.5)
            held[side * count_y + y] = whole_line
            latitude = ((lane - member_of * rows + y * rows).astype(jnp.float32) + 0.5) * (1.0 / total_rows)
            term = whole_line * latitude
            weighted = term if weighted is None else weighted + term
        for m in range(members):
            scores.append(jnp.sum(jnp.where(member_of == m, weighted, 0.0)) * ((levels * total_rows) ** -0.5))
    mean = sum(scores[1:], scores[0]) * (1.0 / len(scores))
    for slot in range(members):
        value = scores[0]
        for k in range(1, len(scores)):
            value = jnp.where(source[slot] == k, scores[k], value)
        weight[slot] = value - mean
    mine = held[lax.axis_index("member") * count_y + lax.axis_index("gridy")]
    for m in range(members):
        overturn[m] = mine[:, m * rows : (m + 1) * rows]


def finish(source, spread, members, rows, count_y, count_x, cols):
    levels = spread.shape[1]
    return pl.pallas_call(
        functools.partial(finish_kernel, count_y, count_x, cols * count_x),
        out_shape=(
            jax.ShapeDtypeStruct((members, levels, rows), jnp.float32),
            jax.ShapeDtypeStruct((members,), jnp.float32),
        ),
        in_specs=in_smem(1) + whole(1),
        out_specs=(whole(1)[0], in_smem(1)[0]),
        scratch_shapes=[pltpu.VMEM((2 * count_y,) + spread.shape[1:], jnp.float32)],
        compiler_params=pltpu.CompilerParams(vmem_limit_bytes=VMEM_LIMIT),
        name="finish",
    )(source, spread)


def pick_kernel(levels, choice, *refs):
    count = len(refs) - 6
    sources, outs, sem = refs[:count], refs[count : count + 5], refs[count + 5]
    slots = outs[0].shape[0]

    def parts(s, source):
        for f in range(4):
            yield source.at[pl.ds(f * levels, levels)], outs[f].at[s]
        yield source.at[4 * levels], outs[4].at[s]

    for s in range(slots):
        for k in range(count):

            @pl.when(choice[s] == k)
            def _():
                for i, (source, target) in enumerate(parts(s, sources[k])):
                    pltpu.make_async_copy(source, target, sem.at[s, i]).start()

    for s in range(slots):
        for i, (source, target) in enumerate(parts(s, sources[0])):
            pltpu.make_async_copy(source, target, sem.at[s, i]).wait()


def pick(choice, sources, slots, levels):
    _, rows, cols = sources[0].shape
    volume = jax.ShapeDtypeStruct((slots, levels, rows, cols), jnp.float32)
    surface = jax.ShapeDtypeStruct((slots, rows, cols), jnp.float32)
    return pl.pallas_call(
        functools.partial(pick_kernel, levels),
        out_shape=(volume,) * 4 + (surface,),
        in_specs=in_smem(1) + in_hbm(len(sources)),
        out_specs=tuple(in_hbm(5)),
        scratch_shapes=[pltpu.SemaphoreType.DMA((slots, 5))],
        name="pick",
    )(choice, *sources)


def shift(value, axis, by):
    count = lax.axis_size(axis)
    return lax.ppermute(value, axis, [(i, (i + by) % count) for i in range(count)])


def exchange_rims(packed):
    to_west, to_east, to_north, to_south = packed
    rows = to_west.shape[1]
    from_east, from_west = shift(to_west, "gridx", -1), shift(to_east, "gridx", 1)
    from_north, from_south = shift(to_south, "gridy", -1), shift(to_north, "gridy", 1)
    low = jnp.concatenate([from_east[:, :CHUNK], from_west[:, :CHUNK]], axis=2)
    high = jnp.concatenate([from_east[:, rows - CHUNK :], from_west[:, rows - CHUNK :]], axis=2)
    north_sides, south_sides = shift(low, "gridy", -1), shift(high, "gridy", 1)
    return from_east, from_west, from_north, from_south, north_sides, south_sides


def from_all(tiles, axes):
    return lax.all_to_all(tiles, axes, split_axis=0, concat_axis=0, tiled=True)


def swap(value):
    return lax.ppermute(value, "member", [(0, 1), (1, 0)])


def shards(temp, salt, uvel, vvel, eta, land_mask, clone_source):
    members, levels, rows, cols = temp.shape
    assert members == 2 and lax.axis_size("member") == 2
    count_y, count_x = lax.axis_size("gridy"), lax.axis_size("gridx")
    total_rows = rows * count_y
    everywhere = ("member", "gridy", "gridx")

    fields = (temp, salt, uvel, vvel, eta, land_mask)
    rims = exchange_rims(pack_rims(*fields))
    tiles, kept = local_sums(clone_source, fields, rims, total_rows, 2 * count_y * count_x)
    tiles = from_all(tiles, everywhere)

    sent, zonal, info = advance(True, clone_source, tiles, kept, None, rows, cols, total_rows)
    arrived = swap(sent)

    def rest():
        other, spread = advance(False, info, tiles, kept, zonal, rows, cols, total_rows)
        spread = from_all(spread, everywhere)
        return (other, *finish(clone_source, spread, members, rows, count_y, count_x, cols))

    def nothing():
        return jnp.zeros_like(sent), jnp.zeros((members, levels, rows), jnp.float32), jnp.zeros((members,), jnp.float32)

    other, overturn, clone_weight = lax.cond(info[members + 1] != 0, rest, nothing)

    def with_second():
        return pick(info, (sent, other, arrived, swap(other)), members, levels)

    def without_second():
        return pick(info, (sent, other, arrived), members, levels)

    picked = lax.cond(info[members] != 0, with_second, without_second)
    return (*picked, overturn, clone_weight)


def solution(mesh):
    volume = P("member", None, "gridy", "gridx")
    in_specs = (volume,) * 4 + (P("member", "gridy", "gridx"), P("gridy", "gridx"), P("member"))
    out_specs = (volume,) * 4 + (P("member", "gridy", "gridx"), P("member", None, "gridy"), P("member"))
    return jax.shard_map(shards, mesh=mesh, in_specs=in_specs, out_specs=out_specs, check_vma=False)
```

```python
import functools

import jax
import jax.numpy as jnp
from jax import lax
from jax.experimental import pallas as pl
from jax.experimental.pallas import tpu as pltpu
from jax.sharding import PartitionSpec as P

STEPS = 2
ITERS = 3

ALPHA_T = 0.8
BETA_S = 0.6
PRESS_K = 0.25
STEP_DT = 0.1
KAPPA = 0.1
VISCOSITY = 0.1
DRAG_K = 0.05
CORI_K = 1.0
SURF_C = 4.0
DIV_K = 0.5
GRAV_K = 0.5

ADV = STEP_DT * 0.5
DIV = DIV_K * 0.5
GRAV = GRAV_K * 0.5

WIDE = 10
TOP = 24
CHUNK = 16
LANE = 128
PER_GROUP = 11
PAIRS = [(a, b) for a in range(4) for b in range(a, 4)]
SUMS = 6 + 6 * len(PAIRS)
VMEM_LIMIT = 24 * 1024 * 1024
WHOLE_VMEM = 60 * 1024 * 1024


def rim_place(plane):
    group, place = divmod(plane, PER_GROUP)
    if place < 6:
        return group, 0, (2 * place + 1) * WIDE
    return group, 1, (2 * (place - 6) + 2) * WIDE


def groups_of(planes):
    return -(-planes // PER_GROUP)


def lanes_like(shape):
    return lax.broadcasted_iota(jnp.int32, shape, len(shape) - 1)


def fetches(fields, planes_of, mask_to, sems, levels):
    members = fields[0].shape[0]
    per_member = []
    for m in range(members):
        parts = [(fields[f].at[m], planes_of(m, pl.ds(f * levels, levels))) for f in range(4)]
        parts.append((fields[4].at[m], planes_of(m, 4 * levels)))
        per_member.append([pltpu.make_async_copy(*part, sems.at[m, i]) for i, part in enumerate(parts)])
    mask_copy = pltpu.make_async_copy(fields[5], mask_to, sems.at[0, 5])
    mask_copy.start()
    for copies in per_member:
        for copy in copies:
            copy.start()
    mask_copy.wait()
    return per_member


def pack_kernel(levels, *refs):
    fields, (to_west, to_east, rows_first, rows_second), (held, mask, sems) = refs[:6], refs[6:10], refs[10:]
    members, _, rows, cols = held.shape
    planes = 4 * levels + 2
    copies = fetches(fields, lambda m, at: held.at[m, at], mask, sems, levels)
    lane = lanes_like((rows, LANE))
    even = lax.broadcasted_iota(jnp.int32, (WIDE, cols), 0) * 0 + lax.rem(lax.axis_index("gridy"), 2) == 0
    for m in range(members):
        for copy in copies[m]:
            copy.wait()
        west_parts = [None] * groups_of(planes)
        east_parts = [None] * groups_of(planes)
        for plane in range(planes):
            value = held[m, plane] if plane < planes - 1 else mask[...].astype(jnp.float32)
            group, _, start = rim_place(plane)
            both = jnp.where(lane < WIDE, value[:, :LANE], value[:, cols - LANE :])
            both = pltpu.roll(both, start, 1)
            is_west = (lane >= start) & (lane < start + WIDE)
            is_east = (lane >= start - WIDE) & (lane < start)
            zero = jnp.zeros_like(both)
            west_parts[group] = jnp.where(is_west, both, zero if west_parts[group] is None else west_parts[group])
            east_parts[group] = jnp.where(is_east, both, zero if east_parts[group] is None else east_parts[group])
            low, high = value[:WIDE], value[rows - WIDE :]
            rows_first[m, plane * WIDE : (plane + 1) * WIDE, :] = jnp.where(even, high, low)
            rows_second[m, plane * WIDE : (plane + 1) * WIDE, :] = jnp.where(even, low, high)
        for group in range(groups_of(planes)):
            where = slice(group * LANE, (group + 1) * LANE)
            to_west[m, :, where] = west_parts[group]
            to_east[m, :, where] = east_parts[group]


def whole(count):
    return [pl.BlockSpec(memory_space=pltpu.VMEM)] * count


def in_hbm(count):
    return [pl.BlockSpec(memory_space=pltpu.HBM)] * count


def in_smem(count):
    return [pl.BlockSpec(memory_space=pltpu.SMEM)] * count


def pack_rims(temp, salt, uvel, vvel, eta, mask):
    members, levels, rows, cols = temp.shape
    planes = 4 * levels + 2
    wide = groups_of(planes) * LANE
    row_pack = -(-planes * WIDE // 8) * 8
    side = jax.ShapeDtypeStruct((members, rows, wide), jnp.float32)
    line = jax.ShapeDtypeStruct((members, row_pack, cols), jnp.float32)
    return pl.pallas_call(
        functools.partial(pack_kernel, levels),
        out_shape=(side, side, line, line),
        in_specs=in_hbm(6),
        out_specs=tuple(whole(4)),
        scratch_shapes=[
            pltpu.VMEM((members, planes - 1, rows, cols), jnp.float32),
            pltpu.VMEM((rows, cols), jnp.int32),
            pltpu.SemaphoreType.DMA((members, 6)),
        ],
        compiler_params=pltpu.CompilerParams(vmem_limit_bytes=WHOLE_VMEM),
        name="pack_rims",
    )(temp, salt, uvel, vvel, eta, mask)


def east_west(value):
    width = value.shape[-1]
    return pltpu.roll(value, width - 1, 1), pltpu.roll(value, 1, 1)


def chunks(first, last):
    return [(a, min(a + CHUNK, last)) for a in range(first, last, CHUNK)]


def assemble(ext, mask, rims, m, levels, total_rows):
    from_east, from_west, rows_first, rows_second, sides_first, sides_second = rims
    planes = 4 * levels + 2
    rows, cols = mask.shape
    tile_row = lax.axis_index("gridy")
    odd_tile = lax.rem(tile_row, 2).astype(jnp.float32)
    keep_south = jnp.where(tile_row > 0, 1.0, 0.0).astype(jnp.float32)
    keep_north = jnp.where(tile_row * rows + rows < total_rows, 1.0, 0.0).astype(jnp.float32)
    north_factors = keep_north * (1.0 - odd_tile), keep_north * odd_tile
    south_factors = keep_south * odd_tile, keep_south * (1.0 - odd_tile)

    def of_north(first, second):
        return north_factors[0] * first + north_factors[1] * second

    def of_south(first, second):
        return south_factors[0] * first + south_factors[1] * second

    wide = groups_of(planes) * LANE
    for group in range(groups_of(planes)):
        where = slice(group * LANE, (group + 1) * LANE)
        where_west = slice(wide + group * LANE, wide + (group + 1) * LANE)
        east = sides_first[m, :, where], sides_second[m, :, where]
        west = sides_first[m, :, where_west], sides_second[m, :, where_west]
        bands = [(TOP - CHUNK, of_south(*east), of_south(*west))]
        for a in range(0, rows, CHUNK):
            bands.append((TOP + a, from_east[m, a : a + CHUNK, where], from_west[m, a : a + CHUNK, where]))
        bands.append((TOP + rows, of_north(*east), of_north(*west)))
        for at, east, west in bands:
            odd = ((lanes_like(east.shape) // WIDE) & 1) == 1
            joined = (jnp.where(odd, east, west), jnp.where(odd, west, east))
            for plane in range(group * PER_GROUP, min((group + 1) * PER_GROUP, planes)):
                _, kind, offset = rim_place(plane)
                ext[plane, at : at + CHUNK, cols : cols + LANE] = pltpu.roll(joined[kind], LANE - offset, 1)
    ext[planes - 1, TOP : TOP + rows, :cols] = mask[...].astype(jnp.float32)
    for plane in range(planes):
        at = slice(plane * WIDE, (plane + 1) * WIDE)
        ext[plane, TOP - WIDE : TOP, :cols] = of_south(rows_first[m, at, :], rows_second[m, at, :])
        ext[plane, TOP + rows : TOP + rows + WIDE, :cols] = of_north(rows_first[m, at, :], rows_second[m, at, :])


def fill_rows(turn, inside, first_row, total_rows):
    shape = (CHUNK, turn.shape[1])
    for a in range(0, turn.shape[0], CHUNK):
        row = first_row + (a - TOP) + lax.broadcasted_iota(jnp.int32, shape, 0)
        latitude = row.astype(jnp.float32) + 0.5
        turn[a : a + CHUNK, :] = STEP_DT * CORI_K * (2.0 * latitude / total_rows - 1.0)
        inside[a : a + CHUNK, :] = jnp.where((row >= 0) & (row < total_rows), 1.0, 0.0)


KEPT = ["tu", "tv", "q", "v0", "v1", "v2"]
KEEP_FLOW = 1.0 - STEP_DT * DRAG_K - 4.0 * VISCOSITY
KEEP_TRACER = 1.0 - 4.0 * KAPPA
PRESS_SCALE = PRESS_K * 0.5 * STEP_DT


class Planes:
    def __init__(self, levels, rows, turn, inside):
        self.levels, self.rows, self.turn, self.inside = levels, rows, turn, inside
        self.views = {}

    def add(self, ref, names, lead=()):
        for i, name in enumerate(names):
            self.views[name] = ref.at[lead + (i,)]

    def get(self, name, a, b):
        return self.views[name][a:b, :]

    def put(self, name, a, b, value):
        self.views[name][a:b, :] = value

    def sides(self, name, a, b):
        here = self.get(name, a, b)
        east, west = east_west(here)
        return here, east, west, self.get(name, a + 1, b + 1), self.get(name, a - 1, b - 1)

    def slopes(self, name, a, b):
        _, east, west, north, south = self.sides(name, a, b)
        return east - west, north - south

    def around(self, name, a, b):
        here, east, west, north, south = self.sides(name, a, b)
        return here, (east + west) + (north + south)

    def main(self):
        return chunks(TOP, TOP + self.rows)

    def near(self):
        return [(TOP - 8, TOP)] + self.main() + [(TOP + self.rows, TOP + self.rows + 8)]

    def masked(self, a, b, value):
        if a >= TOP and b <= TOP + self.rows:
            return value
        return self.inside[a:b, :] * value

    def divergence(self, u_name, v_name, a, b):
        east, west = east_west(self.get(u_name, a, b))
        return DIV * ((east - west) + (self.get(v_name, a + 1, b + 1) - self.get(v_name, a - 1, b - 1)))

    def flow(self, u_name, v_name, press, out_u, out_v, a, b):
        ocean, turn = self.get("ocean", a, b), self.turn[a:b, :]
        u, around_u = self.around(u_name, a, b)
        v, around_v = self.around(v_name, a, b)
        push_u, push_v = turn * v, turn * u
        if press:
            slope_x, slope_y = self.slopes(press, a, b)
            push_u, push_v = push_u - slope_x, push_v + slope_y
        self.put(out_u, a, b, ocean * ((KEEP_FLOW * u + VISCOSITY * around_u) + push_u))
        self.put(out_v, a, b, ocean * ((KEEP_FLOW * v + VISCOSITY * around_v) - push_v))

    def powers(self, first, second, third):
        for a, b in self.near():
            self.put(second, a, b, self.masked(a, b, self.around(first, a, b)[1]))
        for a, b in self.near():
            value = self.around(second, a, b)[1] - 4.0 * self.get(first, a, b)
            self.put(third, a, b, self.masked(a, b, value))

    def next_right_side(self, u_name, v_name, eta_name, press, out_name):
        for a, b in self.near():
            self.flow(u_name, v_name, press, "t2u", "t2v", a, b)
        for a, b in self.near():
            div = self.divergence("t2u", "t2v", a, b)
            value = self.get(eta_name, a, b) - div if eta_name else -div
            self.put(out_name, a, b, self.masked(a, b, value))


def scaled(factor, value):
    return value if factor == 1.0 else factor * value


def surface_start(ext, work):
    levels = work.levels
    low, high = TOP - CHUNK, TOP + work.rows + CHUNK
    for a, b in chunks(low, high):
        su = sv = sp = None
        for l in range(levels):
            factor = PRESS_SCALE * (levels - l)
            dens = (factor * BETA_S) * ext[levels + l, a:b, :] - (factor * ALPHA_T) * ext[l, a:b, :]
            work.put("d%d" % l, a, b, dens)
            u, v = ext[2 * levels + l, a:b, :], ext[3 * levels + l, a:b, :]
            su, sv, sp = (u, v, dens) if l == 0 else (su + u, sv + v, sp + dens)
        work.put("su", a, b, su)
        work.put("sv", a, b, sv)
        work.put("sp", a, b, sp)
    for a, b in work.near():
        carried = None
        for l in range(levels):
            slope_x, slope_y = work.slopes("d%d" % l, a, b)
            term = ext[2 * levels + l, a:b, :] * slope_x + ext[3 * levels + l, a:b, :] * slope_y
            carried = term if l == 0 else carried + term
        here, around = work.around("sp", a, b)
        work.put("q", a, b, work.get("ocean", a, b) * ((KEEP_TRACER * here + KAPPA * around) - ADV * carried))
    for a, b in chunks(low, high):
        work.flow("su", "sv", "sp", "tu", "tv", a, b)
    for a, b in work.near():
        work.put("v0", a, b, work.masked(a, b, work.get("eta", a, b) - work.divergence("tu", "tv", a, b)))


SUM_NAMES = ["su", "sv", "sp", "v3", "pu", "pv", "t2u", "t2v"] + ["w%d_%d" % (i, k) for i in range(4) for k in range(4)]


def sums_kernel(levels, total_rows, *refs):
    fields, rims, out, kept = refs[:6], refs[6:12], refs[12], refs[13]
    planes, turn, inside, red, mask, sems = refs[14:]
    members = kept.shape[0]
    rows, cols = mask.shape
    copies = fetches(fields, lambda m, at: kept.at[m, at, pl.ds(TOP, rows), pl.ds(0, cols)], mask, sems, levels)
    tile_row = lax.axis_index("gridy")
    fill_rows(turn, inside, tile_row * rows, total_rows)
    red[...] = jnp.zeros_like(red)
    for m in range(members):
        assemble(kept.at[m], mask, rims, m, levels, total_rows)
    for copy in sum(copies, []):
        copy.wait()

    def one(m, carry):
        ext = kept.at[m]
        work = Planes(levels, rows, turn, inside)
        work.add(planes, SUM_NAMES + ["d%d" % l for l in range(levels)])
        work.add(kept, ["ext%d" % i for i in range(4 * levels)] + ["eta", "ocean"] + KEPT, (m,))
        surface_start(ext, work)
        work.powers("v0", "v1", "v2")
        for a, b in work.main():
            work.put("v3", a, b, work.around("v2", a, b)[1])
        work.next_right_side("tu", "tv", None, "q", "w0_0")
        for k in range(1, 4):
            name = "v%d" % (k - 1)
            for a, b in work.near():
                ocean = work.get("ocean", a, b)
                slope_x, slope_y = work.slopes(name, a, b)
                work.put("pu", a, b, scaled(-levels * GRAV, ocean * slope_x))
                work.put("pv", a, b, scaled(-levels * GRAV, ocean * slope_y))
            work.next_right_side("pu", "pv", name, None, "w0_%d" % k)
        for k in range(4):
            work.powers("w0_%d" % k, "w1_%d" % k, "w2_%d" % k)
            for a, b in work.main():
                work.put("w3_%d" % k, a, b, work.around("w2_%d" % k, a, b)[1])

        def put_sums(at, first, second, pairs):
            totals = [None] * len(pairs)
            for a in range(TOP, TOP + rows, 8):
                xs = [work.get(name, a, a + 8)[:, :cols] for name in first]
                ys = [work.get(name, a, a + 8)[:, :cols] for name in second]
                for p, (i, j) in enumerate(pairs):
                    term = xs[i] * ys[j]
                    totals[p] = term if totals[p] is None else totals[p] + term
            for p, total in enumerate(totals):
                folded = total[:, :LANE]
                for c in range(LANE, cols, LANE):
                    folded = folded + total[:, c : c + LANE]
                red[m, at + p : at + p + 1, :] = jnp.sum(folded, axis=0, keepdims=True)

        for i in range(6):
            low, high = i // 2, i - i // 2
            put_sums(i, ["v%d" % low], ["v%d" % high], [(0, 0)])
            names = [["w%d_%d" % (which, k) for k in range(4)] for which in (low, high)]
            put_sums(6 + i * len(PAIRS), names[0], names[1], PAIRS)
        return carry

    lax.fori_loop(0, members, one, 0)
    for m in range(members):
        line = jnp.sum(jnp.transpose(red[m]), axis=0, keepdims=True)
        for i in range(out.shape[0]):
            out[i, m : m + 1, :] = line


def plane_shape(rows, cols):
    return (2 * TOP + rows, cols + LANE)


def local_sums(fields, rims, total_rows, copies):
    members, levels, rows, cols = fields[0].shape
    assert SUMS <= LANE and members <= 8
    shape = plane_shape(rows, cols)
    kept = (members, 4 * levels + 2 + len(KEPT)) + shape
    return pl.pallas_call(
        functools.partial(sums_kernel, levels, total_rows),
        out_shape=(jax.ShapeDtypeStruct((copies, members, LANE), jnp.float32), jax.ShapeDtypeStruct(kept, jnp.float32)),
        in_specs=in_hbm(6) + whole(6),
        out_specs=tuple(whole(2)),
        scratch_shapes=[
            pltpu.VMEM((len(SUM_NAMES) + levels,) + shape, jnp.float32),
            pltpu.VMEM(shape, jnp.float32),
            pltpu.VMEM(shape, jnp.float32),
            pltpu.VMEM((members, LANE, LANE), jnp.float32),
            pltpu.VMEM((rows, cols), jnp.int32),
            pltpu.SemaphoreType.DMA((members, 6)),
        ],
        compiler_params=pltpu.CompilerParams(vmem_limit_bytes=VMEM_LIMIT),
        cost_estimate=pl.CostEstimate(flops=10**8, bytes_accessed=4 * 10**6, transcendentals=0),
        name="local_sums",
    )(*fields, *rims)


def krylov(moment):
    n00, n01, n11, n12, n22, x22 = moment
    n02 = n11 - 4.0 * n00
    main, near = 1.0 + 4.0 * SURF_C, SURF_C
    g00 = main * n00 - near * n01
    g01 = main * n01 - near * n11
    g02 = main * n02 - near * n12
    g11 = main * n11 - near * (n12 + 4.0 * n01)
    g12 = main * n12 - near * (n22 + 4.0 * n02)
    g22 = main * n22 - near * x22
    l1, l2 = g01 / g00, g02 / g00
    d1 = g11 - l1 * g01
    d1 = jnp.where(d1 > 3e-7 * g11, d1, jnp.inf)
    e = g12 - l1 * g02
    l12 = e / d1
    d2 = g22 - l2 * g02 - l12 * e
    d2 = jnp.where(d2 > 3e-7 * g22, d2, jnp.inf)
    z0 = n00
    z1 = n01 - l1 * z0
    z2 = n02 - l2 * z0 - l12 * z1
    y2 = z2 / d2
    y1 = z1 / d1 - l12 * y2
    y0 = z0 / g00 - l1 * y1 - l2 * y2
    return [y0, y1, y2]


def weights(read):
    first = krylov([read(i) for i in range(6)])
    lifted = [None] + first
    second = []
    for i in range(6):
        total = None
        for p, (a, b) in enumerate(PAIRS):
            term = read(6 + i * len(PAIRS) + p)
            for k in (a, b):
                if k:
                    term = term * lifted[k]
            if a != b:
                term = 2.0 * term
            total = term if total is None else total + term
        second.append(total)
    return first, krylov(second)


RUN_NAMES = ["pu", "pv", "t2u", "t2v", "eta1", "w0", "w1", "w2", "eta2", "p", "p2", "gu1", "gv1", "gu2", "gv2"]


def whether(*conditions):
    result = jnp.int32(0)
    for condition in conditions:
        result = jnp.where(condition, 1, result)
    return result


def choose(source, theirs, side, members, info):
    mine, away = side * members, (1 - side) * members
    sent = [whether(*[theirs[slot] == mine + m for slot in range(members)]) for m in range(2)]
    here = [whether(*[source[slot] == away + m for slot in range(members)]) for m in range(2)]
    first_sent, first_here = 1 - sent[0], 1 - here[0]
    for slot in range(members):
        own = jnp.where(source[slot] - mine == first_sent, 0, 1)
        far = jnp.where(source[slot] - away == first_here, 2, 3)
        info[slot] = jnp.where((source[slot] >= mine) & (source[slot] < mine + members), own, far)
    info[members] = jnp.maximum(sent[0] * sent[1], here[0] * here[1])
    info[members + 1] = jnp.int32(1)
    return first_sent


def advance_kernel(levels, total_rows, is_first, *refs):
    if is_first:
        source, theirs, tiles, kept, out, zonal, info = refs[:7]
    else:
        info, theirs, tiles, kept, zonal_before, out, spread = refs[:7]
    planes, after, turn, inside, staged, sums, sem = refs[7:14]
    rows, cols = out.shape[1:]
    members = kept.shape[0]
    side, tile_row = lax.axis_index("member"), lax.axis_index("gridy")
    total = tiles[0]
    for i in range(1, tiles.shape[0]):
        total = total + tiles[i]
    staged[0:members, :] = total
    copy = pltpu.make_async_copy(staged, sums, sem)
    copy.start()
    fill_rows(turn, inside, tile_row * rows, total_rows)
    if not is_first:
        zonal = refs[14]
    zonal[...] = jnp.zeros_like(zonal) if is_first else zonal_before[...]
    copy.wait()
    if is_first:
        member = choose(source, theirs, side, members, info)
    else:
        member = whether(*[theirs[slot] == side * members for slot in range(members)])
    ext = kept.at[member]
    work = Planes(levels, rows, turn, inside)
    work.add(planes, RUN_NAMES)
    work.add(kept, ["ext%d" % i for i in range(4 * levels)] + ["eta", "ocean"] + KEPT, (member,))

    def read(i):
        return jnp.full((1, 1), sums[member, i], jnp.float32)

    def combine(factors, names, out_name):
        for a, b in work.near():
            value = None
            for factor, name in zip(factors, names):
                term = factor * work.get(name, a, b)
                value = term if value is None else value + term
            work.put(out_name, a, b, value)

    first, second = weights(read)
    combine(first, ("v0", "v1", "v2"), "eta1")
    for a, b in work.near():
        ocean = work.get("ocean", a, b)
        slope_x, slope_y = work.slopes("eta1", a, b)
        slope_x, slope_y = GRAV * ocean * slope_x, GRAV * ocean * slope_y
        work.put("gu1", a, b, slope_x)
        work.put("gv1", a, b, slope_y)
        work.put("pu", a, b, work.get("tu", a, b) - levels * slope_x)
        work.put("pv", a, b, work.get("tv", a, b) - levels * slope_y)
    work.next_right_side("pu", "pv", "eta1", "q", "w0")
    work.powers("w0", "w1", "w2")
    combine(second, ("w0", "w1", "w2"), "eta2")
    for a, b in work.main():
        ocean = work.get("ocean", a, b)
        slope_x, slope_y = work.slopes("eta2", a, b)
        work.put("gu2", a, b, GRAV * ocean * slope_x)
        work.put("gv2", a, b, GRAV * ocean * slope_y)
        out[4 * levels, a - TOP : b - TOP, :] = work.get("eta2", a, b)[:, :cols]
    low, high = TOP - 8, TOP + rows + 8
    for a, b in chunks(TOP - CHUNK, TOP + rows + CHUNK):
        work.put("p", a, b, jnp.zeros((b - a, cols + LANE), jnp.float32))
        work.put("p2", a, b, jnp.zeros((b - a, cols + LANE), jnp.float32))

    def step(ref, l, press, a, b, width):
        def of(view):
            here = view[a:b, :]
            east, west = east_west(here)
            return here[:, :width], east[:, :width], west[:, :width], view[a + 1 : b + 1, :width], view[a - 1 : b - 1, :width]

        ocean = work.views["ocean"][a:b, :width]
        coriolis = turn[a:b, :width]
        u, east, west, north, south = of(ref.at[2 * levels + l])
        around_u = (east + west) + (north + south)
        v, east, west, north, south = of(ref.at[3 * levels + l])
        around_v = (east + west) + (north + south)
        _, east, west, north, south = of(work.views[press])
        new_u = ocean * ((KEEP_FLOW * u + VISCOSITY * around_u) + (coriolis * v - (east - west)))
        new_v = ocean * ((KEEP_FLOW * v + VISCOSITY * around_v) - (coriolis * u + (north - south)))
        flow_u, flow_v = ADV * u, ADV * v
        results = []
        for at in (l, levels + l):
            here, east, west, north, south = of(ref.at[at])
            carried = flow_u * (east - west) + flow_v * (north - south)
            spread = KEEP_TRACER * here + KAPPA * ((east + west) + (north + south))
            results.append(ocean * (spread - carried))
        return results[0], results[1], new_u, new_v

    def add_press(ref, l, press, a, b):
        dens = (PRESS_SCALE * BETA_S) * ref[levels + l, a:b, :] - (PRESS_SCALE * ALPHA_T) * ref[l, a:b, :]
        work.put(press, a, b, work.get(press, a, b) + dens)

    def level(l, carry):
        for a in range(TOP - CHUNK, TOP + rows + CHUNK, 8):
            add_press(ext, l, "p", a, a + 8)
        for a in range(low, high, 8):
            temp, salt, u, v = step(ext, l, "p", a, a + 8, cols + LANE)
            after[l, a : a + 8, :] = temp
            after[levels + l, a : a + 8, :] = salt
            after[2 * levels + l, a : a + 8, :] = u - work.get("gu1", a, a + 8)
            after[3 * levels + l, a : a + 8, :] = v - work.get("gv1", a, a + 8)
        for a in range(low, high, 8):
            add_press(after, l, "p2", a, a + 8)
        for a in range(TOP, TOP + rows, 8):
            temp, salt, u, v = step(after, l, "p2", a, a + 8, cols)
            here = slice(a - TOP, a - TOP + 8)
            v = v - work.get("gv2", a, a + 8)[:, :cols]
            out[l, here, :] = temp
            out[levels + l, here, :] = salt
            out[2 * levels + l, here, :] = u - work.get("gu2", a, a + 8)[:, :cols]
            out[3 * levels + l, here, :] = v
            row_sum = jnp.sum(v, axis=1, keepdims=True)
            zonal[here, :] = jnp.where(lanes_like((8, LANE)) == member * levels + l, row_sum, zonal[here, :])
        return carry

    lax.fori_loop(0, levels, level, 0)
    if not is_first:
        square = jnp.concatenate([zonal[...]] + [jnp.zeros_like(zonal)] * (LANE // rows - 1), axis=0)
        turned = jnp.transpose(square)[: members * levels]
        line = turned[:levels]
        for m in range(1, members):
            line = line + pltpu.roll(turned, m * rows, 1)[m * levels : (m + 1) * levels]
        for i in range(spread.shape[0]):
            spread[i] = line


def advance(is_first, small, theirs, tiles, kept, zonal, rows, cols, total_rows):
    members, planes = kept.shape[:2]
    levels = (planes - 2 - len(KEPT)) // 4
    assert members * rows == LANE and members * levels == 8
    shape = plane_shape(rows, cols)
    zonal_shape = jax.ShapeDtypeStruct((rows, LANE), jnp.float32)
    out_shape = [jax.ShapeDtypeStruct((4 * levels + 1, rows, cols), jnp.float32)]
    if is_first:
        out_shape += [zonal_shape, jax.ShapeDtypeStruct((members + 2,), jnp.int32)]
    else:
        out_shape += [jax.ShapeDtypeStruct((tiles.shape[0], levels, members * rows), jnp.float32)]
    return pl.pallas_call(
        functools.partial(advance_kernel, levels, total_rows, is_first),
        out_shape=tuple(out_shape),
        in_specs=in_smem(2) + whole(2 if is_first else 3),
        out_specs=tuple(whole(2) + (in_smem(1) if is_first else [])),
        scratch_shapes=[
            pltpu.VMEM((len(RUN_NAMES),) + shape, jnp.float32),
            pltpu.VMEM((4 * levels,) + shape, jnp.float32),
            pltpu.VMEM(shape, jnp.float32),
            pltpu.VMEM(shape, jnp.float32),
            pltpu.VMEM((8, LANE), jnp.float32),
            pltpu.SMEM((8, LANE), jnp.float32),
            pltpu.SemaphoreType.DMA,
        ]
        + ([] if is_first else [pltpu.VMEM((rows, LANE), jnp.float32)]),
        compiler_params=pltpu.CompilerParams(vmem_limit_bytes=VMEM_LIMIT),
        cost_estimate=pl.CostEstimate(flops=10**8, bytes_accessed=4 * 10**6, transcendentals=0),
        name="advance",
    )(small, theirs, tiles, kept, *([] if is_first else [zonal]))


def finish_kernel(count_y, count_x, total_cols, spread, overturn, score, held):
    members, levels, rows = overturn.shape
    total_rows = rows * count_y
    lane = lanes_like(spread.shape[1:])
    member_of = lane // rows
    weighted = None
    for y in range(count_y):
        total = spread[y * count_x]
        for x in range(1, count_x):
            total = total + spread[y * count_x + x]
        lines = [total[0:1]]
        for l in range(1, levels):
            lines.append(lines[-1] + total[l : l + 1])
        lines = jnp.concatenate(lines, axis=0) * (total_cols**-0.5)
        held[y] = lines
        latitude = ((lane - member_of * rows + y * rows).astype(jnp.float32) + 0.5) * (1.0 / total_rows)
        weighted = lines * latitude if weighted is None else weighted + lines * latitude
    mine = held[lax.axis_index("gridy")]
    for m in range(members):
        overturn[m] = mine[:, m * rows : (m + 1) * rows]
        score[m] = jnp.sum(jnp.where(member_of == m, weighted, 0.0)) * ((levels * total_rows) ** -0.5)


def finish(spread, members, rows, count_y, count_x, cols):
    levels = spread.shape[1]
    return pl.pallas_call(
        functools.partial(finish_kernel, count_y, count_x, cols * count_x),
        out_shape=(
            jax.ShapeDtypeStruct((members, levels, rows), jnp.float32),
            jax.ShapeDtypeStruct((members,), jnp.float32),
        ),
        in_specs=whole(1),
        out_specs=(whole(1)[0], in_smem(1)[0]),
        scratch_shapes=[pltpu.VMEM((count_y,) + spread.shape[1:], jnp.float32)],
        compiler_params=pltpu.CompilerParams(vmem_limit_bytes=VMEM_LIMIT),
        name="finish",
    )(spread)


def pick_kernel(levels, choice, source, score, their_score, *refs):
    count = len(refs) - 7
    sources, outs, weight, sem = refs[:count], refs[count : count + 5], refs[count + 5], refs[count + 6]
    slots = outs[0].shape[0]

    def parts(s, source):
        for f in range(4):
            yield source.at[pl.ds(f * levels, levels)], outs[f].at[s]
        yield source.at[4 * levels], outs[4].at[s]

    for s in range(slots):
        for k in range(count):

            @pl.when(choice[s] == k)
            def _():
                for i, (one, target) in enumerate(parts(s, sources[k])):
                    pltpu.make_async_copy(one, target, sem.at[s, i]).start()

    side = lax.axis_index("member")
    mean = (sum(score[m] for m in range(slots)) + sum(their_score[m] for m in range(slots))) * (0.5 / slots)
    for s in range(slots):
        value = jnp.float32(0.0)
        for m in range(slots):
            value = jnp.where(source[s] == side * slots + m, score[m], value)
            value = jnp.where(source[s] == (1 - side) * slots + m, their_score[m], value)
        weight[s] = value - mean
    for s in range(slots):
        for i, (one, target) in enumerate(parts(s, sources[0])):
            pltpu.make_async_copy(one, target, sem.at[s, i]).wait()


def pick(choice, source, score, their_score, sources, slots, levels):
    _, rows, cols = sources[0].shape
    volume = jax.ShapeDtypeStruct((slots, levels, rows, cols), jnp.float32)
    surface = jax.ShapeDtypeStruct((slots, rows, cols), jnp.float32)
    return pl.pallas_call(
        functools.partial(pick_kernel, levels),
        out_shape=(volume,) * 4 + (surface, jax.ShapeDtypeStruct((slots,), jnp.float32)),
        in_specs=in_smem(4) + whole(len(sources)),
        out_specs=tuple(in_hbm(5) + in_smem(1)),
        scratch_shapes=[pltpu.SemaphoreType.DMA((slots, 5))],
        compiler_params=pltpu.CompilerParams(vmem_limit_bytes=VMEM_LIMIT),
        name="pick",
    )(choice, source, score, their_score, *sources)


def shift(value, axis, by):
    count = lax.axis_size(axis)
    return lax.ppermute(value, axis, [(i, (i + by) % count) for i in range(count)])


def exchange_rims(packed):
    to_west, to_east, rows_first, rows_second = packed
    rows = to_west.shape[1]
    count = lax.axis_size("gridy")
    assert count % 2 == 0
    partners = [i ^ 1 for i in range(count)], [min(max(i - 1 + 2 * (i % 2), 0), count - 1) for i in range(count)]

    def pair(value, which):
        return lax.ppermute(value, "gridy", list(enumerate(partners[which])))

    from_east, from_west = shift(to_west, "gridx", -1), shift(to_east, "gridx", 1)
    rows_first, rows_second = pair(rows_first, 0), pair(rows_second, 1)
    low = jnp.concatenate([from_east[:, :CHUNK], from_west[:, :CHUNK]], axis=2)
    high = jnp.concatenate([from_east[:, rows - CHUNK :], from_west[:, rows - CHUNK :]], axis=2)
    even = lax.axis_index("gridy") % 2 == 0
    sides_first = pair(jnp.where(even, high, low), 0)
    sides_second = pair(jnp.where(even, low, high), 1)
    return from_east, from_west, rows_first, rows_second, sides_first, sides_second


def from_all(tiles, axes):
    return lax.all_to_all(tiles, axes, split_axis=0, concat_axis=0, tiled=True)


def swap(value):
    return lax.ppermute(value, "member", [(0, 1), (1, 0)])


def shards(temp, salt, uvel, vvel, eta, land_mask, clone_source):
    members, levels, rows, cols = temp.shape
    assert members == 2 and lax.axis_size("member") == 2
    count_y, count_x = lax.axis_size("gridy"), lax.axis_size("gridx")
    total_rows = rows * count_y
    grid = ("gridy", "gridx")

    their_source = swap(clone_source)
    fields = (temp, salt, uvel, vvel, eta, land_mask)
    rims = exchange_rims(pack_rims(*fields))
    tiles, kept = local_sums(fields, rims, total_rows, count_y * count_x)
    tiles = from_all(tiles, grid)

    sent, zonal, info = advance(True, clone_source, their_source, tiles, kept, None, rows, cols, total_rows)
    arrived = swap(sent)

    def rest():
        other, spread = advance(False, info, their_source, tiles, kept, zonal, rows, cols, total_rows)
        return (other, *finish(from_all(spread, grid), members, rows, count_y, count_x, cols))

    def nothing():
        return jnp.zeros_like(sent), jnp.zeros((members, levels, rows), jnp.float32), jnp.zeros((members,), jnp.float32)

    other, overturn, score = lax.cond(info[members + 1] != 0, rest, nothing)
    their_score = swap(score)

    def with_second():
        sources = (sent, other, arrived, swap(other))
        return pick(info, clone_source, score, their_score, sources, members, levels)

    def without_second():
        return pick(info, clone_source, score, their_score, (sent, other, arrived), members, levels)

    *picked, clone_weight = lax.cond(info[members] != 0, with_second, without_second)
    return (*picked, overturn, clone_weight)


def solution(mesh):
    volume = P("member", None, "gridy", "gridx")
    in_specs = (volume,) * 4 + (P("member", "gridy", "gridx"), P("gridy", "gridx"), P("member"))
    out_specs = (volume,) * 4 + (P("member", "gridy", "gridx"), P("member", None, "gridy"), P("member"))
    return jax.shard_map(shards, mesh=mesh, in_specs=in_specs, out_specs=out_specs, check_vma=False)
```

```python
import functools

import jax
import jax.numpy as jnp
from jax import lax
from jax.experimental import pallas as pl
from jax.experimental.pallas import tpu as pltpu
from jax.sharding import PartitionSpec as P

STEPS = 2
ITERS = 3

ALPHA_T = 0.8
BETA_S = 0.6
PRESS_K = 0.25
STEP_DT = 0.1
KAPPA = 0.1
VISCOSITY = 0.1
DRAG_K = 0.05
CORI_K = 1.0
SURF_C = 4.0
DIV_K = 0.5
GRAV_K = 0.5

ADV = STEP_DT * 0.5
DIV = DIV_K * 0.5
GRAV = GRAV_K * 0.5

WIDE = 10
TOP = 24
CHUNK = 16
LANE = 128
PER_GROUP = 11
PAIRS = [(a, b) for a in range(4) for b in range(a, 4)]
SUMS = 6 + 6 * len(PAIRS)
VMEM_LIMIT = 24 * 1024 * 1024
WHOLE_VMEM = 60 * 1024 * 1024


def rim_place(plane):
    group, place = divmod(plane, PER_GROUP)
    if place < 6:
        return group, 0, (2 * place + 1) * WIDE
    return group, 1, (2 * (place - 6) + 2) * WIDE


def groups_of(planes):
    return -(-planes // PER_GROUP)


def lanes_like(shape):
    return lax.broadcasted_iota(jnp.int32, shape, len(shape) - 1)


def fetches(fields, planes_of, mask_to, sems, levels):
    members = fields[0].shape[0]
    per_member = []
    for m in range(members):
        parts = [(fields[f].at[m], planes_of(m, pl.ds(f * levels, levels))) for f in range(4)]
        parts.append((fields[4].at[m], planes_of(m, 4 * levels)))
        per_member.append([pltpu.make_async_copy(*part, sems.at[m, i]) for i, part in enumerate(parts)])
    mask_copy = pltpu.make_async_copy(fields[5], mask_to, sems.at[0, 5])
    mask_copy.start()
    for copies in per_member:
        for copy in copies:
            copy.start()
    mask_copy.wait()
    return per_member


def pack_kernel(levels, *refs):
    fields, (to_west, to_east, rows_first, rows_second), (held, mask, sems) = refs[:6], refs[6:10], refs[10:]
    members, _, rows, cols = held.shape
    planes = 4 * levels + 2
    copies = fetches(fields, lambda m, at: held.at[m, at], mask, sems, levels)
    lane = lanes_like((rows, LANE))
    even = lax.broadcasted_iota(jnp.int32, (WIDE, cols), 0) * 0 + lax.rem(lax.axis_index("gridy"), 2) == 0
    for m in range(members):
        for copy in copies[m]:
            copy.wait()
        west_parts = [None] * groups_of(planes)
        east_parts = [None] * groups_of(planes)
        for plane in range(planes):
            value = held[m, plane] if plane < planes - 1 else mask[...].astype(jnp.float32)
            group, _, start = rim_place(plane)
            both = jnp.where(lane < WIDE, value[:, :LANE], value[:, cols - LANE :])
            both = pltpu.roll(both, start, 1)
            is_west = (lane >= start) & (lane < start + WIDE)
            is_east = (lane >= start - WIDE) & (lane < start)
            zero = jnp.zeros_like(both)
            west_parts[group] = jnp.where(is_west, both, zero if west_parts[group] is None else west_parts[group])
            east_parts[group] = jnp.where(is_east, both, zero if east_parts[group] is None else east_parts[group])
            low, high = value[:WIDE], value[rows - WIDE :]
            rows_first[m, plane * WIDE : (plane + 1) * WIDE, :] = jnp.where(even, high, low)
            rows_second[m, plane * WIDE : (plane + 1) * WIDE, :] = jnp.where(even, low, high)
        for group in range(groups_of(planes)):
            where = slice(group * LANE, (group + 1) * LANE)
            to_west[m, :, where] = west_parts[group]
            to_east[m, :, where] = east_parts[group]


def whole(count):
    return [pl.BlockSpec(memory_space=pltpu.VMEM)] * count


def in_hbm(count):
    return [pl.BlockSpec(memory_space=pltpu.HBM)] * count


def in_smem(count):
    return [pl.BlockSpec(memory_space=pltpu.SMEM)] * count


def pack_rims(temp, salt, uvel, vvel, eta, mask):
    members, levels, rows, cols = temp.shape
    planes = 4 * levels + 2
    wide = groups_of(planes) * LANE
    row_pack = -(-planes * WIDE // 8) * 8
    side = jax.ShapeDtypeStruct((members, rows, wide), jnp.float32)
    line = jax.ShapeDtypeStruct((members, row_pack, cols), jnp.float32)
    return pl.pallas_call(
        functools.partial(pack_kernel, levels),
        out_shape=(side, side, line, line),
        in_specs=in_hbm(6),
        out_specs=tuple(whole(4)),
        scratch_shapes=[
            pltpu.VMEM((members, planes - 1, rows, cols), jnp.float32),
            pltpu.VMEM((rows, cols), jnp.int32),
            pltpu.SemaphoreType.DMA((members, 6)),
        ],
        compiler_params=pltpu.CompilerParams(vmem_limit_bytes=WHOLE_VMEM),
        name="pack_rims",
    )(temp, salt, uvel, vvel, eta, mask)


def east_west(value):
    width = value.shape[-1]
    return pltpu.roll(value, width - 1, 1), pltpu.roll(value, 1, 1)


def chunks(first, last):
    return [(a, min(a + CHUNK, last)) for a in range(first, last, CHUNK)]


def assemble(ext, mask, rims, m, levels, total_rows):
    from_east, from_west, rows_first, rows_second, sides_first, sides_second = rims
    planes = 4 * levels + 2
    rows, cols = mask.shape
    tile_row = lax.axis_index("gridy")
    odd_tile = lax.rem(tile_row, 2).astype(jnp.float32)
    keep_south = jnp.where(tile_row > 0, 1.0, 0.0).astype(jnp.float32)
    keep_north = jnp.where(tile_row * rows + rows < total_rows, 1.0, 0.0).astype(jnp.float32)
    north_factors = keep_north * (1.0 - odd_tile), keep_north * odd_tile
    south_factors = keep_south * odd_tile, keep_south * (1.0 - odd_tile)

    def of_north(first, second):
        return north_factors[0] * first + north_factors[1] * second

    def of_south(first, second):
        return south_factors[0] * first + south_factors[1] * second

    wide = groups_of(planes) * LANE
    for group in range(groups_of(planes)):
        where = slice(group * LANE, (group + 1) * LANE)
        where_west = slice(wide + group * LANE, wide + (group + 1) * LANE)
        east = sides_first[m, :, where], sides_second[m, :, where]
        west = sides_first[m, :, where_west], sides_second[m, :, where_west]
        bands = [(TOP - CHUNK, of_south(*east), of_south(*west))]
        for a in range(0, rows, CHUNK):
            bands.append((TOP + a, from_east[m, a : a + CHUNK, where], from_west[m, a : a + CHUNK, where]))
        bands.append((TOP + rows, of_north(*east), of_north(*west)))
        for at, east, west in bands:
            odd = ((lanes_like(east.shape) // WIDE) & 1) == 1
            joined = (jnp.where(odd, east, west), jnp.where(odd, west, east))
            for plane in range(group * PER_GROUP, min((group + 1) * PER_GROUP, planes)):
                _, kind, offset = rim_place(plane)
                ext[plane, at : at + CHUNK, cols : cols + LANE] = pltpu.roll(joined[kind], LANE - offset, 1)
    ext[planes - 1, TOP : TOP + rows, :cols] = mask[...].astype(jnp.float32)
    for plane in range(planes):
        at = slice(plane * WIDE, (plane + 1) * WIDE)
        ext[plane, TOP - WIDE : TOP, :cols] = of_south(rows_first[m, at, :], rows_second[m, at, :])
        ext[plane, TOP + rows : TOP + rows + WIDE, :cols] = of_north(rows_first[m, at, :], rows_second[m, at, :])


def fill_rows(turn, inside, first_row, total_rows):
    shape = (CHUNK, turn.shape[1])
    for a in range(0, turn.shape[0], CHUNK):
        row = first_row + (a - TOP) + lax.broadcasted_iota(jnp.int32, shape, 0)
        latitude = row.astype(jnp.float32) + 0.5
        turn[a : a + CHUNK, :] = STEP_DT * CORI_K * (2.0 * latitude / total_rows - 1.0)
        inside[a : a + CHUNK, :] = jnp.where((row >= 0) & (row < total_rows), 1.0, 0.0)


KEPT = ["tu", "tv", "q", "v0", "v1", "v2"]
KEEP_FLOW = 1.0 - STEP_DT * DRAG_K - 4.0 * VISCOSITY
KEEP_TRACER = 1.0 - 4.0 * KAPPA
PRESS_SCALE = PRESS_K * 0.5 * STEP_DT


class Planes:
    def __init__(self, levels, rows, turn, inside):
        self.levels, self.rows, self.turn, self.inside = levels, rows, turn, inside
        self.views = {}

    def add(self, ref, names, lead=()):
        for i, name in enumerate(names):
            self.views[name] = ref.at[lead + (i,)]

    def get(self, name, a, b):
        return self.views[name][a:b, :]

    def put(self, name, a, b, value):
        self.views[name][a:b, :] = value

    def sides(self, name, a, b):
        here = self.get(name, a, b)
        east, west = east_west(here)
        return here, east, west, self.get(name, a + 1, b + 1), self.get(name, a - 1, b - 1)

    def slopes(self, name, a, b):
        _, east, west, north, south = self.sides(name, a, b)
        return east - west, north - south

    def around(self, name, a, b):
        here, east, west, north, south = self.sides(name, a, b)
        return here, (east + west) + (north + south)

    def main(self):
        return chunks(TOP, TOP + self.rows)

    def near(self):
        return [(TOP - 8, TOP)] + self.main() + [(TOP + self.rows, TOP + self.rows + 8)]

    def masked(self, a, b, value):
        if a >= TOP and b <= TOP + self.rows:
            return value
        return self.inside[a:b, :] * value

    def divergence(self, u_name, v_name, a, b):
        east, west = east_west(self.get(u_name, a, b))
        return DIV * ((east - west) + (self.get(v_name, a + 1, b + 1) - self.get(v_name, a - 1, b - 1)))

    def flow(self, u_name, v_name, press, out_u, out_v, a, b):
        ocean, turn = self.get("ocean", a, b), self.turn[a:b, :]
        u, around_u = self.around(u_name, a, b)
        v, around_v = self.around(v_name, a, b)
        push_u, push_v = turn * v, turn * u
        if press:
            slope_x, slope_y = self.slopes(press, a, b)
            push_u, push_v = push_u - slope_x, push_v + slope_y
        self.put(out_u, a, b, ocean * ((KEEP_FLOW * u + VISCOSITY * around_u) + push_u))
        self.put(out_v, a, b, ocean * ((KEEP_FLOW * v + VISCOSITY * around_v) - push_v))

    def powers(self, first, second, third):
        for a, b in self.near():
            self.put(second, a, b, self.masked(a, b, self.around(first, a, b)[1]))
        for a, b in self.near():
            value = self.around(second, a, b)[1] - 4.0 * self.get(first, a, b)
            self.put(third, a, b, self.masked(a, b, value))

    def next_right_side(self, u_name, v_name, eta_name, press, out_name):
        for a, b in self.near():
            self.flow(u_name, v_name, press, "t2u", "t2v", a, b)
        for a, b in self.near():
            div = self.divergence("t2u", "t2v", a, b)
            value = self.get(eta_name, a, b) - div if eta_name else -div
            self.put(out_name, a, b, self.masked(a, b, value))


def scaled(factor, value):
    return value if factor == 1.0 else factor * value


def surface_start(ext, work):
    levels = work.levels
    low, high = TOP - CHUNK, TOP + work.rows + CHUNK
    for a, b in chunks(low, high):
        su = sv = sp = None
        for l in range(levels):
            factor = PRESS_SCALE * (levels - l)
            dens = (factor * BETA_S) * ext[levels + l, a:b, :] - (factor * ALPHA_T) * ext[l, a:b, :]
            work.put("d%d" % l, a, b, dens)
            u, v = ext[2 * levels + l, a:b, :], ext[3 * levels + l, a:b, :]
            su, sv, sp = (u, v, dens) if l == 0 else (su + u, sv + v, sp + dens)
        work.put("su", a, b, su)
        work.put("sv", a, b, sv)
        work.put("sp", a, b, sp)
    for a, b in work.near():
        carried = None
        for l in range(levels):
            slope_x, slope_y = work.slopes("d%d" % l, a, b)
            term = ext[2 * levels + l, a:b, :] * slope_x + ext[3 * levels + l, a:b, :] * slope_y
            carried = term if l == 0 else carried + term
        here, around = work.around("sp", a, b)
        work.put("q", a, b, work.get("ocean", a, b) * ((KEEP_TRACER * here + KAPPA * around) - ADV * carried))
    for a, b in chunks(low, high):
        work.flow("su", "sv", "sp", "tu", "tv", a, b)
    for a, b in work.near():
        work.put("v0", a, b, work.masked(a, b, work.get("eta", a, b) - work.divergence("tu", "tv", a, b)))


SUM_NAMES = ["su", "sv", "sp", "v3", "pu", "pv", "t2u", "t2v"] + ["w%d_%d" % (i, k) for i in range(4) for k in range(4)]


def whether(*conditions):
    result = jnp.int32(0)
    for condition in conditions:
        result = jnp.where(condition, 1, result)
    return result


def choose(source, theirs, side, members, info):
    mine, away = side * members, (1 - side) * members
    sent = [whether(*[theirs[slot] == mine + m for slot in range(members)]) for m in range(2)]
    here = [whether(*[source[slot] == away + m for slot in range(members)]) for m in range(2)]
    first_sent, first_here = 1 - sent[0], 1 - here[0]
    for slot in range(members):
        own = jnp.where(source[slot] - mine == first_sent, 0, 1)
        far = jnp.where(source[slot] - away == first_here, 2, 3)
        info[slot] = jnp.where((source[slot] >= mine) & (source[slot] < mine + members), own, far)
    info[members] = jnp.maximum(sent[0] * sent[1], here[0] * here[1])
    info[members + 1] = jnp.int32(1)
    info[members + 2] = first_sent


def sums_kernel(levels, total_rows, source, theirs, *refs):
    fields, rims, out, kept, info = refs[:6], refs[6:12], refs[12], refs[13], refs[14]
    planes, turn, inside, red, mask, sems = refs[15:]
    members = kept.shape[0]
    rows, cols = mask.shape
    copies = fetches(fields, lambda m, at: kept.at[m, at, pl.ds(TOP, rows), pl.ds(0, cols)], mask, sems, levels)
    tile_row = lax.axis_index("gridy")
    choose(source, theirs, lax.axis_index("member"), members, info)
    fill_rows(turn, inside, tile_row * rows, total_rows)
    red[...] = jnp.zeros_like(red)
    for m in range(members):
        assemble(kept.at[m], mask, rims, m, levels, total_rows)
    for copy in sum(copies, []):
        copy.wait()

    def one(m, carry):
        ext = kept.at[m]
        work = Planes(levels, rows, turn, inside)
        work.add(planes, SUM_NAMES + ["d%d" % l for l in range(levels)])
        work.add(kept, ["ext%d" % i for i in range(4 * levels)] + ["eta", "ocean"] + KEPT, (m,))
        surface_start(ext, work)
        work.powers("v0", "v1", "v2")
        for a, b in work.main():
            work.put("v3", a, b, work.around("v2", a, b)[1])
        work.next_right_side("tu", "tv", None, "q", "w0_0")
        for k in range(1, 4):
            name = "v%d" % (k - 1)
            for a, b in work.near():
                ocean = work.get("ocean", a, b)
                slope_x, slope_y = work.slopes(name, a, b)
                work.put("pu", a, b, scaled(-levels * GRAV, ocean * slope_x))
                work.put("pv", a, b, scaled(-levels * GRAV, ocean * slope_y))
            work.next_right_side("pu", "pv", name, None, "w0_%d" % k)
        for k in range(4):
            work.powers("w0_%d" % k, "w1_%d" % k, "w2_%d" % k)
            for a, b in work.main():
                work.put("w3_%d" % k, a, b, work.around("w2_%d" % k, a, b)[1])

        def put_sums(at, first, second, pairs):
            totals = [None] * len(pairs)
            for a in range(TOP, TOP + rows, 8):
                xs = [work.get(name, a, a + 8)[:, :cols] for name in first]
                ys = [work.get(name, a, a + 8)[:, :cols] for name in second]
                for p, (i, j) in enumerate(pairs):
                    term = xs[i] * ys[j]
                    totals[p] = term if totals[p] is None else totals[p] + term
            for p, total in enumerate(totals):
                folded = total[:, :LANE]
                for c in range(LANE, cols, LANE):
                    folded = folded + total[:, c : c + LANE]
                red[m, at + p : at + p + 1, :] = jnp.sum(folded, axis=0, keepdims=True)

        for i in range(6):
            low, high = i // 2, i - i // 2
            put_sums(i, ["v%d" % low], ["v%d" % high], [(0, 0)])
            names = [["w%d_%d" % (which, k) for k in range(4)] for which in (low, high)]
            put_sums(6 + i * len(PAIRS), names[0], names[1], PAIRS)
        return carry

    lax.fori_loop(0, members, one, 0)
    for m in range(members):
        out[m : m + 1, :] = jnp.sum(jnp.transpose(red[m]), axis=0, keepdims=True)


def plane_shape(rows, cols):
    return (2 * TOP + rows, cols + LANE)


def local_sums(source, theirs, fields, rims, total_rows):
    members, levels, rows, cols = fields[0].shape
    assert SUMS <= LANE and members <= 8
    shape = plane_shape(rows, cols)
    kept = (members, 4 * levels + 2 + len(KEPT)) + shape
    return pl.pallas_call(
        functools.partial(sums_kernel, levels, total_rows),
        out_shape=(
            jax.ShapeDtypeStruct((members, LANE), jnp.float32),
            jax.ShapeDtypeStruct(kept, jnp.float32),
            jax.ShapeDtypeStruct((members + 3,), jnp.int32),
        ),
        in_specs=in_smem(2) + in_hbm(6) + whole(6),
        out_specs=tuple(whole(2) + in_smem(1)),
        scratch_shapes=[
            pltpu.VMEM((len(SUM_NAMES) + levels,) + shape, jnp.float32),
            pltpu.VMEM(shape, jnp.float32),
            pltpu.VMEM(shape, jnp.float32),
            pltpu.VMEM((members, LANE, LANE), jnp.float32),
            pltpu.VMEM((rows, cols), jnp.int32),
            pltpu.SemaphoreType.DMA((members, 6)),
        ],
        compiler_params=pltpu.CompilerParams(vmem_limit_bytes=VMEM_LIMIT),
        cost_estimate=pl.CostEstimate(flops=10**8, bytes_accessed=4 * 10**6, transcendentals=0),
        name="local_sums",
    )(source, theirs, *fields, *rims)


def krylov(moment):
    n00, n01, n11, n12, n22, x22 = moment
    n02 = n11 - 4.0 * n00
    main, near = 1.0 + 4.0 * SURF_C, SURF_C
    g00 = main * n00 - near * n01
    g01 = main * n01 - near * n11
    g02 = main * n02 - near * n12
    g11 = main * n11 - near * (n12 + 4.0 * n01)
    g12 = main * n12 - near * (n22 + 4.0 * n02)
    g22 = main * n22 - near * x22
    l1, l2 = g01 / g00, g02 / g00
    d1 = g11 - l1 * g01
    d1 = jnp.where(d1 > 3e-7 * g11, d1, jnp.inf)
    e = g12 - l1 * g02
    l12 = e / d1
    d2 = g22 - l2 * g02 - l12 * e
    d2 = jnp.where(d2 > 3e-7 * g22, d2, jnp.inf)
    z0 = n00
    z1 = n01 - l1 * z0
    z2 = n02 - l2 * z0 - l12 * z1
    y2 = z2 / d2
    y1 = z1 / d1 - l12 * y2
    y0 = z0 / g00 - l1 * y1 - l2 * y2
    return [y0, y1, y2]


def weights(read):
    first = krylov([read(i) for i in range(6)])
    lifted = [None] + first
    second = []
    for i in range(6):
        total = None
        for p, (a, b) in enumerate(PAIRS):
            term = read(6 + i * len(PAIRS) + p)
            for k in (a, b):
                if k:
                    term = term * lifted[k]
            if a != b:
                term = 2.0 * term
            total = term if total is None else total + term
        second.append(total)
    return first, krylov(second)


RUN_NAMES = ["pu", "pv", "t2u", "t2v", "eta1", "w0", "w1", "w2", "eta2", "p", "p2", "gu1", "gv1", "gu2", "gv2"]


def advance_kernel(levels, total_rows, is_first, *refs):
    if is_first:
        info, tiles, kept, out, zonal = refs[:5]
        scratch = refs[5:]
    else:
        info, tiles, kept, zonal_before, out, spread = refs[:6]
        scratch = refs[6:]
    planes, after, turn, inside, staged, sums, sem = scratch[:7]
    rows, cols = out.shape[1:]
    members = kept.shape[0]
    tile_row = lax.axis_index("gridy")
    total = tiles[0]
    for i in range(1, tiles.shape[0]):
        total = total + tiles[i]
    staged[0:members, :] = total
    copy = pltpu.make_async_copy(staged, sums, sem)
    copy.start()
    fill_rows(turn, inside, tile_row * rows, total_rows)
    if not is_first:
        zonal = scratch[7]
    zonal[...] = jnp.zeros_like(zonal) if is_first else zonal_before[...]
    copy.wait()
    member = info[members + 2] if is_first else 1 - info[members + 2]
    ext = kept.at[member]
    work = Planes(levels, rows, turn, inside)
    work.add(planes, RUN_NAMES)
    work.add(kept, ["ext%d" % i for i in range(4 * levels)] + ["eta", "ocean"] + KEPT, (member,))

    def read(i):
        return jnp.full((1, 1), sums[member, i], jnp.float32)

    def combine(factors, names, out_name):
        for a, b in work.near():
            value = None
            for factor, name in zip(factors, names):
                term = factor * work.get(name, a, b)
                value = term if value is None else value + term
            work.put(out_name, a, b, value)

    first, second = weights(read)
    combine(first, ("v0", "v1", "v2"), "eta1")
    for a, b in work.near():
        ocean = work.get("ocean", a, b)
        slope_x, slope_y = work.slopes("eta1", a, b)
        slope_x, slope_y = GRAV * ocean * slope_x, GRAV * ocean * slope_y
        work.put("gu1", a, b, slope_x)
        work.put("gv1", a, b, slope_y)
        work.put("pu", a, b, work.get("tu", a, b) - levels * slope_x)
        work.put("pv", a, b, work.get("tv", a, b) - levels * slope_y)
    work.next_right_side("pu", "pv", "eta1", "q", "w0")
    work.powers("w0", "w1", "w2")
    combine(second, ("w0", "w1", "w2"), "eta2")
    for a, b in work.main():
        ocean = work.get("ocean", a, b)
        slope_x, slope_y = work.slopes("eta2", a, b)
        work.put("gu2", a, b, GRAV * ocean * slope_x)
        work.put("gv2", a, b, GRAV * ocean * slope_y)
        out[4 * levels, a - TOP : b - TOP, :] = work.get("eta2", a, b)[:, :cols]
    low, high = TOP - 8, TOP + rows + 8
    for a, b in chunks(TOP - CHUNK, TOP + rows + CHUNK):
        work.put("p", a, b, jnp.zeros((b - a, cols + LANE), jnp.float32))
        work.put("p2", a, b, jnp.zeros((b - a, cols + LANE), jnp.float32))

    def step(ref, l, press, a, b, width):
        def of(view):
            here = view[a:b, :]
            east, west = east_west(here)
            return here[:, :width], east[:, :width], west[:, :width], view[a + 1 : b + 1, :width], view[a - 1 : b - 1, :width]

        ocean = work.views["ocean"][a:b, :width]
        coriolis = turn[a:b, :width]
        u, east, west, north, south = of(ref.at[2 * levels + l])
        around_u = (east + west) + (north + south)
        v, east, west, north, south = of(ref.at[3 * levels + l])
        around_v = (east + west) + (north + south)
        _, east, west, north, south = of(work.views[press])
        new_u = ocean * ((KEEP_FLOW * u + VISCOSITY * around_u) + (coriolis * v - (east - west)))
        new_v = ocean * ((KEEP_FLOW * v + VISCOSITY * around_v) - (coriolis * u + (north - south)))
        flow_u, flow_v = ADV * u, ADV * v
        results = []
        for at in (l, levels + l):
            here, east, west, north, south = of(ref.at[at])
            carried = flow_u * (east - west) + flow_v * (north - south)
            spread = KEEP_TRACER * here + KAPPA * ((east + west) + (north + south))
            results.append(ocean * (spread - carried))
        return results[0], results[1], new_u, new_v

    def add_press(ref, l, press, a, b):
        dens = (PRESS_SCALE * BETA_S) * ref[levels + l, a:b, :] - (PRESS_SCALE * ALPHA_T) * ref[l, a:b, :]
        work.put(press, a, b, work.get(press, a, b) + dens)

    def level(l, carry):
        for a in range(TOP - CHUNK, TOP + rows + CHUNK, 8):
            add_press(ext, l, "p", a, a + 8)
        for a in range(low, high, 8):
            temp, salt, u, v = step(ext, l, "p", a, a + 8, cols + LANE)
            after[l, a : a + 8, :] = temp
            after[levels + l, a : a + 8, :] = salt
            after[2 * levels + l, a : a + 8, :] = u - work.get("gu1", a, a + 8)
            after[3 * levels + l, a : a + 8, :] = v - work.get("gv1", a, a + 8)
        for a in range(low, high, 8):
            add_press(after, l, "p2", a, a + 8)
        for a in range(TOP, TOP + rows, 8):
            temp, salt, u, v = step(after, l, "p2", a, a + 8, cols)
            here = slice(a - TOP, a - TOP + 8)
            v = v - work.get("gv2", a, a + 8)[:, :cols]
            out[l, here, :] = temp
            out[levels + l, here, :] = salt
            out[2 * levels + l, here, :] = u - work.get("gu2", a, a + 8)[:, :cols]
            out[3 * levels + l, here, :] = v
            row_sum = jnp.sum(v, axis=1, keepdims=True)
            zonal[here, :] = jnp.where(lanes_like((8, LANE)) == member * levels + l, row_sum, zonal[here, :])
        return carry

    lax.fori_loop(0, levels, level, 0)
    if not is_first:
        square = jnp.concatenate([zonal[...]] + [jnp.zeros_like(zonal)] * (LANE // rows - 1), axis=0)
        turned = jnp.transpose(square)[: members * levels]
        line = turned[:levels]
        for m in range(1, members):
            line = line + pltpu.roll(turned, m * rows, 1)[m * levels : (m + 1) * levels]
        for i in range(spread.shape[0]):
            spread[i] = line


def advance(is_first, info, tiles, kept, zonal, rows, cols, total_rows):
    members, planes = kept.shape[:2]
    levels = (planes - 2 - len(KEPT)) // 4
    assert members * rows == LANE and members * levels == 8
    shape = plane_shape(rows, cols)
    zonal_shape = jax.ShapeDtypeStruct((rows, LANE), jnp.float32)
    out_shape = [jax.ShapeDtypeStruct((4 * levels + 1, rows, cols), jnp.float32)]
    if is_first:
        out_shape += [zonal_shape]
    else:
        out_shape += [jax.ShapeDtypeStruct((tiles.shape[0], levels, members * rows), jnp.float32)]
    return pl.pallas_call(
        functools.partial(advance_kernel, levels, total_rows, is_first),
        out_shape=tuple(out_shape),
        in_specs=in_smem(1) + whole(2 if is_first else 3),
        out_specs=tuple(whole(2)),
        scratch_shapes=[
            pltpu.VMEM((len(RUN_NAMES),) + shape, jnp.float32),
            pltpu.VMEM((4 * levels,) + shape, jnp.float32),
            pltpu.VMEM(shape, jnp.float32),
            pltpu.VMEM(shape, jnp.float32),
            pltpu.VMEM((8, LANE), jnp.float32),
            pltpu.SMEM((8, LANE), jnp.float32),
            pltpu.SemaphoreType.DMA,
        ]
        + ([] if is_first else [pltpu.VMEM((rows, LANE), jnp.float32)]),
        compiler_params=pltpu.CompilerParams(vmem_limit_bytes=VMEM_LIMIT),
        cost_estimate=pl.CostEstimate(flops=10**8, bytes_accessed=4 * 10**6, transcendentals=0),
        name="advance",
    )(info, tiles, kept, *([] if is_first else [zonal]))


def finish_kernel(count_y, count_x, total_cols, spread, overturn, score, held):
    members, levels, rows = overturn.shape
    total_rows = rows * count_y
    lane = lanes_like(spread.shape[1:])
    member_of = lane // rows
    weighted = None
    for y in range(count_y):
        total = spread[y * count_x]
        for x in range(1, count_x):
            total = total + spread[y * count_x + x]
        lines = [total[0:1]]
        for l in range(1, levels):
            lines.append(lines[-1] + total[l : l + 1])
        lines = jnp.concatenate(lines, axis=0) * (total_cols**-0.5)
        held[y] = lines
        latitude = ((lane - member_of * rows + y * rows).astype(jnp.float32) + 0.5) * (1.0 / total_rows)
        weighted = lines * latitude if weighted is None else weighted + lines * latitude
    mine = held[lax.axis_index("gridy")]
    for m in range(members):
        overturn[m] = mine[:, m * rows : (m + 1) * rows]
        score[m] = jnp.sum(jnp.where(member_of == m, weighted, 0.0)) * ((levels * total_rows) ** -0.5)


def finish(spread, members, rows, count_y, count_x, cols):
    levels = spread.shape[1]
    return pl.pallas_call(
        functools.partial(finish_kernel, count_y, count_x, cols * count_x),
        out_shape=(
            jax.ShapeDtypeStruct((members, levels, rows), jnp.float32),
            jax.ShapeDtypeStruct((members,), jnp.float32),
        ),
        in_specs=whole(1),
        out_specs=(whole(1)[0], in_smem(1)[0]),
        scratch_shapes=[pltpu.VMEM((count_y,) + spread.shape[1:], jnp.float32)],
        compiler_params=pltpu.CompilerParams(vmem_limit_bytes=VMEM_LIMIT),
        name="finish",
    )(spread)


def pick_kernel(levels, choice, source, score, their_score, *refs):
    count = len(refs) - 7
    sources, outs, weight, sem = refs[:count], refs[count : count + 5], refs[count + 5], refs[count + 6]
    slots = outs[0].shape[0]

    def parts(s, source):
        for f in range(4):
            yield source.at[pl.ds(f * levels, levels)], outs[f].at[s]
        yield source.at[4 * levels], outs[4].at[s]

    for s in range(slots):
        for k in range(count):

            @pl.when(choice[s] == k)
            def _():
                for i, (one, target) in enumerate(parts(s, sources[k])):
                    pltpu.make_async_copy(one, target, sem.at[s, i]).start()

    side = lax.axis_index("member")
    mean = (sum(score[m] for m in range(slots)) + sum(their_score[m] for m in range(slots))) * (0.5 / slots)
    for s in range(slots):
        value = jnp.float32(0.0)
        for m in range(slots):
            value = jnp.where(source[s] == side * slots + m, score[m], value)
            value = jnp.where(source[s] == (1 - side) * slots + m, their_score[m], value)
        weight[s] = value - mean
    for s in range(slots):
        for i, (one, target) in enumerate(parts(s, sources[0])):
            pltpu.make_async_copy(one, target, sem.at[s, i]).wait()


def pick(choice, source, score, their_score, sources, slots, levels):
    _, rows, cols = sources[0].shape
    volume = jax.ShapeDtypeStruct((slots, levels, rows, cols), jnp.float32)
    surface = jax.ShapeDtypeStruct((slots, rows, cols), jnp.float32)
    return pl.pallas_call(
        functools.partial(pick_kernel, levels),
        out_shape=(volume,) * 4 + (surface, jax.ShapeDtypeStruct((slots,), jnp.float32)),
        in_specs=in_smem(4) + whole(len(sources)),
        out_specs=tuple(in_hbm(5) + in_smem(1)),
        scratch_shapes=[pltpu.SemaphoreType.DMA((slots, 5))],
        compiler_params=pltpu.CompilerParams(vmem_limit_bytes=VMEM_LIMIT),
        name="pick",
    )(choice, source, score, their_score, *sources)


def shift(value, axis, by):
    count = lax.axis_size(axis)
    return lax.ppermute(value, axis, [(i, (i + by) % count) for i in range(count)])


def exchange_rims(packed):
    to_west, to_east, rows_first, rows_second = packed
    rows = to_west.shape[1]
    count = lax.axis_size("gridy")
    assert count % 2 == 0
    partners = [i ^ 1 for i in range(count)], [min(max(i - 1 + 2 * (i % 2), 0), count - 1) for i in range(count)]

    def pair(value, which):
        return lax.ppermute(value, "gridy", list(enumerate(partners[which])))

    from_east, from_west = shift(to_west, "gridx", -1), shift(to_east, "gridx", 1)
    rows_first, rows_second = pair(rows_first, 0), pair(rows_second, 1)
    low = jnp.concatenate([from_east[:, :CHUNK], from_west[:, :CHUNK]], axis=2)
    high = jnp.concatenate([from_east[:, rows - CHUNK :], from_west[:, rows - CHUNK :]], axis=2)
    even = lax.axis_index("gridy") % 2 == 0
    sides_first = pair(jnp.where(even, high, low), 0)
    sides_second = pair(jnp.where(even, low, high), 1)
    return from_east, from_west, rows_first, rows_second, sides_first, sides_second


def from_all(tiles, axes):
    return lax.all_to_all(tiles, axes, split_axis=0, concat_axis=0, tiled=True)


def swap(value):
    return lax.ppermute(value, "member", [(0, 1), (1, 0)])


def shards(temp, salt, uvel, vvel, eta, land_mask, clone_source):
    members, levels, rows, cols = temp.shape
    assert members == 2 and lax.axis_size("member") == 2
    count_y, count_x = lax.axis_size("gridy"), lax.axis_size("gridx")
    total_rows = rows * count_y
    grid = ("gridy", "gridx")

    their_source = swap(clone_source)
    fields = (temp, salt, uvel, vvel, eta, land_mask)
    rims = exchange_rims(pack_rims(*fields))
    tile, kept, info = local_sums(clone_source, their_source, fields, rims, total_rows)
    tiles = from_all(jnp.broadcast_to(tile[None], (count_y * count_x,) + tile.shape), grid)

    sent, zonal = advance(True, info, tiles, kept, None, rows, cols, total_rows)
    arrived = swap(sent)

    def rest():
        other, spread = advance(False, info, tiles, kept, zonal, rows, cols, total_rows)
        return (other, *finish(from_all(spread, grid), members, rows, count_y, count_x, cols))

    def nothing():
        return jnp.zeros_like(sent), jnp.zeros((members, levels, rows), jnp.float32), jnp.zeros((members,), jnp.float32)

    other, overturn, score = lax.cond(info[members + 1] != 0, rest, nothing)
    their_score = swap(score)

    def with_second():
        sources = (sent, other, arrived, swap(other))
        return pick(info, clone_source, score, their_score, sources, members, levels)

    def without_second():
        return pick(info, clone_source, score, their_score, (sent, other, arrived), members, levels)

    *picked, clone_weight = lax.cond(info[members] != 0, with_second, without_second)
    return (*picked, overturn, clone_weight)


def solution(mesh):
    volume = P("member", None, "gridy", "gridx")
    in_specs = (volume,) * 4 + (P("member", "gridy", "gridx"), P("gridy", "gridx"), P("member"))
    out_specs = (volume,) * 4 + (P("member", "gridy", "gridx"), P("member", None, "gridy"), P("member"))
    return jax.shard_map(shards, mesh=mesh, in_specs=in_specs, out_specs=out_specs, check_vma=False)
```

```python
import functools

import jax
import jax.numpy as jnp
from jax import lax
from jax.experimental import pallas as pl
from jax.experimental.pallas import tpu as pltpu
from jax.sharding import PartitionSpec as P

STEPS = 2
ITERS = 3

ALPHA_T = 0.8
BETA_S = 0.6
PRESS_K = 0.25
STEP_DT = 0.1
KAPPA = 0.1
VISCOSITY = 0.1
DRAG_K = 0.05
CORI_K = 1.0
SURF_C = 4.0
DIV_K = 0.5
GRAV_K = 0.5

ADV = STEP_DT * 0.5
DIV = DIV_K * 0.5
GRAV = GRAV_K * 0.5

WIDE = 10
TOP = 24
CHUNK = 16
LANE = 128
PER_GROUP = 11
PAIRS = [(a, b) for a in range(4) for b in range(a, 4)]
SUMS = 6 + 6 * len(PAIRS)
VMEM_LIMIT = 24 * 1024 * 1024
WHOLE_VMEM = 60 * 1024 * 1024


def rim_place(plane):
    group, place = divmod(plane, PER_GROUP)
    if place < 6:
        return group, 0, (2 * place + 1) * WIDE
    return group, 1, (2 * (place - 6) + 2) * WIDE


def groups_of(planes):
    return -(-planes // PER_GROUP)


def lanes_like(shape):
    return lax.broadcasted_iota(jnp.int32, shape, len(shape) - 1)


def fetches(fields, planes_of, mask_to, sems, levels):
    members = fields[0].shape[0]
    per_member = []
    for m in range(members):
        parts = [(fields[f].at[m], planes_of(m, pl.ds(f * levels, levels))) for f in range(4)]
        parts.append((fields[4].at[m], planes_of(m, 4 * levels)))
        per_member.append([pltpu.make_async_copy(*part, sems.at[m, i]) for i, part in enumerate(parts)])
    mask_copy = pltpu.make_async_copy(fields[5], mask_to, sems.at[0, 5])
    mask_copy.start()
    for copies in per_member:
        for copy in copies:
            copy.start()
    mask_copy.wait()
    return per_member


def pack_kernel(levels, *refs):
    fields, (to_west, to_east, rows_first, rows_second), (held, mask, sems) = refs[:6], refs[6:10], refs[10:]
    members, _, rows, cols = held.shape
    planes = 4 * levels + 2
    copies = fetches(fields, lambda m, at: held.at[m, at], mask, sems, levels)
    lane = lanes_like((rows, LANE))
    even = lax.broadcasted_iota(jnp.int32, (WIDE, cols), 0) * 0 + lax.rem(lax.axis_index("gridy"), 2) == 0
    for m in range(members):
        for copy in copies[m]:
            copy.wait()
        west_parts = [None] * groups_of(planes)
        east_parts = [None] * groups_of(planes)
        for plane in range(planes):
            value = held[m, plane] if plane < planes - 1 else mask[...].astype(jnp.float32)
            group, _, start = rim_place(plane)
            both = jnp.where(lane < WIDE, value[:, :LANE], value[:, cols - LANE :])
            both = pltpu.roll(both, start, 1)
            is_west = (lane >= start) & (lane < start + WIDE)
            is_east = (lane >= start - WIDE) & (lane < start)
            zero = jnp.zeros_like(both)
            west_parts[group] = jnp.where(is_west, both, zero if west_parts[group] is None else west_parts[group])
            east_parts[group] = jnp.where(is_east, both, zero if east_parts[group] is None else east_parts[group])
            low, high = value[:WIDE], value[rows - WIDE :]
            rows_first[m, plane * WIDE : (plane + 1) * WIDE, :] = jnp.where(even, high, low)
            rows_second[m, plane * WIDE : (plane + 1) * WIDE, :] = jnp.where(even, low, high)
        for group in range(groups_of(planes)):
            where = slice(group * LANE, (group + 1) * LANE)
            to_west[m, :, where] = west_parts[group]
            to_east[m, :, where] = east_parts[group]


def whole(count):
    return [pl.BlockSpec(memory_space=pltpu.VMEM)] * count


def in_hbm(count):
    return [pl.BlockSpec(memory_space=pltpu.HBM)] * count


def in_smem(count):
    return [pl.BlockSpec(memory_space=pltpu.SMEM)] * count


def pack_rims(temp, salt, uvel, vvel, eta, mask):
    members, levels, rows, cols = temp.shape
    planes = 4 * levels + 2
    wide = groups_of(planes) * LANE
    row_pack = -(-planes * WIDE // 8) * 8
    side = jax.ShapeDtypeStruct((members, rows, wide), jnp.float32)
    line = jax.ShapeDtypeStruct((members, row_pack, cols), jnp.float32)
    return pl.pallas_call(
        functools.partial(pack_kernel, levels),
        out_shape=(side, side, line, line),
        in_specs=in_hbm(6),
        out_specs=tuple(whole(4)),
        scratch_shapes=[
            pltpu.VMEM((members, planes - 1, rows, cols), jnp.float32),
            pltpu.VMEM((rows, cols), jnp.int32),
            pltpu.SemaphoreType.DMA((members, 6)),
        ],
        compiler_params=pltpu.CompilerParams(vmem_limit_bytes=WHOLE_VMEM),
        name="pack_rims",
    )(temp, salt, uvel, vvel, eta, mask)


def east_west(value):
    width = value.shape[-1]
    return pltpu.roll(value, width - 1, 1), pltpu.roll(value, 1, 1)


def chunks(first, last):
    return [(a, min(a + CHUNK, last)) for a in range(first, last, CHUNK)]


def assemble(ext, mask, rims, m, levels, total_rows):
    from_east, from_west, rows_first, rows_second, sides_first, sides_second = rims
    planes = 4 * levels + 2
    rows, cols = mask.shape
    tile_row = lax.axis_index("gridy")
    odd_tile = lax.rem(tile_row, 2).astype(jnp.float32)
    keep_south = jnp.where(tile_row > 0, 1.0, 0.0).astype(jnp.float32)
    keep_north = jnp.where(tile_row * rows + rows < total_rows, 1.0, 0.0).astype(jnp.float32)
    north_factors = keep_north * (1.0 - odd_tile), keep_north * odd_tile
    south_factors = keep_south * odd_tile, keep_south * (1.0 - odd_tile)

    def of_north(first, second):
        return north_factors[0] * first + north_factors[1] * second

    def of_south(first, second):
        return south_factors[0] * first + south_factors[1] * second

    wide = groups_of(planes) * LANE
    for group in range(groups_of(planes)):
        where = slice(group * LANE, (group + 1) * LANE)
        where_west = slice(wide + group * LANE, wide + (group + 1) * LANE)
        east = sides_first[m, :, where], sides_second[m, :, where]
        west = sides_first[m, :, where_west], sides_second[m, :, where_west]
        bands = [(TOP - CHUNK, of_south(*east), of_south(*west))]
        for a in range(0, rows, CHUNK):
            bands.append((TOP + a, from_east[m, a : a + CHUNK, where], from_west[m, a : a + CHUNK, where]))
        bands.append((TOP + rows, of_north(*east), of_north(*west)))
        for at, east, west in bands:
            odd = ((lanes_like(east.shape) // WIDE) & 1) == 1
            joined = (jnp.where(odd, east, west), jnp.where(odd, west, east))
            for plane in range(group * PER_GROUP, min((group + 1) * PER_GROUP, planes)):
                _, kind, offset = rim_place(plane)
                ext[plane, at : at + CHUNK, cols : cols + LANE] = pltpu.roll(joined[kind], LANE - offset, 1)
    ext[planes - 1, TOP : TOP + rows, :cols] = mask[...].astype(jnp.float32)
    for plane in range(planes):
        at = slice(plane * WIDE, (plane + 1) * WIDE)
        ext[plane, TOP - WIDE : TOP, :cols] = of_south(rows_first[m, at, :], rows_second[m, at, :])
        ext[plane, TOP + rows : TOP + rows + WIDE, :cols] = of_north(rows_first[m, at, :], rows_second[m, at, :])


def fill_rows(turn, inside, first_row, total_rows):
    shape = (CHUNK, turn.shape[1])
    for a in range(0, turn.shape[0], CHUNK):
        row = first_row + (a - TOP) + lax.broadcasted_iota(jnp.int32, shape, 0)
        latitude = row.astype(jnp.float32) + 0.5
        turn[a : a + CHUNK, :] = STEP_DT * CORI_K * (2.0 * latitude / total_rows - 1.0)
        inside[a : a + CHUNK, :] = jnp.where((row >= 0) & (row < total_rows), 1.0, 0.0)


KEPT = ["tu", "tv", "q", "v0", "v1", "v2"]
KEEP_FLOW = 1.0 - STEP_DT * DRAG_K - 4.0 * VISCOSITY
KEEP_TRACER = 1.0 - 4.0 * KAPPA
PRESS_SCALE = PRESS_K * 0.5 * STEP_DT


class Planes:
    def __init__(self, levels, rows, turn, inside):
        self.levels, self.rows, self.turn, self.inside = levels, rows, turn, inside
        self.views = {}

    def add(self, ref, names, lead=()):
        for i, name in enumerate(names):
            self.views[name] = ref.at[lead + (i,)]

    def get(self, name, a, b):
        return self.views[name][a:b, :]

    def put(self, name, a, b, value):
        self.views[name][a:b, :] = value

    def sides(self, name, a, b):
        here = self.get(name, a, b)
        east, west = east_west(here)
        return here, east, west, self.get(name, a + 1, b + 1), self.get(name, a - 1, b - 1)

    def slopes(self, name, a, b):
        _, east, west, north, south = self.sides(name, a, b)
        return east - west, north - south

    def around(self, name, a, b):
        here, east, west, north, south = self.sides(name, a, b)
        return here, (east + west) + (north + south)

    def main(self):
        return chunks(TOP, TOP + self.rows)

    def near(self):
        return [(TOP - 8, TOP)] + self.main() + [(TOP + self.rows, TOP + self.rows + 8)]

    def masked(self, a, b, value):
        if a >= TOP and b <= TOP + self.rows:
            return value
        return self.inside[a:b, :] * value

    def divergence(self, u_name, v_name, a, b):
        east, west = east_west(self.get(u_name, a, b))
        return DIV * ((east - west) + (self.get(v_name, a + 1, b + 1) - self.get(v_name, a - 1, b - 1)))

    def flow(self, u_name, v_name, press, out_u, out_v, a, b):
        ocean, turn = self.get("ocean", a, b), self.turn[a:b, :]
        u, around_u = self.around(u_name, a, b)
        v, around_v = self.around(v_name, a, b)
        push_u, push_v = turn * v, turn * u
        if press:
            slope_x, slope_y = self.slopes(press, a, b)
            push_u, push_v = push_u - slope_x, push_v + slope_y
        self.put(out_u, a, b, ocean * ((KEEP_FLOW * u + VISCOSITY * around_u) + push_u))
        self.put(out_v, a, b, ocean * ((KEEP_FLOW * v + VISCOSITY * around_v) - push_v))

    def powers(self, first, second, third):
        for a, b in self.near():
            self.put(second, a, b, self.masked(a, b, self.around(first, a, b)[1]))
        for a, b in self.near():
            value = self.around(second, a, b)[1] - 4.0 * self.get(first, a, b)
            self.put(third, a, b, self.masked(a, b, value))

    def next_right_side(self, u_name, v_name, eta_name, press, out_name):
        for a, b in self.near():
            self.flow(u_name, v_name, press, "t2u", "t2v", a, b)
        for a, b in self.near():
            div = self.divergence("t2u", "t2v", a, b)
            value = self.get(eta_name, a, b) - div if eta_name else -div
            self.put(out_name, a, b, self.masked(a, b, value))


def scaled(factor, value):
    return value if factor == 1.0 else factor * value


def surface_start(ext, work):
    levels = work.levels
    low, high = TOP - CHUNK, TOP + work.rows + CHUNK
    for a, b in chunks(low, high):
        su = sv = sp = None
        for l in range(levels):
            factor = PRESS_SCALE * (levels - l)
            dens = (factor * BETA_S) * ext[levels + l, a:b, :] - (factor * ALPHA_T) * ext[l, a:b, :]
            work.put("d%d" % l, a, b, dens)
            u, v = ext[2 * levels + l, a:b, :], ext[3 * levels + l, a:b, :]
            su, sv, sp = (u, v, dens) if l == 0 else (su + u, sv + v, sp + dens)
        work.put("su", a, b, su)
        work.put("sv", a, b, sv)
        work.put("sp", a, b, sp)
    for a, b in work.near():
        carried = None
        for l in range(levels):
            slope_x, slope_y = work.slopes("d%d" % l, a, b)
            term = ext[2 * levels + l, a:b, :] * slope_x + ext[3 * levels + l, a:b, :] * slope_y
            carried = term if l == 0 else carried + term
        here, around = work.around("sp", a, b)
        work.put("q", a, b, work.get("ocean", a, b) * ((KEEP_TRACER * here + KAPPA * around) - ADV * carried))
    for a, b in chunks(low, high):
        work.flow("su", "sv", "sp", "tu", "tv", a, b)
    for a, b in work.near():
        work.put("v0", a, b, work.masked(a, b, work.get("eta", a, b) - work.divergence("tu", "tv", a, b)))


SUM_NAMES = ["su", "sv", "sp", "v3", "pu", "pv", "t2u", "t2v"] + ["w%d_%d" % (i, k) for i in range(4) for k in range(4)]


def whether(*conditions):
    result = jnp.int32(0)
    for condition in conditions:
        result = jnp.where(condition, 1, result)
    return result


def choose(source, theirs, side, members, info):
    mine, away = side * members, (1 - side) * members
    sent = [whether(*[theirs[slot] == mine + m for slot in range(members)]) for m in range(2)]
    here = [whether(*[source[slot] == away + m for slot in range(members)]) for m in range(2)]
    first_sent, first_here = 1 - sent[0], 1 - here[0]
    for slot in range(members):
        own = jnp.where(source[slot] - mine == first_sent, 0, 1)
        far = jnp.where(source[slot] - away == first_here, 2, 3)
        info[slot] = jnp.where((source[slot] >= mine) & (source[slot] < mine + members), own, far)
    info[members] = jnp.maximum(sent[0] * sent[1], here[0] * here[1])
    info[members + 1] = jnp.int32(1)
    info[members + 2] = first_sent


def sums_kernel(levels, total_rows, source, theirs, *refs):
    fields, rims, out, kept, info = refs[:6], refs[6:12], refs[12], refs[13], refs[14]
    planes, turn, inside, red, mask, sems = refs[15:]
    members = kept.shape[0]
    rows, cols = mask.shape
    copies = fetches(fields, lambda m, at: kept.at[m, at, pl.ds(TOP, rows), pl.ds(0, cols)], mask, sems, levels)
    tile_row = lax.axis_index("gridy")
    choose(source, theirs, lax.axis_index("member"), members, info)
    fill_rows(turn, inside, tile_row * rows, total_rows)
    red[...] = jnp.zeros_like(red)
    for m in range(members):
        assemble(kept.at[m], mask, rims, m, levels, total_rows)
    for copy in sum(copies, []):
        copy.wait()

    def one(m, carry):
        ext = kept.at[m]
        work = Planes(levels, rows, turn, inside)
        work.add(planes, SUM_NAMES + ["d%d" % l for l in range(levels)])
        work.add(kept, ["ext%d" % i for i in range(4 * levels)] + ["eta", "ocean"] + KEPT, (m,))
        surface_start(ext, work)
        work.powers("v0", "v1", "v2")
        for a, b in work.main():
            work.put("v3", a, b, work.around("v2", a, b)[1])
        work.next_right_side("tu", "tv", None, "q", "w0_0")
        for k in range(1, 4):
            name = "v%d" % (k - 1)
            for a, b in work.near():
                ocean = work.get("ocean", a, b)
                slope_x, slope_y = work.slopes(name, a, b)
                work.put("pu", a, b, scaled(-levels * GRAV, ocean * slope_x))
                work.put("pv", a, b, scaled(-levels * GRAV, ocean * slope_y))
            work.next_right_side("pu", "pv", name, None, "w0_%d" % k)
        for k in range(4):
            work.powers("w0_%d" % k, "w1_%d" % k, "w2_%d" % k)
            for a, b in work.main():
                work.put("w3_%d" % k, a, b, work.around("w2_%d" % k, a, b)[1])

        def put_sums(at, first, second, pairs):
            totals = [None] * len(pairs)
            for a in range(TOP, TOP + rows, 8):
                xs = [work.get(name, a, a + 8)[:, :cols] for name in first]
                ys = [work.get(name, a, a + 8)[:, :cols] for name in second]
                for p, (i, j) in enumerate(pairs):
                    term = xs[i] * ys[j]
                    totals[p] = term if totals[p] is None else totals[p] + term
            for p, total in enumerate(totals):
                folded = total[:, :LANE]
                for c in range(LANE, cols, LANE):
                    folded = folded + total[:, c : c + LANE]
                red[m, at + p : at + p + 1, :] = jnp.sum(folded, axis=0, keepdims=True)

        for i in range(6):
            low, high = i // 2, i - i // 2
            put_sums(i, ["v%d" % low], ["v%d" % high], [(0, 0)])
            names = [["w%d_%d" % (which, k) for k in range(4)] for which in (low, high)]
            put_sums(6 + i * len(PAIRS), names[0], names[1], PAIRS)
        return carry

    lax.fori_loop(0, members, one, 0)
    for m in range(members):
        out[m : m + 1, :] = jnp.sum(jnp.transpose(red[m]), axis=0, keepdims=True)


def plane_shape(rows, cols):
    return (2 * TOP + rows, cols + LANE)


def local_sums(source, theirs, fields, rims, total_rows):
    members, levels, rows, cols = fields[0].shape
    assert SUMS <= LANE and members <= 8
    shape = plane_shape(rows, cols)
    kept = (members, 4 * levels + 2 + len(KEPT)) + shape
    return pl.pallas_call(
        functools.partial(sums_kernel, levels, total_rows),
        out_shape=(
            jax.ShapeDtypeStruct((members, LANE), jnp.float32),
            jax.ShapeDtypeStruct(kept, jnp.float32),
            jax.ShapeDtypeStruct((members + 3,), jnp.int32),
        ),
        in_specs=in_smem(2) + in_hbm(6) + whole(6),
        out_specs=tuple(whole(2) + in_smem(1)),
        scratch_shapes=[
            pltpu.VMEM((len(SUM_NAMES) + levels,) + shape, jnp.float32),
            pltpu.VMEM(shape, jnp.float32),
            pltpu.VMEM(shape, jnp.float32),
            pltpu.VMEM((members, LANE, LANE), jnp.float32),
            pltpu.VMEM((rows, cols), jnp.int32),
            pltpu.SemaphoreType.DMA((members, 6)),
        ],
        compiler_params=pltpu.CompilerParams(vmem_limit_bytes=VMEM_LIMIT),
        cost_estimate=pl.CostEstimate(flops=10**8, bytes_accessed=4 * 10**6, transcendentals=0),
        name="local_sums",
    )(source, theirs, *fields, *rims)


def krylov(moment):
    n00, n01, n11, n12, n22, x22 = moment
    n02 = n11 - 4.0 * n00
    main, near = 1.0 + 4.0 * SURF_C, SURF_C
    g00 = main * n00 - near * n01
    g01 = main * n01 - near * n11
    g02 = main * n02 - near * n12
    g11 = main * n11 - near * (n12 + 4.0 * n01)
    g12 = main * n12 - near * (n22 + 4.0 * n02)
    g22 = main * n22 - near * x22
    l1, l2 = g01 / g00, g02 / g00
    d1 = g11 - l1 * g01
    d1 = jnp.where(d1 > 3e-7 * g11, d1, jnp.inf)
    e = g12 - l1 * g02
    l12 = e / d1
    d2 = g22 - l2 * g02 - l12 * e
    d2 = jnp.where(d2 > 3e-7 * g22, d2, jnp.inf)
    z0 = n00
    z1 = n01 - l1 * z0
    z2 = n02 - l2 * z0 - l12 * z1
    y2 = z2 / d2
    y1 = z1 / d1 - l12 * y2
    y0 = z0 / g00 - l1 * y1 - l2 * y2
    return [y0, y1, y2]


def weights(read):
    first = krylov([read(i) for i in range(6)])
    lifted = [None] + first
    second = []
    for i in range(6):
        total = None
        for p, (a, b) in enumerate(PAIRS):
            term = read(6 + i * len(PAIRS) + p)
            for k in (a, b):
                if k:
                    term = term * lifted[k]
            if a != b:
                term = 2.0 * term
            total = term if total is None else total + term
        second.append(total)
    return first, krylov(second)


RUN_NAMES = ["pu", "pv", "t2u", "t2v", "eta1", "w0", "w1", "w2", "eta2", "p2", "gu1", "gv1", "gu2", "gv2"]


def member_planes(kept, member, levels, rows, turn, inside):
    work = Planes(levels, rows, turn, inside)
    work.add(kept, ["ext%d" % i for i in range(4 * levels)] + ["eta", "ocean"] + KEPT, (member,))
    return work


def add_press(planes, l, levels, press, a, b):
    dens = (PRESS_SCALE * BETA_S) * planes[levels + l, a:b, :] - (PRESS_SCALE * ALPHA_T) * planes[l, a:b, :]
    press[a:b, :] = press[a:b, :] + dens


def explicit_step(work, press, views, a, b, width):
    def of(view):
        here = view[a:b, :]
        east, west = east_west(here)
        return here[:, :width], east[:, :width], west[:, :width], view[a + 1 : b + 1, :width], view[a - 1 : b - 1, :width]

    ocean = work.views["ocean"][a:b, :width]
    coriolis = work.turn[a:b, :width]
    u, east, west, north, south = of(views[2])
    around_u = (east + west) + (north + south)
    v, east, west, north, south = of(views[3])
    around_v = (east + west) + (north + south)
    _, east, west, north, south = of(press)
    new_u = ocean * ((KEEP_FLOW * u + VISCOSITY * around_u) + (coriolis * v - (east - west)))
    new_v = ocean * ((KEEP_FLOW * v + VISCOSITY * around_v) - (coriolis * u + (north - south)))
    flow_u, flow_v = ADV * u, ADV * v
    results = []
    for view in views[:2]:
        here, east, west, north, south = of(view)
        carried = flow_u * (east - west) + flow_v * (north - south)
        spread = KEEP_TRACER * here + KAPPA * ((east + west) + (north + south))
        results.append(ocean * (spread - carried))
    return results[0], results[1], new_u, new_v


def step_kernel(levels, total_rows, kept, after, press, turn, inside):
    members = kept.shape[0]
    rows = kept.shape[2] - 2 * TOP
    fill_rows(turn, inside, lax.axis_index("gridy") * rows, total_rows)

    def level(i, carry):
        m, l = i // levels, i % levels
        work = member_planes(kept, m, levels, rows, turn, inside)

        @pl.when(l == 0)
        def _():
            for a, b in chunks(TOP - CHUNK, TOP + rows + CHUNK):
                press[a:b, :] = jnp.zeros((b - a, press.shape[1]), jnp.float32)

        for a in range(TOP - CHUNK, TOP + rows + CHUNK, 8):
            add_press(kept.at[m], l, levels, press, a, a + 8)
        views = [kept.at[m, f * levels + l] for f in range(4)]
        for a in range(TOP - 8, TOP + rows + 8, 8):
            for f, value in enumerate(explicit_step(work, press, views, a, a + 8, press.shape[1])):
                after[m, f * levels + l, a : a + 8, :] = value
        return carry

    lax.fori_loop(0, members * levels, level, 0)


def first_step(kept, levels, total_rows):
    shape = kept.shape[2:]
    return pl.pallas_call(
        functools.partial(step_kernel, levels, total_rows),
        out_shape=jax.ShapeDtypeStruct((kept.shape[0], 4 * levels) + shape, jnp.float32),
        in_specs=whole(1),
        out_specs=whole(1)[0],
        scratch_shapes=[pltpu.VMEM(shape, jnp.float32)] * 3,
        compiler_params=pltpu.CompilerParams(vmem_limit_bytes=VMEM_LIMIT),
        cost_estimate=pl.CostEstimate(flops=10**7, bytes_accessed=10**6, transcendentals=0),
        name="first_step",
    )(kept)


def advance_kernel(levels, total_rows, is_first, parts, *refs):
    info, tiles, kept, after, zonal_before = refs[:5]
    outs, last = refs[5 : 5 + len(parts)], refs[5 + len(parts)]
    planes, flows, turn, inside, staged, sums, sem, zonal = refs[6 + len(parts) :]
    half = levels // 2
    rows, cols = kept.shape[2] - 2 * TOP, kept.shape[3] - LANE
    members = kept.shape[0]
    tile_row = lax.axis_index("gridy")
    total = tiles[0]
    for i in range(1, tiles.shape[0]):
        total = total + tiles[i]
    staged[0:members, :] = total
    copy = pltpu.make_async_copy(staged, sums, sem)
    copy.start()
    fill_rows(turn, inside, tile_row * rows, total_rows)
    zonal[...] = zonal_before[...]
    copy.wait()
    member = info[members + 2] if is_first else 1 - info[members + 2]
    work = member_planes(kept, member, levels, rows, turn, inside)
    work.add(planes, RUN_NAMES)

    def read(i):
        return jnp.full((1, 1), sums[member, i], jnp.float32)

    def combine(factors, names, out_name):
        for a, b in work.near():
            value = None
            for factor, name in zip(factors, names):
                term = factor * work.get(name, a, b)
                value = term if value is None else value + term
            work.put(out_name, a, b, value)

    first, second = weights(read)
    combine(first, ("v0", "v1", "v2"), "eta1")
    for a, b in work.near():
        ocean = work.get("ocean", a, b)
        slope_x, slope_y = work.slopes("eta1", a, b)
        slope_x, slope_y = GRAV * ocean * slope_x, GRAV * ocean * slope_y
        work.put("gu1", a, b, slope_x)
        work.put("gv1", a, b, slope_y)
        work.put("pu", a, b, work.get("tu", a, b) - levels * slope_x)
        work.put("pv", a, b, work.get("tv", a, b) - levels * slope_y)
    work.next_right_side("pu", "pv", "eta1", "q", "w0")
    work.powers("w0", "w1", "w2")
    combine(second, ("w0", "w1", "w2"), "eta2")
    for a, b in work.main():
        ocean = work.get("ocean", a, b)
        slope_x, slope_y = work.slopes("eta2", a, b)
        work.put("gu2", a, b, GRAV * ocean * slope_x)
        work.put("gv2", a, b, GRAV * ocean * slope_y)
        if 0 in parts:
            outs[0][4 * half, a - TOP : b - TOP, :] = work.get("eta2", a, b)[:, :cols]
    low, high = TOP - 8, TOP + rows + 8
    press = work.views["p2"]
    for a, b in work.near():
        press[a:b, :] = jnp.zeros((b - a, cols + LANE), jnp.float32)

    def press_only(l, carry):
        for a in range(low, high, 8):
            add_press(after.at[member], l, levels, press, a, a + 8)
        return carry

    def level_of(out, start):
        def level(l, carry):
            press_only(l, carry)
            for a in range(low, high, 8):
                flows[0, a : a + 8, :] = after[member, 2 * levels + l, a : a + 8, :] - work.get("gu1", a, a + 8)
                flows[1, a : a + 8, :] = after[member, 3 * levels + l, a : a + 8, :] - work.get("gv1", a, a + 8)
            views = [after.at[member, l], after.at[member, levels + l], flows.at[0], flows.at[1]]
            for a in range(TOP, TOP + rows, 8):
                temp, salt, u, v = explicit_step(work, press, views, a, a + 8, cols)
                here = slice(a - TOP, a - TOP + 8)
                v = v - work.get("gv2", a, a + 8)[:, :cols]
                out[l - start, here, :] = temp
                out[half + l - start, here, :] = salt
                out[2 * half + l - start, here, :] = u - work.get("gu2", a, a + 8)[:, :cols]
                out[3 * half + l - start, here, :] = v
                row_sum = jnp.sum(v, axis=1, keepdims=True)
                zonal[here, :] = jnp.where(lanes_like((8, LANE)) == member * levels + l, row_sum, zonal[here, :])
            return carry

        return level

    if parts[0]:
        lax.fori_loop(0, half, press_only, 0)
    for part, out in zip(parts, outs):
        lax.fori_loop(part * half, part * half + half, level_of(out, part * half), 0)
    if is_first:
        last[...] = zonal[...]
    else:
        square = jnp.concatenate([zonal[...]] + [jnp.zeros_like(zonal)] * (LANE // rows - 1), axis=0)
        turned = jnp.transpose(square)[: members * levels]
        line = turned[:levels]
        for m in range(1, members):
            line = line + pltpu.roll(turned, m * rows, 1)[m * levels : (m + 1) * levels]
        for i in range(last.shape[0]):
            last[i] = line


def advance(is_first, parts, info, tiles, kept, after, zonal, total_rows):
    members, _, *shape = kept.shape
    levels = after.shape[1] // 4
    rows, cols = shape[0] - 2 * TOP, shape[1] - LANE
    shape = tuple(shape)
    assert members * rows == LANE and members * levels == 8 and levels % 2 == 0
    out_shape = [jax.ShapeDtypeStruct((2 * levels + (part == 0), rows, cols), jnp.float32) for part in parts]
    last = (rows, LANE) if is_first else (tiles.shape[0], levels, members * rows)
    return pl.pallas_call(
        functools.partial(advance_kernel, levels, total_rows, is_first, parts),
        out_shape=tuple(out_shape) + (jax.ShapeDtypeStruct(last, jnp.float32),),
        in_specs=in_smem(1) + whole(4),
        out_specs=tuple(whole(len(parts) + 1)),
        scratch_shapes=[
            pltpu.VMEM((len(RUN_NAMES),) + shape, jnp.float32),
            pltpu.VMEM((2,) + shape, jnp.float32),
            pltpu.VMEM(shape, jnp.float32),
            pltpu.VMEM(shape, jnp.float32),
            pltpu.VMEM((8, LANE), jnp.float32),
            pltpu.SMEM((8, LANE), jnp.float32),
            pltpu.SemaphoreType.DMA,
            pltpu.VMEM((rows, LANE), jnp.float32),
        ],
        compiler_params=pltpu.CompilerParams(vmem_limit_bytes=VMEM_LIMIT),
        cost_estimate=pl.CostEstimate(flops=10**8, bytes_accessed=4 * 10**6, transcendentals=0),
        name="advance",
    )(info, tiles, kept, after, zonal)


def finish_kernel(count_y, count_x, total_cols, spread, overturn, score, held):
    members, levels, rows = overturn.shape
    total_rows = rows * count_y
    lane = lanes_like(spread.shape[1:])
    member_of = lane // rows
    weighted = None
    for y in range(count_y):
        total = spread[y * count_x]
        for x in range(1, count_x):
            total = total + spread[y * count_x + x]
        lines = [total[0:1]]
        for l in range(1, levels):
            lines.append(lines[-1] + total[l : l + 1])
        lines = jnp.concatenate(lines, axis=0) * (total_cols**-0.5)
        held[y] = lines
        latitude = ((lane - member_of * rows + y * rows).astype(jnp.float32) + 0.5) * (1.0 / total_rows)
        weighted = lines * latitude if weighted is None else weighted + lines * latitude
    mine = held[lax.axis_index("gridy")]
    for m in range(members):
        overturn[m] = mine[:, m * rows : (m + 1) * rows]
        score[m] = jnp.sum(jnp.where(member_of == m, weighted, 0.0)) * ((levels * total_rows) ** -0.5)


def finish(spread, members, rows, count_y, count_x, cols):
    levels = spread.shape[1]
    return pl.pallas_call(
        functools.partial(finish_kernel, count_y, count_x, cols * count_x),
        out_shape=(
            jax.ShapeDtypeStruct((members, levels, rows), jnp.float32),
            jax.ShapeDtypeStruct((members,), jnp.float32),
        ),
        in_specs=whole(1),
        out_specs=(whole(1)[0], in_smem(1)[0]),
        scratch_shapes=[pltpu.VMEM((count_y,) + spread.shape[1:], jnp.float32)],
        compiler_params=pltpu.CompilerParams(vmem_limit_bytes=VMEM_LIMIT),
        name="finish",
    )(spread)


def pick_kernel(levels, choice, source, score, their_score, *refs):
    count = (len(refs) - 7) // 2
    sources = [refs[2 * k : 2 * k + 2] for k in range(count)]
    outs, weight, sem = refs[2 * count : 2 * count + 5], refs[2 * count + 5], refs[2 * count + 6]
    slots = outs[0].shape[0]
    half = levels // 2

    def parts(s, source):
        for part in range(2):
            for f in range(4):
                yield source[part].at[pl.ds(f * half, half)], outs[f].at[s, pl.ds(part * half, half)]
        yield source[0].at[4 * half], outs[4].at[s]

    for s in range(slots):
        for k in range(count):

            @pl.when(choice[s] == k)
            def _():
                for i, (one, target) in enumerate(parts(s, sources[k])):
                    pltpu.make_async_copy(one, target, sem.at[s, i]).start()

    side = lax.axis_index("member")
    mean = (sum(score[m] for m in range(slots)) + sum(their_score[m] for m in range(slots))) * (0.5 / slots)
    for s in range(slots):
        value = jnp.float32(0.0)
        for m in range(slots):
            value = jnp.where(source[s] == side * slots + m, score[m], value)
            value = jnp.where(source[s] == (1 - side) * slots + m, their_score[m], value)
        weight[s] = value - mean
    for s in range(slots):
        for i, (one, target) in enumerate(parts(s, sources[0])):
            pltpu.make_async_copy(one, target, sem.at[s, i]).wait()


def pick(choice, source, score, their_score, sources, slots, levels):
    _, rows, cols = sources[0][0].shape
    volume = jax.ShapeDtypeStruct((slots, levels, rows, cols), jnp.float32)
    surface = jax.ShapeDtypeStruct((slots, rows, cols), jnp.float32)
    return pl.pallas_call(
        functools.partial(pick_kernel, levels),
        out_shape=(volume,) * 4 + (surface, jax.ShapeDtypeStruct((slots,), jnp.float32)),
        in_specs=in_smem(4) + whole(2 * len(sources)),
        out_specs=tuple(in_hbm(5) + in_smem(1)),
        scratch_shapes=[pltpu.SemaphoreType.DMA((slots, 9))],
        compiler_params=pltpu.CompilerParams(vmem_limit_bytes=VMEM_LIMIT),
        name="pick",
    )(choice, source, score, their_score, *sum(sources, ()))


def shift(value, axis, by):
    count = lax.axis_size(axis)
    return lax.ppermute(value, axis, [(i, (i + by) % count) for i in range(count)])


def exchange_rims(packed):
    to_west, to_east, rows_first, rows_second = packed
    rows = to_west.shape[1]
    count = lax.axis_size("gridy")
    assert count % 2 == 0
    partners = [i ^ 1 for i in range(count)], [min(max(i - 1 + 2 * (i % 2), 0), count - 1) for i in range(count)]

    def pair(value, which):
        return lax.ppermute(value, "gridy", list(enumerate(partners[which])))

    from_east, from_west = shift(to_west, "gridx", -1), shift(to_east, "gridx", 1)
    rows_first, rows_second = pair(rows_first, 0), pair(rows_second, 1)
    low = jnp.concatenate([from_east[:, :CHUNK], from_west[:, :CHUNK]], axis=2)
    high = jnp.concatenate([from_east[:, rows - CHUNK :], from_west[:, rows - CHUNK :]], axis=2)
    even = lax.axis_index("gridy") % 2 == 0
    sides_first = pair(jnp.where(even, high, low), 0)
    sides_second = pair(jnp.where(even, low, high), 1)
    return from_east, from_west, rows_first, rows_second, sides_first, sides_second


def from_all(tiles, axes):
    return lax.all_to_all(tiles, axes, split_axis=0, concat_axis=0, tiled=True)


def swap(value):
    return lax.ppermute(value, "member", [(0, 1), (1, 0)])


def shards(temp, salt, uvel, vvel, eta, land_mask, clone_source):
    members, levels, rows, cols = temp.shape
    assert members == 2 and lax.axis_size("member") == 2
    count_y, count_x = lax.axis_size("gridy"), lax.axis_size("gridx")
    total_rows = rows * count_y
    grid = ("gridy", "gridx")

    fields = (temp, salt, uvel, vvel, eta, land_mask)
    packed, their_source = lax.optimization_barrier((pack_rims(*fields), swap(clone_source)))
    rims = exchange_rims(packed)
    tile, kept, info = local_sums(clone_source, their_source, fields, rims, total_rows)
    tiles = from_all(jnp.broadcast_to(tile[None], (count_y * count_x,) + tile.shape), grid)
    after = first_step(kept, levels, total_rows)

    def advanced(is_first, parts, zonal):
        return advance(is_first, parts, info, tiles, kept, after, zonal, total_rows)

    def lower_half():
        low, zonal = advanced(True, (1,), zonal_high)
        arrived_low = swap(low)

        def rest():
            *other, spread = advanced(False, (0, 1), zonal)
            return (*other, *finish(from_all(spread, grid), members, rows, count_y, count_x, cols))

        def nothing():
            surface = jnp.zeros((members, levels, rows), jnp.float32)
            return jnp.zeros_like(high), jnp.zeros_like(low), surface, jnp.zeros((members,), jnp.float32)

        return (low, arrived_low, *lax.cond(always, rest, nothing))

    def no_half():
        low = jnp.zeros((2 * levels, rows, cols), jnp.float32)
        surface = jnp.zeros((members, levels, rows), jnp.float32)
        return low, low, jnp.zeros_like(high), low, surface, jnp.zeros((members,), jnp.float32)

    always = info[members + 1] != 0
    high, zonal_high = advanced(True, (0,), jnp.zeros((rows, LANE), jnp.float32))
    arrived_high = swap(high)
    low, arrived_low, other_high, other_low, overturn, score = lax.cond(always, lower_half, no_half)
    their_score = swap(score)

    def with_second():
        sources = ((high, low), (other_high, other_low), (arrived_high, arrived_low), (swap(other_high), swap(other_low)))
        return pick(info, clone_source, score, their_score, sources, members, levels)

    def without_second():
        sources = ((high, low), (other_high, other_low), (arrived_high, arrived_low))
        return pick(info, clone_source, score, their_score, sources, members, levels)

    *picked, clone_weight = lax.cond(info[members] != 0, with_second, without_second)
    return (*picked, overturn, clone_weight)


def solution(mesh):
    volume = P("member", None, "gridy", "gridx")
    in_specs = (volume,) * 4 + (P("member", "gridy", "gridx"), P("gridy", "gridx"), P("member"))
    out_specs = (volume,) * 4 + (P("member", "gridy", "gridx"), P("member", None, "gridy"), P("member"))
    return jax.shard_map(shards, mesh=mesh, in_specs=in_specs, out_specs=out_specs, check_vma=False)
```

```python
import functools

import jax
import jax.numpy as jnp
from jax import lax
from jax.experimental import pallas as pl
from jax.experimental.pallas import tpu as pltpu
from jax.sharding import PartitionSpec as P

STEPS = 2
ITERS = 3

ALPHA_T = 0.8
BETA_S = 0.6
PRESS_K = 0.25
STEP_DT = 0.1
KAPPA = 0.1
VISCOSITY = 0.1
DRAG_K = 0.05
CORI_K = 1.0
SURF_C = 4.0
DIV_K = 0.5
GRAV_K = 0.5

ADV = STEP_DT * 0.5
DIV = DIV_K * 0.5
GRAV = GRAV_K * 0.5
KEEP_FLOW = 1.0 - STEP_DT * DRAG_K - 4.0 * VISCOSITY
KEEP_TRACER = 1.0 - 4.0 * KAPPA
PRESS_SCALE = PRESS_K * 0.5 * STEP_DT

TOP = 24
CHUNK = 16
LANE = 128
PAIRS = [(a, b) for a in range(4) for b in range(a, 4)]
SUMS = 6 + 6 * len(PAIRS)
VMEM_LIMIT = 24 * 1024 * 1024
WHOLE_VMEM = 60 * 1024 * 1024


def rim_layout(levels):
    widths = [("d%d" % l, 6) for l in range(levels)]
    widths += [("ext%d" % (2 * levels + i), 5) for i in range(2 * levels)]
    widths += [("ext%d" % i, 2) for i in range(2 * levels)]
    widths += [("su", 10), ("sv", 10), ("sp", 10), ("eta", 8), ("ocean", 10)]
    layout, start = [], 0
    for name, width in widths:
        layout.append((name, width, start))
        start += width
    assert start <= LANE
    return layout


def level_sums(ext, levels):
    dens = []
    for l in range(levels):
        factor = PRESS_SCALE * (levels - l)
        dens.append((factor * BETA_S) * ext(levels + l) - (factor * ALPHA_T) * ext(l))
    su, sv, sp = ext(2 * levels), ext(3 * levels), dens[0]
    for l in range(1, levels):
        su, sv, sp = su + ext(2 * levels + l), sv + ext(3 * levels + l), sp + dens[l]
    return dens, su, sv, sp


def lanes_like(shape):
    return lax.broadcasted_iota(jnp.int32, shape, len(shape) - 1)


def fetches(fields, planes_of, mask_to, sems, levels):
    def copies(m):
        parts = [(fields[f].at[m], planes_of(m, pl.ds(f * levels, levels))) for f in range(4)]
        parts.append((fields[4].at[m], planes_of(m, 4 * levels)))
        return [pltpu.make_async_copy(*part, sems.at[m, i]) for i, part in enumerate(parts)]

    mask_copy = pltpu.make_async_copy(fields[5], mask_to, sems.at[0, 5])
    mask_copy.start()
    for m in range(fields[0].shape[0]):
        for copy in copies(m):
            copy.start()
    mask_copy.wait()
    return copies


def pack_kernel(levels, *refs):
    fields, (to_west, to_east, rows_first, rows_second), (held, mask, sems) = refs[:6], refs[6:10], refs[10:]
    members, _, rows, cols = held.shape
    copies = fetches(fields, lambda m, at: held.at[m, at], mask, sems, levels)
    lane = lanes_like((rows, LANE))
    even = lax.broadcasted_iota(jnp.int32, (CHUNK, cols), 0) * 0 + lax.rem(lax.axis_index("gridy"), 2) == 0
    for m in range(members):
        for copy in copies(m):
            copy.wait()
        dens, *sums = level_sums(lambda i: held[m, i], levels)
        planes = dict(zip(["su", "sv", "sp"], sums), eta=held[m, 4 * levels], ocean=mask[...].astype(jnp.float32))
        planes.update({"d%d" % l: dens[l] for l in range(levels)})
        west = east = jnp.zeros((rows, LANE), jnp.float32)
        for name, width, start in rim_layout(levels):
            value = held[m, int(name[3:])] if name.startswith("ext") else planes[name]
            here = (lane >= start) & (lane < start + width)
            both = jnp.where(lane < LANE // 2, value[:, :LANE], value[:, cols - LANE :])
            west = jnp.where(here, pltpu.roll(both, start, 1) if start else both, west)
            east = jnp.where(here, pltpu.roll(both, (start + width) % LANE, 1) if start + width < LANE else both, east)
            low, high = value[:width], value[rows - width :]
            rows_first[m, start : start + width, :] = jnp.where(even[:width], high, low)
            rows_second[m, start : start + width, :] = jnp.where(even[:width], low, high)
        to_west[m] = west
        to_east[m] = east


def whole(count):
    return [pl.BlockSpec(memory_space=pltpu.VMEM)] * count


def in_hbm(count):
    return [pl.BlockSpec(memory_space=pltpu.HBM)] * count


def in_smem(count):
    return [pl.BlockSpec(memory_space=pltpu.SMEM)] * count


def pack_rims(temp, salt, uvel, vvel, eta, mask):
    members, levels, rows, cols = temp.shape
    side = jax.ShapeDtypeStruct((members, rows, LANE), jnp.float32)
    line = jax.ShapeDtypeStruct((members, LANE, cols), jnp.float32)
    return pl.pallas_call(
        functools.partial(pack_kernel, levels),
        out_shape=(side, side, line, line),
        in_specs=in_hbm(6),
        out_specs=tuple(whole(4)),
        scratch_shapes=[
            pltpu.VMEM((members, 4 * levels + 1, rows, cols), jnp.float32),
            pltpu.VMEM((rows, cols), jnp.int32),
            pltpu.SemaphoreType.DMA((members, 6)),
        ],
        compiler_params=pltpu.CompilerParams(vmem_limit_bytes=WHOLE_VMEM),
        name="pack_rims",
    )(temp, salt, uvel, vvel, eta, mask)


def east_west(value):
    width = value.shape[-1]
    return pltpu.roll(value, width - 1, 1), pltpu.roll(value, 1, 1)


def chunks(first, last):
    return [(a, min(a + CHUNK, last)) for a in range(first, last, CHUNK)]


def assemble(views, mask, rims, m, levels, total_rows):
    from_east, from_west, rows_first, rows_second, sides_first, sides_second = rims
    rows, cols = mask.shape
    tile_row = lax.axis_index("gridy")
    odd_tile = lax.rem(tile_row, 2).astype(jnp.float32)
    keep_south = jnp.where(tile_row > 0, 1.0, 0.0).astype(jnp.float32)
    keep_north = jnp.where(tile_row * rows + rows < total_rows, 1.0, 0.0).astype(jnp.float32)
    north_factors = keep_north * (1.0 - odd_tile), keep_north * odd_tile
    south_factors = keep_south * odd_tile, keep_south * (1.0 - odd_tile)

    def of_north(first, second):
        return north_factors[0] * first + north_factors[1] * second

    def of_south(first, second):
        return south_factors[0] * first + south_factors[1] * second

    east = sides_first[m, :, :LANE], sides_second[m, :, :LANE]
    west = sides_first[m, :, LANE:], sides_second[m, :, LANE:]
    bands = [(TOP - CHUNK, of_south(*east), of_south(*west))]
    for a in range(0, rows, CHUNK):
        bands.append((TOP + a, from_east[m, a : a + CHUNK, :], from_west[m, a : a + CHUNK, :]))
    bands.append((TOP + rows, of_north(*east), of_north(*west)))
    is_east = lanes_like((CHUNK, LANE)) < LANE // 2
    layout = rim_layout(levels)
    for at, east, west in bands:
        for name, width, start in layout:
            left = pltpu.roll(east, LANE - start, 1) if start else east
            right = pltpu.roll(west, LANE - width - start, 1) if start + width < LANE else west
            views[name][at : at + CHUNK, cols : cols + LANE] = jnp.where(is_east, left, right)
    for name, width, start in layout:
        at = slice(start, start + width)
        views[name][TOP - width : TOP, :cols] = of_south(rows_first[m, at, :], rows_second[m, at, :])
        views[name][TOP + rows : TOP + rows + width, :cols] = of_north(rows_first[m, at, :], rows_second[m, at, :])
    views["ocean"][TOP : TOP + rows, :cols] = mask[...].astype(jnp.float32)


def fill_rows(turn, inside, first_row, total_rows):
    shape = (CHUNK, turn.shape[1])
    for a in range(0, turn.shape[0], CHUNK):
        row = first_row + (a - TOP) + lax.broadcasted_iota(jnp.int32, shape, 0)
        latitude = row.astype(jnp.float32) + 0.5
        turn[a : a + CHUNK, :] = STEP_DT * CORI_K * (2.0 * latitude / total_rows - 1.0)
        inside[a : a + CHUNK, :] = jnp.where((row >= 0) & (row < total_rows), 1.0, 0.0)


KEPT = ["tu", "tv", "q", "v0", "v1", "v2"]


class Planes:
    def __init__(self, levels, rows, turn, inside):
        self.levels, self.rows, self.turn, self.inside = levels, rows, turn, inside
        self.views = {}

    def add(self, ref, names, lead=()):
        for i, name in enumerate(names):
            self.views[name] = ref.at[lead + (i,)]

    def get(self, name, a, b):
        return self.views[name][a:b, :]

    def put(self, name, a, b, value):
        self.views[name][a:b, :] = value

    def sides(self, name, a, b):
        here = self.get(name, a, b)
        east, west = east_west(here)
        return here, east, west, self.get(name, a + 1, b + 1), self.get(name, a - 1, b - 1)

    def slopes(self, name, a, b):
        _, east, west, north, south = self.sides(name, a, b)
        return east - west, north - south

    def around(self, name, a, b):
        here, east, west, north, south = self.sides(name, a, b)
        return here, (east + west) + (north + south)

    def main(self):
        return chunks(TOP, TOP + self.rows)

    def near(self):
        return [(TOP - 8, TOP)] + self.main() + [(TOP + self.rows, TOP + self.rows + 8)]

    def masked(self, a, b, value):
        if a >= TOP and b <= TOP + self.rows:
            return value
        return self.inside[a:b, :] * value

    def divergence(self, u_name, v_name, a, b):
        east, west = east_west(self.get(u_name, a, b))
        return DIV * ((east - west) + (self.get(v_name, a + 1, b + 1) - self.get(v_name, a - 1, b - 1)))

    def flow(self, u_name, v_name, press, out_u, out_v, a, b):
        ocean, turn = self.get("ocean", a, b), self.turn[a:b, :]
        u, around_u = self.around(u_name, a, b)
        v, around_v = self.around(v_name, a, b)
        push_u, push_v = turn * v, turn * u
        if press:
            slope_x, slope_y = self.slopes(press, a, b)
            push_u, push_v = push_u - slope_x, push_v + slope_y
        self.put(out_u, a, b, ocean * ((KEEP_FLOW * u + VISCOSITY * around_u) + push_u))
        self.put(out_v, a, b, ocean * ((KEEP_FLOW * v + VISCOSITY * around_v) - push_v))

    def powers(self, first, second, third):
        for a, b in self.near():
            self.put(second, a, b, self.masked(a, b, self.around(first, a, b)[1]))
        for a, b in self.near():
            value = self.around(second, a, b)[1] - 4.0 * self.get(first, a, b)
            self.put(third, a, b, self.masked(a, b, value))

    def next_right_side(self, u_name, v_name, eta_name, press, out_name):
        for a, b in self.near():
            self.flow(u_name, v_name, press, "t2u", "t2v", a, b)
        for a, b in self.near():
            div = self.divergence("t2u", "t2v", a, b)
            value = self.get(eta_name, a, b) - div if eta_name else -div
            self.put(out_name, a, b, self.masked(a, b, value))


def scaled(factor, value):
    return value if factor == 1.0 else factor * value


def surface_start(ext, work):
    levels = work.levels
    low, high = TOP - CHUNK, TOP + work.rows + CHUNK
    cols = work.turn.shape[1] - LANE
    for a, b in work.main():
        dens, *sums = level_sums(lambda i: ext[i, a:b, :cols], levels)
        for l in range(levels):
            work.views["d%d" % l][a:b, :cols] = dens[l]
        for name, value in zip(("su", "sv", "sp"), sums):
            work.views[name][a:b, :cols] = value
    for a, b in work.near():
        carried = None
        for l in range(levels):
            slope_x, slope_y = work.slopes("d%d" % l, a, b)
            term = ext[2 * levels + l, a:b, :] * slope_x + ext[3 * levels + l, a:b, :] * slope_y
            carried = term if l == 0 else carried + term
        here, around = work.around("sp", a, b)
        work.put("q", a, b, work.get("ocean", a, b) * ((KEEP_TRACER * here + KAPPA * around) - ADV * carried))
    for a, b in chunks(low, high):
        work.flow("su", "sv", "sp", "tu", "tv", a, b)
    for a, b in work.near():
        work.put("v0", a, b, work.masked(a, b, work.get("eta", a, b) - work.divergence("tu", "tv", a, b)))


SUM_NAMES = ["su", "sv", "sp", "v3", "pu", "pv", "t2u", "t2v"] + ["w%d_%d" % (i, k) for i in range(4) for k in range(4)]


def whether(*conditions):
    result = jnp.int32(0)
    for condition in conditions:
        result = jnp.where(condition, 1, result)
    return result


def choose(source, theirs, side, members, info):
    mine, away = side * members, (1 - side) * members
    sent = [whether(*[theirs[slot] == mine + m for slot in range(members)]) for m in range(2)]
    here = [whether(*[source[slot] == away + m for slot in range(members)]) for m in range(2)]
    first_sent, first_here = 1 - sent[0], 1 - here[0]
    for slot in range(members):
        own = jnp.where(source[slot] - mine == first_sent, 0, 1)
        far = jnp.where(source[slot] - away == first_here, 2, 3)
        info[slot] = jnp.where((source[slot] >= mine) & (source[slot] < mine + members), own, far)
    info[members] = jnp.maximum(sent[0] * sent[1], here[0] * here[1])
    info[members + 1] = jnp.int32(1)
    info[members + 2] = first_sent


def sums_kernel(levels, total_rows, source, theirs, *refs):
    fields, rims, out, kept, info = refs[:6], refs[6:12], refs[12], refs[13], refs[14]
    planes, turn, inside, red, mask, sems = refs[15:]
    members = kept.shape[0]
    rows, cols = mask.shape
    member_copies = fetches(fields, lambda m, at: kept.at[m, at, pl.ds(TOP, rows), pl.ds(0, cols)], mask, sems, levels)
    tile_row = lax.axis_index("gridy")
    choose(source, theirs, lax.axis_index("member"), members, info)
    fill_rows(turn, inside, tile_row * rows, total_rows)
    red[...] = jnp.zeros_like(red)

    def one(m, carry):
        ext = kept.at[m]
        work = Planes(levels, rows, turn, inside)
        work.add(planes, SUM_NAMES + ["d%d" % l for l in range(levels)])
        work.add(kept, ["ext%d" % i for i in range(4 * levels)] + ["eta", "ocean"] + KEPT, (m,))
        assemble(work.views, mask, rims, m, levels, total_rows)
        for copy in member_copies(m):
            copy.wait()
        surface_start(ext, work)
        work.powers("v0", "v1", "v2")
        for a, b in work.main():
            work.put("v3", a, b, work.around("v2", a, b)[1])
        work.next_right_side("tu", "tv", None, "q", "w0_0")
        for k in range(1, 4):
            name = "v%d" % (k - 1)
            for a, b in work.near():
                ocean = work.get("ocean", a, b)
                slope_x, slope_y = work.slopes(name, a, b)
                work.put("pu", a, b, scaled(-levels * GRAV, ocean * slope_x))
                work.put("pv", a, b, scaled(-levels * GRAV, ocean * slope_y))
            work.next_right_side("pu", "pv", name, None, "w0_%d" % k)
        for k in range(4):
            work.powers("w0_%d" % k, "w1_%d" % k, "w2_%d" % k)
            for a, b in work.main():
                work.put("w3_%d" % k, a, b, work.around("w2_%d" % k, a, b)[1])

        def put_sums(at, first, second, pairs):
            totals = [None] * len(pairs)
            for a in range(TOP, TOP + rows, 8):
                xs = [work.get(name, a, a + 8)[:, :cols] for name in first]
                ys = [work.get(name, a, a + 8)[:, :cols] for name in second]
                for p, (i, j) in enumerate(pairs):
                    term = xs[i] * ys[j]
                    totals[p] = term if totals[p] is None else totals[p] + term
            for p, total in enumerate(totals):
                folded = total[:, :LANE]
                for c in range(LANE, cols, LANE):
                    folded = folded + total[:, c : c + LANE]
                red[m, at + p : at + p + 1, :] = jnp.sum(folded, axis=0, keepdims=True)

        for i in range(6):
            low, high = i // 2, i - i // 2
            put_sums(i, ["v%d" % low], ["v%d" % high], [(0, 0)])
            names = [["w%d_%d" % (which, k) for k in range(4)] for which in (low, high)]
            put_sums(6 + i * len(PAIRS), names[0], names[1], PAIRS)
        return carry

    lax.fori_loop(0, members, one, 0)
    for m in range(members):
        out[m : m + 1, :] = jnp.sum(jnp.transpose(red[m]), axis=0, keepdims=True)


def plane_shape(rows, cols):
    return (2 * TOP + rows, cols + LANE)


def local_sums(source, theirs, fields, rims, total_rows):
    members, levels, rows, cols = fields[0].shape
    assert SUMS <= LANE and members <= 8
    shape = plane_shape(rows, cols)
    kept = (members, 4 * levels + 2 + len(KEPT)) + shape
    return pl.pallas_call(
        functools.partial(sums_kernel, levels, total_rows),
        out_shape=(
            jax.ShapeDtypeStruct((members, LANE), jnp.float32),
            jax.ShapeDtypeStruct(kept, jnp.float32),
            jax.ShapeDtypeStruct((members + 3,), jnp.int32),
        ),
        in_specs=in_smem(2) + in_hbm(6) + whole(6),
        out_specs=tuple(whole(2) + in_smem(1)),
        scratch_shapes=[
            pltpu.VMEM((len(SUM_NAMES) + levels,) + shape, jnp.float32),
            pltpu.VMEM(shape, jnp.float32),
            pltpu.VMEM(shape, jnp.float32),
            pltpu.VMEM((members, LANE, LANE), jnp.float32),
            pltpu.VMEM((rows, cols), jnp.int32),
            pltpu.SemaphoreType.DMA((members, 6)),
        ],
        compiler_params=pltpu.CompilerParams(vmem_limit_bytes=VMEM_LIMIT),
        cost_estimate=pl.CostEstimate(flops=10**8, bytes_accessed=4 * 10**6, transcendentals=0),
        name="local_sums",
    )(source, theirs, *fields, *rims)


def krylov(moment):
    n00, n01, n11, n12, n22, x22 = moment
    n02 = n11 - 4.0 * n00
    main, near = 1.0 + 4.0 * SURF_C, SURF_C
    g00 = main * n00 - near * n01
    g01 = main * n01 - near * n11
    g02 = main * n02 - near * n12
    g11 = main * n11 - near * (n12 + 4.0 * n01)
    g12 = main * n12 - near * (n22 + 4.0 * n02)
    g22 = main * n22 - near * x22
    l1, l2 = g01 / g00, g02 / g00
    d1 = g11 - l1 * g01
    d1 = jnp.where(d1 > 3e-7 * g11, d1, jnp.inf)
    e = g12 - l1 * g02
    l12 = e / d1
    d2 = g22 - l2 * g02 - l12 * e
    d2 = jnp.where(d2 > 3e-7 * g22, d2, jnp.inf)
    z0 = n00
    z1 = n01 - l1 * z0
    z2 = n02 - l2 * z0 - l12 * z1
    y2 = z2 / d2
    y1 = z1 / d1 - l12 * y2
    y0 = z0 / g00 - l1 * y1 - l2 * y2
    return [y0, y1, y2]


def weights(read):
    first = krylov([read(i) for i in range(6)])
    lifted = [None] + first
    second = []
    for i in range(6):
        total = None
        for p, (a, b) in enumerate(PAIRS):
            term = read(6 + i * len(PAIRS) + p)
            for k in (a, b):
                if k:
                    term = term * lifted[k]
            if a != b:
                term = 2.0 * term
            total = term if total is None else total + term
        second.append(total)
    return first, krylov(second)


RUN_NAMES = ["pu", "pv", "t2u", "t2v", "eta1", "w0", "w1", "w2", "eta2", "p", "p2", "gu1", "gv1", "gu2", "gv2"]


def advance_kernel(levels, total_rows, is_first, *refs):
    if is_first:
        info, tiles, kept, out, zonal = refs[:5]
        scratch = refs[5:]
    else:
        info, tiles, kept, zonal_before, out, spread = refs[:6]
        scratch = refs[6:]
    planes, after, turn, inside, staged, sums, sem = scratch[:7]
    rows, cols = out.shape[1:]
    members = kept.shape[0]
    tile_row = lax.axis_index("gridy")
    total = tiles[0]
    for i in range(1, tiles.shape[0]):
        total = total + tiles[i]
    staged[0:members, :] = total
    copy = pltpu.make_async_copy(staged, sums, sem)
    copy.start()
    fill_rows(turn, inside, tile_row * rows, total_rows)
    if not is_first:
        zonal = scratch[7]
    zonal[...] = jnp.zeros_like(zonal) if is_first else zonal_before[...]
    copy.wait()
    member = info[members + 2] if is_first else 1 - info[members + 2]
    ext = kept.at[member]
    work = Planes(levels, rows, turn, inside)
    work.add(planes, RUN_NAMES)
    work.add(kept, ["ext%d" % i for i in range(4 * levels)] + ["eta", "ocean"] + KEPT, (member,))

    def read(i):
        return jnp.full((1, 1), sums[member, i], jnp.float32)

    def combine(factors, names, out_name):
        for a, b in work.near():
            value = None
            for factor, name in zip(factors, names):
                term = factor * work.get(name, a, b)
                value = term if value is None else value + term
            work.put(out_name, a, b, value)

    first, second = weights(read)
    combine(first, ("v0", "v1", "v2"), "eta1")
    for a, b in work.near():
        ocean = work.get("ocean", a, b)
        slope_x, slope_y = work.slopes("eta1", a, b)
        slope_x, slope_y = GRAV * ocean * slope_x, GRAV * ocean * slope_y
        work.put("gu1", a, b, slope_x)
        work.put("gv1", a, b, slope_y)
        work.put("pu", a, b, work.get("tu", a, b) - levels * slope_x)
        work.put("pv", a, b, work.get("tv", a, b) - levels * slope_y)
    work.next_right_side("pu", "pv", "eta1", "q", "w0")
    work.powers("w0", "w1", "w2")
    combine(second, ("w0", "w1", "w2"), "eta2")
    for a, b in work.main():
        ocean = work.get("ocean", a, b)
        slope_x, slope_y = work.slopes("eta2", a, b)
        work.put("gu2", a, b, GRAV * ocean * slope_x)
        work.put("gv2", a, b, GRAV * ocean * slope_y)
        out[4 * levels, a - TOP : b - TOP, :] = work.get("eta2", a, b)[:, :cols]
    low, high = TOP - 8, TOP + rows + 8
    for a, b in chunks(TOP - CHUNK, TOP + rows + CHUNK):
        work.put("p", a, b, jnp.zeros((b - a, cols + LANE), jnp.float32))
        work.put("p2", a, b, jnp.zeros((b - a, cols + LANE), jnp.float32))

    def step(ref, l, press, a, b, width):
        def of(view):
            here = view[a:b, :]
            east, west = east_west(here)
            return here[:, :width], east[:, :width], west[:, :width], view[a + 1 : b + 1, :width], view[a - 1 : b - 1, :width]

        ocean = work.views["ocean"][a:b, :width]
        coriolis = turn[a:b, :width]
        u, east, west, north, south = of(ref.at[2 * levels + l])
        around_u = (east + west) + (north + south)
        v, east, west, north, south = of(ref.at[3 * levels + l])
        around_v = (east + west) + (north + south)
        _, east, west, north, south = of(work.views[press])
        new_u = ocean * ((KEEP_FLOW * u + VISCOSITY * around_u) + (coriolis * v - (east - west)))
        new_v = ocean * ((KEEP_FLOW * v + VISCOSITY * around_v) - (coriolis * u + (north - south)))
        flow_u, flow_v = ADV * u, ADV * v
        results = []
        for at in (l, levels + l):
            here, east, west, north, south = of(ref.at[at])
            carried = flow_u * (east - west) + flow_v * (north - south)
            spread = KEEP_TRACER * here + KAPPA * ((east + west) + (north + south))
            results.append(ocean * (spread - carried))
        return results[0], results[1], new_u, new_v

    def add_press(ref, l, press, a, b):
        dens = (PRESS_SCALE * BETA_S) * ref[levels + l, a:b, :] - (PRESS_SCALE * ALPHA_T) * ref[l, a:b, :]
        work.put(press, a, b, work.get(press, a, b) + dens)

    def level(l, carry):
        for a in range(TOP - CHUNK, TOP + rows + CHUNK, 8):
            add_press(ext, l, "p", a, a + 8)
        for a in range(low, high, 8):
            temp, salt, u, v = step(ext, l, "p", a, a + 8, cols + LANE)
            after[l, a : a + 8, :] = temp
            after[levels + l, a : a + 8, :] = salt
            after[2 * levels + l, a : a + 8, :] = u - work.get("gu1", a, a + 8)
            after[3 * levels + l, a : a + 8, :] = v - work.get("gv1", a, a + 8)
        for a in range(low, high, 8):
            add_press(after, l, "p2", a, a + 8)
        for a in range(TOP, TOP + rows, 8):
            temp, salt, u, v = step(after, l, "p2", a, a + 8, cols)
            here = slice(a - TOP, a - TOP + 8)
            v = v - work.get("gv2", a, a + 8)[:, :cols]
            out[l, here, :] = temp
            out[levels + l, here, :] = salt
            out[2 * levels + l, here, :] = u - work.get("gu2", a, a + 8)[:, :cols]
            out[3 * levels + l, here, :] = v
            row_sum = jnp.sum(v, axis=1, keepdims=True)
            zonal[here, :] = jnp.where(lanes_like((8, LANE)) == member * levels + l, row_sum, zonal[here, :])
        return carry

    lax.fori_loop(0, levels, level, 0)
    if not is_first:
        square = jnp.concatenate([zonal[...]] + [jnp.zeros_like(zonal)] * (LANE // rows - 1), axis=0)
        turned = jnp.transpose(square)[: members * levels]
        line = turned[:levels]
        for m in range(1, members):
            line = line + pltpu.roll(turned, m * rows, 1)[m * levels : (m + 1) * levels]
        for i in range(spread.shape[0]):
            spread[i] = line


def advance(is_first, info, tiles, kept, zonal, rows, cols, total_rows):
    members, planes = kept.shape[:2]
    levels = (planes - 2 - len(KEPT)) // 4
    assert members * rows == LANE and members * levels == 8
    shape = plane_shape(rows, cols)
    zonal_shape = jax.ShapeDtypeStruct((rows, LANE), jnp.float32)
    out_shape = [jax.ShapeDtypeStruct((4 * levels + 1, rows, cols), jnp.float32)]
    if is_first:
        out_shape += [zonal_shape]
    else:
        out_shape += [jax.ShapeDtypeStruct((tiles.shape[0], levels, members * rows), jnp.float32)]
    return pl.pallas_call(
        functools.partial(advance_kernel, levels, total_rows, is_first),
        out_shape=tuple(out_shape),
        in_specs=in_smem(1) + whole(2 if is_first else 3),
        out_specs=tuple(whole(2)),
        scratch_shapes=[
            pltpu.VMEM((len(RUN_NAMES),) + shape, jnp.float32),
            pltpu.VMEM((4 * levels,) + shape, jnp.float32),
            pltpu.VMEM(shape, jnp.float32),
            pltpu.VMEM(shape, jnp.float32),
            pltpu.VMEM((8, LANE), jnp.float32),
            pltpu.SMEM((8, LANE), jnp.float32),
            pltpu.SemaphoreType.DMA,
        ]
        + ([] if is_first else [pltpu.VMEM((rows, LANE), jnp.float32)]),
        compiler_params=pltpu.CompilerParams(vmem_limit_bytes=VMEM_LIMIT),
        cost_estimate=pl.CostEstimate(flops=10**8, bytes_accessed=4 * 10**6, transcendentals=0),
        name="advance",
    )(info, tiles, kept, *([] if is_first else [zonal]))


def finish_kernel(count_y, count_x, total_cols, spread, overturn, score, held):
    members, levels, rows = overturn.shape
    total_rows = rows * count_y
    lane = lanes_like(spread.shape[1:])
    member_of = lane // rows
    weighted = None
    for y in range(count_y):
        total = spread[y * count_x]
        for x in range(1, count_x):
            total = total + spread[y * count_x + x]
        lines = [total[0:1]]
        for l in range(1, levels):
            lines.append(lines[-1] + total[l : l + 1])
        lines = jnp.concatenate(lines, axis=0) * (total_cols**-0.5)
        held[y] = lines
        latitude = ((lane - member_of * rows + y * rows).astype(jnp.float32) + 0.5) * (1.0 / total_rows)
        weighted = lines * latitude if weighted is None else weighted + lines * latitude
    mine = held[lax.axis_index("gridy")]
    for m in range(members):
        overturn[m] = mine[:, m * rows : (m + 1) * rows]
        score[m] = jnp.sum(jnp.where(member_of == m, weighted, 0.0)) * ((levels * total_rows) ** -0.5)


def finish(spread, members, rows, count_y, count_x, cols):
    levels = spread.shape[1]
    return pl.pallas_call(
        functools.partial(finish_kernel, count_y, count_x, cols * count_x),
        out_shape=(
            jax.ShapeDtypeStruct((members, levels, rows), jnp.float32),
            jax.ShapeDtypeStruct((members,), jnp.float32),
        ),
        in_specs=whole(1),
        out_specs=(whole(1)[0], in_smem(1)[0]),
        scratch_shapes=[pltpu.VMEM((count_y,) + spread.shape[1:], jnp.float32)],
        compiler_params=pltpu.CompilerParams(vmem_limit_bytes=VMEM_LIMIT),
        name="finish",
    )(spread)


def pick_kernel(levels, choice, source, score, their_score, *refs):
    count = len(refs) - 7
    sources, outs, weight, sem = refs[:count], refs[count : count + 5], refs[count + 5], refs[count + 6]
    slots = outs[0].shape[0]

    def parts(s, source):
        for f in range(4):
            yield source.at[pl.ds(f * levels, levels)], outs[f].at[s]
        yield source.at[4 * levels], outs[4].at[s]

    for s in range(slots):
        for k in range(count):

            @pl.when(choice[s] == k)
            def _():
                for i, (one, target) in enumerate(parts(s, sources[k])):
                    pltpu.make_async_copy(one, target, sem.at[s, i]).start()

    side = lax.axis_index("member")
    mean = (sum(score[m] for m in range(slots)) + sum(their_score[m] for m in range(slots))) * (0.5 / slots)
    for s in range(slots):
        value = jnp.float32(0.0)
        for m in range(slots):
            value = jnp.where(source[s] == side * slots + m, score[m], value)
            value = jnp.where(source[s] == (1 - side) * slots + m, their_score[m], value)
        weight[s] = value - mean
    for s in range(slots):
        for i, (one, target) in enumerate(parts(s, sources[0])):
            pltpu.make_async_copy(one, target, sem.at[s, i]).wait()


def pick(choice, source, score, their_score, sources, slots, levels):
    _, rows, cols = sources[0].shape
    volume = jax.ShapeDtypeStruct((slots, levels, rows, cols), jnp.float32)
    surface = jax.ShapeDtypeStruct((slots, rows, cols), jnp.float32)
    return pl.pallas_call(
        functools.partial(pick_kernel, levels),
        out_shape=(volume,) * 4 + (surface, jax.ShapeDtypeStruct((slots,), jnp.float32)),
        in_specs=in_smem(4) + whole(len(sources)),
        out_specs=tuple(in_hbm(5) + in_smem(1)),
        scratch_shapes=[pltpu.SemaphoreType.DMA((slots, 5))],
        compiler_params=pltpu.CompilerParams(vmem_limit_bytes=VMEM_LIMIT),
        name="pick",
    )(choice, source, score, their_score, *sources)


def shift(value, axis, by):
    count = lax.axis_size(axis)
    return lax.ppermute(value, axis, [(i, (i + by) % count) for i in range(count)])


def exchange_rims(packed):
    to_west, to_east, rows_first, rows_second = packed
    rows = to_west.shape[1]
    count = lax.axis_size("gridy")
    assert count % 2 == 0
    partners = [i ^ 1 for i in range(count)], [min(max(i - 1 + 2 * (i % 2), 0), count - 1) for i in range(count)]

    def pair(value, which):
        return lax.ppermute(value, "gridy", list(enumerate(partners[which])))

    from_east, from_west = shift(to_west, "gridx", -1), shift(to_east, "gridx", 1)
    rows_first, rows_second = pair(rows_first, 0), pair(rows_second, 1)
    low = jnp.concatenate([from_east[:, :CHUNK], from_west[:, :CHUNK]], axis=2)
    high = jnp.concatenate([from_east[:, rows - CHUNK :], from_west[:, rows - CHUNK :]], axis=2)
    even = lax.axis_index("gridy") % 2 == 0
    sides_first = pair(jnp.where(even, high, low), 0)
    sides_second = pair(jnp.where(even, low, high), 1)
    return from_east, from_west, rows_first, rows_second, sides_first, sides_second


def from_all(tiles, axes):
    return lax.all_to_all(tiles, axes, split_axis=0, concat_axis=0, tiled=True)


def swap(value):
    return lax.ppermute(value, "member", [(0, 1), (1, 0)])


def shards(temp, salt, uvel, vvel, eta, land_mask, clone_source):
    members, levels, rows, cols = temp.shape
    assert members == 2 and lax.axis_size("member") == 2
    count_y, count_x = lax.axis_size("gridy"), lax.axis_size("gridx")
    total_rows = rows * count_y
    grid = ("gridy", "gridx")

    fields = (temp, salt, uvel, vvel, eta, land_mask)
    packed, their_source = lax.optimization_barrier((pack_rims(*fields), swap(clone_source)))
    rims = exchange_rims(packed)
    tile, kept, info = local_sums(clone_source, their_source, fields, rims, total_rows)
    tiles = from_all(jnp.broadcast_to(tile[None], (count_y * count_x,) + tile.shape), grid)

    sent, zonal = advance(True, info, tiles, kept, None, rows, cols, total_rows)
    arrived = swap(sent)

    def rest():
        other, spread = advance(False, info, tiles, kept, zonal, rows, cols, total_rows)
        return (other, *finish(from_all(spread, grid), members, rows, count_y, count_x, cols))

    def nothing():
        return jnp.zeros_like(sent), jnp.zeros((members, levels, rows), jnp.float32), jnp.zeros((members,), jnp.float32)

    other, overturn, score = lax.cond(info[members + 1] != 0, rest, nothing)
    their_score = swap(score)

    def with_second():
        sources = (sent, other, arrived, swap(other))
        return pick(info, clone_source, score, their_score, sources, members, levels)

    def without_second():
        return pick(info, clone_source, score, their_score, (sent, other, arrived), members, levels)

    *picked, clone_weight = lax.cond(info[members] != 0, with_second, without_second)
    return (*picked, overturn, clone_weight)


def solution(mesh):
    volume = P("member", None, "gridy", "gridx")
    in_specs = (volume,) * 4 + (P("member", "gridy", "gridx"), P("gridy", "gridx"), P("member"))
    out_specs = (volume,) * 4 + (P("member", "gridy", "gridx"), P("member", None, "gridy"), P("member"))
    return jax.shard_map(shards, mesh=mesh, in_specs=in_specs, out_specs=out_specs, check_vma=False)
```

```python
import functools

import jax
import jax.numpy as jnp
from jax import lax
from jax.experimental import pallas as pl
from jax.experimental.pallas import tpu as pltpu
from jax.sharding import PartitionSpec as P

STEPS = 2
ITERS = 3

ALPHA_T = 0.8
BETA_S = 0.6
PRESS_K = 0.25
STEP_DT = 0.1
KAPPA = 0.1
VISCOSITY = 0.1
DRAG_K = 0.05
CORI_K = 1.0
SURF_C = 4.0
DIV_K = 0.5
GRAV_K = 0.5

ADV = STEP_DT * 0.5
DIV = DIV_K * 0.5
GRAV = GRAV_K * 0.5

WIDE = 10
TOP = 24
CHUNK = 16
CHUNK_2D = 8
CHUNK_3D = 16
LANE = 128
PER_GROUP = 11
PAIRS = [(a, b) for a in range(4) for b in range(a, 4)]
SUMS = 6 + 6 * len(PAIRS)
VMEM_LIMIT = 24 * 1024 * 1024
WHOLE_VMEM = 60 * 1024 * 1024


def rim_place(plane):
    group, place = divmod(plane, PER_GROUP)
    if place < 6:
        return group, 0, (2 * place + 1) * WIDE
    return group, 1, (2 * (place - 6) + 2) * WIDE


def groups_of(planes):
    return -(-planes // PER_GROUP)


def lanes_like(shape):
    return lax.broadcasted_iota(jnp.int32, shape, len(shape) - 1)


def fetches(fields, planes_of, mask_to, sems, levels):
    members = fields[0].shape[0]
    per_member = []
    for m in range(members):
        parts = [(fields[f].at[m], planes_of(m, pl.ds(f * levels, levels))) for f in range(4)]
        parts.append((fields[4].at[m], planes_of(m, 4 * levels)))
        per_member.append([pltpu.make_async_copy(*part, sems.at[m, i]) for i, part in enumerate(parts)])
    mask_copy = pltpu.make_async_copy(fields[5], mask_to, sems.at[0, 5])
    mask_copy.start()
    for copies in per_member:
        for copy in copies:
            copy.start()
    mask_copy.wait()
    return per_member


def pack_kernel(levels, *refs):
    fields, (to_west, to_east, rows_first, rows_second), (held, mask, sems) = refs[:6], refs[6:10], refs[10:]
    members, _, rows, cols = held.shape
    planes = 4 * levels + 2
    copies = fetches(fields, lambda m, at: held.at[m, at], mask, sems, levels)
    lane = lanes_like((rows, LANE))
    even = lax.broadcasted_iota(jnp.int32, (WIDE, cols), 0) * 0 + lax.rem(lax.axis_index("gridy"), 2) == 0
    for m in range(members):
        for copy in copies[m]:
            copy.wait()
        west_parts = [None] * groups_of(planes)
        east_parts = [None] * groups_of(planes)
        for plane in range(planes):
            value = held[m, plane] if plane < planes - 1 else mask[...].astype(jnp.float32)
            group, _, start = rim_place(plane)
            both = jnp.where(lane < WIDE, value[:, :LANE], value[:, cols - LANE :])
            both = pltpu.roll(both, start, 1)
            is_west = (lane >= start) & (lane < start + WIDE)
            is_east = (lane >= start - WIDE) & (lane < start)
            zero = jnp.zeros_like(both)
            west_parts[group] = jnp.where(is_west, both, zero if west_parts[group] is None else west_parts[group])
            east_parts[group] = jnp.where(is_east, both, zero if east_parts[group] is None else east_parts[group])
            low, high = value[:WIDE], value[rows - WIDE :]
            rows_first[m, plane * WIDE : (plane + 1) * WIDE, :] = jnp.where(even, high, low)
            rows_second[m, plane * WIDE : (plane + 1) * WIDE, :] = jnp.where(even, low, high)
        for group in range(groups_of(planes)):
            where = slice(group * LANE, (group + 1) * LANE)
            to_west[m, :, where] = west_parts[group]
            to_east[m, :, where] = east_parts[group]


def whole(count):
    return [pl.BlockSpec(memory_space=pltpu.VMEM)] * count


def in_hbm(count):
    return [pl.BlockSpec(memory_space=pltpu.HBM)] * count


def in_smem(count):
    return [pl.BlockSpec(memory_space=pltpu.SMEM)] * count


def pack_rims(temp, salt, uvel, vvel, eta, mask):
    members, levels, rows, cols = temp.shape
    planes = 4 * levels + 2
    wide = groups_of(planes) * LANE
    row_pack = -(-planes * WIDE // 8) * 8
    side = jax.ShapeDtypeStruct((members, rows, wide), jnp.float32)
    line = jax.ShapeDtypeStruct((members, row_pack, cols), jnp.float32)
    return pl.pallas_call(
        functools.partial(pack_kernel, levels),
        out_shape=(side, side, line, line),
        in_specs=in_hbm(6),
        out_specs=tuple(whole(4)),
        scratch_shapes=[
            pltpu.VMEM((members, planes - 1, rows, cols), jnp.float32),
            pltpu.VMEM((rows, cols), jnp.int32),
            pltpu.SemaphoreType.DMA((members, 6)),
        ],
        compiler_params=pltpu.CompilerParams(vmem_limit_bytes=WHOLE_VMEM),
        name="pack_rims",
    )(temp, salt, uvel, vvel, eta, mask)


def east_west(value):
    width = value.shape[-1]
    return pltpu.roll(value, width - 1, 1), pltpu.roll(value, 1, 1)


def chunks(first, last, size=CHUNK_2D):
    return [(a, min(a + size, last)) for a in range(first, last, size)]


def assemble(ext, mask, rims, m, levels, total_rows):
    from_east, from_west, rows_first, rows_second, sides_first, sides_second = rims
    planes = 4 * levels + 2
    rows, cols = mask.shape
    tile_row = lax.axis_index("gridy")
    odd_tile = lax.rem(tile_row, 2).astype(jnp.float32)
    keep_south = jnp.where(tile_row > 0, 1.0, 0.0).astype(jnp.float32)
    keep_north = jnp.where(tile_row * rows + rows < total_rows, 1.0, 0.0).astype(jnp.float32)
    north_factors = keep_north * (1.0 - odd_tile), keep_north * odd_tile
    south_factors = keep_south * odd_tile, keep_south * (1.0 - odd_tile)

    def of_north(first, second):
        return north_factors[0] * first + north_factors[1] * second

    def of_south(first, second):
        return south_factors[0] * first + south_factors[1] * second

    wide = groups_of(planes) * LANE
    for group in range(groups_of(planes)):
        where = slice(group * LANE, (group + 1) * LANE)
        where_west = slice(wide + group * LANE, wide + (group + 1) * LANE)
        east = sides_first[m, :, where], sides_second[m, :, where]
        west = sides_first[m, :, where_west], sides_second[m, :, where_west]
        bands = [(TOP - CHUNK, of_south(*east), of_south(*west))]
        for a in range(0, rows, CHUNK):
            bands.append((TOP + a, from_east[m, a : a + CHUNK, where], from_west[m, a : a + CHUNK, where]))
        bands.append((TOP + rows, of_north(*east), of_north(*west)))
        for at, east, west in bands:
            odd = ((lanes_like(east.shape) // WIDE) & 1) == 1
            joined = (jnp.where(odd, east, west), jnp.where(odd, west, east))
            for plane in range(group * PER_GROUP, min((group + 1) * PER_GROUP, planes)):
                _, kind, offset = rim_place(plane)
                ext[plane, at : at + CHUNK, cols : cols + LANE] = pltpu.roll(joined[kind], LANE - offset, 1)
    ext[planes - 1, TOP : TOP + rows, :cols] = mask[...].astype(jnp.float32)
    for plane in range(planes):
        at = slice(plane * WIDE, (plane + 1) * WIDE)
        ext[plane, TOP - WIDE : TOP, :cols] = of_south(rows_first[m, at, :], rows_second[m, at, :])
        ext[plane, TOP + rows : TOP + rows + WIDE, :cols] = of_north(rows_first[m, at, :], rows_second[m, at, :])


def fill_rows(turn, inside, first_row, total_rows):
    shape = (CHUNK, turn.shape[1])
    for a in range(0, turn.shape[0], CHUNK):
        row = first_row + (a - TOP) + lax.broadcasted_iota(jnp.int32, shape, 0)
        latitude = row.astype(jnp.float32) + 0.5
        turn[a : a + CHUNK, :] = STEP_DT * CORI_K * (2.0 * latitude / total_rows - 1.0)
        inside[a : a + CHUNK, :] = jnp.where((row >= 0) & (row < total_rows), 1.0, 0.0)


KEPT = ["tu", "tv", "q", "v0", "v1", "v2"]
KEEP_FLOW = 1.0 - STEP_DT * DRAG_K - 4.0 * VISCOSITY
KEEP_TRACER = 1.0 - 4.0 * KAPPA
PRESS_SCALE = PRESS_K * 0.5 * STEP_DT


class Planes:
    def __init__(self, levels, rows, turn, inside):
        self.levels, self.rows, self.turn, self.inside = levels, rows, turn, inside
        self.views = {}

    def add(self, ref, names, lead=()):
        for i, name in enumerate(names):
            self.views[name] = ref.at[lead + (i,)]

    def get(self, name, a, b):
        return self.views[name][a:b, :]

    def put(self, name, a, b, value):
        self.views[name][a:b, :] = value

    def sides(self, name, a, b):
        here = self.get(name, a, b)
        east, west = east_west(here)
        return here, east, west, self.get(name, a + 1, b + 1), self.get(name, a - 1, b - 1)

    def slopes(self, name, a, b):
        _, east, west, north, south = self.sides(name, a, b)
        return east - west, north - south

    def around(self, name, a, b):
        here, east, west, north, south = self.sides(name, a, b)
        return here, (east + west) + (north + south)

    def main(self):
        return chunks(TOP, TOP + self.rows)

    def near(self):
        return [(TOP - 8, TOP)] + self.main() + [(TOP + self.rows, TOP + self.rows + 8)]

    def masked(self, a, b, value):
        if a >= TOP and b <= TOP + self.rows:
            return value
        return self.inside[a:b, :] * value

    def divergence(self, u_name, v_name, a, b):
        east, west = east_west(self.get(u_name, a, b))
        return DIV * ((east - west) + (self.get(v_name, a + 1, b + 1) - self.get(v_name, a - 1, b - 1)))

    def flow(self, u_name, v_name, press, out_u, out_v, a, b):
        ocean, turn = self.get("ocean", a, b), self.turn[a:b, :]
        u, around_u = self.around(u_name, a, b)
        v, around_v = self.around(v_name, a, b)
        push_u, push_v = turn * v, turn * u
        if press:
            slope_x, slope_y = self.slopes(press, a, b)
            push_u, push_v = push_u - slope_x, push_v + slope_y
        self.put(out_u, a, b, ocean * ((KEEP_FLOW * u + VISCOSITY * around_u) + push_u))
        self.put(out_v, a, b, ocean * ((KEEP_FLOW * v + VISCOSITY * around_v) - push_v))

    def powers(self, first, second, third):
        for a, b in self.near():
            self.put(second, a, b, self.masked(a, b, self.around(first, a, b)[1]))
        for a, b in self.near():
            value = self.around(second, a, b)[1] - 4.0 * self.get(first, a, b)
            self.put(third, a, b, self.masked(a, b, value))

    def next_right_side(self, u_name, v_name, eta_name, press, out_name):
        for a, b in self.near():
            self.flow(u_name, v_name, press, "t2u", "t2v", a, b)
        for a, b in self.near():
            div = self.divergence("t2u", "t2v", a, b)
            value = self.get(eta_name, a, b) - div if eta_name else -div
            self.put(out_name, a, b, self.masked(a, b, value))


def scaled(factor, value):
    return value if factor == 1.0 else factor * value


def surface_start(ext, work):
    levels = work.levels
    low, high = TOP - CHUNK, TOP + work.rows + CHUNK
    for a, b in chunks(low, high):
        su = sv = sp = None
        for l in range(levels):
            factor = PRESS_SCALE * (levels - l)
            dens = (factor * BETA_S) * ext[levels + l, a:b, :] - (factor * ALPHA_T) * ext[l, a:b, :]
            work.put("d%d" % l, a, b, dens)
            u, v = ext[2 * levels + l, a:b, :], ext[3 * levels + l, a:b, :]
            su, sv, sp = (u, v, dens) if l == 0 else (su + u, sv + v, sp + dens)
        work.put("su", a, b, su)
        work.put("sv", a, b, sv)
        work.put("sp", a, b, sp)
    for a, b in work.near():
        carried = None
        for l in range(levels):
            slope_x, slope_y = work.slopes("d%d" % l, a, b)
            term = ext[2 * levels + l, a:b, :] * slope_x + ext[3 * levels + l, a:b, :] * slope_y
            carried = term if l == 0 else carried + term
        here, around = work.around("sp", a, b)
        work.put("q", a, b, work.get("ocean", a, b) * ((KEEP_TRACER * here + KAPPA * around) - ADV * carried))
    for a, b in chunks(low, high):
        work.flow("su", "sv", "sp", "tu", "tv", a, b)
    for a, b in work.near():
        work.put("v0", a, b, work.masked(a, b, work.get("eta", a, b) - work.divergence("tu", "tv", a, b)))


SUM_NAMES = ["su", "sv", "sp", "v3", "pu", "pv", "t2u", "t2v"] + ["w%d_%d" % (i, k) for i in range(4) for k in range(4)]


def whether(*conditions):
    result = jnp.int32(0)
    for condition in conditions:
        result = jnp.where(condition, 1, result)
    return result


def choose(source, theirs, side, members, info):
    mine, away = side * members, (1 - side) * members
    sent = [whether(*[theirs[slot] == mine + m for slot in range(members)]) for m in range(2)]
    here = [whether(*[source[slot] == away + m for slot in range(members)]) for m in range(2)]
    first_sent, first_here = 1 - sent[0], 1 - here[0]
    for slot in range(members):
        own = jnp.where(source[slot] - mine == first_sent, 0, 1)
        far = jnp.where(source[slot] - away == first_here, 2, 3)
        info[slot] = jnp.where((source[slot] >= mine) & (source[slot] < mine + members), own, far)
    info[members] = jnp.maximum(sent[0] * sent[1], here[0] * here[1])
    info[members + 1] = jnp.int32(1)
    info[members + 2] = first_sent


def sums_kernel(levels, total_rows, source, theirs, *refs):
    fields, rims, out, kept, info = refs[:6], refs[6:12], refs[12], refs[13], refs[14]
    planes, turn, inside, red, mask, sems = refs[15:]
    members = kept.shape[0]
    rows, cols = mask.shape
    copies = fetches(fields, lambda m, at: kept.at[m, at, pl.ds(TOP, rows), pl.ds(0, cols)], mask, sems, levels)
    tile_row = lax.axis_index("gridy")
    choose(source, theirs, lax.axis_index("member"), members, info)
    fill_rows(turn, inside, tile_row * rows, total_rows)
    red[...] = jnp.zeros_like(red)
    for m in range(members):
        assemble(kept.at[m], mask, rims, m, levels, total_rows)
    for copy in sum(copies, []):
        copy.wait()

    def one(m, carry):
        ext = kept.at[m]
        work = Planes(levels, rows, turn, inside)
        work.add(planes, SUM_NAMES + ["d%d" % l for l in range(levels)])
        work.add(kept, ["ext%d" % i for i in range(4 * levels)] + ["eta", "ocean"] + KEPT, (m,))
        surface_start(ext, work)
        work.powers("v0", "v1", "v2")
        for a, b in work.main():
            work.put("v3", a, b, work.around("v2", a, b)[1])
        work.next_right_side("tu", "tv", None, "q", "w0_0")
        for k in range(1, 4):
            name = "v%d" % (k - 1)
            for a, b in work.near():
                ocean = work.get("ocean", a, b)
                slope_x, slope_y = work.slopes(name, a, b)
                work.put("pu", a, b, scaled(-levels * GRAV, ocean * slope_x))
                work.put("pv", a, b, scaled(-levels * GRAV, ocean * slope_y))
            work.next_right_side("pu", "pv", name, None, "w0_%d" % k)
        for k in range(4):
            work.powers("w0_%d" % k, "w1_%d" % k, "w2_%d" % k)
            for a, b in work.main():
                work.put("w3_%d" % k, a, b, work.around("w2_%d" % k, a, b)[1])

        def put_sums(at, first, second, pairs):
            totals = [None] * len(pairs)
            for a in range(TOP, TOP + rows, 8):
                xs = [work.get(name, a, a + 8)[:, :cols] for name in first]
                ys = [work.get(name, a, a + 8)[:, :cols] for name in second]
                for p, (i, j) in enumerate(pairs):
                    term = xs[i] * ys[j]
                    totals[p] = term if totals[p] is None else totals[p] + term
            for p, total in enumerate(totals):
                folded = total[:, :LANE]
                for c in range(LANE, cols, LANE):
                    folded = folded + total[:, c : c + LANE]
                red[m, at + p : at + p + 1, :] = jnp.sum(folded, axis=0, keepdims=True)

        for i in range(6):
            low, high = i // 2, i - i // 2
            put_sums(i, ["v%d" % low], ["v%d" % high], [(0, 0)])
            names = [["w%d_%d" % (which, k) for k in range(4)] for which in (low, high)]
            put_sums(6 + i * len(PAIRS), names[0], names[1], PAIRS)
        return carry

    lax.fori_loop(0, members, one, 0)
    for m in range(members):
        out[m : m + 1, :] = jnp.sum(jnp.transpose(red[m]), axis=0, keepdims=True)


def plane_shape(rows, cols):
    return (2 * TOP + rows, cols + LANE)


def local_sums(source, theirs, fields, rims, total_rows):
    members, levels, rows, cols = fields[0].shape
    assert SUMS <= LANE and members <= 8
    shape = plane_shape(rows, cols)
    kept = (members, 4 * levels + 2 + len(KEPT)) + shape
    return pl.pallas_call(
        functools.partial(sums_kernel, levels, total_rows),
        out_shape=(
            jax.ShapeDtypeStruct((members, LANE), jnp.float32),
            jax.ShapeDtypeStruct(kept, jnp.float32),
            jax.ShapeDtypeStruct((members + 3,), jnp.int32),
        ),
        in_specs=in_smem(2) + in_hbm(6) + whole(6),
        out_specs=tuple(whole(2) + in_smem(1)),
        scratch_shapes=[
            pltpu.VMEM((len(SUM_NAMES) + levels,) + shape, jnp.float32),
            pltpu.VMEM(shape, jnp.float32),
            pltpu.VMEM(shape, jnp.float32),
            pltpu.VMEM((members, LANE, LANE), jnp.float32),
            pltpu.VMEM((rows, cols), jnp.int32),
            pltpu.SemaphoreType.DMA((members, 6)),
        ],
        compiler_params=pltpu.CompilerParams(vmem_limit_bytes=VMEM_LIMIT),
        cost_estimate=pl.CostEstimate(flops=10**8, bytes_accessed=4 * 10**6, transcendentals=0),
        name="local_sums",
    )(source, theirs, *fields, *rims)


def krylov(moment):
    n00, n01, n11, n12, n22, x22 = moment
    n02 = n11 - 4.0 * n00
    main, near = 1.0 + 4.0 * SURF_C, SURF_C
    g00 = main * n00 - near * n01
    g01 = main * n01 - near * n11
    g02 = main * n02 - near * n12
    g11 = main * n11 - near * (n12 + 4.0 * n01)
    g12 = main * n12 - near * (n22 + 4.0 * n02)
    g22 = main * n22 - near * x22
    l1, l2 = g01 / g00, g02 / g00
    d1 = g11 - l1 * g01
    d1 = jnp.where(d1 > 3e-7 * g11, d1, jnp.inf)
    e = g12 - l1 * g02
    l12 = e / d1
    d2 = g22 - l2 * g02 - l12 * e
    d2 = jnp.where(d2 > 3e-7 * g22, d2, jnp.inf)
    z0 = n00
    z1 = n01 - l1 * z0
    z2 = n02 - l2 * z0 - l12 * z1
    y2 = z2 / d2
    y1 = z1 / d1 - l12 * y2
    y0 = z0 / g00 - l1 * y1 - l2 * y2
    return [y0, y1, y2]


def weights(read):
    first = krylov([read(i) for i in range(6)])
    lifted = [None] + first
    second = []
    for i in range(6):
        total = None
        for p, (a, b) in enumerate(PAIRS):
            term = read(6 + i * len(PAIRS) + p)
            for k in (a, b):
                if k:
                    term = term * lifted[k]
            if a != b:
                term = 2.0 * term
            total = term if total is None else total + term
        second.append(total)
    return first, krylov(second)


RUN_NAMES = ["pu", "pv", "t2u", "t2v", "eta1", "w0", "w1", "w2", "eta2", "p", "p2", "gu1", "gv1", "gu2", "gv2"]


def advance_kernel(levels, total_rows, is_first, *refs):
    if is_first:
        info, tiles, kept, out, zonal = refs[:5]
        scratch = refs[5:]
    else:
        info, tiles, kept, zonal_before, out, spread = refs[:6]
        scratch = refs[6:]
    planes, after, turn, inside, staged, sums, sem = scratch[:7]
    rows, cols = out.shape[1:]
    members = kept.shape[0]
    tile_row = lax.axis_index("gridy")
    total = tiles[0]
    for i in range(1, tiles.shape[0]):
        total = total + tiles[i]
    staged[0:members, :] = total
    copy = pltpu.make_async_copy(staged, sums, sem)
    copy.start()
    fill_rows(turn, inside, tile_row * rows, total_rows)
    if not is_first:
        zonal = scratch[7]
    zonal[...] = jnp.zeros_like(zonal) if is_first else zonal_before[...]
    copy.wait()
    member = info[members + 2] if is_first else 1 - info[members + 2]
    ext = kept.at[member]
    work = Planes(levels, rows, turn, inside)
    work.add(planes, RUN_NAMES)
    work.add(kept, ["ext%d" % i for i in range(4 * levels)] + ["eta", "ocean"] + KEPT, (member,))

    def read(i):
        return jnp.full((1, 1), sums[member, i], jnp.float32)

    def combine(factors, names, out_name):
        for a, b in work.near():
            value = None
            for factor, name in zip(factors, names):
                term = factor * work.get(name, a, b)
                value = term if value is None else value + term
            work.put(out_name, a, b, value)

    first, second = weights(read)
    combine(first, ("v0", "v1", "v2"), "eta1")
    for a, b in work.near():
        ocean = work.get("ocean", a, b)
        slope_x, slope_y = work.slopes("eta1", a, b)
        slope_x, slope_y = GRAV * ocean * slope_x, GRAV * ocean * slope_y
        work.put("gu1", a, b, slope_x)
        work.put("gv1", a, b, slope_y)
        work.put("pu", a, b, work.get("tu", a, b) - levels * slope_x)
        work.put("pv", a, b, work.get("tv", a, b) - levels * slope_y)
    work.next_right_side("pu", "pv", "eta1", "q", "w0")
    work.powers("w0", "w1", "w2")
    combine(second, ("w0", "w1", "w2"), "eta2")
    for a, b in work.main():
        ocean = work.get("ocean", a, b)
        slope_x, slope_y = work.slopes("eta2", a, b)
        work.put("gu2", a, b, GRAV * ocean * slope_x)
        work.put("gv2", a, b, GRAV * ocean * slope_y)
        out[4 * levels, a - TOP : b - TOP, :] = work.get("eta2", a, b)[:, :cols]
    low, high = TOP - 8, TOP + rows + 8
    for a, b in chunks(TOP - CHUNK, TOP + rows + CHUNK):
        work.put("p", a, b, jnp.zeros((b - a, cols + LANE), jnp.float32))
        work.put("p2", a, b, jnp.zeros((b - a, cols + LANE), jnp.float32))

    def step(ref, l, press, a, b, width):
        def of(view):
            here = view[a:b, :]
            east, west = east_west(here)
            return here[:, :width], east[:, :width], west[:, :width], view[a + 1 : b + 1, :width], view[a - 1 : b - 1, :width]

        ocean = work.views["ocean"][a:b, :width]
        coriolis = turn[a:b, :width]
        u, east, west, north, south = of(ref.at[2 * levels + l])
        around_u = (east + west) + (north + south)
        v, east, west, north, south = of(ref.at[3 * levels + l])
        around_v = (east + west) + (north + south)
        _, east, west, north, south = of(work.views[press])
        new_u = ocean * ((KEEP_FLOW * u + VISCOSITY * around_u) + (coriolis * v - (east - west)))
        new_v = ocean * ((KEEP_FLOW * v + VISCOSITY * around_v) - (coriolis * u + (north - south)))
        flow_u, flow_v = ADV * u, ADV * v
        results = []
        for at in (l, levels + l):
            here, east, west, north, south = of(ref.at[at])
            carried = flow_u * (east - west) + flow_v * (north - south)
            spread = KEEP_TRACER * here + KAPPA * ((east + west) + (north + south))
            results.append(ocean * (spread - carried))
        return results[0], results[1], new_u, new_v

    def add_press(ref, l, press, a, b):
        dens = (PRESS_SCALE * BETA_S) * ref[levels + l, a:b, :] - (PRESS_SCALE * ALPHA_T) * ref[l, a:b, :]
        work.put(press, a, b, work.get(press, a, b) + dens)

    def level(l, carry):
        for a, b in chunks(TOP - CHUNK, TOP + rows + CHUNK, CHUNK_3D):
            add_press(ext, l, "p", a, b)
        for a, b in chunks(low, high, CHUNK_3D):
            temp, salt, u, v = step(ext, l, "p", a, b, cols + LANE)
            after[l, a:b, :] = temp
            after[levels + l, a:b, :] = salt
            after[2 * levels + l, a:b, :] = u - work.get("gu1", a, b)
            after[3 * levels + l, a:b, :] = v - work.get("gv1", a, b)
        for a, b in chunks(low, high, CHUNK_3D):
            add_press(after, l, "p2", a, b)
        for a, b in chunks(TOP, TOP + rows, CHUNK_3D):
            temp, salt, u, v = step(after, l, "p2", a, b, cols)
            here = slice(a - TOP, b - TOP)
            v = v - work.get("gv2", a, b)[:, :cols]
            out[l, here, :] = temp
            out[levels + l, here, :] = salt
            out[2 * levels + l, here, :] = u - work.get("gu2", a, b)[:, :cols]
            out[3 * levels + l, here, :] = v
            row_sum = jnp.sum(v, axis=1, keepdims=True)
            zonal[here, :] = jnp.where(lanes_like((b - a, LANE)) == member * levels + l, row_sum, zonal[here, :])
        return carry

    lax.fori_loop(0, levels, level, 0)
    if not is_first:
        square = jnp.concatenate([zonal[...]] + [jnp.zeros_like(zonal)] * (LANE // rows - 1), axis=0)
        turned = jnp.transpose(square)[: members * levels]
        line = turned[:levels]
        for m in range(1, members):
            line = line + pltpu.roll(turned, m * rows, 1)[m * levels : (m + 1) * levels]
        for i in range(spread.shape[0]):
            spread[i] = line


def advance(is_first, info, tiles, kept, zonal, rows, cols, total_rows):
    members, planes = kept.shape[:2]
    levels = (planes - 2 - len(KEPT)) // 4
    assert members * rows == LANE and members * levels == 8
    shape = plane_shape(rows, cols)
    zonal_shape = jax.ShapeDtypeStruct((rows, LANE), jnp.float32)
    out_shape = [jax.ShapeDtypeStruct((4 * levels + 1, rows, cols), jnp.float32)]
    if is_first:
        out_shape += [zonal_shape]
    else:
        out_shape += [jax.ShapeDtypeStruct((tiles.shape[0], levels, members * rows), jnp.float32)]
    return pl.pallas_call(
        functools.partial(advance_kernel, levels, total_rows, is_first),
        out_shape=tuple(out_shape),
        in_specs=in_smem(1) + whole(2 if is_first else 3),
        out_specs=tuple(whole(2)),
        scratch_shapes=[
            pltpu.VMEM((len(RUN_NAMES),) + shape, jnp.float32),
            pltpu.VMEM((4 * levels,) + shape, jnp.float32),
            pltpu.VMEM(shape, jnp.float32),
            pltpu.VMEM(shape, jnp.float32),
            pltpu.VMEM((8, LANE), jnp.float32),
            pltpu.SMEM((8, LANE), jnp.float32),
            pltpu.SemaphoreType.DMA,
        ]
        + ([] if is_first else [pltpu.VMEM((rows, LANE), jnp.float32)]),
        compiler_params=pltpu.CompilerParams(vmem_limit_bytes=VMEM_LIMIT),
        cost_estimate=pl.CostEstimate(flops=10**8, bytes_accessed=4 * 10**6, transcendentals=0),
        name="advance",
    )(info, tiles, kept, *([] if is_first else [zonal]))


def finish_kernel(count_y, count_x, total_cols, spread, overturn, score, held):
    members, levels, rows = overturn.shape
    total_rows = rows * count_y
    lane = lanes_like(spread.shape[1:])
    member_of = lane // rows
    weighted = None
    for y in range(count_y):
        total = spread[y * count_x]
        for x in range(1, count_x):
            total = total + spread[y * count_x + x]
        lines = [total[0:1]]
        for l in range(1, levels):
            lines.append(lines[-1] + total[l : l + 1])
        lines = jnp.concatenate(lines, axis=0) * (total_cols**-0.5)
        held[y] = lines
        latitude = ((lane - member_of * rows + y * rows).astype(jnp.float32) + 0.5) * (1.0 / total_rows)
        weighted = lines * latitude if weighted is None else weighted + lines * latitude
    mine = held[lax.axis_index("gridy")]
    for m in range(members):
        overturn[m] = mine[:, m * rows : (m + 1) * rows]
        score[m] = jnp.sum(jnp.where(member_of == m, weighted, 0.0)) * ((levels * total_rows) ** -0.5)


def finish(spread, members, rows, count_y, count_x, cols):
    levels = spread.shape[1]
    return pl.pallas_call(
        functools.partial(finish_kernel, count_y, count_x, cols * count_x),
        out_shape=(
            jax.ShapeDtypeStruct((members, levels, rows), jnp.float32),
            jax.ShapeDtypeStruct((members,), jnp.float32),
        ),
        in_specs=whole(1),
        out_specs=(whole(1)[0], in_smem(1)[0]),
        scratch_shapes=[pltpu.VMEM((count_y,) + spread.shape[1:], jnp.float32)],
        compiler_params=pltpu.CompilerParams(vmem_limit_bytes=VMEM_LIMIT),
        name="finish",
    )(spread)


def pick_kernel(levels, choice, source, score, their_score, *refs):
    count = len(refs) - 7
    sources, outs, weight, sem = refs[:count], refs[count : count + 5], refs[count + 5], refs[count + 6]
    slots = outs[0].shape[0]

    def parts(s, source):
        for f in range(4):
            yield source.at[pl.ds(f * levels, levels)], outs[f].at[s]
        yield source.at[4 * levels], outs[4].at[s]

    for s in range(slots):
        for k in range(count):

            @pl.when(choice[s] == k)
            def _():
                for i, (one, target) in enumerate(parts(s, sources[k])):
                    pltpu.make_async_copy(one, target, sem.at[s, i]).start()

    side = lax.axis_index("member")
    mean = (sum(score[m] for m in range(slots)) + sum(their_score[m] for m in range(slots))) * (0.5 / slots)
    for s in range(slots):
        value = jnp.float32(0.0)
        for m in range(slots):
            value = jnp.where(source[s] == side * slots + m, score[m], value)
            value = jnp.where(source[s] == (1 - side) * slots + m, their_score[m], value)
        weight[s] = value - mean
    for s in range(slots):
        for i, (one, target) in enumerate(parts(s, sources[0])):
            pltpu.make_async_copy(one, target, sem.at[s, i]).wait()


def pick(choice, source, score, their_score, sources, slots, levels):
    _, rows, cols = sources[0].shape
    volume = jax.ShapeDtypeStruct((slots, levels, rows, cols), jnp.float32)
    surface = jax.ShapeDtypeStruct((slots, rows, cols), jnp.float32)
    return pl.pallas_call(
        functools.partial(pick_kernel, levels),
        out_shape=(volume,) * 4 + (surface, jax.ShapeDtypeStruct((slots,), jnp.float32)),
        in_specs=in_smem(4) + whole(len(sources)),
        out_specs=tuple(in_hbm(5) + in_smem(1)),
        scratch_shapes=[pltpu.SemaphoreType.DMA((slots, 5))],
        compiler_params=pltpu.CompilerParams(vmem_limit_bytes=VMEM_LIMIT),
        name="pick",
    )(choice, source, score, their_score, *sources)


def shift(value, axis, by):
    count = lax.axis_size(axis)
    return lax.ppermute(value, axis, [(i, (i + by) % count) for i in range(count)])


def exchange_rims(packed):
    to_west, to_east, rows_first, rows_second = packed
    rows = to_west.shape[1]
    count = lax.axis_size("gridy")
    assert count % 2 == 0
    partners = [i ^ 1 for i in range(count)], [min(max(i - 1 + 2 * (i % 2), 0), count - 1) for i in range(count)]

    def pair(value, which):
        return lax.ppermute(value, "gridy", list(enumerate(partners[which])))

    from_east, from_west = shift(to_west, "gridx", -1), shift(to_east, "gridx", 1)
    rows_first, rows_second = pair(rows_first, 0), pair(rows_second, 1)
    low = jnp.concatenate([from_east[:, :CHUNK], from_west[:, :CHUNK]], axis=2)
    high = jnp.concatenate([from_east[:, rows - CHUNK :], from_west[:, rows - CHUNK :]], axis=2)
    even = lax.axis_index("gridy") % 2 == 0
    sides_first = pair(jnp.where(even, high, low), 0)
    sides_second = pair(jnp.where(even, low, high), 1)
    return from_east, from_west, rows_first, rows_second, sides_first, sides_second


def from_all(tiles, axes):
    return lax.all_to_all(tiles, axes, split_axis=0, concat_axis=0, tiled=True)


def swap(value):
    return lax.ppermute(value, "member", [(0, 1), (1, 0)])


def shards(temp, salt, uvel, vvel, eta, land_mask, clone_source):
    members, levels, rows, cols = temp.shape
    assert members == 2 and lax.axis_size("member") == 2
    count_y, count_x = lax.axis_size("gridy"), lax.axis_size("gridx")
    total_rows = rows * count_y
    grid = ("gridy", "gridx")

    fields = (temp, salt, uvel, vvel, eta, land_mask)
    packed, their_source = lax.optimization_barrier((pack_rims(*fields), swap(clone_source)))
    rims = exchange_rims(packed)
    tile, kept, info = local_sums(clone_source, their_source, fields, rims, total_rows)
    tiles = from_all(jnp.broadcast_to(tile[None], (count_y * count_x,) + tile.shape), grid)

    sent, zonal = advance(True, info, tiles, kept, None, rows, cols, total_rows)
    arrived = swap(sent)

    def rest():
        other, spread = advance(False, info, tiles, kept, zonal, rows, cols, total_rows)
        return (other, *finish(from_all(spread, grid), members, rows, count_y, count_x, cols))

    def nothing():
        return jnp.zeros_like(sent), jnp.zeros((members, levels, rows), jnp.float32), jnp.zeros((members,), jnp.float32)

    other, overturn, score = lax.cond(info[members + 1] != 0, rest, nothing)
    their_score = swap(score)

    def with_second():
        sources = (sent, other, arrived, swap(other))
        return pick(info, clone_source, score, their_score, sources, members, levels)

    def without_second():
        return pick(info, clone_source, score, their_score, (sent, other, arrived), members, levels)

    *picked, clone_weight = lax.cond(info[members] != 0, with_second, without_second)
    return (*picked, overturn, clone_weight)


def solution(mesh):
    volume = P("member", None, "gridy", "gridx")
    in_specs = (volume,) * 4 + (P("member", "gridy", "gridx"), P("gridy", "gridx"), P("member"))
    out_specs = (volume,) * 4 + (P("member", "gridy", "gridx"), P("member", None, "gridy"), P("member"))
    return jax.shard_map(shards, mesh=mesh, in_specs=in_specs, out_specs=out_specs, check_vma=False)
```

```python
import functools

import jax
import jax.numpy as jnp
from jax import lax
from jax.experimental import pallas as pl
from jax.experimental.pallas import tpu as pltpu
from jax.sharding import PartitionSpec as P

STEPS = 2
ITERS = 3

ALPHA_T = 0.8
BETA_S = 0.6
PRESS_K = 0.25
STEP_DT = 0.1
KAPPA = 0.1
VISCOSITY = 0.1
DRAG_K = 0.05
CORI_K = 1.0
SURF_C = 4.0
DIV_K = 0.5
GRAV_K = 0.5

ADV = STEP_DT * 0.5
DIV = DIV_K * 0.5
GRAV = GRAV_K * 0.5

WIDE = 10
TOP = 24
CHUNK = 16
CHUNK_2D = 8
CHUNK_3D = 32
LANE = 128
PER_GROUP = 11
PAIRS = [(a, b) for a in range(4) for b in range(a, 4)]
SUMS = 6 + 6 * len(PAIRS)
VMEM_LIMIT = 24 * 1024 * 1024
WHOLE_VMEM = 60 * 1024 * 1024


def rim_place(plane):
    group, place = divmod(plane, PER_GROUP)
    if place < 6:
        return group, 0, (2 * place + 1) * WIDE
    return group, 1, (2 * (place - 6) + 2) * WIDE


def groups_of(planes):
    return -(-planes // PER_GROUP)


def lanes_like(shape):
    return lax.broadcasted_iota(jnp.int32, shape, len(shape) - 1)


def fetches(fields, planes_of, mask_to, sems, levels):
    members = fields[0].shape[0]
    per_member = []
    for m in range(members):
        parts = [(fields[f].at[m], planes_of(m, pl.ds(f * levels, levels))) for f in range(4)]
        parts.append((fields[4].at[m], planes_of(m, 4 * levels)))
        per_member.append([pltpu.make_async_copy(*part, sems.at[m, i]) for i, part in enumerate(parts)])
    mask_copy = pltpu.make_async_copy(fields[5], mask_to, sems.at[0, 5])
    mask_copy.start()
    for copies in per_member:
        for copy in copies:
            copy.start()
    mask_copy.wait()
    return per_member


def pack_kernel(levels, *refs):
    fields, (to_west, to_east, rows_first, rows_second), (held, mask, sems) = refs[:6], refs[6:10], refs[10:]
    members, _, rows, cols = held.shape
    planes = 4 * levels + 2
    copies = fetches(fields, lambda m, at: held.at[m, at], mask, sems, levels)
    lane = lanes_like((rows, LANE))
    even = lax.broadcasted_iota(jnp.int32, (WIDE, cols), 0) * 0 + lax.rem(lax.axis_index("gridy"), 2) == 0
    for m in range(members):
        for copy in copies[m]:
            copy.wait()
        west_parts = [None] * groups_of(planes)
        east_parts = [None] * groups_of(planes)
        for plane in range(planes):
            value = held[m, plane] if plane < planes - 1 else mask[...].astype(jnp.float32)
            group, _, start = rim_place(plane)
            both = jnp.where(lane < WIDE, value[:, :LANE], value[:, cols - LANE :])
            both = pltpu.roll(both, start, 1)
            is_west = (lane >= start) & (lane < start + WIDE)
            is_east = (lane >= start - WIDE) & (lane < start)
            zero = jnp.zeros_like(both)
            west_parts[group] = jnp.where(is_west, both, zero if west_parts[group] is None else west_parts[group])
            east_parts[group] = jnp.where(is_east, both, zero if east_parts[group] is None else east_parts[group])
            low, high = value[:WIDE], value[rows - WIDE :]
            rows_first[m, plane * WIDE : (plane + 1) * WIDE, :] = jnp.where(even, high, low)
            rows_second[m, plane * WIDE : (plane + 1) * WIDE, :] = jnp.where(even, low, high)
        for group in range(groups_of(planes)):
            where = slice(group * LANE, (group + 1) * LANE)
            to_west[m, :, where] = west_parts[group]
            to_east[m, :, where] = east_parts[group]


def whole(count):
    return [pl.BlockSpec(memory_space=pltpu.VMEM)] * count


def in_hbm(count):
    return [pl.BlockSpec(memory_space=pltpu.HBM)] * count


def in_smem(count):
    return [pl.BlockSpec(memory_space=pltpu.SMEM)] * count


def pack_rims(temp, salt, uvel, vvel, eta, mask):
    members, levels, rows, cols = temp.shape
    planes = 4 * levels + 2
    wide = groups_of(planes) * LANE
    row_pack = -(-planes * WIDE // 8) * 8
    side = jax.ShapeDtypeStruct((members, rows, wide), jnp.float32)
    line = jax.ShapeDtypeStruct((members, row_pack, cols), jnp.float32)
    return pl.pallas_call(
        functools.partial(pack_kernel, levels),
        out_shape=(side, side, line, line),
        in_specs=in_hbm(6),
        out_specs=tuple(whole(4)),
        scratch_shapes=[
            pltpu.VMEM((members, planes - 1, rows, cols), jnp.float32),
            pltpu.VMEM((rows, cols), jnp.int32),
            pltpu.SemaphoreType.DMA((members, 6)),
        ],
        compiler_params=pltpu.CompilerParams(vmem_limit_bytes=WHOLE_VMEM),
        name="pack_rims",
    )(temp, salt, uvel, vvel, eta, mask)


def east_west(value):
    width = value.shape[-1]
    return pltpu.roll(value, width - 1, 1), pltpu.roll(value, 1, 1)


def chunks(first, last, size=CHUNK_2D):
    return [(a, min(a + size, last)) for a in range(first, last, size)]


def assemble(ext, fields, rims, m, levels, total_rows):
    from_east, from_west, rows_first, rows_second, sides_first, sides_second = rims
    planes = 4 * levels + 2
    rows, cols = fields[5].shape
    tile_row = lax.axis_index("gridy")
    odd_tile = lax.rem(tile_row, 2).astype(jnp.float32)
    keep_south = jnp.where(tile_row > 0, 1.0, 0.0).astype(jnp.float32)
    keep_north = jnp.where(tile_row * rows + rows < total_rows, 1.0, 0.0).astype(jnp.float32)
    north_factors = keep_north * (1.0 - odd_tile), keep_north * odd_tile
    south_factors = keep_south * odd_tile, keep_south * (1.0 - odd_tile)

    def of_north(first, second):
        return north_factors[0] * first + north_factors[1] * second

    def of_south(first, second):
        return south_factors[0] * first + south_factors[1] * second

    wide = groups_of(planes) * LANE
    for group in range(groups_of(planes)):
        where = slice(group * LANE, (group + 1) * LANE)
        where_west = slice(wide + group * LANE, wide + (group + 1) * LANE)
        east = sides_first[m, :, where], sides_second[m, :, where]
        west = sides_first[m, :, where_west], sides_second[m, :, where_west]
        bands = [(TOP - CHUNK, of_south(*east), of_south(*west))]
        for a in range(0, rows, CHUNK):
            bands.append((TOP + a, from_east[m, a : a + CHUNK, where], from_west[m, a : a + CHUNK, where]))
        bands.append((TOP + rows, of_north(*east), of_north(*west)))
        for at, east, west in bands:
            odd = ((lanes_like(east.shape) // WIDE) & 1) == 1
            joined = (jnp.where(odd, east, west), jnp.where(odd, west, east))
            for plane in range(group * PER_GROUP, min((group + 1) * PER_GROUP, planes)):
                _, kind, offset = rim_place(plane)
                ext[plane, at : at + CHUNK, cols : cols + LANE] = pltpu.roll(joined[kind], LANE - offset, 1)
    for plane in range(planes):
        if plane < 4 * levels:
            value = fields[plane // levels][m, plane % levels]
        else:
            value = fields[4][m] if plane == 4 * levels else fields[5][...].astype(jnp.float32)
        ext[plane, TOP : TOP + rows, :cols] = value
        at = slice(plane * WIDE, (plane + 1) * WIDE)
        ext[plane, TOP - WIDE : TOP, :cols] = of_south(rows_first[m, at, :], rows_second[m, at, :])
        ext[plane, TOP + rows : TOP + rows + WIDE, :cols] = of_north(rows_first[m, at, :], rows_second[m, at, :])


def fill_rows(turn, inside, first_row, total_rows):
    shape = (CHUNK, turn.shape[1])
    for a in range(0, turn.shape[0], CHUNK):
        row = first_row + (a - TOP) + lax.broadcasted_iota(jnp.int32, shape, 0)
        latitude = row.astype(jnp.float32) + 0.5
        turn[a : a + CHUNK, :] = STEP_DT * CORI_K * (2.0 * latitude / total_rows - 1.0)
        inside[a : a + CHUNK, :] = jnp.where((row >= 0) & (row < total_rows), 1.0, 0.0)


KEPT = ["tu", "tv", "q", "v0", "v1", "v2"]
KEEP_FLOW = 1.0 - STEP_DT * DRAG_K - 4.0 * VISCOSITY
KEEP_TRACER = 1.0 - 4.0 * KAPPA
PRESS_SCALE = PRESS_K * 0.5 * STEP_DT


class Planes:
    def __init__(self, levels, rows, turn, inside):
        self.levels, self.rows, self.turn, self.inside = levels, rows, turn, inside
        self.views = {}

    def add(self, ref, names, lead=()):
        for i, name in enumerate(names):
            self.views[name] = ref.at[lead + (i,)]

    def get(self, name, a, b):
        return self.views[name][a:b, :]

    def put(self, name, a, b, value):
        self.views[name][a:b, :] = value

    def sides(self, name, a, b):
        here = self.get(name, a, b)
        east, west = east_west(here)
        return here, east, west, self.get(name, a + 1, b + 1), self.get(name, a - 1, b - 1)

    def slopes(self, name, a, b):
        _, east, west, north, south = self.sides(name, a, b)
        return east - west, north - south

    def around(self, name, a, b):
        here, east, west, north, south = self.sides(name, a, b)
        return here, (east + west) + (north + south)

    def main(self):
        return chunks(TOP, TOP + self.rows)

    def near(self):
        return [(TOP - 8, TOP)] + self.main() + [(TOP + self.rows, TOP + self.rows + 8)]

    def masked(self, a, b, value):
        if a >= TOP and b <= TOP + self.rows:
            return value
        return self.inside[a:b, :] * value

    def divergence(self, u_name, v_name, a, b):
        east, west = east_west(self.get(u_name, a, b))
        return DIV * ((east - west) + (self.get(v_name, a + 1, b + 1) - self.get(v_name, a - 1, b - 1)))

    def flow(self, u_name, v_name, press, out_u, out_v, a, b):
        ocean, turn = self.get("ocean", a, b), self.turn[a:b, :]
        u, around_u = self.around(u_name, a, b)
        v, around_v = self.around(v_name, a, b)
        push_u, push_v = turn * v, turn * u
        if press:
            slope_x, slope_y = self.slopes(press, a, b)
            push_u, push_v = push_u - slope_x, push_v + slope_y
        self.put(out_u, a, b, ocean * ((KEEP_FLOW * u + VISCOSITY * around_u) + push_u))
        self.put(out_v, a, b, ocean * ((KEEP_FLOW * v + VISCOSITY * around_v) - push_v))

    def powers(self, first, second, third):
        for a, b in self.near():
            self.put(second, a, b, self.masked(a, b, self.around(first, a, b)[1]))
        for a, b in self.near():
            value = self.around(second, a, b)[1] - 4.0 * self.get(first, a, b)
            self.put(third, a, b, self.masked(a, b, value))

    def next_right_side(self, u_name, v_name, eta_name, press, out_name):
        for a, b in self.near():
            self.flow(u_name, v_name, press, "t2u", "t2v", a, b)
        for a, b in self.near():
            div = self.divergence("t2u", "t2v", a, b)
            value = self.get(eta_name, a, b) - div if eta_name else -div
            self.put(out_name, a, b, self.masked(a, b, value))


def scaled(factor, value):
    return value if factor == 1.0 else factor * value


def surface_start(ext, work):
    levels = work.levels
    low, high = TOP - CHUNK, TOP + work.rows + CHUNK
    for a, b in chunks(low, high):
        su = sv = sp = None
        for l in range(levels):
            factor = PRESS_SCALE * (levels - l)
            dens = (factor * BETA_S) * ext[levels + l, a:b, :] - (factor * ALPHA_T) * ext[l, a:b, :]
            work.put("d%d" % l, a, b, dens)
            u, v = ext[2 * levels + l, a:b, :], ext[3 * levels + l, a:b, :]
            su, sv, sp = (u, v, dens) if l == 0 else (su + u, sv + v, sp + dens)
        work.put("su", a, b, su)
        work.put("sv", a, b, sv)
        work.put("sp", a, b, sp)
    for a, b in work.near():
        carried = None
        for l in range(levels):
            slope_x, slope_y = work.slopes("d%d" % l, a, b)
            term = ext[2 * levels + l, a:b, :] * slope_x + ext[3 * levels + l, a:b, :] * slope_y
            carried = term if l == 0 else carried + term
        here, around = work.around("sp", a, b)
        work.put("q", a, b, work.get("ocean", a, b) * ((KEEP_TRACER * here + KAPPA * around) - ADV * carried))
    for a, b in chunks(low, high):
        work.flow("su", "sv", "sp", "tu", "tv", a, b)
    for a, b in work.near():
        work.put("v0", a, b, work.masked(a, b, work.get("eta", a, b) - work.divergence("tu", "tv", a, b)))


SUM_NAMES = ["su", "sv", "sp", "v3", "pu", "pv", "t2u", "t2v"] + ["w%d_%d" % (i, k) for i in range(4) for k in range(4)]


def whether(*conditions):
    result = jnp.int32(0)
    for condition in conditions:
        result = jnp.where(condition, 1, result)
    return result


def choose(source, theirs, side, members, info):
    mine, away = side * members, (1 - side) * members
    sent = [whether(*[theirs[slot] == mine + m for slot in range(members)]) for m in range(2)]
    here = [whether(*[source[slot] == away + m for slot in range(members)]) for m in range(2)]
    first_sent, first_here = 1 - sent[0], 1 - here[0]
    for slot in range(members):
        own = jnp.where(source[slot] - mine == first_sent, 0, 1)
        far = jnp.where(source[slot] - away == first_here, 2, 3)
        info[slot] = jnp.where((source[slot] >= mine) & (source[slot] < mine + members), own, far)
    info[members] = jnp.maximum(sent[0] * sent[1], here[0] * here[1])
    info[members + 1] = jnp.int32(1)
    info[members + 2] = first_sent


def sums_kernel(levels, total_rows, source, theirs, *refs):
    fields, rims, out, kept, info = refs[:6], refs[6:12], refs[12], refs[13], refs[14]
    planes, turn, inside, red = refs[15:]
    members = kept.shape[0]
    rows, cols = fields[5].shape
    tile_row = lax.axis_index("gridy")
    choose(source, theirs, lax.axis_index("member"), members, info)
    fill_rows(turn, inside, tile_row * rows, total_rows)
    red[...] = jnp.zeros_like(red)

    def one(m, carry):
        ext = kept.at[m]
        assemble(ext, fields, rims, m, levels, total_rows)
        work = Planes(levels, rows, turn, inside)
        work.add(planes, SUM_NAMES + ["d%d" % l for l in range(levels)])
        work.add(kept, ["ext%d" % i for i in range(4 * levels)] + ["eta", "ocean"] + KEPT, (m,))
        surface_start(ext, work)
        work.powers("v0", "v1", "v2")
        for a, b in work.main():
            work.put("v3", a, b, work.around("v2", a, b)[1])
        work.next_right_side("tu", "tv", None, "q", "w0_0")
        for k in range(1, 4):
            name = "v%d" % (k - 1)
            for a, b in work.near():
                ocean = work.get("ocean", a, b)
                slope_x, slope_y = work.slopes(name, a, b)
                work.put("pu", a, b, scaled(-levels * GRAV, ocean * slope_x))
                work.put("pv", a, b, scaled(-levels * GRAV, ocean * slope_y))
            work.next_right_side("pu", "pv", name, None, "w0_%d" % k)
        for k in range(4):
            work.powers("w0_%d" % k, "w1_%d" % k, "w2_%d" % k)
            for a, b in work.main():
                work.put("w3_%d" % k, a, b, work.around("w2_%d" % k, a, b)[1])

        def put_sums(at, first, second, pairs):
            totals = [None] * len(pairs)
            for a in range(TOP, TOP + rows, 8):
                xs = [work.get(name, a, a + 8)[:, :cols] for name in first]
                ys = [work.get(name, a, a + 8)[:, :cols] for name in second]
                for p, (i, j) in enumerate(pairs):
                    term = xs[i] * ys[j]
                    totals[p] = term if totals[p] is None else totals[p] + term
            for p, total in enumerate(totals):
                folded = total[:, :LANE]
                for c in range(LANE, cols, LANE):
                    folded = folded + total[:, c : c + LANE]
                red[m, at + p : at + p + 1, :] = jnp.sum(folded, axis=0, keepdims=True)

        for i in range(6):
            low, high = i // 2, i - i // 2
            put_sums(i, ["v%d" % low], ["v%d" % high], [(0, 0)])
            names = [["w%d_%d" % (which, k) for k in range(4)] for which in (low, high)]
            put_sums(6 + i * len(PAIRS), names[0], names[1], PAIRS)
        return carry

    lax.fori_loop(0, members, one, 0)
    for m in range(members):
        out[m : m + 1, :] = jnp.sum(jnp.transpose(red[m]), axis=0, keepdims=True)


def plane_shape(rows, cols):
    return (2 * TOP + rows, cols + LANE)


def local_sums(source, theirs, fields, rims, total_rows):
    members, levels, rows, cols = fields[0].shape
    assert SUMS <= LANE and members <= 8
    shape = plane_shape(rows, cols)
    kept = (members, 4 * levels + 2 + len(KEPT)) + shape
    return pl.pallas_call(
        functools.partial(sums_kernel, levels, total_rows),
        out_shape=(
            jax.ShapeDtypeStruct((members, LANE), jnp.float32),
            jax.ShapeDtypeStruct(kept, jnp.float32),
            jax.ShapeDtypeStruct((members + 3,), jnp.int32),
        ),
        in_specs=in_smem(2) + whole(12),
        out_specs=tuple(whole(2) + in_smem(1)),
        scratch_shapes=[
            pltpu.VMEM((len(SUM_NAMES) + levels,) + shape, jnp.float32),
            pltpu.VMEM(shape, jnp.float32),
            pltpu.VMEM(shape, jnp.float32),
            pltpu.VMEM((members, LANE, LANE), jnp.float32),
        ],
        compiler_params=pltpu.CompilerParams(vmem_limit_bytes=VMEM_LIMIT),
        cost_estimate=pl.CostEstimate(flops=10**8, bytes_accessed=4 * 10**6, transcendentals=0),
        name="local_sums",
    )(source, theirs, *fields, *rims)


def krylov(moment):
    n00, n01, n11, n12, n22, x22 = moment
    n02 = n11 - 4.0 * n00
    main, near = 1.0 + 4.0 * SURF_C, SURF_C
    g00 = main * n00 - near * n01
    g01 = main * n01 - near * n11
    g02 = main * n02 - near * n12
    g11 = main * n11 - near * (n12 + 4.0 * n01)
    g12 = main * n12 - near * (n22 + 4.0 * n02)
    g22 = main * n22 - near * x22
    l1, l2 = g01 / g00, g02 / g00
    d1 = g11 - l1 * g01
    d1 = jnp.where(d1 > 3e-7 * g11, d1, jnp.inf)
    e = g12 - l1 * g02
    l12 = e / d1
    d2 = g22 - l2 * g02 - l12 * e
    d2 = jnp.where(d2 > 3e-7 * g22, d2, jnp.inf)
    z0 = n00
    z1 = n01 - l1 * z0
    z2 = n02 - l2 * z0 - l12 * z1
    y2 = z2 / d2
    y1 = z1 / d1 - l12 * y2
    y0 = z0 / g00 - l1 * y1 - l2 * y2
    return [y0, y1, y2]


def weights(read):
    first = krylov([read(i) for i in range(6)])
    lifted = [None] + first
    second = []
    for i in range(6):
        total = None
        for p, (a, b) in enumerate(PAIRS):
            term = read(6 + i * len(PAIRS) + p)
            for k in (a, b):
                if k:
                    term = term * lifted[k]
            if a != b:
                term = 2.0 * term
            total = term if total is None else total + term
        second.append(total)
    return first, krylov(second)


RUN_NAMES = ["pu", "pv", "t2u", "t2v", "eta1", "w0", "w1", "w2", "eta2", "p", "p2", "gu1", "gv1", "gu2", "gv2"]


def advance_kernel(levels, total_rows, is_first, *refs):
    if is_first:
        info, tiles, kept, out, zonal = refs[:5]
        scratch = refs[5:]
    else:
        info, tiles, kept, zonal_before, out, spread = refs[:6]
        scratch = refs[6:]
    planes, after, turn, inside, staged, sums, sem = scratch[:7]
    rows, cols = out.shape[1:]
    members = kept.shape[0]
    tile_row = lax.axis_index("gridy")
    total = tiles[0]
    for i in range(1, tiles.shape[0]):
        total = total + tiles[i]
    staged[0:members, :] = total
    copy = pltpu.make_async_copy(staged, sums, sem)
    copy.start()
    fill_rows(turn, inside, tile_row * rows, total_rows)
    if not is_first:
        zonal = scratch[7]
    zonal[...] = jnp.zeros_like(zonal) if is_first else zonal_before[...]
    copy.wait()
    member = info[members + 2] if is_first else 1 - info[members + 2]
    ext = kept.at[member]
    work = Planes(levels, rows, turn, inside)
    work.add(planes, RUN_NAMES)
    work.add(kept, ["ext%d" % i for i in range(4 * levels)] + ["eta", "ocean"] + KEPT, (member,))

    def read(i):
        return jnp.full((1, 1), sums[member, i], jnp.float32)

    def combine(factors, names, out_name):
        for a, b in work.near():
            value = None
            for factor, name in zip(factors, names):
                term = factor * work.get(name, a, b)
                value = term if value is None else value + term
            work.put(out_name, a, b, value)

    first, second = weights(read)
    combine(first, ("v0", "v1", "v2"), "eta1")
    for a, b in work.near():
        ocean = work.get("ocean", a, b)
        slope_x, slope_y = work.slopes("eta1", a, b)
        slope_x, slope_y = GRAV * ocean * slope_x, GRAV * ocean * slope_y
        work.put("gu1", a, b, slope_x)
        work.put("gv1", a, b, slope_y)
        work.put("pu", a, b, work.get("tu", a, b) - levels * slope_x)
        work.put("pv", a, b, work.get("tv", a, b) - levels * slope_y)
    work.next_right_side("pu", "pv", "eta1", "q", "w0")
    work.powers("w0", "w1", "w2")
    combine(second, ("w0", "w1", "w2"), "eta2")
    for a, b in work.main():
        ocean = work.get("ocean", a, b)
        slope_x, slope_y = work.slopes("eta2", a, b)
        work.put("gu2", a, b, GRAV * ocean * slope_x)
        work.put("gv2", a, b, GRAV * ocean * slope_y)
        out[4 * levels, a - TOP : b - TOP, :] = work.get("eta2", a, b)[:, :cols]
    low, high = TOP - 8, TOP + rows + 8
    for a, b in chunks(TOP - CHUNK, TOP + rows + CHUNK):
        work.put("p", a, b, jnp.zeros((b - a, cols + LANE), jnp.float32))
        work.put("p2", a, b, jnp.zeros((b - a, cols + LANE), jnp.float32))

    def step(ref, l, press, a, b, width):
        def of(view):
            here = view[a:b, :]
            east, west = east_west(here)
            return here[:, :width], east[:, :width], west[:, :width], view[a + 1 : b + 1, :width], view[a - 1 : b - 1, :width]

        ocean = work.views["ocean"][a:b, :width]
        coriolis = turn[a:b, :width]
        u, east, west, north, south = of(ref.at[2 * levels + l])
        around_u = (east + west) + (north + south)
        v, east, west, north, south = of(ref.at[3 * levels + l])
        around_v = (east + west) + (north + south)
        _, east, west, north, south = of(work.views[press])
        new_u = ocean * ((KEEP_FLOW * u + VISCOSITY * around_u) + (coriolis * v - (east - west)))
        new_v = ocean * ((KEEP_FLOW * v + VISCOSITY * around_v) - (coriolis * u + (north - south)))
        flow_u, flow_v = ADV * u, ADV * v
        results = []
        for at in (l, levels + l):
            here, east, west, north, south = of(ref.at[at])
            carried = flow_u * (east - west) + flow_v * (north - south)
            spread = KEEP_TRACER * here + KAPPA * ((east + west) + (north + south))
            results.append(ocean * (spread - carried))
        return results[0], results[1], new_u, new_v

    def add_press(ref, l, press, a, b):
        dens = (PRESS_SCALE * BETA_S) * ref[levels + l, a:b, :] - (PRESS_SCALE * ALPHA_T) * ref[l, a:b, :]
        work.put(press, a, b, work.get(press, a, b) + dens)

    def level(l, carry):
        for a, b in chunks(TOP - CHUNK, TOP + rows + CHUNK, CHUNK_3D):
            add_press(ext, l, "p", a, b)
        for a, b in chunks(low, high, CHUNK_3D):
            temp, salt, u, v = step(ext, l, "p", a, b, cols + LANE)
            after[l, a:b, :] = temp
            after[levels + l, a:b, :] = salt
            after[2 * levels + l, a:b, :] = u - work.get("gu1", a, b)
            after[3 * levels + l, a:b, :] = v - work.get("gv1", a, b)
        for a, b in chunks(low, high, CHUNK_3D):
            add_press(after, l, "p2", a, b)
        for a, b in chunks(TOP, TOP + rows, CHUNK_3D):
            temp, salt, u, v = step(after, l, "p2", a, b, cols)
            here = slice(a - TOP, b - TOP)
            v = v - work.get("gv2", a, b)[:, :cols]
            out[l, here, :] = temp
            out[levels + l, here, :] = salt
            out[2 * levels + l, here, :] = u - work.get("gu2", a, b)[:, :cols]
            out[3 * levels + l, here, :] = v
            row_sum = jnp.sum(v, axis=1, keepdims=True)
            zonal[here, :] = jnp.where(lanes_like((b - a, LANE)) == member * levels + l, row_sum, zonal[here, :])
        return carry

    lax.fori_loop(0, levels, level, 0)
    if not is_first:
        square = jnp.concatenate([zonal[...]] + [jnp.zeros_like(zonal)] * (LANE // rows - 1), axis=0)
        turned = jnp.transpose(square)[: members * levels]
        line = turned[:levels]
        for m in range(1, members):
            line = line + pltpu.roll(turned, m * rows, 1)[m * levels : (m + 1) * levels]
        for i in range(spread.shape[0]):
            spread[i] = line


def advance(is_first, info, tiles, kept, zonal, rows, cols, total_rows):
    members, planes = kept.shape[:2]
    levels = (planes - 2 - len(KEPT)) // 4
    assert members * rows == LANE and members * levels == 8
    shape = plane_shape(rows, cols)
    zonal_shape = jax.ShapeDtypeStruct((rows, LANE), jnp.float32)
    out_shape = [jax.ShapeDtypeStruct((4 * levels + 1, rows, cols), jnp.float32)]
    if is_first:
        out_shape += [zonal_shape]
    else:
        out_shape += [jax.ShapeDtypeStruct((tiles.shape[0], levels, members * rows), jnp.float32)]
    return pl.pallas_call(
        functools.partial(advance_kernel, levels, total_rows, is_first),
        out_shape=tuple(out_shape),
        in_specs=in_smem(1) + whole(2 if is_first else 3),
        out_specs=tuple(whole(2)),
        scratch_shapes=[
            pltpu.VMEM((len(RUN_NAMES),) + shape, jnp.float32),
            pltpu.VMEM((4 * levels,) + shape, jnp.float32),
            pltpu.VMEM(shape, jnp.float32),
            pltpu.VMEM(shape, jnp.float32),
            pltpu.VMEM((8, LANE), jnp.float32),
            pltpu.SMEM((8, LANE), jnp.float32),
            pltpu.SemaphoreType.DMA,
        ]
        + ([] if is_first else [pltpu.VMEM((rows, LANE), jnp.float32)]),
        compiler_params=pltpu.CompilerParams(vmem_limit_bytes=VMEM_LIMIT),
        cost_estimate=pl.CostEstimate(flops=10**8, bytes_accessed=4 * 10**6, transcendentals=0),
        name="advance",
    )(info, tiles, kept, *([] if is_first else [zonal]))


def finish_kernel(count_y, count_x, total_cols, spread, overturn, score, held):
    members, levels, rows = overturn.shape
    total_rows = rows * count_y
    lane = lanes_like(spread.shape[1:])
    member_of = lane // rows
    weighted = None
    for y in range(count_y):
        total = spread[y * count_x]
        for x in range(1, count_x):
            total = total + spread[y * count_x + x]
        lines = [total[0:1]]
        for l in range(1, levels):
            lines.append(lines[-1] + total[l : l + 1])
        lines = jnp.concatenate(lines, axis=0) * (total_cols**-0.5)
        held[y] = lines
        latitude = ((lane - member_of * rows + y * rows).astype(jnp.float32) + 0.5) * (1.0 / total_rows)
        weighted = lines * latitude if weighted is None else weighted + lines * latitude
    mine = held[lax.axis_index("gridy")]
    for m in range(members):
        overturn[m] = mine[:, m * rows : (m + 1) * rows]
        score[m] = jnp.sum(jnp.where(member_of == m, weighted, 0.0)) * ((levels * total_rows) ** -0.5)


def finish(spread, members, rows, count_y, count_x, cols):
    levels = spread.shape[1]
    return pl.pallas_call(
        functools.partial(finish_kernel, count_y, count_x, cols * count_x),
        out_shape=(
            jax.ShapeDtypeStruct((members, levels, rows), jnp.float32),
            jax.ShapeDtypeStruct((members,), jnp.float32),
        ),
        in_specs=whole(1),
        out_specs=(whole(1)[0], in_smem(1)[0]),
        scratch_shapes=[pltpu.VMEM((count_y,) + spread.shape[1:], jnp.float32)],
        compiler_params=pltpu.CompilerParams(vmem_limit_bytes=VMEM_LIMIT),
        name="finish",
    )(spread)


def pick_kernel(levels, choice, source, score, their_score, *refs):
    count = len(refs) - 7
    sources, outs, weight, sem = refs[:count], refs[count : count + 5], refs[count + 5], refs[count + 6]
    slots = outs[0].shape[0]

    def parts(s, source):
        for f in range(4):
            yield source.at[pl.ds(f * levels, levels)], outs[f].at[s]
        yield source.at[4 * levels], outs[4].at[s]

    for s in range(slots):
        for k in range(count):

            @pl.when(choice[s] == k)
            def _():
                for i, (one, target) in enumerate(parts(s, sources[k])):
                    pltpu.make_async_copy(one, target, sem.at[s, i]).start()

    side = lax.axis_index("member")
    mean = (sum(score[m] for m in range(slots)) + sum(their_score[m] for m in range(slots))) * (0.5 / slots)
    for s in range(slots):
        value = jnp.float32(0.0)
        for m in range(slots):
            value = jnp.where(source[s] == side * slots + m, score[m], value)
            value = jnp.where(source[s] == (1 - side) * slots + m, their_score[m], value)
        weight[s] = value - mean
    for s in range(slots):
        for i, (one, target) in enumerate(parts(s, sources[0])):
            pltpu.make_async_copy(one, target, sem.at[s, i]).wait()


def pick(choice, source, score, their_score, sources, slots, levels):
    _, rows, cols = sources[0].shape
    volume = jax.ShapeDtypeStruct((slots, levels, rows, cols), jnp.float32)
    surface = jax.ShapeDtypeStruct((slots, rows, cols), jnp.float32)
    return pl.pallas_call(
        functools.partial(pick_kernel, levels),
        out_shape=(volume,) * 4 + (surface, jax.ShapeDtypeStruct((slots,), jnp.float32)),
        in_specs=in_smem(4) + whole(len(sources)),
        out_specs=tuple(in_hbm(5) + in_smem(1)),
        scratch_shapes=[pltpu.SemaphoreType.DMA((slots, 5))],
        compiler_params=pltpu.CompilerParams(vmem_limit_bytes=VMEM_LIMIT),
        name="pick",
    )(choice, source, score, their_score, *sources)


def shift(value, axis, by):
    count = lax.axis_size(axis)
    return lax.ppermute(value, axis, [(i, (i + by) % count) for i in range(count)])


def exchange_rims(packed, clone_source):
    to_west, to_east, rows_first, rows_second = packed
    rows = to_west.shape[1]
    count = lax.axis_size("gridy")
    assert count % 2 == 0
    partners = [i ^ 1 for i in range(count)], [min(max(i - 1 + 2 * (i % 2), 0), count - 1) for i in range(count)]

    def pair(value, which):
        return lax.ppermute(value, "gridy", list(enumerate(partners[which])))

    from_east, from_west = shift(to_west, "gridx", -1), shift(to_east, "gridx", 1)
    rows_first, rows_second = pair(rows_first, 0), pair(rows_second, 1)
    low = jnp.concatenate([from_east[:, :CHUNK], from_west[:, :CHUNK]], axis=2)
    high = jnp.concatenate([from_east[:, rows - CHUNK :], from_west[:, rows - CHUNK :]], axis=2)
    low, high, their_source = lax.optimization_barrier((low, high, swap(clone_source)))
    even = lax.axis_index("gridy") % 2 == 0
    sides_first = pair(jnp.where(even, high, low), 0)
    sides_second = pair(jnp.where(even, low, high), 1)
    return (from_east, from_west, rows_first, rows_second, sides_first, sides_second), their_source


def from_all(tiles, axes):
    return lax.all_to_all(tiles, axes, split_axis=0, concat_axis=0, tiled=True)


def swap(value):
    return lax.ppermute(value, "member", [(0, 1), (1, 0)])


def shards(temp, salt, uvel, vvel, eta, land_mask, clone_source):
    members, levels, rows, cols = temp.shape
    assert members == 2 and lax.axis_size("member") == 2
    count_y, count_x = lax.axis_size("gridy"), lax.axis_size("gridx")
    total_rows = rows * count_y
    grid = ("gridy", "gridx")

    fields = (temp, salt, uvel, vvel, eta, land_mask)
    rims, their_source = exchange_rims(pack_rims(*fields), clone_source)
    tile, kept, info = local_sums(clone_source, their_source, fields, rims, total_rows)
    tiles = from_all(jnp.broadcast_to(tile[None], (count_y * count_x,) + tile.shape), grid)

    sent, zonal = advance(True, info, tiles, kept, None, rows, cols, total_rows)
    arrived = swap(sent)

    def rest():
        other, spread = advance(False, info, tiles, kept, zonal, rows, cols, total_rows)
        return (other, *finish(from_all(spread, grid), members, rows, count_y, count_x, cols))

    def nothing():
        return jnp.zeros_like(sent), jnp.zeros((members, levels, rows), jnp.float32), jnp.zeros((members,), jnp.float32)

    other, overturn, score = lax.cond(info[members + 1] != 0, rest, nothing)
    their_score = swap(score)

    def with_second():
        sources = (sent, other, arrived, swap(other))
        return pick(info, clone_source, score, their_score, sources, members, levels)

    def without_second():
        return pick(info, clone_source, score, their_score, (sent, other, arrived), members, levels)

    *picked, clone_weight = lax.cond(info[members] != 0, with_second, without_second)
    return (*picked, overturn, clone_weight)


def solution(mesh):
    volume = P("member", None, "gridy", "gridx")
    in_specs = (volume,) * 4 + (P("member", "gridy", "gridx"), P("gridy", "gridx"), P("member"))
    out_specs = (volume,) * 4 + (P("member", "gridy", "gridx"), P("member", None, "gridy"), P("member"))
    return jax.shard_map(shards, mesh=mesh, in_specs=in_specs, out_specs=out_specs, check_vma=False)
```

```python
import functools

import jax
import jax.numpy as jnp
from jax import lax
from jax.experimental import pallas as pl
from jax.experimental.pallas import tpu as pltpu
from jax.sharding import PartitionSpec as P

STEPS = 2
ITERS = 3

ALPHA_T = 0.8
BETA_S = 0.6
PRESS_K = 0.25
STEP_DT = 0.1
KAPPA = 0.1
VISCOSITY = 0.1
DRAG_K = 0.05
CORI_K = 1.0
SURF_C = 4.0
DIV_K = 0.5
GRAV_K = 0.5

ADV = STEP_DT * 0.5
DIV = DIV_K * 0.5
GRAV = GRAV_K * 0.5

WIDE = 10
TOP = 24
CHUNK = 16
CHUNK_2D = 8
CHUNK_3D = 64
LANE = 128
PER_GROUP = 11
PAIRS = [(a, b) for a in range(4) for b in range(a, 4)]
SUMS = 6 + 6 * len(PAIRS)
VMEM_LIMIT = 24 * 1024 * 1024
WHOLE_VMEM = 60 * 1024 * 1024


def rim_place(plane):
    group, place = divmod(plane, PER_GROUP)
    if place < 6:
        return group, 0, (2 * place + 1) * WIDE
    return group, 1, (2 * (place - 6) + 2) * WIDE


def groups_of(planes):
    return -(-planes // PER_GROUP)


def lanes_like(shape):
    return lax.broadcasted_iota(jnp.int32, shape, len(shape) - 1)


def fetches(fields, planes_of, mask_to, sems, levels):
    members = fields[0].shape[0]
    per_member = []
    for m in range(members):
        parts = [(fields[f].at[m], planes_of(m, pl.ds(f * levels, levels))) for f in range(4)]
        parts.append((fields[4].at[m], planes_of(m, 4 * levels)))
        per_member.append([pltpu.make_async_copy(*part, sems.at[m, i]) for i, part in enumerate(parts)])
    mask_copy = pltpu.make_async_copy(fields[5], mask_to, sems.at[0, 5])
    mask_copy.start()
    for copies in per_member:
        for copy in copies:
            copy.start()
    mask_copy.wait()
    return per_member


def pack_columns_kernel(levels, *refs):
    fields, (to_west, to_east), (held, mask, sems) = refs[:6], refs[6:8], refs[8:]
    members, _, rows, cols = held.shape
    planes = 4 * levels + 2
    copies = fetches(fields, lambda m, at: held.at[m, at], mask, sems, levels)
    lane = lanes_like((rows, LANE))
    for m in range(members):
        for copy in copies[m]:
            copy.wait()
        west_parts = [jnp.zeros((rows, LANE), jnp.float32)] * groups_of(planes)
        east_parts = list(west_parts)
        for plane in range(planes):
            value = held[m, plane] if plane < planes - 1 else mask[...].astype(jnp.float32)
            group, _, start = rim_place(plane)
            both = jnp.where(lane < WIDE, value[:, :LANE], value[:, cols - LANE :])
            both = pltpu.roll(both, start, 1)
            is_west = (lane >= start) & (lane < start + WIDE)
            is_east = (lane >= start - WIDE) & (lane < start)
            west_parts[group] = jnp.where(is_west, both, west_parts[group])
            east_parts[group] = jnp.where(is_east, both, east_parts[group])
        for group in range(groups_of(planes)):
            where = slice(group * LANE, (group + 1) * LANE)
            to_west[m, :, where] = west_parts[group]
            to_east[m, :, where] = east_parts[group]


def pack_rows_kernel(levels, *refs):
    fields, (rows_first, rows_second), (held, mask, sems) = refs[:6], refs[6:8], refs[8:]
    members, _, rows, cols = held.shape
    planes = 4 * levels + 2
    copies = fetches(fields, lambda m, at: held.at[m, at], mask, sems, levels)
    even = lax.broadcasted_iota(jnp.int32, (WIDE, cols), 0) * 0 + lax.rem(lax.axis_index("gridy"), 2) == 0
    for m in range(members):
        for copy in copies[m]:
            copy.wait()
        for plane in range(planes):
            value = held[m, plane] if plane < planes - 1 else mask[...].astype(jnp.float32)
            low, high = value[:WIDE], value[rows - WIDE :]
            rows_first[m, plane * WIDE : (plane + 1) * WIDE, :] = jnp.where(even, high, low)
            rows_second[m, plane * WIDE : (plane + 1) * WIDE, :] = jnp.where(even, low, high)


def whole(count):
    return [pl.BlockSpec(memory_space=pltpu.VMEM)] * count


def in_hbm(count):
    return [pl.BlockSpec(memory_space=pltpu.HBM)] * count


def in_smem(count):
    return [pl.BlockSpec(memory_space=pltpu.SMEM)] * count


def pack(kernel, shape, fields, name):
    members, levels, rows, cols = fields[0].shape
    return pl.pallas_call(
        functools.partial(kernel, levels),
        out_shape=(jax.ShapeDtypeStruct(shape, jnp.float32),) * 2,
        in_specs=in_hbm(6),
        out_specs=tuple(whole(2)),
        scratch_shapes=[
            pltpu.VMEM((members, 4 * levels + 1, rows, cols), jnp.float32),
            pltpu.VMEM((rows, cols), jnp.int32),
            pltpu.SemaphoreType.DMA((members, 6)),
        ],
        compiler_params=pltpu.CompilerParams(vmem_limit_bytes=WHOLE_VMEM),
        cost_estimate=pl.CostEstimate(flops=10**6, bytes_accessed=10**6, transcendentals=0),
        name=name,
    )(*fields)


def pack_columns(fields):
    members, levels, rows, _ = fields[0].shape
    wide = groups_of(4 * levels + 2) * LANE
    return pack(pack_columns_kernel, (members, rows, wide), fields, "pack_columns")


def pack_rows(fields):
    members, levels, _, cols = fields[0].shape
    height = -(-(4 * levels + 2) * WIDE // 8) * 8
    return pack(pack_rows_kernel, (members, height, cols), fields, "pack_rows")


def east_west(value):
    width = value.shape[-1]
    return pltpu.roll(value, width - 1, 1), pltpu.roll(value, 1, 1)


def chunks(first, last, size=CHUNK_2D):
    return [(a, min(a + size, last)) for a in range(first, last, size)]


def assemble(ext, fields, rims, m, levels, total_rows):
    from_east, from_west, rows_first, rows_second, sides_first, sides_second = rims
    planes = 4 * levels + 2
    rows, cols = fields[5].shape
    tile_row = lax.axis_index("gridy")
    odd_tile = lax.rem(tile_row, 2).astype(jnp.float32)
    keep_south = jnp.where(tile_row > 0, 1.0, 0.0).astype(jnp.float32)
    keep_north = jnp.where(tile_row * rows + rows < total_rows, 1.0, 0.0).astype(jnp.float32)
    north_factors = keep_north * (1.0 - odd_tile), keep_north * odd_tile
    south_factors = keep_south * odd_tile, keep_south * (1.0 - odd_tile)

    def of_north(first, second):
        return north_factors[0] * first + north_factors[1] * second

    def of_south(first, second):
        return south_factors[0] * first + south_factors[1] * second

    wide = groups_of(planes) * LANE
    for group in range(groups_of(planes)):
        where = slice(group * LANE, (group + 1) * LANE)
        where_west = slice(wide + group * LANE, wide + (group + 1) * LANE)
        east = sides_first[m, :, where], sides_second[m, :, where]
        west = sides_first[m, :, where_west], sides_second[m, :, where_west]
        bands = [(TOP - CHUNK, of_south(*east), of_south(*west))]
        for a in range(0, rows, CHUNK):
            bands.append((TOP + a, from_east[m, a : a + CHUNK, where], from_west[m, a : a + CHUNK, where]))
        bands.append((TOP + rows, of_north(*east), of_north(*west)))
        for at, east, west in bands:
            odd = ((lanes_like(east.shape) // WIDE) & 1) == 1
            joined = (jnp.where(odd, east, west), jnp.where(odd, west, east))
            for plane in range(group * PER_GROUP, min((group + 1) * PER_GROUP, planes)):
                _, kind, offset = rim_place(plane)
                ext[plane, at : at + CHUNK, cols : cols + LANE] = pltpu.roll(joined[kind], LANE - offset, 1)
    for plane in range(planes):
        if plane < 4 * levels:
            value = fields[plane // levels][m, plane % levels]
        else:
            value = fields[4][m] if plane == 4 * levels else fields[5][...].astype(jnp.float32)
        ext[plane, TOP : TOP + rows, :cols] = value
        at = slice(plane * WIDE, (plane + 1) * WIDE)
        ext[plane, TOP - WIDE : TOP, :cols] = of_south(rows_first[m, at, :], rows_second[m, at, :])
        ext[plane, TOP + rows : TOP + rows + WIDE, :cols] = of_north(rows_first[m, at, :], rows_second[m, at, :])


def fill_rows(turn, inside, first_row, total_rows):
    shape = (CHUNK, turn.shape[1])
    for a in range(0, turn.shape[0], CHUNK):
        row = first_row + (a - TOP) + lax.broadcasted_iota(jnp.int32, shape, 0)
        latitude = row.astype(jnp.float32) + 0.5
        turn[a : a + CHUNK, :] = STEP_DT * CORI_K * (2.0 * latitude / total_rows - 1.0)
        inside[a : a + CHUNK, :] = jnp.where((row >= 0) & (row < total_rows), 1.0, 0.0)


KEPT = ["tu", "tv", "q", "v0", "v1", "v2"]
KEEP_FLOW = 1.0 - STEP_DT * DRAG_K - 4.0 * VISCOSITY
KEEP_TRACER = 1.0 - 4.0 * KAPPA
PRESS_SCALE = PRESS_K * 0.5 * STEP_DT


class Planes:
    def __init__(self, levels, rows, turn, inside):
        self.levels, self.rows, self.turn, self.inside = levels, rows, turn, inside
        self.views = {}

    def add(self, ref, names, lead=()):
        for i, name in enumerate(names):
            self.views[name] = ref.at[lead + (i,)]

    def get(self, name, a, b):
        return self.views[name][a:b, :]

    def put(self, name, a, b, value):
        self.views[name][a:b, :] = value

    def sides(self, name, a, b):
        here = self.get(name, a, b)
        east, west = east_west(here)
        return here, east, west, self.get(name, a + 1, b + 1), self.get(name, a - 1, b - 1)

    def slopes(self, name, a, b):
        _, east, west, north, south = self.sides(name, a, b)
        return east - west, north - south

    def around(self, name, a, b):
        here, east, west, north, south = self.sides(name, a, b)
        return here, (east + west) + (north + south)

    def main(self):
        return chunks(TOP, TOP + self.rows)

    def near(self):
        return [(TOP - 8, TOP)] + self.main() + [(TOP + self.rows, TOP + self.rows + 8)]

    def masked(self, a, b, value):
        if a >= TOP and b <= TOP + self.rows:
            return value
        return self.inside[a:b, :] * value

    def divergence(self, u_name, v_name, a, b):
        east, west = east_west(self.get(u_name, a, b))
        return DIV * ((east - west) + (self.get(v_name, a + 1, b + 1) - self.get(v_name, a - 1, b - 1)))

    def flow(self, u_name, v_name, press, out_u, out_v, a, b):
        ocean, turn = self.get("ocean", a, b), self.turn[a:b, :]
        u, around_u = self.around(u_name, a, b)
        v, around_v = self.around(v_name, a, b)
        push_u, push_v = turn * v, turn * u
        if press:
            slope_x, slope_y = self.slopes(press, a, b)
            push_u, push_v = push_u - slope_x, push_v + slope_y
        self.put(out_u, a, b, ocean * ((KEEP_FLOW * u + VISCOSITY * around_u) + push_u))
        self.put(out_v, a, b, ocean * ((KEEP_FLOW * v + VISCOSITY * around_v) - push_v))

    def powers(self, first, second, third):
        for a, b in self.near():
            self.put(second, a, b, self.masked(a, b, self.around(first, a, b)[1]))
        for a, b in self.near():
            value = self.around(second, a, b)[1] - 4.0 * self.get(first, a, b)
            self.put(third, a, b, self.masked(a, b, value))

    def next_right_side(self, u_name, v_name, eta_name, press, out_name):
        for a, b in self.near():
            self.flow(u_name, v_name, press, "t2u", "t2v", a, b)
        for a, b in self.near():
            div = self.divergence("t2u", "t2v", a, b)
            value = self.get(eta_name, a, b) - div if eta_name else -div
            self.put(out_name, a, b, self.masked(a, b, value))


def scaled(factor, value):
    return value if factor == 1.0 else factor * value


def surface_start(ext, work):
    levels = work.levels
    low, high = TOP - CHUNK, TOP + work.rows + CHUNK
    for a, b in chunks(low, high):
        su = sv = sp = None
        for l in range(levels):
            factor = PRESS_SCALE * (levels - l)
            dens = (factor * BETA_S) * ext[levels + l, a:b, :] - (factor * ALPHA_T) * ext[l, a:b, :]
            work.put("d%d" % l, a, b, dens)
            u, v = ext[2 * levels + l, a:b, :], ext[3 * levels + l, a:b, :]
            su, sv, sp = (u, v, dens) if l == 0 else (su + u, sv + v, sp + dens)
        work.put("su", a, b, su)
        work.put("sv", a, b, sv)
        work.put("sp", a, b, sp)
    for a, b in work.near():
        carried = None
        for l in range(levels):
            slope_x, slope_y = work.slopes("d%d" % l, a, b)
            term = ext[2 * levels + l, a:b, :] * slope_x + ext[3 * levels + l, a:b, :] * slope_y
            carried = term if l == 0 else carried + term
        here, around = work.around("sp", a, b)
        work.put("q", a, b, work.get("ocean", a, b) * ((KEEP_TRACER * here + KAPPA * around) - ADV * carried))
    for a, b in chunks(low, high):
        work.flow("su", "sv", "sp", "tu", "tv", a, b)
    for a, b in work.near():
        work.put("v0", a, b, work.masked(a, b, work.get("eta", a, b) - work.divergence("tu", "tv", a, b)))


SUM_NAMES = ["su", "sv", "sp", "v3", "pu", "pv", "t2u", "t2v"] + ["w%d_%d" % (i, k) for i in range(4) for k in range(4)]


def whether(*conditions):
    result = jnp.int32(0)
    for condition in conditions:
        result = jnp.where(condition, 1, result)
    return result


def choose(source, theirs, side, members, info):
    mine, away = side * members, (1 - side) * members
    sent = [whether(*[theirs[slot] == mine + m for slot in range(members)]) for m in range(2)]
    here = [whether(*[source[slot] == away + m for slot in range(members)]) for m in range(2)]
    first_sent, first_here = 1 - sent[0], 1 - here[0]
    for slot in range(members):
        own = jnp.where(source[slot] - mine == first_sent, 0, 1)
        far = jnp.where(source[slot] - away == first_here, 2, 3)
        info[slot] = jnp.where((source[slot] >= mine) & (source[slot] < mine + members), own, far)
    info[members] = jnp.maximum(sent[0] * sent[1], here[0] * here[1])
    info[members + 1] = jnp.int32(1)
    info[members + 2] = first_sent


def sums_kernel(levels, total_rows, source, theirs, *refs):
    fields, rims, out, kept, info = refs[:6], refs[6:12], refs[12], refs[13], refs[14]
    planes, turn, inside, red = refs[15:]
    members = kept.shape[0]
    rows, cols = fields[5].shape
    tile_row = lax.axis_index("gridy")
    choose(source, theirs, lax.axis_index("member"), members, info)
    fill_rows(turn, inside, tile_row * rows, total_rows)
    red[...] = jnp.zeros_like(red)

    def one(m, carry):
        ext = kept.at[m]
        assemble(ext, fields, rims, m, levels, total_rows)
        work = Planes(levels, rows, turn, inside)
        work.add(planes, SUM_NAMES + ["d%d" % l for l in range(levels)])
        work.add(kept, ["ext%d" % i for i in range(4 * levels)] + ["eta", "ocean"] + KEPT, (m,))
        surface_start(ext, work)
        work.powers("v0", "v1", "v2")
        for a, b in work.main():
            work.put("v3", a, b, work.around("v2", a, b)[1])
        work.next_right_side("tu", "tv", None, "q", "w0_0")
        for k in range(1, 4):
            name = "v%d" % (k - 1)
            for a, b in work.near():
                ocean = work.get("ocean", a, b)
                slope_x, slope_y = work.slopes(name, a, b)
                work.put("pu", a, b, scaled(-levels * GRAV, ocean * slope_x))
                work.put("pv", a, b, scaled(-levels * GRAV, ocean * slope_y))
            work.next_right_side("pu", "pv", name, None, "w0_%d" % k)
        for k in range(4):
            work.powers("w0_%d" % k, "w1_%d" % k, "w2_%d" % k)
            for a, b in work.main():
                work.put("w3_%d" % k, a, b, work.around("w2_%d" % k, a, b)[1])

        def put_sums(at, first, second, pairs):
            totals = [None] * len(pairs)
            for a in range(TOP, TOP + rows, 8):
                xs = [work.get(name, a, a + 8)[:, :cols] for name in first]
                ys = [work.get(name, a, a + 8)[:, :cols] for name in second]
                for p, (i, j) in enumerate(pairs):
                    term = xs[i] * ys[j]
                    totals[p] = term if totals[p] is None else totals[p] + term
            for p, total in enumerate(totals):
                folded = total[:, :LANE]
                for c in range(LANE, cols, LANE):
                    folded = folded + total[:, c : c + LANE]
                red[m, at + p : at + p + 1, :] = jnp.sum(folded, axis=0, keepdims=True)

        for i in range(6):
            low, high = i // 2, i - i // 2
            put_sums(i, ["v%d" % low], ["v%d" % high], [(0, 0)])
            names = [["w%d_%d" % (which, k) for k in range(4)] for which in (low, high)]
            put_sums(6 + i * len(PAIRS), names[0], names[1], PAIRS)
        return carry

    lax.fori_loop(0, members, one, 0)
    for m in range(members):
        out[m : m + 1, :] = jnp.sum(jnp.transpose(red[m]), axis=0, keepdims=True)


def plane_shape(rows, cols):
    return (2 * TOP + rows, cols + LANE)


def local_sums(source, theirs, fields, rims, total_rows):
    members, levels, rows, cols = fields[0].shape
    assert SUMS <= LANE and members <= 8
    shape = plane_shape(rows, cols)
    kept = (members, 4 * levels + 2 + len(KEPT)) + shape
    return pl.pallas_call(
        functools.partial(sums_kernel, levels, total_rows),
        out_shape=(
            jax.ShapeDtypeStruct((members, LANE), jnp.float32),
            jax.ShapeDtypeStruct(kept, jnp.float32),
            jax.ShapeDtypeStruct((members + 3,), jnp.int32),
        ),
        in_specs=in_smem(2) + whole(12),
        out_specs=tuple(whole(2) + in_smem(1)),
        scratch_shapes=[
            pltpu.VMEM((len(SUM_NAMES) + levels,) + shape, jnp.float32),
            pltpu.VMEM(shape, jnp.float32),
            pltpu.VMEM(shape, jnp.float32),
            pltpu.VMEM((members, LANE, LANE), jnp.float32),
        ],
        compiler_params=pltpu.CompilerParams(vmem_limit_bytes=VMEM_LIMIT),
        cost_estimate=pl.CostEstimate(flops=10**8, bytes_accessed=4 * 10**6, transcendentals=0),
        name="local_sums",
    )(source, theirs, *fields, *rims)


def krylov(moment):
    n00, n01, n11, n12, n22, x22 = moment
    n02 = n11 - 4.0 * n00
    main, near = 1.0 + 4.0 * SURF_C, SURF_C
    g00 = main * n00 - near * n01
    g01 = main * n01 - near * n11
    g02 = main * n02 - near * n12
    g11 = main * n11 - near * (n12 + 4.0 * n01)
    g12 = main * n12 - near * (n22 + 4.0 * n02)
    g22 = main * n22 - near * x22
    l1, l2 = g01 / g00, g02 / g00
    d1 = g11 - l1 * g01
    d1 = jnp.where(d1 > 3e-7 * g11, d1, jnp.inf)
    e = g12 - l1 * g02
    l12 = e / d1
    d2 = g22 - l2 * g02 - l12 * e
    d2 = jnp.where(d2 > 3e-7 * g22, d2, jnp.inf)
    z0 = n00
    z1 = n01 - l1 * z0
    z2 = n02 - l2 * z0 - l12 * z1
    y2 = z2 / d2
    y1 = z1 / d1 - l12 * y2
    y0 = z0 / g00 - l1 * y1 - l2 * y2
    return [y0, y1, y2]


def weights(read):
    first = krylov([read(i) for i in range(6)])
    lifted = [None] + first
    second = []
    for i in range(6):
        total = None
        for p, (a, b) in enumerate(PAIRS):
            term = read(6 + i * len(PAIRS) + p)
            for k in (a, b):
                if k:
                    term = term * lifted[k]
            if a != b:
                term = 2.0 * term
            total = term if total is None else total + term
        second.append(total)
    return first, krylov(second)


RUN_NAMES = ["pu", "pv", "t2u", "t2v", "eta1", "w0", "w1", "w2", "eta2", "p", "p2", "gu1", "gv1", "gu2", "gv2"]


def advance_kernel(levels, total_rows, is_first, *refs):
    if is_first:
        info, tiles, kept, out, zonal = refs[:5]
        scratch = refs[5:]
    else:
        info, tiles, kept, zonal_before, out, spread = refs[:6]
        scratch = refs[6:]
    planes, after, turn, inside, staged, sums, sem = scratch[:7]
    rows, cols = out.shape[1:]
    members = kept.shape[0]
    tile_row = lax.axis_index("gridy")
    total = tiles[0]
    for i in range(1, tiles.shape[0]):
        total = total + tiles[i]
    staged[0:members, :] = total
    copy = pltpu.make_async_copy(staged, sums, sem)
    copy.start()
    fill_rows(turn, inside, tile_row * rows, total_rows)
    if not is_first:
        zonal = scratch[7]
    zonal[...] = jnp.zeros_like(zonal) if is_first else zonal_before[...]
    copy.wait()
    member = info[members + 2] if is_first else 1 - info[members + 2]
    ext = kept.at[member]
    work = Planes(levels, rows, turn, inside)
    work.add(planes, RUN_NAMES)
    work.add(kept, ["ext%d" % i for i in range(4 * levels)] + ["eta", "ocean"] + KEPT, (member,))

    def read(i):
        return jnp.full((1, 1), sums[member, i], jnp.float32)

    def combine(factors, names, out_name):
        for a, b in work.near():
            value = None
            for factor, name in zip(factors, names):
                term = factor * work.get(name, a, b)
                value = term if value is None else value + term
            work.put(out_name, a, b, value)

    first, second = weights(read)
    combine(first, ("v0", "v1", "v2"), "eta1")
    for a, b in work.near():
        ocean = work.get("ocean", a, b)
        slope_x, slope_y = work.slopes("eta1", a, b)
        slope_x, slope_y = GRAV * ocean * slope_x, GRAV * ocean * slope_y
        work.put("gu1", a, b, slope_x)
        work.put("gv1", a, b, slope_y)
        work.put("pu", a, b, work.get("tu", a, b) - levels * slope_x)
        work.put("pv", a, b, work.get("tv", a, b) - levels * slope_y)
    work.next_right_side("pu", "pv", "eta1", "q", "w0")
    work.powers("w0", "w1", "w2")
    combine(second, ("w0", "w1", "w2"), "eta2")
    for a, b in work.main():
        ocean = work.get("ocean", a, b)
        slope_x, slope_y = work.slopes("eta2", a, b)
        work.put("gu2", a, b, GRAV * ocean * slope_x)
        work.put("gv2", a, b, GRAV * ocean * slope_y)
        out[4 * levels, a - TOP : b - TOP, :] = work.get("eta2", a, b)[:, :cols]
    low, high = TOP - 8, TOP + rows + 8
    for a, b in chunks(TOP - CHUNK, TOP + rows + CHUNK):
        work.put("p", a, b, jnp.zeros((b - a, cols + LANE), jnp.float32))
        work.put("p2", a, b, jnp.zeros((b - a, cols + LANE), jnp.float32))

    def step(ref, l, press, a, b, width):
        def of(view):
            here = view[a:b, :]
            east, west = east_west(here)
            return here[:, :width], east[:, :width], west[:, :width], view[a + 1 : b + 1, :width], view[a - 1 : b - 1, :width]

        ocean = work.views["ocean"][a:b, :width]
        coriolis = turn[a:b, :width]
        u, east, west, north, south = of(ref.at[2 * levels + l])
        around_u = (east + west) + (north + south)
        v, east, west, north, south = of(ref.at[3 * levels + l])
        around_v = (east + west) + (north + south)
        _, east, west, north, south = of(work.views[press])
        new_u = ocean * ((KEEP_FLOW * u + VISCOSITY * around_u) + (coriolis * v - (east - west)))
        new_v = ocean * ((KEEP_FLOW * v + VISCOSITY * around_v) - (coriolis * u + (north - south)))
        flow_u, flow_v = ADV * u, ADV * v
        results = []
        for at in (l, levels + l):
            here, east, west, north, south = of(ref.at[at])
            carried = flow_u * (east - west) + flow_v * (north - south)
            spread = KEEP_TRACER * here + KAPPA * ((east + west) + (north + south))
            results.append(ocean * (spread - carried))
        return results[0], results[1], new_u, new_v

    def add_press(ref, l, press, a, b):
        dens = (PRESS_SCALE * BETA_S) * ref[levels + l, a:b, :] - (PRESS_SCALE * ALPHA_T) * ref[l, a:b, :]
        work.put(press, a, b, work.get(press, a, b) + dens)

    def level(l, carry):
        for a, b in chunks(TOP - CHUNK, TOP + rows + CHUNK, CHUNK_3D):
            add_press(ext, l, "p", a, b)
        for a, b in chunks(low, high, CHUNK_3D):
            temp, salt, u, v = step(ext, l, "p", a, b, cols + LANE)
            after[l, a:b, :] = temp
            after[levels + l, a:b, :] = salt
            after[2 * levels + l, a:b, :] = u - work.get("gu1", a, b)
            after[3 * levels + l, a:b, :] = v - work.get("gv1", a, b)
        for a, b in chunks(low, high, CHUNK_3D):
            add_press(after, l, "p2", a, b)
        for a, b in chunks(TOP, TOP + rows, CHUNK_3D):
            temp, salt, u, v = step(after, l, "p2", a, b, cols)
            here = slice(a - TOP, b - TOP)
            v = v - work.get("gv2", a, b)[:, :cols]
            out[l, here, :] = temp
            out[levels + l, here, :] = salt
            out[2 * levels + l, here, :] = u - work.get("gu2", a, b)[:, :cols]
            out[3 * levels + l, here, :] = v
            row_sum = jnp.sum(v, axis=1, keepdims=True)
            zonal[here, :] = jnp.where(lanes_like((b - a, LANE)) == member * levels + l, row_sum, zonal[here, :])
        return carry

    lax.fori_loop(0, levels, level, 0)
    if not is_first:
        square = jnp.concatenate([zonal[...]] + [jnp.zeros_like(zonal)] * (LANE // rows - 1), axis=0)
        turned = jnp.transpose(square)[: members * levels]
        line = turned[:levels]
        for m in range(1, members):
            line = line + pltpu.roll(turned, m * rows, 1)[m * levels : (m + 1) * levels]
        for i in range(spread.shape[0]):
            spread[i] = line


def advance(is_first, info, tiles, kept, zonal, rows, cols, total_rows):
    members, planes = kept.shape[:2]
    levels = (planes - 2 - len(KEPT)) // 4
    assert members * rows == LANE and members * levels == 8
    shape = plane_shape(rows, cols)
    zonal_shape = jax.ShapeDtypeStruct((rows, LANE), jnp.float32)
    out_shape = [jax.ShapeDtypeStruct((4 * levels + 1, rows, cols), jnp.float32)]
    if is_first:
        out_shape += [zonal_shape]
    else:
        out_shape += [jax.ShapeDtypeStruct((tiles.shape[0], levels, members * rows), jnp.float32)]
    return pl.pallas_call(
        functools.partial(advance_kernel, levels, total_rows, is_first),
        out_shape=tuple(out_shape),
        in_specs=in_smem(1) + whole(2 if is_first else 3),
        out_specs=tuple(whole(2)),
        scratch_shapes=[
            pltpu.VMEM((len(RUN_NAMES),) + shape, jnp.float32),
            pltpu.VMEM((4 * levels,) + shape, jnp.float32),
            pltpu.VMEM(shape, jnp.float32),
            pltpu.VMEM(shape, jnp.float32),
            pltpu.VMEM((8, LANE), jnp.float32),
            pltpu.SMEM((8, LANE), jnp.float32),
            pltpu.SemaphoreType.DMA,
        ]
        + ([] if is_first else [pltpu.VMEM((rows, LANE), jnp.float32)]),
        compiler_params=pltpu.CompilerParams(vmem_limit_bytes=VMEM_LIMIT),
        cost_estimate=pl.CostEstimate(flops=10**8, bytes_accessed=4 * 10**6, transcendentals=0),
        name="advance",
    )(info, tiles, kept, *([] if is_first else [zonal]))


def finish_kernel(count_y, count_x, total_cols, spread, overturn, score, held):
    members, levels, rows = overturn.shape
    total_rows = rows * count_y
    lane = lanes_like(spread.shape[1:])
    member_of = lane // rows
    weighted = None
    for y in range(count_y):
        total = spread[y * count_x]
        for x in range(1, count_x):
            total = total + spread[y * count_x + x]
        lines = [total[0:1]]
        for l in range(1, levels):
            lines.append(lines[-1] + total[l : l + 1])
        lines = jnp.concatenate(lines, axis=0) * (total_cols**-0.5)
        held[y] = lines
        latitude = ((lane - member_of * rows + y * rows).astype(jnp.float32) + 0.5) * (1.0 / total_rows)
        weighted = lines * latitude if weighted is None else weighted + lines * latitude
    mine = held[lax.axis_index("gridy")]
    for m in range(members):
        overturn[m] = mine[:, m * rows : (m + 1) * rows]
        score[m] = jnp.sum(jnp.where(member_of == m, weighted, 0.0)) * ((levels * total_rows) ** -0.5)


def finish(spread, members, rows, count_y, count_x, cols):
    levels = spread.shape[1]
    return pl.pallas_call(
        functools.partial(finish_kernel, count_y, count_x, cols * count_x),
        out_shape=(
            jax.ShapeDtypeStruct((members, levels, rows), jnp.float32),
            jax.ShapeDtypeStruct((members,), jnp.float32),
        ),
        in_specs=whole(1),
        out_specs=(whole(1)[0], in_smem(1)[0]),
        scratch_shapes=[pltpu.VMEM((count_y,) + spread.shape[1:], jnp.float32)],
        compiler_params=pltpu.CompilerParams(vmem_limit_bytes=VMEM_LIMIT),
        name="finish",
    )(spread)


def pick_kernel(levels, choice, source, score, their_score, *refs):
    count = len(refs) - 7
    sources, outs, weight, sem = refs[:count], refs[count : count + 5], refs[count + 5], refs[count + 6]
    slots = outs[0].shape[0]

    def parts(s, source):
        for f in range(4):
            yield source.at[pl.ds(f * levels, levels)], outs[f].at[s]
        yield source.at[4 * levels], outs[4].at[s]

    for s in range(slots):
        for k in range(count):

            @pl.when(choice[s] == k)
            def _():
                for i, (one, target) in enumerate(parts(s, sources[k])):
                    pltpu.make_async_copy(one, target, sem.at[s, i]).start()

    side = lax.axis_index("member")
    mean = (sum(score[m] for m in range(slots)) + sum(their_score[m] for m in range(slots))) * (0.5 / slots)
    for s in range(slots):
        value = jnp.float32(0.0)
        for m in range(slots):
            value = jnp.where(source[s] == side * slots + m, score[m], value)
            value = jnp.where(source[s] == (1 - side) * slots + m, their_score[m], value)
        weight[s] = value - mean
    for s in range(slots):
        for i, (one, target) in enumerate(parts(s, sources[0])):
            pltpu.make_async_copy(one, target, sem.at[s, i]).wait()


def pick(choice, source, score, their_score, sources, slots, levels):
    _, rows, cols = sources[0].shape
    volume = jax.ShapeDtypeStruct((slots, levels, rows, cols), jnp.float32)
    surface = jax.ShapeDtypeStruct((slots, rows, cols), jnp.float32)
    return pl.pallas_call(
        functools.partial(pick_kernel, levels),
        out_shape=(volume,) * 4 + (surface, jax.ShapeDtypeStruct((slots,), jnp.float32)),
        in_specs=in_smem(4) + whole(len(sources)),
        out_specs=tuple(in_hbm(5) + in_smem(1)),
        scratch_shapes=[pltpu.SemaphoreType.DMA((slots, 5))],
        compiler_params=pltpu.CompilerParams(vmem_limit_bytes=VMEM_LIMIT),
        name="pick",
    )(choice, source, score, their_score, *sources)


def shift(value, axis, by):
    count = lax.axis_size(axis)
    return lax.ppermute(value, axis, [(i, (i + by) % count) for i in range(count)])


def exchange_rims(fields, clone_source):
    to_west, to_east = pack_columns(fields)
    rows = to_west.shape[1]
    count = lax.axis_size("gridy")
    assert count % 2 == 0
    partners = [i ^ 1 for i in range(count)], [min(max(i - 1 + 2 * (i % 2), 0), count - 1) for i in range(count)]

    def pair(value, which):
        return lax.ppermute(value, "gridy", list(enumerate(partners[which])))

    from_east, from_west = shift(to_west, "gridx", -1), shift(to_east, "gridx", 1)
    rows_first, rows_second = pack_rows(fields)
    rows_first, rows_second = pair(rows_first, 0), pair(rows_second, 1)
    low = jnp.concatenate([from_east[:, :CHUNK], from_west[:, :CHUNK]], axis=2)
    high = jnp.concatenate([from_east[:, rows - CHUNK :], from_west[:, rows - CHUNK :]], axis=2)
    low, high, their_source = lax.optimization_barrier((low, high, swap(clone_source)))
    even = lax.axis_index("gridy") % 2 == 0
    sides_first = pair(jnp.where(even, high, low), 0)
    sides_second = pair(jnp.where(even, low, high), 1)
    return (from_east, from_west, rows_first, rows_second, sides_first, sides_second), their_source


def from_all(tiles, axes):
    return lax.all_to_all(tiles, axes, split_axis=0, concat_axis=0, tiled=True)


def swap(value):
    return lax.ppermute(value, "member", [(0, 1), (1, 0)])


def shards(temp, salt, uvel, vvel, eta, land_mask, clone_source):
    members, levels, rows, cols = temp.shape
    assert members == 2 and lax.axis_size("member") == 2
    count_y, count_x = lax.axis_size("gridy"), lax.axis_size("gridx")
    total_rows = rows * count_y
    grid = ("gridy", "gridx")

    fields = (temp, salt, uvel, vvel, eta, land_mask)
    rims, their_source = exchange_rims(fields, clone_source)
    tile, kept, info = local_sums(clone_source, their_source, fields, rims, total_rows)
    tiles = from_all(jnp.broadcast_to(tile[None], (count_y * count_x,) + tile.shape), grid)

    sent, zonal = advance(True, info, tiles, kept, None, rows, cols, total_rows)
    arrived = swap(sent)

    def rest():
        other, spread = advance(False, info, tiles, kept, zonal, rows, cols, total_rows)
        return (other, *finish(from_all(spread, grid), members, rows, count_y, count_x, cols))

    def nothing():
        return jnp.zeros_like(sent), jnp.zeros((members, levels, rows), jnp.float32), jnp.zeros((members,), jnp.float32)

    other, overturn, score = lax.cond(info[members + 1] != 0, rest, nothing)
    their_score = swap(score)

    def with_second():
        sources = (sent, other, arrived, swap(other))
        return pick(info, clone_source, score, their_score, sources, members, levels)

    def without_second():
        return pick(info, clone_source, score, their_score, (sent, other, arrived), members, levels)

    *picked, clone_weight = lax.cond(info[members] != 0, with_second, without_second)
    return (*picked, overturn, clone_weight)


def solution(mesh):
    volume = P("member", None, "gridy", "gridx")
    in_specs = (volume,) * 4 + (P("member", "gridy", "gridx"), P("gridy", "gridx"), P("member"))
    out_specs = (volume,) * 4 + (P("member", "gridy", "gridx"), P("member", None, "gridy"), P("member"))
    return jax.shard_map(shards, mesh=mesh, in_specs=in_specs, out_specs=out_specs, check_vma=False)
```

```python
import functools

import jax
import jax.numpy as jnp
from jax import lax
from jax.experimental import pallas as pl
from jax.experimental.pallas import tpu as pltpu
from jax.sharding import PartitionSpec as P

STEPS = 2
ITERS = 3

ALPHA_T = 0.8
BETA_S = 0.6
PRESS_K = 0.25
STEP_DT = 0.1
KAPPA = 0.1
VISCOSITY = 0.1
DRAG_K = 0.05
CORI_K = 1.0
SURF_C = 4.0
DIV_K = 0.5
GRAV_K = 0.5

ADV = STEP_DT * 0.5
DIV = DIV_K * 0.5
GRAV = GRAV_K * 0.5

WIDE = 10
TOP = 24
CHUNK = 16
CHUNK_2D = 8
CHUNK_3D = 32
LANE = 128
PER_GROUP = 11
PAIRS = [(a, b) for a in range(4) for b in range(a, 4)]
SUMS = 6 + 6 * len(PAIRS)
VMEM_LIMIT = 24 * 1024 * 1024
WHOLE_VMEM = 60 * 1024 * 1024


def rim_place(plane):
    group, place = divmod(plane, PER_GROUP)
    if place < 6:
        return group, 0, (2 * place + 1) * WIDE
    return group, 1, (2 * (place - 6) + 2) * WIDE


def groups_of(planes):
    return -(-planes // PER_GROUP)


def lanes_like(shape):
    return lax.broadcasted_iota(jnp.int32, shape, len(shape) - 1)


def fetches(fields, planes_of, mask_to, sems, levels):
    members = fields[0].shape[0]
    per_member = []
    for m in range(members):
        parts = [(fields[f].at[m], planes_of(m, pl.ds(f * levels, levels))) for f in range(4)]
        parts.append((fields[4].at[m], planes_of(m, 4 * levels)))
        per_member.append([pltpu.make_async_copy(*part, sems.at[m, i]) for i, part in enumerate(parts)])
    mask_copy = pltpu.make_async_copy(fields[5], mask_to, sems.at[0, 5])
    mask_copy.start()
    for copies in per_member:
        for copy in copies:
            copy.start()
    mask_copy.wait()
    return per_member


def pack_kernel(levels, *refs):
    fields, (to_west, to_east, rows_first, rows_second), (held, mask, sems) = refs[:6], refs[6:10], refs[10:]
    members, _, rows, cols = held.shape
    planes = 4 * levels + 2
    copies = fetches(fields, lambda m, at: held.at[m, at], mask, sems, levels)
    lane = lanes_like((rows, LANE))
    even = lax.broadcasted_iota(jnp.int32, (WIDE, cols), 0) * 0 + lax.rem(lax.axis_index("gridy"), 2) == 0
    for m in range(members):
        for copy in copies[m]:
            copy.wait()
        west_parts = [None] * groups_of(planes)
        east_parts = [None] * groups_of(planes)
        for plane in range(planes):
            value = held[m, plane] if plane < planes - 1 else mask[...].astype(jnp.float32)
            group, _, start = rim_place(plane)
            both = jnp.where(lane < WIDE, value[:, :LANE], value[:, cols - LANE :])
            both = pltpu.roll(both, start, 1)
            is_west = (lane >= start) & (lane < start + WIDE)
            is_east = (lane >= start - WIDE) & (lane < start)
            zero = jnp.zeros_like(both)
            west_parts[group] = jnp.where(is_west, both, zero if west_parts[group] is None else west_parts[group])
            east_parts[group] = jnp.where(is_east, both, zero if east_parts[group] is None else east_parts[group])
            low, high = value[:WIDE], value[rows - WIDE :]
            rows_first[m, plane * WIDE : (plane + 1) * WIDE, :] = jnp.where(even, high, low)
            rows_second[m, plane * WIDE : (plane + 1) * WIDE, :] = jnp.where(even, low, high)
        for group in range(groups_of(planes)):
            where = slice(group * LANE, (group + 1) * LANE)
            to_west[m, :, where] = west_parts[group]
            to_east[m, :, where] = east_parts[group]


def whole(count):
    return [pl.BlockSpec(memory_space=pltpu.VMEM)] * count


def in_hbm(count):
    return [pl.BlockSpec(memory_space=pltpu.HBM)] * count


def in_smem(count):
    return [pl.BlockSpec(memory_space=pltpu.SMEM)] * count


def pack_rims(temp, salt, uvel, vvel, eta, mask):
    members, levels, rows, cols = temp.shape
    planes = 4 * levels + 2
    wide = groups_of(planes) * LANE
    row_pack = -(-planes * WIDE // 8) * 8
    side = jax.ShapeDtypeStruct((members, rows, wide), jnp.float32)
    line = jax.ShapeDtypeStruct((members, row_pack, cols), jnp.float32)
    return pl.pallas_call(
        functools.partial(pack_kernel, levels),
        out_shape=(side, side, line, line),
        in_specs=in_hbm(6),
        out_specs=tuple(whole(4)),
        scratch_shapes=[
            pltpu.VMEM((members, planes - 1, rows, cols), jnp.float32),
            pltpu.VMEM((rows, cols), jnp.int32),
            pltpu.SemaphoreType.DMA((members, 6)),
        ],
        compiler_params=pltpu.CompilerParams(vmem_limit_bytes=WHOLE_VMEM),
        name="pack_rims",
    )(temp, salt, uvel, vvel, eta, mask)


def east_west(value):
    width = value.shape[-1]
    return pltpu.roll(value, width - 1, 1), pltpu.roll(value, 1, 1)


def chunks(first, last, size=CHUNK_2D):
    return [(a, min(a + size, last)) for a in range(first, last, size)]


def assemble(ext, fields, rims, m, levels, total_rows):
    from_east, from_west, rows_first, rows_second, sides_first, sides_second = rims
    planes = 4 * levels + 2
    rows, cols = fields[5].shape
    tile_row = lax.axis_index("gridy")
    odd_tile = lax.rem(tile_row, 2).astype(jnp.float32)
    keep_south = jnp.where(tile_row > 0, 1.0, 0.0).astype(jnp.float32)
    keep_north = jnp.where(tile_row * rows + rows < total_rows, 1.0, 0.0).astype(jnp.float32)
    north_factors = keep_north * (1.0 - odd_tile), keep_north * odd_tile
    south_factors = keep_south * odd_tile, keep_south * (1.0 - odd_tile)

    def of_north(first, second):
        return north_factors[0] * first + north_factors[1] * second

    def of_south(first, second):
        return south_factors[0] * first + south_factors[1] * second

    wide = groups_of(planes) * LANE
    for group in range(groups_of(planes)):
        where = slice(group * LANE, (group + 1) * LANE)
        where_west = slice(wide + group * LANE, wide + (group + 1) * LANE)
        east = sides_first[m, :, where], sides_second[m, :, where]
        west = sides_first[m, :, where_west], sides_second[m, :, where_west]
        bands = [(TOP - CHUNK, of_south(*east), of_south(*west))]
        for a in range(0, rows, CHUNK):
            bands.append((TOP + a, from_east[m, a : a + CHUNK, where], from_west[m, a : a + CHUNK, where]))
        bands.append((TOP + rows, of_north(*east), of_north(*west)))
        for at, east, west in bands:
            odd = ((lanes_like(east.shape) // WIDE) & 1) == 1
            joined = (jnp.where(odd, east, west), jnp.where(odd, west, east))
            for plane in range(group * PER_GROUP, min((group + 1) * PER_GROUP, planes)):
                _, kind, offset = rim_place(plane)
                ext[plane, at : at + CHUNK, cols : cols + LANE] = pltpu.roll(joined[kind], LANE - offset, 1)
    for plane in range(planes):
        if plane < 4 * levels:
            value = fields[plane // levels][m, plane % levels]
        else:
            value = fields[4][m] if plane == 4 * levels else fields[5][...].astype(jnp.float32)
        ext[plane, TOP : TOP + rows, :cols] = value
        at = slice(plane * WIDE, (plane + 1) * WIDE)
        ext[plane, TOP - WIDE : TOP, :cols] = of_south(rows_first[m, at, :], rows_second[m, at, :])
        ext[plane, TOP + rows : TOP + rows + WIDE, :cols] = of_north(rows_first[m, at, :], rows_second[m, at, :])


def fill_rows(turn, inside, first_row, total_rows):
    shape = (CHUNK, turn.shape[1])
    for a in range(0, turn.shape[0], CHUNK):
        row = first_row + (a - TOP) + lax.broadcasted_iota(jnp.int32, shape, 0)
        latitude = row.astype(jnp.float32) + 0.5
        turn[a : a + CHUNK, :] = STEP_DT * CORI_K * (2.0 * latitude / total_rows - 1.0)
        inside[a : a + CHUNK, :] = jnp.where((row >= 0) & (row < total_rows), 1.0, 0.0)


KEPT = ["tu", "tv", "q", "v0", "v1", "v2"]
KEEP_FLOW = 1.0 - STEP_DT * DRAG_K - 4.0 * VISCOSITY
KEEP_TRACER = 1.0 - 4.0 * KAPPA
PRESS_SCALE = PRESS_K * 0.5 * STEP_DT


class Planes:
    def __init__(self, levels, rows, turn, inside):
        self.levels, self.rows, self.turn, self.inside = levels, rows, turn, inside
        self.views = {}

    def add(self, ref, names, lead=()):
        for i, name in enumerate(names):
            self.views[name] = ref.at[lead + (i,)]

    def get(self, name, a, b):
        return self.views[name][a:b, :]

    def put(self, name, a, b, value):
        self.views[name][a:b, :] = value

    def sides(self, name, a, b):
        here = self.get(name, a, b)
        east, west = east_west(here)
        return here, east, west, self.get(name, a + 1, b + 1), self.get(name, a - 1, b - 1)

    def slopes(self, name, a, b):
        _, east, west, north, south = self.sides(name, a, b)
        return east - west, north - south

    def around(self, name, a, b):
        here, east, west, north, south = self.sides(name, a, b)
        return here, (east + west) + (north + south)

    def main(self):
        return chunks(TOP, TOP + self.rows)

    def near(self):
        return [(TOP - 8, TOP)] + self.main() + [(TOP + self.rows, TOP + self.rows + 8)]

    def masked(self, a, b, value):
        if a >= TOP and b <= TOP + self.rows:
            return value
        return self.inside[a:b, :] * value

    def divergence(self, u_name, v_name, a, b):
        east, west = east_west(self.get(u_name, a, b))
        return DIV * ((east - west) + (self.get(v_name, a + 1, b + 1) - self.get(v_name, a - 1, b - 1)))

    def flow(self, u_name, v_name, press, out_u, out_v, a, b):
        ocean, turn = self.get("ocean", a, b), self.turn[a:b, :]
        u, around_u = self.around(u_name, a, b)
        v, around_v = self.around(v_name, a, b)
        push_u, push_v = turn * v, turn * u
        if press:
            slope_x, slope_y = self.slopes(press, a, b)
            push_u, push_v = push_u - slope_x, push_v + slope_y
        self.put(out_u, a, b, ocean * ((KEEP_FLOW * u + VISCOSITY * around_u) + push_u))
        self.put(out_v, a, b, ocean * ((KEEP_FLOW * v + VISCOSITY * around_v) - push_v))

    def powers(self, first, second, third):
        for a, b in self.near():
            self.put(second, a, b, self.masked(a, b, self.around(first, a, b)[1]))
        for a, b in self.near():
            value = self.around(second, a, b)[1] - 4.0 * self.get(first, a, b)
            self.put(third, a, b, self.masked(a, b, value))

    def next_right_side(self, u_name, v_name, eta_name, press, out_name):
        for a, b in self.near():
            self.flow(u_name, v_name, press, "t2u", "t2v", a, b)
        for a, b in self.near():
            div = self.divergence("t2u", "t2v", a, b)
            value = self.get(eta_name, a, b) - div if eta_name else -div
            self.put(out_name, a, b, self.masked(a, b, value))


def scaled(factor, value):
    return value if factor == 1.0 else factor * value


def surface_start(ext, work):
    levels = work.levels
    low, high = TOP - CHUNK, TOP + work.rows + CHUNK
    for a, b in chunks(low, high):
        su = sv = sp = None
        for l in range(levels):
            factor = PRESS_SCALE * (levels - l)
            dens = (factor * BETA_S) * ext[levels + l, a:b, :] - (factor * ALPHA_T) * ext[l, a:b, :]
            work.put("d%d" % l, a, b, dens)
            u, v = ext[2 * levels + l, a:b, :], ext[3 * levels + l, a:b, :]
            su, sv, sp = (u, v, dens) if l == 0 else (su + u, sv + v, sp + dens)
        work.put("su", a, b, su)
        work.put("sv", a, b, sv)
        work.put("sp", a, b, sp)
    for a, b in work.near():
        carried = None
        for l in range(levels):
            slope_x, slope_y = work.slopes("d%d" % l, a, b)
            term = ext[2 * levels + l, a:b, :] * slope_x + ext[3 * levels + l, a:b, :] * slope_y
            carried = term if l == 0 else carried + term
        here, around = work.around("sp", a, b)
        work.put("q", a, b, work.get("ocean", a, b) * ((KEEP_TRACER * here + KAPPA * around) - ADV * carried))
    for a, b in chunks(low, high):
        work.flow("su", "sv", "sp", "tu", "tv", a, b)
    for a, b in work.near():
        work.put("v0", a, b, work.masked(a, b, work.get("eta", a, b) - work.divergence("tu", "tv", a, b)))


SUM_NAMES = ["su", "sv", "sp", "v3", "pu", "pv", "t2u", "t2v"] + ["w%d_%d" % (i, k) for i in range(4) for k in range(4)]


def whether(*conditions):
    result = jnp.int32(0)
    for condition in conditions:
        result = jnp.where(condition, 1, result)
    return result


def choose(source, theirs, side, members, info):
    mine, away = side * members, (1 - side) * members
    sent = [whether(*[theirs[slot] == mine + m for slot in range(members)]) for m in range(2)]
    here = [whether(*[source[slot] == away + m for slot in range(members)]) for m in range(2)]
    first_sent, first_here = 1 - sent[0], 1 - here[0]
    for slot in range(members):
        own = jnp.where(source[slot] - mine == first_sent, 0, 1)
        far = jnp.where(source[slot] - away == first_here, 2, 3)
        info[slot] = jnp.where((source[slot] >= mine) & (source[slot] < mine + members), own, far)
    info[members] = jnp.maximum(sent[0] * sent[1], here[0] * here[1])
    info[members + 1] = jnp.int32(1)
    info[members + 2] = first_sent


def sums_kernel(levels, total_rows, source, theirs, *refs):
    fields, rims, out, kept, info = refs[:6], refs[6:12], refs[12], refs[13], refs[14]
    planes, turn, inside, red = refs[15:]
    members = kept.shape[0]
    rows, cols = fields[5].shape
    tile_row = lax.axis_index("gridy")
    choose(source, theirs, lax.axis_index("member"), members, info)
    fill_rows(turn, inside, tile_row * rows, total_rows)
    red[...] = jnp.zeros_like(red)

    def one(m, carry):
        ext = kept.at[m]
        assemble(ext, fields, rims, m, levels, total_rows)
        work = Planes(levels, rows, turn, inside)
        work.add(planes, SUM_NAMES + ["d%d" % l for l in range(levels)])
        work.add(kept, ["ext%d" % i for i in range(4 * levels)] + ["eta", "ocean"] + KEPT, (m,))
        surface_start(ext, work)
        work.powers("v0", "v1", "v2")
        for a, b in work.main():
            work.put("v3", a, b, work.around("v2", a, b)[1])
        work.next_right_side("tu", "tv", None, "q", "w0_0")
        for k in range(1, 4):
            name = "v%d" % (k - 1)
            for a, b in work.near():
                ocean = work.get("ocean", a, b)
                slope_x, slope_y = work.slopes(name, a, b)
                work.put("pu", a, b, scaled(-levels * GRAV, ocean * slope_x))
                work.put("pv", a, b, scaled(-levels * GRAV, ocean * slope_y))
            work.next_right_side("pu", "pv", name, None, "w0_%d" % k)
        for k in range(4):
            work.powers("w0_%d" % k, "w1_%d" % k, "w2_%d" % k)
            for a, b in work.main():
                work.put("w3_%d" % k, a, b, work.around("w2_%d" % k, a, b)[1])

        def put_sums(at, first, second, pairs):
            totals = [None] * len(pairs)
            for a in range(TOP, TOP + rows, 8):
                xs = [work.get(name, a, a + 8)[:, :cols] for name in first]
                ys = [work.get(name, a, a + 8)[:, :cols] for name in second]
                for p, (i, j) in enumerate(pairs):
                    term = xs[i] * ys[j]
                    totals[p] = term if totals[p] is None else totals[p] + term
            for p, total in enumerate(totals):
                folded = total[:, :LANE]
                for c in range(LANE, cols, LANE):
                    folded = folded + total[:, c : c + LANE]
                red[m, at + p : at + p + 1, :] = jnp.sum(folded, axis=0, keepdims=True)

        for i in range(6):
            low, high = i // 2, i - i // 2
            put_sums(i, ["v%d" % low], ["v%d" % high], [(0, 0)])
            names = [["w%d_%d" % (which, k) for k in range(4)] for which in (low, high)]
            put_sums(6 + i * len(PAIRS), names[0], names[1], PAIRS)
        return carry

    for m in range(members):
        one(m, 0)
    for m in range(members):
        out[m : m + 1, :] = jnp.sum(jnp.transpose(red[m]), axis=0, keepdims=True)


def plane_shape(rows, cols):
    return (2 * TOP + rows, cols + LANE)


def local_sums(source, theirs, fields, rims, total_rows):
    members, levels, rows, cols = fields[0].shape
    assert SUMS <= LANE and members <= 8
    shape = plane_shape(rows, cols)
    kept = (members, 4 * levels + 2 + len(KEPT)) + shape
    return pl.pallas_call(
        functools.partial(sums_kernel, levels, total_rows),
        out_shape=(
            jax.ShapeDtypeStruct((members, LANE), jnp.float32),
            jax.ShapeDtypeStruct(kept, jnp.float32),
            jax.ShapeDtypeStruct((members + 3,), jnp.int32),
        ),
        in_specs=in_smem(2) + whole(12),
        out_specs=tuple(whole(2) + in_smem(1)),
        scratch_shapes=[
            pltpu.VMEM((len(SUM_NAMES) + levels,) + shape, jnp.float32),
            pltpu.VMEM(shape, jnp.float32),
            pltpu.VMEM(shape, jnp.float32),
            pltpu.VMEM((members, LANE, LANE), jnp.float32),
        ],
        compiler_params=pltpu.CompilerParams(vmem_limit_bytes=VMEM_LIMIT),
        cost_estimate=pl.CostEstimate(flops=10**8, bytes_accessed=4 * 10**6, transcendentals=0),
        name="local_sums",
    )(source, theirs, *fields, *rims)


def krylov(moment):
    n00, n01, n11, n12, n22, x22 = moment
    n02 = n11 - 4.0 * n00
    main, near = 1.0 + 4.0 * SURF_C, SURF_C
    g00 = main * n00 - near * n01
    g01 = main * n01 - near * n11
    g02 = main * n02 - near * n12
    g11 = main * n11 - near * (n12 + 4.0 * n01)
    g12 = main * n12 - near * (n22 + 4.0 * n02)
    g22 = main * n22 - near * x22
    l1, l2 = g01 / g00, g02 / g00
    d1 = g11 - l1 * g01
    d1 = jnp.where(d1 > 3e-7 * g11, d1, jnp.inf)
    e = g12 - l1 * g02
    l12 = e / d1
    d2 = g22 - l2 * g02 - l12 * e
    d2 = jnp.where(d2 > 3e-7 * g22, d2, jnp.inf)
    z0 = n00
    z1 = n01 - l1 * z0
    z2 = n02 - l2 * z0 - l12 * z1
    y2 = z2 / d2
    y1 = z1 / d1 - l12 * y2
    y0 = z0 / g00 - l1 * y1 - l2 * y2
    return [y0, y1, y2]


def weights(read):
    first = krylov([read(i) for i in range(6)])
    lifted = [None] + first
    second = []
    for i in range(6):
        total = None
        for p, (a, b) in enumerate(PAIRS):
            term = read(6 + i * len(PAIRS) + p)
            for k in (a, b):
                if k:
                    term = term * lifted[k]
            if a != b:
                term = 2.0 * term
            total = term if total is None else total + term
        second.append(total)
    return first, krylov(second)


RUN_NAMES = ["pu", "pv", "t2u", "t2v", "eta1", "w0", "w1", "w2", "eta2", "p", "p2", "gu1", "gv1", "gu2", "gv2"]


def advance_kernel(levels, total_rows, is_first, *refs):
    if is_first:
        info, tiles, kept, out, zonal = refs[:5]
        scratch = refs[5:]
    else:
        info, tiles, kept, zonal_before, out, spread = refs[:6]
        scratch = refs[6:]
    planes, after, turn, inside, staged, sums, sem = scratch[:7]
    rows, cols = out.shape[1:]
    members = kept.shape[0]
    tile_row = lax.axis_index("gridy")
    total = tiles[0]
    for i in range(1, tiles.shape[0]):
        total = total + tiles[i]
    staged[0:members, :] = total
    copy = pltpu.make_async_copy(staged, sums, sem)
    copy.start()
    fill_rows(turn, inside, tile_row * rows, total_rows)
    if not is_first:
        zonal = scratch[7]
    zonal[...] = jnp.zeros_like(zonal) if is_first else zonal_before[...]
    copy.wait()
    member = info[members + 2] if is_first else 1 - info[members + 2]
    ext = kept.at[member]
    work = Planes(levels, rows, turn, inside)
    work.add(planes, RUN_NAMES)
    work.add(kept, ["ext%d" % i for i in range(4 * levels)] + ["eta", "ocean"] + KEPT, (member,))

    def read(i):
        return jnp.full((1, 1), sums[member, i], jnp.float32)

    def combine(factors, names, out_name):
        for a, b in work.near():
            value = None
            for factor, name in zip(factors, names):
                term = factor * work.get(name, a, b)
                value = term if value is None else value + term
            work.put(out_name, a, b, value)

    first, second = weights(read)
    combine(first, ("v0", "v1", "v2"), "eta1")
    for a, b in work.near():
        ocean = work.get("ocean", a, b)
        slope_x, slope_y = work.slopes("eta1", a, b)
        slope_x, slope_y = GRAV * ocean * slope_x, GRAV * ocean * slope_y
        work.put("gu1", a, b, slope_x)
        work.put("gv1", a, b, slope_y)
        work.put("pu", a, b, work.get("tu", a, b) - levels * slope_x)
        work.put("pv", a, b, work.get("tv", a, b) - levels * slope_y)
    work.next_right_side("pu", "pv", "eta1", "q", "w0")
    work.powers("w0", "w1", "w2")
    combine(second, ("w0", "w1", "w2"), "eta2")
    for a, b in work.main():
        ocean = work.get("ocean", a, b)
        slope_x, slope_y = work.slopes("eta2", a, b)
        work.put("gu2", a, b, GRAV * ocean * slope_x)
        work.put("gv2", a, b, GRAV * ocean * slope_y)
        out[4 * levels, a - TOP : b - TOP, :] = work.get("eta2", a, b)[:, :cols]
    low, high = TOP - 8, TOP + rows + 8
    for a, b in chunks(TOP - CHUNK, TOP + rows + CHUNK):
        work.put("p", a, b, jnp.zeros((b - a, cols + LANE), jnp.float32))
        work.put("p2", a, b, jnp.zeros((b - a, cols + LANE), jnp.float32))

    def step(ref, l, press, a, b, width):
        def of(view):
            here = view[a:b, :]
            east, west = east_west(here)
            return here[:, :width], east[:, :width], west[:, :width], view[a + 1 : b + 1, :width], view[a - 1 : b - 1, :width]

        ocean = work.views["ocean"][a:b, :width]
        coriolis = turn[a:b, :width]
        u, east, west, north, south = of(ref.at[2 * levels + l])
        around_u = (east + west) + (north + south)
        v, east, west, north, south = of(ref.at[3 * levels + l])
        around_v = (east + west) + (north + south)
        _, east, west, north, south = of(work.views[press])
        new_u = ocean * ((KEEP_FLOW * u + VISCOSITY * around_u) + (coriolis * v - (east - west)))
        new_v = ocean * ((KEEP_FLOW * v + VISCOSITY * around_v) - (coriolis * u + (north - south)))
        flow_u, flow_v = ADV * u, ADV * v
        results = []
        for at in (l, levels + l):
            here, east, west, north, south = of(ref.at[at])
            carried = flow_u * (east - west) + flow_v * (north - south)
            spread = KEEP_TRACER * here + KAPPA * ((east + west) + (north + south))
            results.append(ocean * (spread - carried))
        return results[0], results[1], new_u, new_v

    def add_press(ref, l, press, a, b):
        dens = (PRESS_SCALE * BETA_S) * ref[levels + l, a:b, :] - (PRESS_SCALE * ALPHA_T) * ref[l, a:b, :]
        work.put(press, a, b, work.get(press, a, b) + dens)

    def level(l, carry):
        for a, b in chunks(TOP - CHUNK, TOP + rows + CHUNK, CHUNK_3D):
            add_press(ext, l, "p", a, b)
        for a, b in chunks(low, high, CHUNK_3D):
            temp, salt, u, v = step(ext, l, "p", a, b, cols + LANE)
            after[l, a:b, :] = temp
            after[levels + l, a:b, :] = salt
            after[2 * levels + l, a:b, :] = u - work.get("gu1", a, b)
            after[3 * levels + l, a:b, :] = v - work.get("gv1", a, b)
        for a, b in chunks(low, high, CHUNK_3D):
            add_press(after, l, "p2", a, b)
        for a, b in chunks(TOP, TOP + rows, CHUNK_3D):
            temp, salt, u, v = step(after, l, "p2", a, b, cols)
            here = slice(a - TOP, b - TOP)
            v = v - work.get("gv2", a, b)[:, :cols]
            out[l, here, :] = temp
            out[levels + l, here, :] = salt
            out[2 * levels + l, here, :] = u - work.get("gu2", a, b)[:, :cols]
            out[3 * levels + l, here, :] = v
            row_sum = jnp.sum(v, axis=1, keepdims=True)
            zonal[here, :] = jnp.where(lanes_like((b - a, LANE)) == member * levels + l, row_sum, zonal[here, :])
        return carry

    for l in range(levels):
        level(l, 0)
    if not is_first:
        square = jnp.concatenate([zonal[...]] + [jnp.zeros_like(zonal)] * (LANE // rows - 1), axis=0)
        turned = jnp.transpose(square)[: members * levels]
        line = turned[:levels]
        for m in range(1, members):
            line = line + pltpu.roll(turned, m * rows, 1)[m * levels : (m + 1) * levels]
        for i in range(spread.shape[0]):
            spread[i] = line


def advance(is_first, info, tiles, kept, zonal, rows, cols, total_rows):
    members, planes = kept.shape[:2]
    levels = (planes - 2 - len(KEPT)) // 4
    assert members * rows == LANE and members * levels == 8
    shape = plane_shape(rows, cols)
    zonal_shape = jax.ShapeDtypeStruct((rows, LANE), jnp.float32)
    out_shape = [jax.ShapeDtypeStruct((4 * levels + 1, rows, cols), jnp.float32)]
    if is_first:
        out_shape += [zonal_shape]
    else:
        out_shape += [jax.ShapeDtypeStruct((tiles.shape[0], levels, members * rows), jnp.float32)]
    return pl.pallas_call(
        functools.partial(advance_kernel, levels, total_rows, is_first),
        out_shape=tuple(out_shape),
        in_specs=in_smem(1) + whole(2 if is_first else 3),
        out_specs=tuple(whole(2)),
        scratch_shapes=[
            pltpu.VMEM((len(RUN_NAMES),) + shape, jnp.float32),
            pltpu.VMEM((4 * levels,) + shape, jnp.float32),
            pltpu.VMEM(shape, jnp.float32),
            pltpu.VMEM(shape, jnp.float32),
            pltpu.VMEM((8, LANE), jnp.float32),
            pltpu.SMEM((8, LANE), jnp.float32),
            pltpu.SemaphoreType.DMA,
        ]
        + ([] if is_first else [pltpu.VMEM((rows, LANE), jnp.float32)]),
        compiler_params=pltpu.CompilerParams(vmem_limit_bytes=VMEM_LIMIT),
        cost_estimate=pl.CostEstimate(flops=10**8, bytes_accessed=4 * 10**6, transcendentals=0),
        name="advance",
    )(info, tiles, kept, *([] if is_first else [zonal]))


def finish_kernel(count_y, count_x, total_cols, spread, overturn, score, held):
    members, levels, rows = overturn.shape
    total_rows = rows * count_y
    lane = lanes_like(spread.shape[1:])
    member_of = lane // rows
    weighted = None
    for y in range(count_y):
        total = spread[y * count_x]
        for x in range(1, count_x):
            total = total + spread[y * count_x + x]
        lines = [total[0:1]]
        for l in range(1, levels):
            lines.append(lines[-1] + total[l : l + 1])
        lines = jnp.concatenate(lines, axis=0) * (total_cols**-0.5)
        held[y] = lines
        latitude = ((lane - member_of * rows + y * rows).astype(jnp.float32) + 0.5) * (1.0 / total_rows)
        weighted = lines * latitude if weighted is None else weighted + lines * latitude
    mine = held[lax.axis_index("gridy")]
    for m in range(members):
        overturn[m] = mine[:, m * rows : (m + 1) * rows]
        score[m] = jnp.sum(jnp.where(member_of == m, weighted, 0.0)) * ((levels * total_rows) ** -0.5)


def finish(spread, members, rows, count_y, count_x, cols):
    levels = spread.shape[1]
    return pl.pallas_call(
        functools.partial(finish_kernel, count_y, count_x, cols * count_x),
        out_shape=(
            jax.ShapeDtypeStruct((members, levels, rows), jnp.float32),
            jax.ShapeDtypeStruct((members,), jnp.float32),
        ),
        in_specs=whole(1),
        out_specs=(whole(1)[0], in_smem(1)[0]),
        scratch_shapes=[pltpu.VMEM((count_y,) + spread.shape[1:], jnp.float32)],
        compiler_params=pltpu.CompilerParams(vmem_limit_bytes=VMEM_LIMIT),
        name="finish",
    )(spread)


def pick_kernel(levels, choice, source, score, their_score, *refs):
    count = len(refs) - 7
    sources, outs, weight, sem = refs[:count], refs[count : count + 5], refs[count + 5], refs[count + 6]
    slots = outs[0].shape[0]

    def parts(s, source):
        for f in range(4):
            yield source.at[pl.ds(f * levels, levels)], outs[f].at[s]
        yield source.at[4 * levels], outs[4].at[s]

    for s in range(slots):
        for k in range(count):

            @pl.when(choice[s] == k)
            def _():
                for i, (one, target) in enumerate(parts(s, sources[k])):
                    pltpu.make_async_copy(one, target, sem.at[s, i]).start()

    side = lax.axis_index("member")
    mean = (sum(score[m] for m in range(slots)) + sum(their_score[m] for m in range(slots))) * (0.5 / slots)
    for s in range(slots):
        value = jnp.float32(0.0)
        for m in range(slots):
            value = jnp.where(source[s] == side * slots + m, score[m], value)
            value = jnp.where(source[s] == (1 - side) * slots + m, their_score[m], value)
        weight[s] = value - mean
    for s in range(slots):
        for i, (one, target) in enumerate(parts(s, sources[0])):
            pltpu.make_async_copy(one, target, sem.at[s, i]).wait()


def pick(choice, source, score, their_score, sources, slots, levels):
    _, rows, cols = sources[0].shape
    volume = jax.ShapeDtypeStruct((slots, levels, rows, cols), jnp.float32)
    surface = jax.ShapeDtypeStruct((slots, rows, cols), jnp.float32)
    return pl.pallas_call(
        functools.partial(pick_kernel, levels),
        out_shape=(volume,) * 4 + (surface, jax.ShapeDtypeStruct((slots,), jnp.float32)),
        in_specs=in_smem(4) + whole(len(sources)),
        out_specs=tuple(in_hbm(5) + in_smem(1)),
        scratch_shapes=[pltpu.SemaphoreType.DMA((slots, 5))],
        compiler_params=pltpu.CompilerParams(vmem_limit_bytes=VMEM_LIMIT),
        name="pick",
    )(choice, source, score, their_score, *sources)


def shift(value, axis, by):
    count = lax.axis_size(axis)
    return lax.ppermute(value, axis, [(i, (i + by) % count) for i in range(count)])


def exchange_rims(packed, clone_source):
    to_west, to_east, rows_first, rows_second = packed
    rows = to_west.shape[1]
    count = lax.axis_size("gridy")
    assert count % 2 == 0
    partners = [i ^ 1 for i in range(count)], [min(max(i - 1 + 2 * (i % 2), 0), count - 1) for i in range(count)]

    def pair(value, which):
        return lax.ppermute(value, "gridy", list(enumerate(partners[which])))

    from_east, from_west = shift(to_west, "gridx", -1), shift(to_east, "gridx", 1)
    rows_first, rows_second = pair(rows_first, 0), pair(rows_second, 1)
    low = jnp.concatenate([from_east[:, :CHUNK], from_west[:, :CHUNK]], axis=2)
    high = jnp.concatenate([from_east[:, rows - CHUNK :], from_west[:, rows - CHUNK :]], axis=2)
    low, high, their_source = lax.optimization_barrier((low, high, swap(clone_source)))
    even = lax.axis_index("gridy") % 2 == 0
    sides_first = pair(jnp.where(even, high, low), 0)
    sides_second = pair(jnp.where(even, low, high), 1)
    return (from_east, from_west, rows_first, rows_second, sides_first, sides_second), their_source


def from_all(tiles, axes):
    return lax.all_to_all(tiles, axes, split_axis=0, concat_axis=0, tiled=True)


def swap(value):
    return lax.ppermute(value, "member", [(0, 1), (1, 0)])


def shards(temp, salt, uvel, vvel, eta, land_mask, clone_source):
    members, levels, rows, cols = temp.shape
    assert members == 2 and lax.axis_size("member") == 2
    count_y, count_x = lax.axis_size("gridy"), lax.axis_size("gridx")
    total_rows = rows * count_y
    grid = ("gridy", "gridx")

    fields = (temp, salt, uvel, vvel, eta, land_mask)
    rims, their_source = exchange_rims(pack_rims(*fields), clone_source)
    tile, kept, info = local_sums(clone_source, their_source, fields, rims, total_rows)
    tiles = from_all(jnp.broadcast_to(tile[None], (count_y * count_x,) + tile.shape), grid)

    sent, zonal = advance(True, info, tiles, kept, None, rows, cols, total_rows)
    arrived = swap(sent)

    def rest():
        other, spread = advance(False, info, tiles, kept, zonal, rows, cols, total_rows)
        return (other, *finish(from_all(spread, grid), members, rows, count_y, count_x, cols))

    def nothing():
        return jnp.zeros_like(sent), jnp.zeros((members, levels, rows), jnp.float32), jnp.zeros((members,), jnp.float32)

    other, overturn, score = lax.cond(info[members + 1] != 0, rest, nothing)
    their_score = swap(score)

    def with_second():
        sources = (sent, other, arrived, swap(other))
        return pick(info, clone_source, score, their_score, sources, members, levels)

    def without_second():
        return pick(info, clone_source, score, their_score, (sent, other, arrived), members, levels)

    *picked, clone_weight = lax.cond(info[members] != 0, with_second, without_second)
    return (*picked, overturn, clone_weight)


def solution(mesh):
    volume = P("member", None, "gridy", "gridx")
    in_specs = (volume,) * 4 + (P("member", "gridy", "gridx"), P("gridy", "gridx"), P("member"))
    out_specs = (volume,) * 4 + (P("member", "gridy", "gridx"), P("member", None, "gridy"), P("member"))
    return jax.shard_map(shards, mesh=mesh, in_specs=in_specs, out_specs=out_specs, check_vma=False)
```
